32 devices in a mesh: samp: 2 (over y), row: 2 (over x), col: 8 (over z, core).
Axes of the slice: x: 2, y: 2, z: 4, core: 2. Of those that a mesh axis runs over, the one named last changes fastest.
Arguments:
- tokens: bfloat16 [8, 512, 768], P('samp', 'col'), may hold values from -110 to 110
- restype: int32 [512], P('col'), may hold values from 0 to 31
- type_table: bfloat16 [32, 768], replicated, may hold values from -8 to 8
- key_mask: int32 [512], P('col'), may hold values 0 or 1
- pair: bfloat16 [512, 512, 128], P('row', 'col'), may hold values from -160 to 160
- w_bias: bfloat16 [128, 16], replicated, may hold values from -0.5 to 0.5
- w_query: bfloat16 [768, 768], replicated, may hold values from -2 to 2
- w_key: bfloat16 [768, 768], replicated, may hold values from -2 to 2
- w_value: bfloat16 [768, 768], replicated, may hold values from -0.21875 to 0.21875
- w_gate: bfloat16 [768, 768], replicated, may hold values from -0.21875 to 0.21875
- cotangent: bfloat16 [8, 512, 768], P('samp', 'col'), may hold values from -6 to 6
Outputs:
- token_grad: bfloat16 [8, 512, 768], P('samp', 'col')
- pair_grad: bfloat16 [512, 512, 128], P('row', 'col')
- bias_weight_grad: float32 [128, 16], replicated
The draws below stay inside these ranges and needn't reach their ends.
All inputs are finite; a program needn't handle non-finite values. No bound on the sum of `key_mask` on one device may be relied on, other than what follows from the above.
Results may differ from the reference program's by a relative error of at most 0.034.
The reference program's roundings to bfloat16 on the way count: a program that leaves them out, or rounds other values in their place, can miss the bound.
Values may be sent and summed in bfloat16 or wider, within the bound.
No kernel may reach another device: no remote copies, remote signals or barrier semaphores. Data moves between devices by JAX's collectives and lax.ppermute only.
A program may use at most 128 MiB of HBM per device.

```python
import math
import jax
import jax.numpy as jnp
from jax import lax

D = 768
H = 16
CH = 48
C = 128
NTYPE = 32
TOKENS = 512
SAMPLES = 8
N_ROW = 2


def shared_base(key):
    return jnp.clip(jax.random.normal(jax.random.fold_in(key, 21), (D, D), jnp.float32), -5.0, 5.0)


def draw_tokens(key, part):
    key = jax.random.fold_in(key, 11)
    first, second, third = jax.random.split(key, 3)
    channel_scale = jnp.exp(jax.random.uniform(second, (D,), jnp.float32) * math.log(10.0))
    token_scale = jnp.exp(jax.random.uniform(third, (SAMPLES, TOKENS, 1), jnp.float32) * math.log(2.0))
    base = jnp.clip(jax.random.normal(first, (SAMPLES, TOKENS, D), jnp.float32), -5.0, 5.0)
    return (base * channel_scale * token_scale).astype(jnp.bfloat16)


def draw_pair(key, part):
    key = jax.random.fold_in(key, 12)
    first, second, third = jax.random.split(key, 3)
    channel_scale = jnp.exp(jax.random.uniform(second, (C,), jnp.float32) * math.log(10.0))
    row_scale = jnp.exp(jax.random.uniform(third, (TOKENS, 1, 1), jnp.float32) * math.log(3.0))
    base = jnp.clip(jax.random.normal(first, (TOKENS, TOKENS, C), jnp.float32), -5.0, 5.0)
    return (base * channel_scale * row_scale).astype(jnp.bfloat16)


def draw_w_query(key, part):
    base = shared_base(key)
    return (base / math.sqrt(D)).astype(jnp.bfloat16)


def draw_w_key(key, part):
    key = jax.random.fold_in(key, 32)
    fresh = jnp.clip(jax.random.normal(key, (D, D), jnp.float32), -5.0, 5.0)
    return (fresh / math.sqrt(D)).astype(jnp.bfloat16)


def touch_ends(drawn, key, smallest, top_value):
    longest = drawn.shape.index(max(drawn.shape))
    spots = []
    for shift in (0, 1):
        where = [jax.random.randint(jax.random.fold_in(key, axis), (), 0, length) for axis, length in enumerate(drawn.shape)]
        where[longest] = (where[longest] + shift) % drawn.shape[longest]
        spots.append(tuple(where))
    return drawn.at[spots[0]].set(smallest).at[spots[1]].set(top_value)


def steps_of(key, shape, cuts, smallest, high):
    def one(dim, parts):
        draws = jax.random.uniform(jax.random.fold_in(jax.random.fold_in(key, 6), dim), (parts,), jnp.float32, smallest / len(cuts), high / len(cuts))
        return jnp.repeat(jnp.exp(draws), shape[dim] // parts).reshape((-1,) + (1,) * (len(shape) - dim - 1))

    level = one(*cuts[0])
    for cut in cuts[1:]:
        level = level * one(*cut)
    return level


def noise(key, dims, spread, reach, shards=(), kind=jnp.bfloat16):
    gain = steps_of(key, dims, shards, -0.22, 0.18) if shards else 1.0
    entries = jax.random.normal(key, dims, jnp.float32) * spread * gain
    return jnp.minimum(jnp.maximum(entries, -reach), reach).astype(kind)


def setup_inputs(seed: int = 0) -> dict:
    key_of = jax.random.split(jax.random.key(seed), 12)
    return {
        "tokens": draw_tokens(jax.random.fold_in(key_of[11], 71), 0),
        "restype": touch_ends(jax.random.randint(key_of[1], (TOKENS,), 0, NTYPE), jax.random.fold_in(key_of[1], 1), 0, NTYPE - 1).astype(jnp.int32),
        "type_table": noise(key_of[2], (NTYPE, D), 2.0, 8.0),
        "key_mask": touch_ends((jax.random.randint(key_of[3], (TOKENS,), 0, 8) < 7).astype(jnp.int32), jax.random.fold_in(key_of[3], 1), 0, 1),
        "pair": draw_pair(jax.random.fold_in(key_of[11], 71), 0),
        "w_bias": noise(key_of[5], (C, H), C ** -0.5, 0.5),
        "w_query": draw_w_query(jax.random.fold_in(key_of[11], 71), 0),
        "w_key": draw_w_key(jax.random.fold_in(key_of[11], 71), 0),
        "w_value": noise(key_of[8], (D, D), D ** -0.5, 0.21875),
        "w_gate": noise(key_of[9], (D, D), D ** -0.5, 0.21875),
        "cotangent": noise(key_of[10], (SAMPLES, TOKENS, D), 1.0, 6.0, ((0, 2), (1, 8))),
    }


def token_norm(tokens, restype, type_table):
    onehot = (restype[:, None] == jnp.arange(NTYPE, dtype=jnp.int32)[None, :]).astype(jnp.bfloat16)
    embedded = tokens.astype(jnp.float32) + jnp.dot(onehot, type_table, preferred_element_type=jnp.float32)
    centred = embedded - lax.optimization_barrier(jnp.mean(embedded, axis=-1, keepdims=True))
    inv_std = lax.rsqrt(lax.optimization_barrier(jnp.mean(centred * centred, axis=-1, keepdims=True)) + 1e-05)
    return (centred * inv_std, inv_std)

def pair_norm(block):
    values = block.astype(jnp.float32)
    centred = values - lax.optimization_barrier(jnp.mean(values, axis=-1, keepdims=True))
    inv_std = lax.rsqrt(lax.optimization_barrier(jnp.mean(centred * centred, axis=-1, keepdims=True)) + 1e-05)
    return (centred * inv_std, inv_std)

def norm_back(grad_in, normed, inv_std):
    return inv_std * (grad_in - lax.optimization_barrier(jnp.mean(grad_in, axis=-1, keepdims=True)) - normed * lax.optimization_barrier(jnp.mean(grad_in * normed, axis=-1, keepdims=True)))

def reference(tokens, restype, type_table, key_mask, pair, w_bias, w_query, w_key, w_value, w_gate, cotangent):
    normed, inv_std = token_norm(tokens, restype, type_table)
    act = normed.astype(jnp.bfloat16)
    bias_weight = w_bias.astype(jnp.float32)
    block_rows = TOKENS // N_ROW
    blocks = pair.reshape(N_ROW, block_rows, TOKENS, C)

    def block_bias(block):
        pair_normed, pair_inv = pair_norm(block)
        return jnp.einsum('ijc,ch->hij', pair_normed, bias_weight, precision=lax.Precision.HIGHEST)
    bias = lax.map(block_bias, blocks)
    bias = jnp.transpose(bias, (1, 0, 2, 3)).reshape(H, TOKENS, TOKENS)
    keep = key_mask == 1
    w_query_f = w_query.astype(jnp.float32)
    w_key_f = w_key.astype(jnp.float32)
    w_value_f = w_value.astype(jnp.float32)

    def one_sample(grad_bias, inputs):
        act_s, grad_s = inputs
        queries = jnp.dot(act_s, w_query, preferred_element_type=jnp.float32).astype(jnp.bfloat16)
        key_proj = jnp.dot(act_s, w_key, preferred_element_type=jnp.float32).astype(jnp.bfloat16)
        value_proj = jnp.dot(act_s, w_value, preferred_element_type=jnp.float32).astype(jnp.bfloat16)
        gate_lin = jnp.dot(act_s, w_gate, preferred_element_type=jnp.float32).astype(jnp.bfloat16)
        query_heads = queries.astype(jnp.float32).reshape(TOKENS, H, CH)
        key_heads = key_proj.astype(jnp.float32).reshape(TOKENS, H, CH)
        value_heads = value_proj.astype(jnp.float32).reshape(TOKENS, H, CH)
        scores = jnp.einsum('ihc,jhc->hij', query_heads, key_heads) / math.sqrt(CH) + bias
        scores = jnp.where(keep[None, None, :], scores, -1000000000.0)
        top = lax.optimization_barrier(jnp.max(scores, axis=-1, keepdims=True))
        expo = jnp.exp(scores - top)
        totals = lax.optimization_barrier(jnp.sum(expo, axis=-1))
        attended = jnp.einsum('hij,jhc->ihc', expo.astype(jnp.bfloat16).astype(jnp.float32), value_heads)
        attended = attended / jnp.transpose(totals)[:, :, None]
        flat_out = attended.reshape(TOKENS, D)
        sig_gate = jax.nn.sigmoid(gate_lin.astype(jnp.float32))
        grad_f = grad_s.astype(jnp.float32)
        grad_out = (grad_f * sig_gate).astype(jnp.bfloat16)
        grad_gate = (grad_f * flat_out * sig_gate * (1.0 - sig_gate)).astype(jnp.bfloat16)
        grad_heads = grad_out.astype(jnp.float32).reshape(TOKENS, H, CH)
        delta = jnp.transpose(lax.optimization_barrier(jnp.sum(grad_heads * attended, axis=-1)))
        probs = expo / totals[:, :, None]
        grad_pre = jnp.einsum('ihc,jhc->hij', grad_heads, value_heads)
        grad_scores = probs * (grad_pre - delta[:, :, None])
        rounded = grad_scores.astype(jnp.bfloat16).astype(jnp.float32)
        grad_query = (jnp.einsum('hij,jhc->ihc', rounded, key_heads) / math.sqrt(CH)).reshape(TOKENS, D)
        grad_key = (jnp.einsum('hij,ihc->jhc', rounded, query_heads) / math.sqrt(CH)).reshape(TOKENS, D)
        grad_value = jnp.einsum('hij,ihc->jhc', probs.astype(jnp.bfloat16).astype(jnp.float32), grad_heads).reshape(TOKENS, D)
        grad_act = jnp.dot(grad_query, w_query_f.T, precision=lax.Precision.HIGHEST)
        grad_act = grad_act + jnp.dot(grad_key, w_key_f.T, precision=lax.Precision.HIGHEST)
        grad_act = grad_act + jnp.dot(grad_value, w_value_f.T, precision=lax.Precision.HIGHEST)
        grad_act = grad_act + jnp.dot(grad_gate, w_gate.T, preferred_element_type=jnp.float32)
        return (grad_bias + grad_scores, grad_act)
    grad_bias, grad_act = lax.scan(one_sample, jnp.zeros((H, TOKENS, TOKENS), jnp.float32), (act, cotangent))
    token_grad = norm_back(grad_act, normed, inv_std).astype(jnp.bfloat16)
    bias_blocks = jnp.transpose(grad_bias.reshape(H, N_ROW, block_rows, TOKENS), (1, 0, 2, 3))

    def block_grads(inputs):
        block, grad_block = inputs
        pair_normed, pair_inv = pair_norm(block)
        grad_normed = jnp.einsum('hij,ch->ijc', grad_block, bias_weight, precision=lax.Precision.HIGHEST)
        grad_pair = norm_back(grad_normed, pair_normed, pair_inv)
        weight_part = jnp.einsum('ijc,hij->ch', pair_normed, grad_block, precision=lax.Precision.HIGHEST)
        return ((grad_pair * (TOKENS / SAMPLES)).astype(jnp.bfloat16), weight_part)
    pair_blocks, weight_parts = lax.map(block_grads, (blocks, bias_blocks))
    pair_grad = pair_blocks.reshape(TOKENS, TOKENS, C)
    bias_weight_grad = lax.optimization_barrier(jnp.sum(weight_parts, axis=0)) / SAMPLES
    return (token_grad, pair_grad, bias_weight_grad)
```

```python
import math

import jax
import jax.numpy as jnp
from jax import lax
from jax.experimental import pallas as pl
from jax.experimental.pallas import tpu as pltpu
from jax.sharding import PartitionSpec as P

D = 768
H = 16
CH = 48
NTYPE = 32


def broadcast(block, axis, source):
    block = jnp.where(lax.axis_index(axis) == source, block, jnp.zeros_like(block))
    return lax.psum(block, axis)


def token_norm(tokens, restype, type_table):
    onehot = (restype[:, None] == jnp.arange(NTYPE, dtype=jnp.int32)[None, :]).astype(jnp.bfloat16)
    embedded = tokens.astype(jnp.float32) + jnp.dot(
        onehot, type_table, preferred_element_type=jnp.float32
    )
    centred = embedded - jnp.mean(embedded, axis=-1, keepdims=True)
    inv_std = lax.rsqrt(jnp.mean(centred * centred, axis=-1, keepdims=True) + 1e-05)
    return (centred * inv_std, inv_std)


def pair_norm(block):
    values = block.astype(jnp.float32)
    centred = values - jnp.mean(values, axis=-1, keepdims=True)
    inv_std = lax.rsqrt(jnp.mean(centred * centred, axis=-1, keepdims=True) + 1e-05)
    return (centred * inv_std, inv_std)


def norm_back(grad_in, normed, inv_std):
    return inv_std * (
        grad_in
        - jnp.mean(grad_in, axis=-1, keepdims=True)
        - normed * jnp.mean(grad_in * normed, axis=-1, keepdims=True)
    )


def project(rows_in, weight):
    return jnp.einsum("std,de->ste", rows_in, weight, preferred_element_type=jnp.float32).astype(
        jnp.bfloat16
    )


def back_project(grads, weight):
    return jnp.einsum(
        "ste,de->std", grads, weight.astype(jnp.float32), precision=lax.Precision.HIGHEST
    )


def pair_back(grad_bias, pair_normed, pair_inv, bias_weight):
    grad_normed = jnp.einsum("hij,ch->ijc", grad_bias, bias_weight, precision=lax.Precision.HIGHEST)
    return norm_back(grad_normed, pair_normed, pair_inv)


def body_any(
    tokens, restype, type_table, key_mask, pair, w_bias, w_query, w_key, w_value, w_gate, cotangent
):
    n_row = lax.axis_size("row")
    n_col = lax.axis_size("col")
    n_samp = lax.axis_size("samp")
    samp_dev = tokens.shape[0]
    tok_col = tokens.shape[1]
    spread = n_col // n_row
    row_count = tok_col * spread
    total_tokens = tok_col * n_col
    row_index = lax.axis_index("row")
    col_index = lax.axis_index("col")
    is_owner = col_index // spread == row_index
    own_start = col_index % spread * tok_col
    normed, inv_std = token_norm(tokens, restype, type_table)
    own_act = normed.astype(jnp.bfloat16)
    key_proj = project(own_act, w_key)
    value_proj = project(own_act, w_value)
    stacked = jnp.stack([own_act, cotangent])
    pieces = [broadcast(stacked, "col", row_index * spread + member) for member in range(spread)]
    gathered = jnp.concatenate(pieces, axis=2)
    query_side = gathered[0]
    grad_rows = gathered[1]
    queries = project(query_side, w_query)
    gate_lin = project(query_side, w_gate)
    pair_normed, pair_inv = pair_norm(pair)
    bias_weight = w_bias.astype(jnp.float32)
    bias = jnp.einsum("ijc,ch->hij", pair_normed, bias_weight, precision=lax.Precision.HIGHEST)
    query_heads = queries.reshape(samp_dev, row_count, H, CH)
    key_heads = key_proj.reshape(samp_dev, tok_col, H, CH)
    value_heads = value_proj.reshape(samp_dev, tok_col, H, CH)
    scores = (
        jnp.einsum("sihc,sjhc->shij", query_heads, key_heads, preferred_element_type=jnp.float32)
        / math.sqrt(CH)
        + bias[None]
    )
    scores = jnp.where(key_mask[None, None, None, :] == 1, scores, -1000000000.0)
    top = lax.pmax(jnp.max(scores, axis=-1), "col")
    expo = jnp.exp(scores - top[..., None])
    partial_out = jnp.einsum(
        "shij,sjhc->sihc",
        expo.astype(jnp.bfloat16),
        value_heads,
        preferred_element_type=jnp.float32,
    )
    totals, summed = lax.psum(
        (jnp.sum(expo, axis=-1), partial_out.reshape(samp_dev, row_count, D)), "col"
    )
    attended = (
        summed.reshape(samp_dev, row_count, H, CH) / jnp.transpose(totals, (0, 2, 1))[..., None]
    )
    flat_out = attended.reshape(samp_dev, row_count, D)
    sig_gate = jax.nn.sigmoid(gate_lin.astype(jnp.float32))
    grad_f = grad_rows.astype(jnp.float32)
    grad_out = (grad_f * sig_gate).astype(jnp.bfloat16)
    grad_gate = (grad_f * flat_out * sig_gate * (1.0 - sig_gate)).astype(jnp.bfloat16)
    gate_piece = lax.dynamic_slice_in_dim(grad_gate, own_start, tok_col, 1)
    gate_term = jnp.where(
        is_owner,
        jnp.einsum("ste,de->std", gate_piece, w_gate, preferred_element_type=jnp.float32),
        0.0,
    )
    grad_heads = grad_out.reshape(samp_dev, row_count, H, CH)
    delta = jnp.transpose(jnp.sum(grad_heads.astype(jnp.float32) * attended, axis=-1), (0, 2, 1))
    probs = expo / totals[..., None]
    grad_pre = jnp.einsum(
        "sihc,sjhc->shij", grad_heads, value_heads, preferred_element_type=jnp.float32
    )
    grad_scores = probs * (grad_pre - delta[..., None])
    rounded = grad_scores.astype(jnp.bfloat16)
    grad_query = (
        jnp.einsum("shij,sjhc->sihc", rounded, key_heads, preferred_element_type=jnp.float32)
        / math.sqrt(CH)
    ).reshape(samp_dev, row_count, D)
    grad_key = (
        jnp.einsum("shij,sihc->sjhc", rounded, query_heads, preferred_element_type=jnp.float32)
        / math.sqrt(CH)
    ).reshape(samp_dev, tok_col, D)
    grad_value = jnp.einsum(
        "shij,sihc->sjhc",
        probs.astype(jnp.bfloat16),
        grad_heads,
        preferred_element_type=jnp.float32,
    ).reshape(samp_dev, tok_col, D)
    bias_local = jnp.sum(grad_scores, axis=0)
    blank = jnp.zeros((samp_dev, total_tokens, D), jnp.float32)
    mine = lax.psum_scatter(
        lax.dynamic_update_slice_in_dim(blank, grad_query, row_index * row_count, 1),
        "col",
        scatter_dimension=1,
        tiled=True,
    )
    query_all, key_all, value_all, gate_all = lax.psum(
        (mine, grad_key, grad_value, gate_term), "row"
    )
    grad_act = (
        back_project(query_all, w_query)
        + back_project(key_all, w_key)
        + back_project(value_all, w_value)
        + gate_all
    )
    token_grad = norm_back(grad_act, normed, inv_std).astype(jnp.bfloat16)
    samples = samp_dev * n_samp
    grad_bias = lax.psum(bias_local, "samp")
    grad_pair = pair_back(grad_bias, pair_normed, pair_inv, bias_weight)
    pair_grad = (grad_pair * (total_tokens / samples)).astype(jnp.bfloat16)
    weight_part = jnp.einsum("ijc,hij->ch", pair_normed, grad_bias, precision=lax.Precision.HIGHEST)
    weight_sum = lax.psum(weight_part, ("row", "col"))
    bias_weight_grad = weight_sum / samples
    return (token_grad, pair_grad, bias_weight_grad)


EPS = 1e-05
SCALE = 1.0 / math.sqrt(CH)
NT = (((1,), (1,)), ((), ()))
TN = (((0,), (0,)), ((), ()))
MASKED = -65504.0


def params(megabytes):
    return pltpu.CompilerParams(vmem_limit_bytes=megabytes * 1024 * 1024)


def matmul(left, right):
    return jnp.dot(left, right, preferred_element_type=jnp.float32)


def matmul_nt(left, right):
    return lax.dot_general(left, right, NT, preferred_element_type=jnp.float32)


def matmul_tn(left, right):
    return lax.dot_general(left, right, TN, preferred_element_type=jnp.float32)


def halves(values):
    high = values.astype(jnp.bfloat16)
    low = (values - high.astype(jnp.float32)).astype(jnp.bfloat16)
    return high, low


def unit_rows(values):
    centred = values - jnp.mean(values, axis=-1, keepdims=True)
    inv_std = lax.rsqrt(jnp.mean(centred * centred, axis=-1, keepdims=True) + EPS)
    return centred * inv_std, inv_std


def embed_rows(tokens_ref, types_ref, table_ref):
    count, length, width = tokens_ref.shape
    index = lax.broadcasted_iota(jnp.int32, (NTYPE, length), 0)
    onehot = jnp.where(types_ref[...] == index, 1.0, 0.0).astype(jnp.bfloat16)
    added = matmul_tn(onehot, table_ref[...])
    embedded = tokens_ref[...].astype(jnp.float32) + added[None]
    return unit_rows(embedded.reshape(count * length, width))


def token_kernel(
    row_ref, tokens_ref, types_ref, table_ref, wq_ref, wk_ref, wv_ref, wg_ref, cot_ref, out_ref
):
    normed, _ = embed_rows(tokens_ref, types_ref, table_ref)
    act = normed.astype(jnp.bfloat16)
    heads, _, _, count = out_ref.shape

    def store(slot, rounded):
        out_ref[:, slot] = rounded.T.reshape(heads, CH, count)

    for slot, ref in enumerate((wq_ref, wk_ref, wv_ref)):
        store(slot, matmul(act, ref[...]).astype(jnp.bfloat16))
    gate = matmul(act, wg_ref[...]).astype(jnp.bfloat16).astype(jnp.float32)
    cot = cot_ref[...].reshape(gate.shape).astype(jnp.float32)
    store(3, (cot * jax.nn.sigmoid(gate)).astype(jnp.bfloat16))


def token_messages(row, tokens, types, table, weights, cotangent, n_row, n_col):
    samp_dev, tok_col, _ = tokens.shape
    width = D // n_row
    whole3 = lambda i, r: (0, 0, 0)
    whole2 = lambda i, r: (0, 0)
    weight_spec = pl.BlockSpec((D, width), lambda i, r: (0, r[0]))
    shape = (n_col, 4, CH, samp_dev * tok_col)
    return pl.pallas_call(
        token_kernel,
        out_shape=jax.ShapeDtypeStruct(shape, jnp.bfloat16),
        grid_spec=pltpu.PrefetchScalarGridSpec(
            num_scalar_prefetch=1,
            grid=(1,),
            in_specs=[
                pl.BlockSpec(tokens.shape, whole3),
                pl.BlockSpec(types.shape, whole2),
                pl.BlockSpec(table.shape, whole2),
                weight_spec,
                weight_spec,
                weight_spec,
                weight_spec,
                pl.BlockSpec((samp_dev, tok_col, width), lambda i, r: (0, 0, r[0])),
            ],
            out_specs=pl.BlockSpec(shape, lambda i, r: (0, 0, 0, 0)),
        ),
        compiler_params=params(56),
        cost_estimate=pl.CostEstimate(
            flops=2 * samp_dev * tok_col * D * width * 4, bytes_accessed=4_000_000, transcendentals=0
        ),
        name="token_messages",
    )(row, tokens, types, table, *weights, cotangent)


def own_kernel(
    row_ref, tokens_ref, types_ref, table_ref, wg_ref, cot_ref, slope_ref, normed_ref, inv_ref
):
    normed, inv_std = embed_rows(tokens_ref, types_ref, table_ref)
    gate = matmul(normed.astype(jnp.bfloat16), wg_ref[...]).astype(jnp.bfloat16)
    sig = jax.nn.sigmoid(gate.astype(jnp.float32))
    cot = cot_ref[...].reshape(gate.shape).astype(jnp.float32)
    slope_ref[...] = (cot * sig * (1.0 - sig)).T
    normed_ref[...] = normed.T
    inv_ref[...] = jnp.broadcast_to(inv_std, (inv_std.shape[0], 128)).T[:8]


def own_rows(row, tokens, types, table, w_gate, cotangent, half):
    _, tok_col, _ = tokens.shape
    count = half * tok_col
    part_spec = pl.BlockSpec((half, tok_col, D), lambda i, r: (r[0], 0, 0))
    whole2 = lambda i, r: (0, 0)
    return pl.pallas_call(
        own_kernel,
        out_shape=[
            jax.ShapeDtypeStruct((D, count), jnp.float32),
            jax.ShapeDtypeStruct((D, count), jnp.float32),
            jax.ShapeDtypeStruct((8, count), jnp.float32),
        ],
        grid_spec=pltpu.PrefetchScalarGridSpec(
            num_scalar_prefetch=1,
            grid=(1,),
            in_specs=[
                part_spec,
                pl.BlockSpec(types.shape, whole2),
                pl.BlockSpec(table.shape, whole2),
                pl.BlockSpec(w_gate.shape, whole2),
                part_spec,
            ],
            out_specs=[
                pl.BlockSpec((D, count), whole2),
                pl.BlockSpec((D, count), whole2),
                pl.BlockSpec((8, count), whole2),
            ],
        ),
        compiler_params=params(56),
        cost_estimate=pl.CostEstimate(
            flops=2 * count * D * D, bytes_accessed=3_000_000, transcendentals=0
        ),
        name="own_rows",
    )(row, tokens, types, table, w_gate, cotangent)


def pair_columns(pair_ref, k, many):
    _, _, length, width = pair_ref.shape
    blocks = [pair_ref[p, pl.ds(k, many)] for p in range(2)]
    rows = jnp.concatenate(blocks, axis=1).reshape(many * 2 * length, width)
    values = rows.T.astype(jnp.float32)
    centred = values - jnp.mean(values, axis=0, keepdims=True)
    inv_std = lax.rsqrt(jnp.mean(centred * centred, axis=0, keepdims=True) + EPS)
    return centred, inv_std


def bias_kernel(pair_ref, weight_ref, mask_ref, out_ref, flat_ref):
    _, count, length, width = pair_ref.shape
    whole = flat_ref.shape[0] // H
    weight = jnp.concatenate([weight_ref[...]] * 2, axis=1)
    many = 4
    base = pl.program_id(0) * count

    def step(n, carry):
        k = n * many
        centred, inv_std = pair_columns(pair_ref, k, many)
        bias = matmul(weight, jnp.concatenate(halves(centred), axis=0)) * inv_std
        for m in range(many):
            lanes = slice(m * 2 * length, (m + 1) * 2 * length)
            flat_ref[pl.ds(base + k + m, H, stride=whole), :] = bias[:, lanes]
        return carry

    lax.fori_loop(0, count // many, step, 0, unroll=2)

    @pl.when(pl.program_id(0) == pl.num_programs(0) - 1)
    def _():
        keep = jnp.broadcast_to(mask_ref[...].astype(jnp.float32), (128, length)).T
        keep = jnp.concatenate([keep] * (2 * whole // 128), axis=1) == 1.0
        for h in range(H):
            turned = flat_ref[h * whole : (h + 1) * whole, :].T
            bias = jnp.concatenate([turned[:length], turned[length:]], axis=1)
            out_ref[h] = jnp.where(keep, bias, MASKED)


def pair_bias(pair, weight_t, mask):
    row_count, tok_col, width = pair.shape
    steps = 4
    whole = row_count // 2
    count = whole // steps
    return pl.pallas_call(
        bias_kernel,
        out_shape=jax.ShapeDtypeStruct((H, tok_col, row_count), jnp.float32),
        grid=(steps,),
        in_specs=[
            pl.BlockSpec((2, count, tok_col, width), lambda i: (0, i, 0, 0)),
            pl.BlockSpec(weight_t.shape, lambda i: (0, 0)),
            pl.BlockSpec(mask.shape, lambda i: (0, 0)),
        ],
        out_specs=pl.BlockSpec((H, tok_col, row_count), lambda i: (0, 0, 0)),
        scratch_shapes=[pltpu.VMEM((H * whole, 2 * tok_col), jnp.float32)],
        compiler_params=params(24),
        cost_estimate=pl.CostEstimate(
            flops=row_count * tok_col * width * 3000, bytes_accessed=5_000_000, transcendentals=0
        ),
        name="pair_bias",
    )(pair.reshape(2, whole, tok_col, width), weight_t, mask)


def shift_of(top):
    return jnp.floor(jnp.clip(14.0 - jnp.log2(top), -100.0, 100.0))


def attention_kernel(tokens_ref, bias_ref, back_ref, grad_bias_ref, sum_ref):
    n_col = tokens_ref.shape[0]
    tok_col, row_count = bias_ref.shape[1:]
    half = back_ref.shape[2] // tok_col
    n_row = bias_ref.shape[0] // n_col
    step = pl.program_id(0)

    @pl.when(step == 0)
    def _():
        sum_ref[...] = jnp.zeros_like(sum_ref)

    outs = []
    for sample in range(half):
        lanes = slice(sample * tok_col, (sample + 1) * tok_col)

        def side(slot):
            return jnp.concatenate([tokens_ref[c, slot, :, lanes] for c in range(n_col)], axis=1)

        query_t, key_t, value_t, grad_t = [side(slot) for slot in range(4)]
        key = key_t.T
        value = value_t.T
        attended_parts, grad_query_parts = [], []
        grad_key = jnp.zeros(key_t.shape, jnp.float32)
        grad_value = jnp.zeros(key_t.shape, jnp.float32)
        for block in range(n_row):
            cols = slice(block * row_count, (block + 1) * row_count)
            heads = slice(block * n_col, (block + 1) * n_col)
            bias = bias_ref[heads].reshape(n_col * tok_col, row_count)
            query_b = query_t[:, cols]
            grad_b = grad_t[:, cols]
            scores = matmul(key, query_b) * SCALE + bias
            scores = jnp.where(bias < -60000.0, -1000000000.0, scores)
            expo = jnp.exp(scores - jnp.max(scores, axis=0, keepdims=True))
            share = 1.0 / jnp.sum(expo, axis=0, keepdims=True)
            attended = matmul(value_t, expo.astype(jnp.bfloat16)) * share
            delta = jnp.sum(grad_b.astype(jnp.float32) * attended, axis=0, keepdims=True)
            probs = expo * share
            grad_scores = probs * (matmul(value, grad_b) - delta)
            rounded = grad_scores.astype(jnp.bfloat16)
            attended_parts.append(attended)
            grad_query_parts.append(matmul(key_t, rounded) * SCALE)
            grad_key = grad_key + matmul_nt(query_b, rounded)
            grad_value = grad_value + matmul_nt(grad_b, probs.astype(jnp.bfloat16))
            sum_ref[heads] += grad_scores.reshape(n_col, tok_col, row_count)
        outs.append(
            (
                jnp.concatenate(grad_query_parts, axis=1),
                grad_key * SCALE,
                grad_value,
                jnp.concatenate(attended_parts, axis=1),
            )
        )
    spare = jnp.zeros((8 - 4, half * tok_col), jnp.float32)
    tops = [jnp.max(jnp.abs(out[slot]), axis=0, keepdims=True) for slot in range(4) for out in outs]
    shifts = shift_of(jnp.concatenate(tops, axis=0))
    scales = jnp.exp2(shifts)
    scaled = [
        [out[slot] * scales[slot * half + n : slot * half + n + 1] for n, out in enumerate(outs)]
        for slot in range(4)
    ]
    for c in range(n_col):
        lanes = slice(c * tok_col, (c + 1) * tok_col)
        for slot in range(4):
            back_ref[c, slot * CH : (slot + 1) * CH, :] = jnp.concatenate(
                [part[:, lanes] for part in scaled[slot]], axis=1
            )
        tails = [
            jnp.concatenate([shifts[slot * half + n :, lanes][:1] for n in range(half)], axis=1)
            for slot in range(4)
        ]
        back_ref[c, 4 * CH :, :] = jnp.concatenate(tails + [spare], axis=0)

    @pl.when(step == pl.num_programs(0) - 1)
    def _():
        for head in range(n_row * n_col):
            sums = sum_ref[head]
            shift = shift_of(jnp.max(jnp.abs(sums), axis=0, keepdims=True))
            grad_bias_ref[head, :tok_col, :] = sums * jnp.exp2(shift)
            grad_bias_ref[head, tok_col:, :] = jnp.broadcast_to(shift, (8, row_count))


def attention(arrived, bias, n_row):
    n_col, _, _, held = arrived.shape
    _, tok_col, row_count = bias.shape
    half = held // tok_col // n_row
    width = half * tok_col
    back_shape = (n_row * n_col, 4 * CH + 8, width)
    bias_shape = (n_row * n_col, tok_col + 8, row_count)
    return pl.pallas_call(
        attention_kernel,
        out_shape=[
            jax.ShapeDtypeStruct(back_shape, jnp.float32),
            jax.ShapeDtypeStruct(bias_shape, jnp.float32),
        ],
        grid=(n_row,),
        in_specs=[
            pl.BlockSpec((n_col, 4, CH, width), lambda i: (0, 0, 0, i)),
            pl.BlockSpec(bias.shape, lambda i: (0, 0, 0)),
        ],
        out_specs=[
            pl.BlockSpec((n_col, 4 * CH + 8, width), lambda i: (i, 0, 0)),
            pl.BlockSpec(bias_shape, lambda i: (0, 0, 0)),
        ],
        scratch_shapes=[pltpu.VMEM(bias.shape, jnp.float32)],
        compiler_params=params(24),
        cost_estimate=pl.CostEstimate(
            flops=8_000_000_000, bytes_accessed=6_000_000, transcendentals=1_000_000
        ),
        name="attention",
    )(arrived, bias)


def back_kernel(
    back_ref, slope_ref, normed_ref, inv_ref, wq_ref, wk_ref, wv_ref, wg_ref, out_ref
):
    count = back_ref.shape[-1]

    def side(slot):
        scale = jnp.exp2(-back_ref[:, 4 * CH + slot : 4 * CH + slot + 1, :])
        return (back_ref[:, slot * CH : (slot + 1) * CH, :] * scale).reshape(D, count)

    total = jnp.zeros((D, count), jnp.float32)
    for slot, ref in enumerate((wq_ref, wk_ref, wv_ref)):
        parts = matmul(ref[...], jnp.concatenate(halves(side(slot)), axis=1))
        total = total + (parts[:, :count] + parts[:, count:])
    total = total + matmul(wg_ref[...], (side(3) * slope_ref[...]).astype(jnp.bfloat16))
    normed = normed_ref[...]
    result = inv_ref[:1] * (
        total
        - jnp.mean(total, axis=0, keepdims=True)
        - normed * jnp.mean(total * normed, axis=0, keepdims=True)
    )
    out_ref[...] = result.T.astype(jnp.bfloat16)


def token_back(back, slope, normed, inv_std, weights):
    count = back.shape[-1]
    return pl.pallas_call(
        back_kernel,
        out_shape=jax.ShapeDtypeStruct((count, D), jnp.bfloat16),
        compiler_params=params(56),
        cost_estimate=pl.CostEstimate(
            flops=20 * count * D * D, bytes_accessed=8_000_000, transcendentals=0
        ),
        name="token_back",
    )(back, slope, normed, inv_std, *weights)


def pair_back_kernel(factor, pair_ref, grads_ref, weight_ref, out_ref, part_ref, flat_ref):
    _, count, length, width = pair_ref.shape
    whole = flat_ref.shape[0] // H
    weight = weight_ref[...].astype(jnp.float32)
    weight = halves(weight - jnp.mean(weight, axis=1, keepdims=True))
    weight = jnp.concatenate([weight[0], weight[0], weight[1], weight[1]], axis=0).T
    many = 4
    base = pl.program_id(0) * count

    @pl.when(pl.program_id(0) == 0)
    def _():
        part_ref[...] = jnp.zeros_like(part_ref)
        for h in range(H):
            grads = grads_ref[h]
            both = jnp.concatenate([grads[:, :whole], grads[:, whole:]], axis=0)
            flat_ref[h * whole : (h + 1) * whole, :] = both.T

    def step(n, carry):
        k = n * many
        centred, inv_std = pair_columns(pair_ref, k, many)
        normed = centred * inv_std
        grads = jnp.concatenate(
            [flat_ref[pl.ds(base + k + m, H, stride=whole), :] for m in range(many)], axis=1
        )
        grads = jnp.concatenate(halves(grads), axis=0)
        grad_in = matmul(weight, jnp.concatenate([grads, grads], axis=0))
        overlap = jnp.mean(grad_in * normed, axis=0, keepdims=True)
        result = (grad_in - normed * overlap) * (inv_std * factor)
        result = result.astype(jnp.bfloat16).T.reshape(many, 2 * length, width)
        for p in range(2):
            out_ref[p, pl.ds(k, many)] = result[:, p * length : (p + 1) * length]
        return carry + matmul_nt(jnp.concatenate(halves(normed), axis=0), grads)

    parts = jnp.zeros((2 * width, 2 * H), jnp.float32)
    parts = lax.fori_loop(0, count // many, step, parts, unroll=2)
    parts = parts[:, :H] + parts[:, H:]
    part_ref[...] += (parts[:width] + parts[width:]).T


def pair_backward(pair, grads, weight_t, factor):
    row_count, tok_col, width = pair.shape
    steps = 4
    whole = row_count // 2
    pair_spec = pl.BlockSpec((2, whole // steps, tok_col, width), lambda i: (0, i, 0, 0))
    pair_grad, part = pl.pallas_call(
        lambda *refs: pair_back_kernel(factor, *refs),
        out_shape=[
            jax.ShapeDtypeStruct((2, whole, tok_col, width), jnp.bfloat16),
            jax.ShapeDtypeStruct((H, width), jnp.float32),
        ],
        grid=(steps,),
        in_specs=[
            pair_spec,
            pl.BlockSpec(grads.shape, lambda i: (0, 0, 0)),
            pl.BlockSpec(weight_t.shape, lambda i: (0, 0)),
        ],
        out_specs=[pair_spec, pl.BlockSpec((H, width), lambda i: (0, 0))],
        scratch_shapes=[pltpu.VMEM((H * whole, 2 * tok_col), jnp.float32)],
        compiler_params=params(24),
        cost_estimate=pl.CostEstimate(
            flops=row_count * tok_col * width * 5000, bytes_accessed=11_000_000, transcendentals=0
        ),
        name="pair_backward",
    )(pair.reshape(2, whole, tok_col, width), grads, weight_t)
    return pair_grad.reshape(pair.shape), part


def unscaled(block, rows):
    block = block.astype(jnp.float32)
    return block[:, :rows] * jnp.exp2(-block[:, rows : rows + 1])


def swap(block, axis):
    return lax.ppermute(block, axis, [(0, 1), (1, 0)])


def body_heads(
    tokens, restype, type_table, key_mask, pair, w_bias, w_query, w_key, w_value, w_gate, cotangent
):
    n_row = lax.axis_size("row")
    n_col = lax.axis_size("col")
    n_samp = lax.axis_size("samp")
    samp_dev = tokens.shape[0]
    tok_col = tokens.shape[1]
    row_count = pair.shape[0]
    total_tokens = tok_col * n_col
    half = samp_dev // n_row
    row_index = lax.axis_index("row")
    row = row_index.astype(jnp.int32).reshape(1)
    types = restype.reshape(1, tok_col)
    weight_t = w_bias.T
    weights = (w_query, w_key, w_value, w_gate)

    message = token_messages(
        row, tokens, types, type_table, weights, cotangent, n_row, n_col
    )
    message, bias_weight = lax.optimization_barrier((message, weight_t))
    arrived = lax.all_to_all(message, "col", 0, 0, tiled=True)
    bias = pair_bias(pair, bias_weight, key_mask.reshape(1, tok_col))
    arrived, bias = lax.optimization_barrier((arrived, bias.astype(jnp.float16)))
    bias = lax.all_to_all(bias, ("row", "col"), 0, 0, tiled=True).astype(jnp.float32)
    slope, normed, inv_std = own_rows(row, tokens, types, type_table, w_gate, cotangent, half)

    back, grad_bias = attention(arrived, bias, n_row)
    grad_bias = lax.all_to_all(
        grad_bias.astype(jnp.float16), ("row", "col"), 0, 0, tiled=True
    )
    other_bias = swap(grad_bias, "samp")
    back = lax.all_to_all(back.astype(jnp.float16), ("row", "col"), 0, 0, tiled=True)
    grads = unscaled(grad_bias, tok_col) + unscaled(other_bias, tok_col)

    samples = samp_dev * n_samp
    pair_grad, part = pair_backward(pair, grads, weight_t, total_tokens / samples)
    parts = lax.all_to_all(
        jnp.broadcast_to(part[None], (H,) + part.shape), ("row", "col"), 0, 0, tiled=True
    )
    bias_weight_grad = jnp.sum(parts, axis=0).T / samples

    back, part = lax.optimization_barrier((back, part))
    back = back.astype(jnp.float32)
    token_half = token_back(back, slope, normed, inv_std, weights)
    token_half = token_half.reshape(half, tok_col, D)
    other = swap(token_half, "row")
    first = row_index == 0
    token_grad = jnp.concatenate(
        [jnp.where(first, token_half, other), jnp.where(first, other, token_half)], axis=0
    )
    return (token_grad, pair_grad, bias_weight_grad)


def body(*args):
    n_row = lax.axis_size("row")
    n_col = lax.axis_size("col")
    tokens = args[0]
    pair = args[4]
    fits = n_row == 2 and n_row * n_col == H and lax.axis_size("samp") == 2
    square = pair.shape[0] * n_row == pair.shape[1] * n_col
    if fits and square and tokens.shape[0] == 4 and tokens.shape[1] == 64:
        return body_heads(*args)
    return body_any(*args)


def solution(mesh):
    placed = (
        P("samp", "col", None),
        P("col"),
        P(),
        P("col"),
        P("row", "col", None),
        P(),
        P(),
        P(),
        P(),
        P(),
        P("samp", "col", None),
    )
    return jax.shard_map(
        body,
        mesh=mesh,
        in_specs=placed,
        out_specs=(P("samp", "col", None), P("row", "col", None), P()),
        check_vma=False,
    )
```

```python
import math

import jax
import jax.numpy as jnp
from jax import lax
from jax.experimental import pallas as pl
from jax.experimental.pallas import tpu as pltpu
from jax.sharding import PartitionSpec as P

D = 768
H = 16
CH = 48
NTYPE = 32


def broadcast(block, axis, source):
    block = jnp.where(lax.axis_index(axis) == source, block, jnp.zeros_like(block))
    return lax.psum(block, axis)


def token_norm(tokens, restype, type_table):
    onehot = (restype[:, None] == jnp.arange(NTYPE, dtype=jnp.int32)[None, :]).astype(jnp.bfloat16)
    embedded = tokens.astype(jnp.float32) + jnp.dot(
        onehot, type_table, preferred_element_type=jnp.float32
    )
    centred = embedded - jnp.mean(embedded, axis=-1, keepdims=True)
    inv_std = lax.rsqrt(jnp.mean(centred * centred, axis=-1, keepdims=True) + 1e-05)
    return (centred * inv_std, inv_std)


def pair_norm(block):
    values = block.astype(jnp.float32)
    centred = values - jnp.mean(values, axis=-1, keepdims=True)
    inv_std = lax.rsqrt(jnp.mean(centred * centred, axis=-1, keepdims=True) + 1e-05)
    return (centred * inv_std, inv_std)


def norm_back(grad_in, normed, inv_std):
    return inv_std * (
        grad_in
        - jnp.mean(grad_in, axis=-1, keepdims=True)
        - normed * jnp.mean(grad_in * normed, axis=-1, keepdims=True)
    )


def project(rows_in, weight):
    return jnp.einsum("std,de->ste", rows_in, weight, preferred_element_type=jnp.float32).astype(
        jnp.bfloat16
    )


def back_project(grads, weight):
    return jnp.einsum(
        "ste,de->std", grads, weight.astype(jnp.float32), precision=lax.Precision.HIGHEST
    )


def pair_back(grad_bias, pair_normed, pair_inv, bias_weight):
    grad_normed = jnp.einsum("hij,ch->ijc", grad_bias, bias_weight, precision=lax.Precision.HIGHEST)
    return norm_back(grad_normed, pair_normed, pair_inv)


def body_any(
    tokens, restype, type_table, key_mask, pair, w_bias, w_query, w_key, w_value, w_gate, cotangent
):
    n_row = lax.axis_size("row")
    n_col = lax.axis_size("col")
    n_samp = lax.axis_size("samp")
    samp_dev = tokens.shape[0]
    tok_col = tokens.shape[1]
    spread = n_col // n_row
    row_count = tok_col * spread
    total_tokens = tok_col * n_col
    row_index = lax.axis_index("row")
    col_index = lax.axis_index("col")
    is_owner = col_index // spread == row_index
    own_start = col_index % spread * tok_col
    normed, inv_std = token_norm(tokens, restype, type_table)
    own_act = normed.astype(jnp.bfloat16)
    key_proj = project(own_act, w_key)
    value_proj = project(own_act, w_value)
    stacked = jnp.stack([own_act, cotangent])
    pieces = [broadcast(stacked, "col", row_index * spread + member) for member in range(spread)]
    gathered = jnp.concatenate(pieces, axis=2)
    query_side = gathered[0]
    grad_rows = gathered[1]
    queries = project(query_side, w_query)
    gate_lin = project(query_side, w_gate)
    pair_normed, pair_inv = pair_norm(pair)
    bias_weight = w_bias.astype(jnp.float32)
    bias = jnp.einsum("ijc,ch->hij", pair_normed, bias_weight, precision=lax.Precision.HIGHEST)
    query_heads = queries.reshape(samp_dev, row_count, H, CH)
    key_heads = key_proj.reshape(samp_dev, tok_col, H, CH)
    value_heads = value_proj.reshape(samp_dev, tok_col, H, CH)
    scores = (
        jnp.einsum("sihc,sjhc->shij", query_heads, key_heads, preferred_element_type=jnp.float32)
        / math.sqrt(CH)
        + bias[None]
    )
    scores = jnp.where(key_mask[None, None, None, :] == 1, scores, -1000000000.0)
    top = lax.pmax(jnp.max(scores, axis=-1), "col")
    expo = jnp.exp(scores - top[..., None])
    partial_out = jnp.einsum(
        "shij,sjhc->sihc",
        expo.astype(jnp.bfloat16),
        value_heads,
        preferred_element_type=jnp.float32,
    )
    totals, summed = lax.psum(
        (jnp.sum(expo, axis=-1), partial_out.reshape(samp_dev, row_count, D)), "col"
    )
    attended = (
        summed.reshape(samp_dev, row_count, H, CH) / jnp.transpose(totals, (0, 2, 1))[..., None]
    )
    flat_out = attended.reshape(samp_dev, row_count, D)
    sig_gate = jax.nn.sigmoid(gate_lin.astype(jnp.float32))
    grad_f = grad_rows.astype(jnp.float32)
    grad_out = (grad_f * sig_gate).astype(jnp.bfloat16)
    grad_gate = (grad_f * flat_out * sig_gate * (1.0 - sig_gate)).astype(jnp.bfloat16)
    gate_piece = lax.dynamic_slice_in_dim(grad_gate, own_start, tok_col, 1)
    gate_term = jnp.where(
        is_owner,
        jnp.einsum("ste,de->std", gate_piece, w_gate, preferred_element_type=jnp.float32),
        0.0,
    )
    grad_heads = grad_out.reshape(samp_dev, row_count, H, CH)
    delta = jnp.transpose(jnp.sum(grad_heads.astype(jnp.float32) * attended, axis=-1), (0, 2, 1))
    probs = expo / totals[..., None]
    grad_pre = jnp.einsum(
        "sihc,sjhc->shij", grad_heads, value_heads, preferred_element_type=jnp.float32
    )
    grad_scores = probs * (grad_pre - delta[..., None])
    rounded = grad_scores.astype(jnp.bfloat16)
    grad_query = (
        jnp.einsum("shij,sjhc->sihc", rounded, key_heads, preferred_element_type=jnp.float32)
        / math.sqrt(CH)
    ).reshape(samp_dev, row_count, D)
    grad_key = (
        jnp.einsum("shij,sihc->sjhc", rounded, query_heads, preferred_element_type=jnp.float32)
        / math.sqrt(CH)
    ).reshape(samp_dev, tok_col, D)
    grad_value = jnp.einsum(
        "shij,sihc->sjhc",
        probs.astype(jnp.bfloat16),
        grad_heads,
        preferred_element_type=jnp.float32,
    ).reshape(samp_dev, tok_col, D)
    bias_local = jnp.sum(grad_scores, axis=0)
    blank = jnp.zeros((samp_dev, total_tokens, D), jnp.float32)
    mine = lax.psum_scatter(
        lax.dynamic_update_slice_in_dim(blank, grad_query, row_index * row_count, 1),
        "col",
        scatter_dimension=1,
        tiled=True,
    )
    query_all, key_all, value_all, gate_all = lax.psum(
        (mine, grad_key, grad_value, gate_term), "row"
    )
    grad_act = (
        back_project(query_all, w_query)
        + back_project(key_all, w_key)
        + back_project(value_all, w_value)
        + gate_all
    )
    token_grad = norm_back(grad_act, normed, inv_std).astype(jnp.bfloat16)
    samples = samp_dev * n_samp
    grad_bias = lax.psum(bias_local, "samp")
    grad_pair = pair_back(grad_bias, pair_normed, pair_inv, bias_weight)
    pair_grad = (grad_pair * (total_tokens / samples)).astype(jnp.bfloat16)
    weight_part = jnp.einsum("ijc,hij->ch", pair_normed, grad_bias, precision=lax.Precision.HIGHEST)
    weight_sum = lax.psum(weight_part, ("row", "col"))
    bias_weight_grad = weight_sum / samples
    return (token_grad, pair_grad, bias_weight_grad)


EPS = 1e-05
SCALE = 1.0 / math.sqrt(CH)
NT = (((1,), (1,)), ((), ()))
TN = (((0,), (0,)), ((), ()))
MASKED = -65504.0


def params(megabytes):
    return pltpu.CompilerParams(vmem_limit_bytes=megabytes * 1024 * 1024)


def matmul(left, right):
    return jnp.dot(left, right, preferred_element_type=jnp.float32)


def matmul_nt(left, right):
    return lax.dot_general(left, right, NT, preferred_element_type=jnp.float32)


def matmul_tn(left, right):
    return lax.dot_general(left, right, TN, preferred_element_type=jnp.float32)


def halves(values):
    high = values.astype(jnp.bfloat16)
    low = (values - high.astype(jnp.float32)).astype(jnp.bfloat16)
    return high, low


def unit_rows(values):
    centred = values - jnp.mean(values, axis=-1, keepdims=True)
    inv_std = lax.rsqrt(jnp.mean(centred * centred, axis=-1, keepdims=True) + EPS)
    return centred * inv_std, inv_std


def embed_rows(tokens_ref, types_ref, table_ref):
    count, length, width = tokens_ref.shape
    index = lax.broadcasted_iota(jnp.int32, (NTYPE, length), 0)
    onehot = jnp.where(types_ref[...] == index, 1.0, 0.0).astype(jnp.bfloat16)
    added = matmul_tn(onehot, table_ref[...])
    embedded = tokens_ref[...].astype(jnp.float32) + added[None]
    return unit_rows(embedded.reshape(count * length, width))


def token_kernel(row_ref, col_ref, tokens_ref, types_ref, table_ref, *refs):
    wq_ref, wk_ref, wv_ref, wg_ref, cot_ref = refs[:5]
    out_refs, side_ref = refs[5:-1], refs[-1]
    normed, _ = embed_rows(tokens_ref, types_ref, table_ref)
    act = normed.astype(jnp.bfloat16)
    for slot, ref in enumerate((wq_ref, wk_ref, wv_ref)):
        side_ref[slot] = matmul(act, ref[...]).astype(jnp.bfloat16).T
    gate = matmul(act, wg_ref[...]).astype(jnp.bfloat16).astype(jnp.float32)
    cot = cot_ref[...].reshape(gate.shape).astype(jnp.float32)
    side_ref[3] = (cot * jax.nn.sigmoid(gate)).astype(jnp.bfloat16).T
    for offset, out_ref in enumerate(out_refs):
        for core in range(2):
            start = pl.multiple_of((col_ref[0] ^ (2 * offset + core)) * CH, 16)
            out_ref[core] = side_ref[:, pl.ds(start, CH), :]


def token_messages(row, col, tokens, types, table, weights, cotangent, n_row, n_col):
    samp_dev, tok_col, _ = tokens.shape
    width = D // n_row
    held = samp_dev * tok_col
    whole3 = lambda i, r, c: (0, 0, 0)
    whole2 = lambda i, r, c: (0, 0)
    weight_spec = pl.BlockSpec((D, width), lambda i, r, c: (0, r[0]))
    shape = (2, 4, CH, held)
    count = n_col // 2
    return pl.pallas_call(
        token_kernel,
        out_shape=[jax.ShapeDtypeStruct(shape, jnp.bfloat16)] * count,
        grid_spec=pltpu.PrefetchScalarGridSpec(
            num_scalar_prefetch=2,
            grid=(1,),
            in_specs=[
                pl.BlockSpec(tokens.shape, whole3),
                pl.BlockSpec(types.shape, whole2),
                pl.BlockSpec(table.shape, whole2),
                weight_spec,
                weight_spec,
                weight_spec,
                weight_spec,
                pl.BlockSpec((samp_dev, tok_col, width), lambda i, r, c: (0, 0, r[0])),
            ],
            out_specs=[pl.BlockSpec(shape, lambda i, r, c: (0, 0, 0, 0))] * count,
            scratch_shapes=[pltpu.VMEM((4, width, held), jnp.bfloat16)],
        ),
        compiler_params=params(56),
        cost_estimate=pl.CostEstimate(
            flops=4_000_000_000, bytes_accessed=4_000_000, transcendentals=0
        ),
        name="token_messages",
    )(row, col, tokens, types, table, *weights, cotangent)


def own_kernel(
    row_ref, tokens_ref, types_ref, table_ref, wg_ref, cot_ref, slope_ref, normed_ref, inv_ref
):
    normed, inv_std = embed_rows(tokens_ref, types_ref, table_ref)
    gate = matmul(normed.astype(jnp.bfloat16), wg_ref[...]).astype(jnp.bfloat16)
    sig = jax.nn.sigmoid(gate.astype(jnp.float32))
    cot = cot_ref[...].reshape(gate.shape).astype(jnp.float32)
    slope_ref[...] = (cot * sig * (1.0 - sig)).T
    normed_ref[...] = normed.T
    inv_ref[...] = jnp.broadcast_to(inv_std, (inv_std.shape[0], 128)).T[:8]


def own_rows(row, tokens, types, table, w_gate, cotangent, half):
    _, tok_col, _ = tokens.shape
    count = half * tok_col
    part_spec = pl.BlockSpec((half, tok_col, D), lambda i, r: (r[0], 0, 0))
    whole2 = lambda i, r: (0, 0)
    return pl.pallas_call(
        own_kernel,
        out_shape=[
            jax.ShapeDtypeStruct((D, count), jnp.float32),
            jax.ShapeDtypeStruct((D, count), jnp.float32),
            jax.ShapeDtypeStruct((8, count), jnp.float32),
        ],
        grid_spec=pltpu.PrefetchScalarGridSpec(
            num_scalar_prefetch=1,
            grid=(1,),
            in_specs=[
                part_spec,
                pl.BlockSpec(types.shape, whole2),
                pl.BlockSpec(table.shape, whole2),
                pl.BlockSpec(w_gate.shape, whole2),
                part_spec,
            ],
            out_specs=[
                pl.BlockSpec((D, count), whole2),
                pl.BlockSpec((D, count), whole2),
                pl.BlockSpec((8, count), whole2),
            ],
        ),
        compiler_params=params(56),
        cost_estimate=pl.CostEstimate(
            flops=3_000_000_000, bytes_accessed=3_000_000, transcendentals=0
        ),
        name="own_rows",
    )(row, tokens, types, table, w_gate, cotangent)


MANY = 4


def pair_columns(pair_ref, k, many):
    _, _, length, width = pair_ref.shape
    blocks = [pair_ref[p, pl.ds(k, many)] for p in range(2)]
    rows = jnp.concatenate(blocks, axis=1).reshape(many * 2 * length, width)
    same = lax.broadcasted_iota(jnp.int32, (width, width), 0) == lax.broadcasted_iota(
        jnp.int32, (width, width), 1
    )
    centring = (jnp.where(same, 1.0, 0.0) - 1.0 / width).astype(jnp.bfloat16)
    centred = matmul_nt(centring, rows)
    return centred, lax.rsqrt(jnp.mean(centred * centred, axis=0, keepdims=True) + EPS)


def bias_kernel(pair_ref, weight_ref, mask_ref, out_ref, flat_ref):
    _, count, length, width = pair_ref.shape
    whole = flat_ref.shape[0] // H
    weight = jnp.concatenate([weight_ref[...]] * 2, axis=1)
    base = pl.program_id(0) * count

    def step(n, carry):
        k = n * MANY
        centred, inv_std = pair_columns(pair_ref, k, MANY)
        bias = matmul(weight, jnp.concatenate(halves(centred), axis=0)) * inv_std
        for m in range(MANY):
            lanes = slice(m * 2 * length, (m + 1) * 2 * length)
            flat_ref[pl.ds(base + k + m, H, stride=whole), :] = bias[:, lanes]
        return carry

    lax.fori_loop(0, count // MANY, step, 0, unroll=2)

    @pl.when(pl.program_id(0) == pl.num_programs(0) - 1)
    def _():
        keep = jnp.broadcast_to(mask_ref[...].astype(jnp.float32), (128, length)).T
        keep = jnp.concatenate([keep] * (2 * whole // 128), axis=1) == 1.0
        for h in range(H):
            turned = flat_ref[h * whole : (h + 1) * whole, :].T
            bias = jnp.concatenate([turned[:length], turned[length:]], axis=1)
            out_ref[h] = jnp.where(keep, bias, MASKED)


STEPS = 4


def split_spec(shape):
    block = (shape[0] // STEPS,) + tuple(shape[1:])
    return pl.BlockSpec(block, lambda i: (i,) + (0,) * (len(shape) - 1))


def whole_spec(shape):
    return pl.BlockSpec(tuple(shape), lambda i: (0,) * len(shape))


def pair_spec(pair):
    row_count, tok_col, width = pair.shape
    block = (2, row_count // 2 // STEPS, tok_col, width)
    return pl.BlockSpec(block, lambda i: (0, i, 0, 0))


def pair_bias(pair, weight_t, mask):
    row_count, tok_col, width = pair.shape
    whole = row_count // 2
    return pl.pallas_call(
        bias_kernel,
        out_shape=jax.ShapeDtypeStruct((H, tok_col, row_count), jnp.float32),
        grid=(STEPS,),
        in_specs=[pair_spec(pair), whole_spec(weight_t.shape), whole_spec(mask.shape)],
        out_specs=whole_spec((H, tok_col, row_count)),
        scratch_shapes=[pltpu.VMEM((H * whole, 2 * tok_col), jnp.float32)],
        compiler_params=params(24),
        cost_estimate=pl.CostEstimate(
            flops=6_000_000_000, bytes_accessed=5_000_000, transcendentals=0
        ),
        name="pair_bias",
    )(pair.reshape(2, whole, tok_col, width), weight_t, mask)


def norm_kernel(pair_ref, normed_ref, inv_ref):
    def step(n, carry):
        centred, inv_std = pair_columns(pair_ref, n * MANY, MANY)
        normed_ref[n] = jnp.concatenate(halves(centred * inv_std), axis=0)
        inv_ref[n] = jnp.broadcast_to(inv_std, inv_ref.shape[1:])
        return carry

    lax.fori_loop(0, normed_ref.shape[0], step, 0, unroll=2)


def pair_units(pair):
    row_count, tok_col, width = pair.shape
    whole = row_count // 2
    chunks, lanes = whole // MANY, MANY * 2 * tok_col
    shapes = [(chunks, 2 * width, lanes), (chunks, 8, lanes)]
    return pl.pallas_call(
        norm_kernel,
        out_shape=[
            jax.ShapeDtypeStruct(shapes[0], jnp.bfloat16),
            jax.ShapeDtypeStruct(shapes[1], jnp.float32),
        ],
        grid=(STEPS,),
        in_specs=[pair_spec(pair)],
        out_specs=[split_spec(shape) for shape in shapes],
        compiler_params=params(56),
        cost_estimate=pl.CostEstimate(
            flops=6_000_000_000, bytes_accessed=12_000_000, transcendentals=0
        ),
        name="pair_units",
    )(pair.reshape(2, whole, tok_col, width))


def shift_of(top):
    return jnp.floor(jnp.clip(14.0 - jnp.log2(top), -100.0, 100.0))


def attention_kernel(col_ref, *refs):
    other_ref, bias_ref, back_ref, grad_bias_ref, sum_ref, tokens_ref = refs[-6:]
    col = col_ref[0]
    for offset, ref in enumerate(refs[:-6]):
        tokens_ref[col ^ (2 * offset)] = ref[0]
        tokens_ref[col ^ (2 * offset + 1)] = other_ref[offset]
    n_col = tokens_ref.shape[0]
    tok_col, row_count = bias_ref.shape[1:]
    half = back_ref.shape[2] // tok_col
    n_row = bias_ref.shape[0] // n_col
    step = pl.program_id(0)

    @pl.when(step == 0)
    def _():
        sum_ref[...] = jnp.zeros_like(sum_ref)

    outs = []
    for sample in range(half):
        lanes = slice(sample * tok_col, (sample + 1) * tok_col)

        def side(slot):
            return jnp.concatenate([tokens_ref[c, slot, :, lanes] for c in range(n_col)], axis=1)

        query_t, key_t, value_t, grad_t = [side(slot) for slot in range(4)]
        key = key_t.T
        value = value_t.T
        attended_parts, grad_query_parts = [], []
        grad_key = jnp.zeros(key_t.shape, jnp.float32)
        grad_value = jnp.zeros(key_t.shape, jnp.float32)
        for block in range(n_row):
            cols = slice(block * row_count, (block + 1) * row_count)
            heads = slice(block * n_col, (block + 1) * n_col)
            bias = bias_ref[heads].reshape(n_col * tok_col, row_count)
            query_b = query_t[:, cols]
            grad_b = grad_t[:, cols]
            scores = matmul(key, query_b) * SCALE + bias
            scores = jnp.where(bias < -60000.0, -1000000000.0, scores)
            expo = jnp.exp(scores - jnp.max(scores, axis=0, keepdims=True))
            share = 1.0 / jnp.sum(expo, axis=0, keepdims=True)
            attended = matmul(value_t, expo.astype(jnp.bfloat16)) * share
            delta = jnp.sum(grad_b.astype(jnp.float32) * attended, axis=0, keepdims=True)
            probs = expo * share
            grad_scores = probs * (matmul(value, grad_b) - delta)
            rounded = grad_scores.astype(jnp.bfloat16)
            attended_parts.append(attended)
            grad_query_parts.append(matmul(key_t, rounded) * SCALE)
            grad_key = grad_key + matmul_nt(query_b, rounded)
            grad_value = grad_value + matmul_nt(grad_b, probs.astype(jnp.bfloat16))
            sum_ref[heads] += grad_scores.reshape(n_col, tok_col, row_count)
        outs.append(
            (
                jnp.concatenate(grad_query_parts, axis=1),
                grad_key * SCALE,
                grad_value,
                jnp.concatenate(attended_parts, axis=1),
            )
        )
    spare = jnp.zeros((8 - 4, half * tok_col), jnp.float32)
    tops = [jnp.max(jnp.abs(out[slot]), axis=0, keepdims=True) for slot in range(4) for out in outs]
    shifts = shift_of(jnp.concatenate(tops, axis=0))
    scales = jnp.exp2(shifts)
    scaled = [
        [out[slot] * scales[slot * half + n : slot * half + n + 1] for n, out in enumerate(outs)]
        for slot in range(4)
    ]
    for c in range(n_col):
        lanes = slice(c * tok_col, (c + 1) * tok_col)
        for slot in range(4):
            back_ref[c, slot * CH : (slot + 1) * CH, :] = jnp.concatenate(
                [part[:, lanes] for part in scaled[slot]], axis=1
            )
        tails = [
            jnp.concatenate([shifts[slot * half + n :, lanes][:1] for n in range(half)], axis=1)
            for slot in range(4)
        ]
        back_ref[c, 4 * CH :, :] = jnp.concatenate(tails + [spare], axis=0)

    @pl.when(step == pl.num_programs(0) - 1)
    def _():
        for head in range(n_row * n_col):
            sums = sum_ref[head]
            shift = shift_of(jnp.max(jnp.abs(sums), axis=0, keepdims=True))
            grad_bias_ref[head, :tok_col, :] = sums * jnp.exp2(shift)
            grad_bias_ref[head, tok_col:, :] = jnp.broadcast_to(shift, (8, row_count))


def attention(col, arrived, other, bias, n_row):
    count = len(arrived)
    n_col = 2 * count
    _, tok_col, row_count = bias.shape
    half = arrived[0].shape[-1] // tok_col // n_row
    width = half * tok_col
    back_shape = (n_row * n_col, 4 * CH + 8, width)
    bias_shape = (n_row * n_col, tok_col + 8, row_count)
    return pl.pallas_call(
        attention_kernel,
        out_shape=[
            jax.ShapeDtypeStruct(back_shape, jnp.float32),
            jax.ShapeDtypeStruct(bias_shape, jnp.float32),
        ],
        grid_spec=pltpu.PrefetchScalarGridSpec(
            num_scalar_prefetch=1,
            grid=(n_row,),
            in_specs=[pl.BlockSpec((1, 4, CH, width), lambda i, r: (0, 0, 0, i))] * count
            + [
                pl.BlockSpec((count, 4, CH, width), lambda i, r: (0, 0, 0, i)),
                pl.BlockSpec(bias.shape, lambda i, r: (0, 0, 0)),
            ],
            out_specs=[
                pl.BlockSpec((n_col, 4 * CH + 8, width), lambda i, r: (i, 0, 0)),
                pl.BlockSpec(bias_shape, lambda i, r: (0, 0, 0)),
            ],
            scratch_shapes=[
                pltpu.VMEM(bias.shape, jnp.float32),
                pltpu.VMEM((n_col, 4, CH, width), jnp.bfloat16),
            ],
        ),
        compiler_params=params(24),
        cost_estimate=pl.CostEstimate(
            flops=8_000_000_000, bytes_accessed=6_000_000, transcendentals=1_000_000
        ),
        name="attention",
    )(col, *arrived, other, bias)


def back_kernel(*refs):
    slope_ref, normed_ref, inv_ref, wq_ref, wk_ref, wv_ref, wg_ref = refs[-11:-4]
    out_ref, parts_ref, gate_ref, total_ref = refs[-4:]
    back_ref = refs[0]
    count = normed_ref.shape[-1]
    step = pl.program_id(0)
    rows = wq_ref.shape[0]

    @pl.when(step == 0)
    def _():
        for slot in range(4):
            scale = jnp.exp2(-back_ref[:, 4 * CH + slot : 4 * CH + slot + 1, :])
            values = back_ref[:, slot * CH : (slot + 1) * CH, :] * scale
            values = values.reshape(gate_ref.shape)
            if slot < 3:
                parts_ref[slot] = jnp.concatenate(halves(values), axis=1)
            else:
                gate_ref[...] = (values * slope_ref[...]).astype(jnp.bfloat16)

    total = matmul(wg_ref[...], gate_ref[...])
    for slot, ref in enumerate((wq_ref, wk_ref, wv_ref)):
        parts = matmul(ref[...], parts_ref[slot])
        total = total + (parts[:, :count] + parts[:, count:])
    total_ref[pl.ds(pl.multiple_of(step * rows, 8), rows), :] = total

    @pl.when(step == pl.num_programs(0) - 1)
    def _():
        whole = total_ref[...]
        normed = normed_ref[...]
        result = inv_ref[:1] * (
            whole
            - jnp.mean(whole, axis=0, keepdims=True)
            - normed * jnp.mean(whole * normed, axis=0, keepdims=True)
        )
        out_ref[...] = result.T.astype(jnp.bfloat16)


def token_back(back, slope, normed, inv_std, weights):
    count = normed.shape[-1]
    steps = 2
    whole = lambda shape: pl.BlockSpec(shape, lambda i: (0,) * len(shape))
    weight_spec = pl.BlockSpec((D // steps, D), lambda i: (i, 0))
    return pl.pallas_call(
        back_kernel,
        out_shape=jax.ShapeDtypeStruct((count, D), jnp.bfloat16),
        grid=(steps,),
        in_specs=[whole(array.shape) for array in (back, slope, normed, inv_std)]
        + [weight_spec] * 4,
        out_specs=whole((count, D)),
        scratch_shapes=[
            pltpu.VMEM((3, D, 2 * count), jnp.bfloat16),
            pltpu.VMEM((D, count), jnp.bfloat16),
            pltpu.VMEM((D, count), jnp.float32),
        ],
        compiler_params=params(40),
        cost_estimate=pl.CostEstimate(
            flops=4_000_000_000, bytes_accessed=8_000_000, transcendentals=0
        ),
        name="token_back",
    )(back, slope, normed, inv_std, *weights)


def flatten(grads_ref, flat_ref):
    whole = flat_ref.shape[0] // H
    for h in range(H):
        grads = grads_ref[h]
        both = jnp.concatenate([grads[:, :whole], grads[:, whole:]], axis=0)
        flat_ref[h * whole : (h + 1) * whole, :] = both.T


def flat_columns(flat_ref, k, many):
    whole = flat_ref.shape[0] // H
    grads = [flat_ref[pl.ds(k + m, H, stride=whole), :] for m in range(many)]
    return jnp.concatenate(halves(jnp.concatenate(grads, axis=1)), axis=0)


def pair_weight_kernel(normed_ref, grads_ref, part_ref, flat_ref):
    chunks, width, _ = normed_ref.shape
    base = pl.program_id(0) * chunks

    @pl.when(pl.program_id(0) == 0)
    def _():
        part_ref[...] = jnp.zeros_like(part_ref)
        flatten(grads_ref, flat_ref)

    def step(n, carry):
        return carry + matmul_nt(normed_ref[n], flat_columns(flat_ref, (base + n) * MANY, MANY))

    parts = lax.fori_loop(0, chunks, step, jnp.zeros((width, 2 * H), jnp.float32), unroll=2)
    parts = parts[:, :H] + parts[:, H:]
    part_ref[...] += (parts[: width // 2] + parts[width // 2 :]).T


def pair_back_kernel(factor, normed_ref, inv_ref, grads_ref, weight_ref, out_ref, flat_ref):
    _, count, length, width = out_ref.shape
    weight = weight_ref[...].astype(jnp.float32)
    weight = halves(weight - jnp.mean(weight, axis=1, keepdims=True))
    weight = jnp.concatenate([weight[0], weight[0], weight[1], weight[1]], axis=0).T
    base = pl.program_id(0) * count

    @pl.when(pl.program_id(0) == 0)
    def _():
        flatten(grads_ref, flat_ref)

    def step(n, carry):
        k = n * MANY
        normed = normed_ref[n].astype(jnp.float32)
        normed = normed[:width] + normed[width:]
        grads = flat_columns(flat_ref, base + k, MANY)
        grad_in = matmul(weight, jnp.concatenate([grads, grads], axis=0))
        overlap = jnp.mean(grad_in * normed, axis=0, keepdims=True)
        result = (grad_in - normed * overlap) * (inv_ref[n, :1] * factor)
        result = result.astype(jnp.bfloat16).T.reshape(MANY, 2 * length, width)
        for p in range(2):
            out_ref[p, pl.ds(k, MANY)] = result[:, p * length : (p + 1) * length]
        return carry

    lax.fori_loop(0, count // MANY, step, 0, unroll=2)


def pair_weight(normed, grads):
    heads, length, rows = grads.shape
    part_shape = (H, normed.shape[1] // 2)
    return pl.pallas_call(
        pair_weight_kernel,
        out_shape=jax.ShapeDtypeStruct(part_shape, jnp.float32),
        grid=(STEPS,),
        in_specs=[split_spec(normed.shape), whole_spec(grads.shape)],
        out_specs=whole_spec(part_shape),
        scratch_shapes=[pltpu.VMEM((H * rows // 2, 2 * length), jnp.float32)],
        compiler_params=params(24),
        cost_estimate=pl.CostEstimate(
            flops=5_000_000_000, bytes_accessed=100_000, transcendentals=0
        ),
        name="pair_weight",
    )(normed, grads)


def pair_backward(shape, normed, inv_std, grads, weight_t, factor):
    row_count, tok_col, width = shape
    whole = row_count // 2
    pair_grad = pl.pallas_call(
        lambda *refs: pair_back_kernel(factor, *refs),
        out_shape=jax.ShapeDtypeStruct((2, whole, tok_col, width), jnp.bfloat16),
        grid=(STEPS,),
        in_specs=[
            split_spec(normed.shape),
            split_spec(inv_std.shape),
            whole_spec(grads.shape),
            whole_spec(weight_t.shape),
        ],
        out_specs=pl.BlockSpec((2, whole // STEPS, tok_col, width), lambda i: (0, i, 0, 0)),
        scratch_shapes=[pltpu.VMEM((H * whole, 2 * tok_col), jnp.float32)],
        compiler_params=params(24),
        cost_estimate=pl.CostEstimate(
            flops=8_000_000_000, bytes_accessed=100_000, transcendentals=0
        ),
        name="pair_backward",
    )(normed, inv_std, grads, weight_t)
    return pair_grad.reshape(shape)


def unscaled(block, rows):
    block = block.astype(jnp.float32)
    return block[:, :rows] * jnp.exp2(-block[:, rows : rows + 1])


def swap(block, axis):
    return lax.ppermute(block, axis, [(0, 1), (1, 0)])


def body_heads(
    tokens, restype, type_table, key_mask, pair, w_bias, w_query, w_key, w_value, w_gate, cotangent
):
    n_row = lax.axis_size("row")
    n_col = lax.axis_size("col")
    n_samp = lax.axis_size("samp")
    samp_dev = tokens.shape[0]
    tok_col = tokens.shape[1]
    row_count = pair.shape[0]
    total_tokens = tok_col * n_col
    half = samp_dev // n_row
    row_index = lax.axis_index("row")
    row = row_index.astype(jnp.int32).reshape(1)
    col = lax.axis_index("col").astype(jnp.int32).reshape(1)
    types = restype.reshape(1, tok_col)
    weight_t = w_bias.T
    weights = (w_query, w_key, w_value, w_gate)
    samples = samp_dev * n_samp

    def send(block, offset):
        return lax.ppermute(block, "col", [(c, c ^ offset) for c in range(n_col)])

    def by_chip(blocks):
        return [blocks[0]] + [send(blocks[n], 2 * n) for n in range(1, n_col // 2)]

    def across(blocks):
        return send(jnp.stack([block[1] for block in blocks]), 1)

    messages = token_messages(
        row, col, tokens, types, type_table, weights, cotangent, n_row, n_col
    )
    arrived = by_chip(messages)
    bias = pair_bias(pair, weight_t, key_mask.reshape(1, tok_col))
    bias, arrived, types = lax.optimization_barrier(
        (bias.astype(jnp.float16), arrived, types)
    )
    own = own_rows(row, tokens, types, type_table, w_gate, cotangent, half)
    bias = lax.all_to_all(bias, ("row", "col"), 0, 0, tiled=True)
    other = across(arrived)
    bias, other, own = lax.optimization_barrier((bias, other, own))

    back, grad_bias = attention(col, arrived, other, bias.astype(jnp.float32), n_row)
    grad_bias = lax.all_to_all(
        grad_bias.astype(jnp.float16), ("row", "col"), 0, 0, tiled=True
    )
    back, late_pair = lax.optimization_barrier((back.astype(jnp.float16), pair))
    pair_normed, pair_inv = pair_units(late_pair)
    back, _, pair_normed = lax.optimization_barrier((back, grad_bias, pair_normed))
    back = lax.all_to_all(back, ("row", "col"), 0, 0, tiled=True)

    other_bias = swap(grad_bias, "samp")
    own_bias = unscaled(grad_bias, tok_col)
    part = pair_weight(pair_normed, own_bias)
    samp_part = swap(part, "samp")
    row_part = swap(part, "row")
    both_part = lax.ppermute(part, ("samp", "row"), [(n, 3 - n) for n in range(4)])
    other_bias, part = lax.optimization_barrier((other_bias, part))
    grads = own_bias + unscaled(other_bias, tok_col)
    part = (part + samp_part) + (row_part + both_part)
    grads, part = lax.optimization_barrier((grads, part))
    sums = (send(part, 1), send(part, 2), send(part, 3))
    pair_grad = pair_backward(
        pair.shape, pair_normed, pair_inv, grads, weight_t, total_tokens / samples
    )

    pair_grad, back, sums = lax.optimization_barrier((pair_grad, back, sums))
    part = (part + sums[0]) + (sums[1] + sums[2])
    last = send(part, 4)
    token_half = token_back(back.astype(jnp.float32), *own, weights)
    token_half, last = lax.optimization_barrier((token_half, last))
    part = part + last
    token_half = token_half.reshape(half, tok_col, D)
    other_half = swap(token_half, "row")
    first = row_index == 0
    token_grad = jnp.concatenate(
        [jnp.where(first, token_half, other_half), jnp.where(first, other_half, token_half)],
        axis=0,
    )
    return (token_grad, pair_grad, part.T / samples)


def body(*args):
    n_row = lax.axis_size("row")
    n_col = lax.axis_size("col")
    tokens = args[0]
    pair = args[4]
    fits = n_row == 2 and n_col == 8 and n_row * n_col == H and lax.axis_size("samp") == 2
    square = pair.shape[0] * n_row == pair.shape[1] * n_col
    if fits and square and tokens.shape[0] == 4 and tokens.shape[1] == 64:
        return body_heads(*args)
    return body_any(*args)


def solution(mesh):
    placed = (
        P("samp", "col", None),
        P("col"),
        P(),
        P("col"),
        P("row", "col", None),
        P(),
        P(),
        P(),
        P(),
        P(),
        P("samp", "col", None),
    )
    return jax.shard_map(
        body,
        mesh=mesh,
        in_specs=placed,
        out_specs=(P("samp", "col", None), P("row", "col", None), P()),
        check_vma=False,
    )
```

```python
import math

import jax
import jax.numpy as jnp
from jax import lax
from jax.experimental import pallas as pl
from jax.experimental.pallas import tpu as pltpu
from jax.sharding import PartitionSpec as P

D = 768
H = 16
CH = 48
NTYPE = 32


def broadcast(block, axis, source):
    block = jnp.where(lax.axis_index(axis) == source, block, jnp.zeros_like(block))
    return lax.psum(block, axis)


def token_norm(tokens, restype, type_table):
    onehot = (restype[:, None] == jnp.arange(NTYPE, dtype=jnp.int32)[None, :]).astype(jnp.bfloat16)
    embedded = tokens.astype(jnp.float32) + jnp.dot(
        onehot, type_table, preferred_element_type=jnp.float32
    )
    centred = embedded - jnp.mean(embedded, axis=-1, keepdims=True)
    inv_std = lax.rsqrt(jnp.mean(centred * centred, axis=-1, keepdims=True) + 1e-05)
    return (centred * inv_std, inv_std)


def pair_norm(block):
    values = block.astype(jnp.float32)
    centred = values - jnp.mean(values, axis=-1, keepdims=True)
    inv_std = lax.rsqrt(jnp.mean(centred * centred, axis=-1, keepdims=True) + 1e-05)
    return (centred * inv_std, inv_std)


def norm_back(grad_in, normed, inv_std):
    return inv_std * (
        grad_in
        - jnp.mean(grad_in, axis=-1, keepdims=True)
        - normed * jnp.mean(grad_in * normed, axis=-1, keepdims=True)
    )


def project(rows_in, weight):
    return jnp.einsum("std,de->ste", rows_in, weight, preferred_element_type=jnp.float32).astype(
        jnp.bfloat16
    )


def back_project(grads, weight):
    return jnp.einsum(
        "ste,de->std", grads, weight.astype(jnp.float32), precision=lax.Precision.HIGHEST
    )


def pair_back(grad_bias, pair_normed, pair_inv, bias_weight):
    grad_normed = jnp.einsum("hij,ch->ijc", grad_bias, bias_weight, precision=lax.Precision.HIGHEST)
    return norm_back(grad_normed, pair_normed, pair_inv)


def body_any(
    tokens, restype, type_table, key_mask, pair, w_bias, w_query, w_key, w_value, w_gate, cotangent
):
    n_row = lax.axis_size("row")
    n_col = lax.axis_size("col")
    n_samp = lax.axis_size("samp")
    samp_dev = tokens.shape[0]
    tok_col = tokens.shape[1]
    spread = n_col // n_row
    row_count = tok_col * spread
    total_tokens = tok_col * n_col
    row_index = lax.axis_index("row")
    col_index = lax.axis_index("col")
    is_owner = col_index // spread == row_index
    own_start = col_index % spread * tok_col
    normed, inv_std = token_norm(tokens, restype, type_table)
    own_act = normed.astype(jnp.bfloat16)
    key_proj = project(own_act, w_key)
    value_proj = project(own_act, w_value)
    stacked = jnp.stack([own_act, cotangent])
    pieces = [broadcast(stacked, "col", row_index * spread + member) for member in range(spread)]
    gathered = jnp.concatenate(pieces, axis=2)
    query_side = gathered[0]
    grad_rows = gathered[1]
    queries = project(query_side, w_query)
    gate_lin = project(query_side, w_gate)
    pair_normed, pair_inv = pair_norm(pair)
    bias_weight = w_bias.astype(jnp.float32)
    bias = jnp.einsum("ijc,ch->hij", pair_normed, bias_weight, precision=lax.Precision.HIGHEST)
    query_heads = queries.reshape(samp_dev, row_count, H, CH)
    key_heads = key_proj.reshape(samp_dev, tok_col, H, CH)
    value_heads = value_proj.reshape(samp_dev, tok_col, H, CH)
    scores = (
        jnp.einsum("sihc,sjhc->shij", query_heads, key_heads, preferred_element_type=jnp.float32)
        / math.sqrt(CH)
        + bias[None]
    )
    scores = jnp.where(key_mask[None, None, None, :] == 1, scores, -1000000000.0)
    top = lax.pmax(jnp.max(scores, axis=-1), "col")
    expo = jnp.exp(scores - top[..., None])
    partial_out = jnp.einsum(
        "shij,sjhc->sihc",
        expo.astype(jnp.bfloat16),
        value_heads,
        preferred_element_type=jnp.float32,
    )
    totals, summed = lax.psum(
        (jnp.sum(expo, axis=-1), partial_out.reshape(samp_dev, row_count, D)), "col"
    )
    attended = (
        summed.reshape(samp_dev, row_count, H, CH) / jnp.transpose(totals, (0, 2, 1))[..., None]
    )
    flat_out = attended.reshape(samp_dev, row_count, D)
    sig_gate = jax.nn.sigmoid(gate_lin.astype(jnp.float32))
    grad_f = grad_rows.astype(jnp.float32)
    grad_out = (grad_f * sig_gate).astype(jnp.bfloat16)
    grad_gate = (grad_f * flat_out * sig_gate * (1.0 - sig_gate)).astype(jnp.bfloat16)
    gate_piece = lax.dynamic_slice_in_dim(grad_gate, own_start, tok_col, 1)
    gate_term = jnp.where(
        is_owner,
        jnp.einsum("ste,de->std", gate_piece, w_gate, preferred_element_type=jnp.float32),
        0.0,
    )
    grad_heads = grad_out.reshape(samp_dev, row_count, H, CH)
    delta = jnp.transpose(jnp.sum(grad_heads.astype(jnp.float32) * attended, axis=-1), (0, 2, 1))
    probs = expo / totals[..., None]
    grad_pre = jnp.einsum(
        "sihc,sjhc->shij", grad_heads, value_heads, preferred_element_type=jnp.float32
    )
    grad_scores = probs * (grad_pre - delta[..., None])
    rounded = grad_scores.astype(jnp.bfloat16)
    grad_query = (
        jnp.einsum("shij,sjhc->sihc", rounded, key_heads, preferred_element_type=jnp.float32)
        / math.sqrt(CH)
    ).reshape(samp_dev, row_count, D)
    grad_key = (
        jnp.einsum("shij,sihc->sjhc", rounded, query_heads, preferred_element_type=jnp.float32)
        / math.sqrt(CH)
    ).reshape(samp_dev, tok_col, D)
    grad_value = jnp.einsum(
        "shij,sihc->sjhc",
        probs.astype(jnp.bfloat16),
        grad_heads,
        preferred_element_type=jnp.float32,
    ).reshape(samp_dev, tok_col, D)
    bias_local = jnp.sum(grad_scores, axis=0)
    blank = jnp.zeros((samp_dev, total_tokens, D), jnp.float32)
    mine = lax.psum_scatter(
        lax.dynamic_update_slice_in_dim(blank, grad_query, row_index * row_count, 1),
        "col",
        scatter_dimension=1,
        tiled=True,
    )
    query_all, key_all, value_all, gate_all = lax.psum(
        (mine, grad_key, grad_value, gate_term), "row"
    )
    grad_act = (
        back_project(query_all, w_query)
        + back_project(key_all, w_key)
        + back_project(value_all, w_value)
        + gate_all
    )
    token_grad = norm_back(grad_act, normed, inv_std).astype(jnp.bfloat16)
    samples = samp_dev * n_samp
    grad_bias = lax.psum(bias_local, "samp")
    grad_pair = pair_back(grad_bias, pair_normed, pair_inv, bias_weight)
    pair_grad = (grad_pair * (total_tokens / samples)).astype(jnp.bfloat16)
    weight_part = jnp.einsum("ijc,hij->ch", pair_normed, grad_bias, precision=lax.Precision.HIGHEST)
    weight_sum = lax.psum(weight_part, ("row", "col"))
    bias_weight_grad = weight_sum / samples
    return (token_grad, pair_grad, bias_weight_grad)


EPS = 1e-05
SCALE = 1.0 / math.sqrt(CH)
NT = (((1,), (1,)), ((), ()))
TN = (((0,), (0,)), ((), ()))
MASKED = -65504.0


def params(megabytes):
    return pltpu.CompilerParams(vmem_limit_bytes=megabytes * 1024 * 1024)


def matmul(left, right):
    return jnp.dot(left, right, preferred_element_type=jnp.float32)


def matmul_nt(left, right):
    return lax.dot_general(left, right, NT, preferred_element_type=jnp.float32)


def matmul_tn(left, right):
    return lax.dot_general(left, right, TN, preferred_element_type=jnp.float32)


def halves(values):
    high = values.astype(jnp.bfloat16)
    low = (values - high.astype(jnp.float32)).astype(jnp.bfloat16)
    return high, low


def unit_rows(values):
    centred = values - jnp.mean(values, axis=-1, keepdims=True)
    inv_std = lax.rsqrt(jnp.mean(centred * centred, axis=-1, keepdims=True) + EPS)
    return centred * inv_std, inv_std


def embed_rows(tokens_ref, types_ref, table_ref):
    count, length, width = tokens_ref.shape
    index = lax.broadcasted_iota(jnp.int32, (NTYPE, length), 0)
    onehot = jnp.where(types_ref[...] == index, 1.0, 0.0).astype(jnp.bfloat16)
    added = matmul_tn(onehot, table_ref[...])
    embedded = tokens_ref[...].astype(jnp.float32) + added[None]
    return unit_rows(embedded.reshape(count * length, width))


def token_kernel(row_ref, col_ref, tokens_ref, types_ref, table_ref, *refs):
    wq_ref, wk_ref, wv_ref, wg_ref, cot_ref = refs[:5]
    out_refs, side_ref = refs[5:-1], refs[-1]
    normed, _ = embed_rows(tokens_ref, types_ref, table_ref)
    act = normed.astype(jnp.bfloat16)
    for slot, ref in enumerate((wq_ref, wk_ref, wv_ref)):
        side_ref[slot] = matmul(act, ref[...]).astype(jnp.bfloat16).T
    gate = matmul(act, wg_ref[...]).astype(jnp.bfloat16).astype(jnp.float32)
    cot = cot_ref[...].reshape(gate.shape).astype(jnp.float32)
    side_ref[3] = (cot * jax.nn.sigmoid(gate)).astype(jnp.bfloat16).T
    for offset, out_ref in enumerate(out_refs):
        for core in range(2):
            start = pl.multiple_of((col_ref[0] ^ (2 * offset + core)) * CH, 16)
            out_ref[core] = side_ref[:, pl.ds(start, CH), :]


def token_messages(row, col, tokens, types, table, weights, cotangent, n_row, n_col):
    samp_dev, tok_col, _ = tokens.shape
    width = D // n_row
    held = samp_dev * tok_col
    whole3 = lambda i, r, c: (0, 0, 0)
    whole2 = lambda i, r, c: (0, 0)
    weight_spec = pl.BlockSpec((D, width), lambda i, r, c: (0, r[0]))
    shape = (2, 4, CH, held)
    count = n_col // 2
    return pl.pallas_call(
        token_kernel,
        out_shape=[jax.ShapeDtypeStruct(shape, jnp.bfloat16)] * count,
        grid_spec=pltpu.PrefetchScalarGridSpec(
            num_scalar_prefetch=2,
            grid=(1,),
            in_specs=[
                pl.BlockSpec(tokens.shape, whole3),
                pl.BlockSpec(types.shape, whole2),
                pl.BlockSpec(table.shape, whole2),
                weight_spec,
                weight_spec,
                weight_spec,
                weight_spec,
                pl.BlockSpec((samp_dev, tok_col, width), lambda i, r, c: (0, 0, r[0])),
            ],
            out_specs=[pl.BlockSpec(shape, lambda i, r, c: (0, 0, 0, 0))] * count,
            scratch_shapes=[pltpu.VMEM((4, width, held), jnp.bfloat16)],
        ),
        compiler_params=params(56),
        cost_estimate=pl.CostEstimate(
            flops=4_000_000_000, bytes_accessed=4_000_000, transcendentals=0
        ),
        name="token_messages",
    )(row, col, tokens, types, table, *weights, cotangent)


def own_kernel(
    row_ref, tokens_ref, types_ref, table_ref, wg_ref, cot_ref, slope_ref, normed_ref, inv_ref
):
    normed, inv_std = embed_rows(tokens_ref, types_ref, table_ref)
    gate = matmul(normed.astype(jnp.bfloat16), wg_ref[...]).astype(jnp.bfloat16)
    sig = jax.nn.sigmoid(gate.astype(jnp.float32))
    cot = cot_ref[...].reshape(gate.shape).astype(jnp.float32)
    slope_ref[...] = (cot * sig * (1.0 - sig)).T
    normed_ref[...] = normed.T
    inv_ref[...] = jnp.broadcast_to(inv_std, (inv_std.shape[0], 128)).T[:8]


def own_rows(row, tokens, types, table, w_gate, cotangent, half):
    _, tok_col, _ = tokens.shape
    count = half * tok_col
    part_spec = pl.BlockSpec((half, tok_col, D), lambda i, r: (r[0], 0, 0))
    whole2 = lambda i, r: (0, 0)
    return pl.pallas_call(
        own_kernel,
        out_shape=[
            jax.ShapeDtypeStruct((D, count), jnp.float32),
            jax.ShapeDtypeStruct((D, count), jnp.float32),
            jax.ShapeDtypeStruct((8, count), jnp.float32),
        ],
        grid_spec=pltpu.PrefetchScalarGridSpec(
            num_scalar_prefetch=1,
            grid=(1,),
            in_specs=[
                part_spec,
                pl.BlockSpec(types.shape, whole2),
                pl.BlockSpec(table.shape, whole2),
                pl.BlockSpec(w_gate.shape, whole2),
                part_spec,
            ],
            out_specs=[
                pl.BlockSpec((D, count), whole2),
                pl.BlockSpec((D, count), whole2),
                pl.BlockSpec((8, count), whole2),
            ],
        ),
        compiler_params=params(56),
        cost_estimate=pl.CostEstimate(
            flops=3_000_000_000, bytes_accessed=3_000_000, transcendentals=0
        ),
        name="own_rows",
    )(row, tokens, types, table, w_gate, cotangent)


MANY = 4
PARTS = 2


def pair_columns(pair_ref, k, many):
    _, _, length, width = pair_ref.shape
    blocks = [pair_ref[p, pl.ds(k, many)] for p in range(2)]
    rows = jnp.concatenate(blocks, axis=1).reshape(many * 2 * length, width)
    same = lax.broadcasted_iota(jnp.int32, (width, width), 0) == lax.broadcasted_iota(
        jnp.int32, (width, width), 1
    )
    centring = (jnp.where(same, 1.0, 0.0) - 1.0 / width).astype(jnp.bfloat16)
    centred = matmul_nt(centring, rows)
    return centred, lax.rsqrt(jnp.mean(centred * centred, axis=0, keepdims=True) + EPS)


def bias_kernel(pair_ref, weight_ref, mask_ref, out_ref, flat_ref):
    _, count, length, width = pair_ref.shape
    whole = flat_ref.shape[0] // H
    weight = jnp.concatenate([weight_ref[...]] * 2, axis=1)
    base = pl.program_id(0) * count

    def step(n, carry):
        k = n * MANY
        centred, inv_std = pair_columns(pair_ref, k, MANY)
        bias = matmul(weight, jnp.concatenate(halves(centred), axis=0)) * inv_std
        for m in range(MANY):
            lanes = slice(m * 2 * length, (m + 1) * 2 * length)
            flat_ref[pl.ds(base + k + m, H, stride=whole), :] = bias[:, lanes]
        return carry

    lax.fori_loop(0, count // MANY, step, 0, unroll=2)

    @pl.when(pl.program_id(0) == pl.num_programs(0) - 1)
    def _():
        keep = jnp.broadcast_to(mask_ref[...].astype(jnp.float32), (128, length)).T
        keep = jnp.concatenate([keep] * (2 * whole // 128), axis=1) == 1.0
        for h in range(H):
            turned = flat_ref[h * whole : (h + 1) * whole, :].T
            bias = jnp.concatenate([turned[:length], turned[length:]], axis=1)
            out_ref[h] = jnp.where(keep, bias, MASKED)


STEPS = 4


def split_spec(shape):
    block = (shape[0] // STEPS,) + tuple(shape[1:])
    return pl.BlockSpec(block, lambda i: (i,) + (0,) * (len(shape) - 1))


def whole_spec(shape):
    return pl.BlockSpec(tuple(shape), lambda i: (0,) * len(shape))


def pair_spec(pair):
    row_count, tok_col, width = pair.shape
    block = (2, row_count // 2 // STEPS, tok_col, width)
    return pl.BlockSpec(block, lambda i: (0, i, 0, 0))


def pair_bias(pair, weight_t, mask):
    row_count, tok_col, width = pair.shape
    whole = row_count // 2
    return pl.pallas_call(
        bias_kernel,
        out_shape=jax.ShapeDtypeStruct((H, tok_col, row_count), jnp.float32),
        grid=(STEPS,),
        in_specs=[pair_spec(pair), whole_spec(weight_t.shape), whole_spec(mask.shape)],
        out_specs=whole_spec((H, tok_col, row_count)),
        scratch_shapes=[pltpu.VMEM((H * whole, 2 * tok_col), jnp.float32)],
        compiler_params=params(24),
        cost_estimate=pl.CostEstimate(
            flops=6_000_000_000, bytes_accessed=5_000_000, transcendentals=0
        ),
        name="pair_bias",
    )(pair.reshape(2, whole, tok_col, width), weight_t, mask)


def norm_kernel(pair_ref, normed_ref, inv_ref):
    def step(n, carry):
        centred, inv_std = pair_columns(pair_ref, n * MANY, MANY)
        normed_ref[n] = jnp.concatenate(halves(centred * inv_std), axis=0)
        inv_ref[n] = jnp.broadcast_to(inv_std, inv_ref.shape[1:])
        return carry

    lax.fori_loop(0, normed_ref.shape[0], step, 0, unroll=2)


def pair_units(pair):
    row_count, tok_col, width = pair.shape
    whole = row_count // 2
    chunks, lanes = whole // MANY, MANY * 2 * tok_col
    shapes = [(chunks, 2 * width, lanes), (chunks, 8, lanes)]
    return pl.pallas_call(
        norm_kernel,
        out_shape=[
            jax.ShapeDtypeStruct(shapes[0], jnp.bfloat16),
            jax.ShapeDtypeStruct(shapes[1], jnp.float32),
        ],
        grid=(STEPS,),
        in_specs=[pair_spec(pair)],
        out_specs=[split_spec(shape) for shape in shapes],
        compiler_params=params(56),
        cost_estimate=pl.CostEstimate(
            flops=6_000_000_000, bytes_accessed=12_000_000, transcendentals=0
        ),
        name="pair_units",
    )(pair.reshape(2, whole, tok_col, width))


def shift_of(top):
    return jnp.floor(jnp.clip(14.0 - jnp.log2(top), -100.0, 100.0))


def attention_kernel(col_ref, *refs):
    other_ref, bias_ref, back_ref, grad_bias_ref, sum_ref, tokens_ref = refs[-6:]
    col = col_ref[0]
    for offset, ref in enumerate(refs[:-6]):
        tokens_ref[col ^ (2 * offset)] = ref[0]
        tokens_ref[col ^ (2 * offset + 1)] = other_ref[offset]
    n_col = tokens_ref.shape[0]
    tok_col, row_count = bias_ref.shape[1:]
    half = back_ref.shape[2] // tok_col
    n_row = bias_ref.shape[0] // n_col
    step = pl.program_id(0)

    @pl.when(step == 0)
    def _():
        sum_ref[...] = jnp.zeros_like(sum_ref)

    outs = []
    for sample in range(half):
        lanes = slice(sample * tok_col, (sample + 1) * tok_col)

        def side(slot):
            return jnp.concatenate([tokens_ref[c, slot, :, lanes] for c in range(n_col)], axis=1)

        query_t, key_t, value_t, grad_t = [side(slot) for slot in range(4)]
        key = key_t.T
        value = value_t.T
        attended_parts, grad_query_parts = [], []
        grad_key = jnp.zeros(key_t.shape, jnp.float32)
        grad_value = jnp.zeros(key_t.shape, jnp.float32)
        for block in range(n_row):
            cols = slice(block * row_count, (block + 1) * row_count)
            heads = slice(block * n_col, (block + 1) * n_col)
            bias = bias_ref[heads].reshape(n_col * tok_col, row_count)
            query_b = query_t[:, cols]
            grad_b = grad_t[:, cols]
            scores = matmul(key, query_b) * SCALE + bias
            scores = jnp.where(bias < -60000.0, -1000000000.0, scores)
            expo = jnp.exp(scores - jnp.max(scores, axis=0, keepdims=True))
            share = 1.0 / jnp.sum(expo, axis=0, keepdims=True)
            attended = matmul(value_t, expo.astype(jnp.bfloat16)) * share
            delta = jnp.sum(grad_b.astype(jnp.float32) * attended, axis=0, keepdims=True)
            probs = expo * share
            grad_scores = probs * (matmul(value, grad_b) - delta)
            rounded = grad_scores.astype(jnp.bfloat16)
            attended_parts.append(attended)
            grad_query_parts.append(matmul(key_t, rounded) * SCALE)
            grad_key = grad_key + matmul_nt(query_b, rounded)
            grad_value = grad_value + matmul_nt(grad_b, probs.astype(jnp.bfloat16))
            sum_ref[heads] += grad_scores.reshape(n_col, tok_col, row_count)
        outs.append(
            (
                jnp.concatenate(grad_query_parts, axis=1),
                grad_key * SCALE,
                grad_value,
                jnp.concatenate(attended_parts, axis=1),
            )
        )
    spare = jnp.zeros((8 - 4, half * tok_col), jnp.float32)
    tops = [jnp.max(jnp.abs(out[slot]), axis=0, keepdims=True) for slot in range(4) for out in outs]
    shifts = shift_of(jnp.concatenate(tops, axis=0))
    scales = jnp.exp2(shifts)
    scaled = [
        [out[slot] * scales[slot * half + n : slot * half + n + 1] for n, out in enumerate(outs)]
        for slot in range(4)
    ]
    for c in range(n_col):
        lanes = slice(c * tok_col, (c + 1) * tok_col)
        for slot in range(4):
            back_ref[c, slot * CH : (slot + 1) * CH, :] = jnp.concatenate(
                [part[:, lanes] for part in scaled[slot]], axis=1
            )
        tails = [
            jnp.concatenate([shifts[slot * half + n :, lanes][:1] for n in range(half)], axis=1)
            for slot in range(4)
        ]
        back_ref[c, 4 * CH :, :] = jnp.concatenate(tails + [spare], axis=0)

    @pl.when(step == pl.num_programs(0) - 1)
    def _():
        piece = row_count // 2 // PARTS
        for head in range(n_row * n_col):
            sums = sum_ref[head]
            sums = jnp.concatenate(
                [
                    sums[:, (p * PARTS + n) * piece : (p * PARTS + n + 1) * piece]
                    for n in range(PARTS)
                    for p in range(2)
                ],
                axis=1,
            )
            shift = shift_of(jnp.max(jnp.abs(sums), axis=0, keepdims=True))
            grad_bias_ref[head, :tok_col, :] = sums * jnp.exp2(shift)
            grad_bias_ref[head, tok_col:, :] = jnp.broadcast_to(shift, (8, row_count))


def attention(col, arrived, other, bias, n_row):
    count = len(arrived)
    n_col = 2 * count
    _, tok_col, row_count = bias.shape
    half = arrived[0].shape[-1] // tok_col // n_row
    width = half * tok_col
    back_shape = (n_row * n_col, 4 * CH + 8, width)
    bias_shape = (n_row * n_col, tok_col + 8, row_count)
    return pl.pallas_call(
        attention_kernel,
        out_shape=[
            jax.ShapeDtypeStruct(back_shape, jnp.float32),
            jax.ShapeDtypeStruct(bias_shape, jnp.float32),
        ],
        grid_spec=pltpu.PrefetchScalarGridSpec(
            num_scalar_prefetch=1,
            grid=(n_row,),
            in_specs=[pl.BlockSpec((1, 4, CH, width), lambda i, r: (0, 0, 0, i))] * count
            + [
                pl.BlockSpec((count, 4, CH, width), lambda i, r: (0, 0, 0, i)),
                pl.BlockSpec(bias.shape, lambda i, r: (0, 0, 0)),
            ],
            out_specs=[
                pl.BlockSpec((n_col, 4 * CH + 8, width), lambda i, r: (i, 0, 0)),
                pl.BlockSpec(bias_shape, lambda i, r: (0, 0, 0)),
            ],
            scratch_shapes=[
                pltpu.VMEM(bias.shape, jnp.float32),
                pltpu.VMEM((n_col, 4, CH, width), jnp.bfloat16),
            ],
        ),
        compiler_params=params(24),
        cost_estimate=pl.CostEstimate(
            flops=8_000_000_000, bytes_accessed=6_000_000, transcendentals=1_000_000
        ),
        name="attention",
    )(col, *arrived, other, bias)


def back_kernel(*refs):
    slope_ref, normed_ref, inv_ref, wq_ref, wk_ref, wv_ref, wg_ref = refs[-11:-4]
    out_ref, parts_ref, gate_ref, total_ref = refs[-4:]
    back_ref = refs[0]
    count = normed_ref.shape[-1]
    step = pl.program_id(0)
    rows = wq_ref.shape[0]

    @pl.when(step == 0)
    def _():
        for slot in range(4):
            scale = jnp.exp2(-back_ref[:, 4 * CH + slot : 4 * CH + slot + 1, :])
            values = back_ref[:, slot * CH : (slot + 1) * CH, :] * scale
            values = values.reshape(gate_ref.shape)
            if slot < 3:
                parts_ref[slot] = jnp.concatenate(halves(values), axis=1)
            else:
                gate_ref[...] = (values * slope_ref[...]).astype(jnp.bfloat16)

    total = matmul(wg_ref[...], gate_ref[...])
    for slot, ref in enumerate((wq_ref, wk_ref, wv_ref)):
        parts = matmul(ref[...], parts_ref[slot])
        total = total + (parts[:, :count] + parts[:, count:])
    total_ref[pl.ds(pl.multiple_of(step * rows, 8), rows), :] = total

    @pl.when(step == pl.num_programs(0) - 1)
    def _():
        whole = total_ref[...]
        normed = normed_ref[...]
        result = inv_ref[:1] * (
            whole
            - jnp.mean(whole, axis=0, keepdims=True)
            - normed * jnp.mean(whole * normed, axis=0, keepdims=True)
        )
        out_ref[...] = result.T.astype(jnp.bfloat16)


def token_back(back, slope, normed, inv_std, weights):
    count = normed.shape[-1]
    steps = 2
    whole = lambda shape: pl.BlockSpec(shape, lambda i: (0,) * len(shape))
    weight_spec = pl.BlockSpec((D // steps, D), lambda i: (i, 0))
    return pl.pallas_call(
        back_kernel,
        out_shape=jax.ShapeDtypeStruct((count, D), jnp.bfloat16),
        grid=(steps,),
        in_specs=[whole(array.shape) for array in (back, slope, normed, inv_std)]
        + [weight_spec] * 4,
        out_specs=whole((count, D)),
        scratch_shapes=[
            pltpu.VMEM((3, D, 2 * count), jnp.bfloat16),
            pltpu.VMEM((D, count), jnp.bfloat16),
            pltpu.VMEM((D, count), jnp.float32),
        ],
        compiler_params=params(40),
        cost_estimate=pl.CostEstimate(
            flops=4_000_000_000, bytes_accessed=8_000_000, transcendentals=0
        ),
        name="token_back",
    )(back, slope, normed, inv_std, *weights)


def flatten(grads_ref, flat_ref):
    whole = flat_ref.shape[0] // H
    for h in range(H):
        grads = grads_ref[h]
        both = jnp.concatenate([grads[:, :whole], grads[:, whole:]], axis=0)
        flat_ref[h * whole : (h + 1) * whole, :] = both.T


def flat_columns(flat_ref, k, many):
    whole = flat_ref.shape[0] // H
    grads = [flat_ref[pl.ds(k + m, H, stride=whole), :] for m in range(many)]
    return jnp.concatenate(halves(jnp.concatenate(grads, axis=1)), axis=0)


def pair_back_kernel(factor, normed_ref, inv_ref, grads_ref, weight_ref, *refs):
    out_ref, part_ref, flat_ref = refs[-3:]
    _, count, length, width = out_ref.shape
    weight = weight_ref[...].astype(jnp.float32)
    weight = halves(weight - jnp.mean(weight, axis=1, keepdims=True))
    weight = jnp.concatenate([weight[0], weight[0], weight[1], weight[1]], axis=0).T
    base = pl.program_id(0) * count

    @pl.when(pl.program_id(0) == 0)
    def _():
        part_ref[...] = jnp.zeros_like(part_ref)
        flatten(grads_ref, flat_ref)

    def step(n, carry):
        k = n * MANY
        both = normed_ref[n]
        normed = both[:width].astype(jnp.float32) + both[width:].astype(jnp.float32)
        grads = flat_columns(flat_ref, base + k, MANY)
        grad_in = matmul(weight, jnp.concatenate([grads, grads], axis=0))
        overlap = jnp.mean(grad_in * normed, axis=0, keepdims=True)
        result = (grad_in - normed * overlap) * (inv_ref[n, :1] * factor)
        result = result.astype(jnp.bfloat16).T.reshape(MANY, 2 * length, width)
        for p in range(2):
            out_ref[p, pl.ds(k, MANY)] = result[:, p * length : (p + 1) * length]
        return carry + matmul_nt(both, grads)

    parts = jnp.zeros((2 * width, 2 * H), jnp.float32)
    parts = lax.fori_loop(0, count // MANY, step, parts, unroll=2)
    parts = parts[:, :H] + parts[:, H:]
    part_ref[...] += (parts[:width] + parts[width:]).T


def pair_backward(number, so_far, shape, normed, inv_std, grads, weight_t, factor):
    row_count, tok_col, width = shape
    whole = row_count // 2
    steps = STEPS // PARTS
    first = number * steps

    def split(shape):
        block = (shape[0] // STEPS,) + tuple(shape[1:])
        return pl.BlockSpec(block, lambda i: (i + first,) + (0,) * (len(shape) - 1))

    previous = [] if so_far is None else [so_far]
    return pl.pallas_call(
        lambda *refs: pair_back_kernel(factor, *refs),
        out_shape=[
            jax.ShapeDtypeStruct((2, whole, tok_col, width), jnp.bfloat16),
            jax.ShapeDtypeStruct((H, width), jnp.float32),
        ],
        grid=(steps,),
        in_specs=[
            split(normed.shape),
            split(inv_std.shape),
            whole_spec(grads.shape),
            whole_spec(weight_t.shape),
        ]
        + [pl.BlockSpec(memory_space=pl.ANY)] * len(previous),
        out_specs=[
            pl.BlockSpec((2, whole // STEPS, tok_col, width), lambda i: (0, i + first, 0, 0)),
            whole_spec((H, width)),
        ],
        scratch_shapes=[pltpu.VMEM((H * whole // PARTS, 2 * tok_col), jnp.float32)],
        input_output_aliases={4: 0} if previous else {},
        compiler_params=params(24),
        cost_estimate=pl.CostEstimate(
            flops=6_000_000_000, bytes_accessed=100_000, transcendentals=0
        ),
        name="pair_backward",
    )(normed, inv_std, grads, weight_t, *previous)


def unscaled(block, rows):
    block = block.astype(jnp.float32)
    return block[:, :rows] * jnp.exp2(-block[:, rows : rows + 1])


def swap(block, axis):
    return lax.ppermute(block, axis, [(0, 1), (1, 0)])


def body_heads(
    tokens, restype, type_table, key_mask, pair, w_bias, w_query, w_key, w_value, w_gate, cotangent
):
    n_row = lax.axis_size("row")
    n_col = lax.axis_size("col")
    n_samp = lax.axis_size("samp")
    samp_dev = tokens.shape[0]
    tok_col = tokens.shape[1]
    row_count = pair.shape[0]
    total_tokens = tok_col * n_col
    half = samp_dev // n_row
    row_index = lax.axis_index("row")
    row = row_index.astype(jnp.int32).reshape(1)
    col = lax.axis_index("col").astype(jnp.int32).reshape(1)
    types = restype.reshape(1, tok_col)
    weight_t = w_bias.T
    weights = (w_query, w_key, w_value, w_gate)
    samples = samp_dev * n_samp

    def send(block, offset):
        return lax.ppermute(block, "col", [(c, c ^ offset) for c in range(n_col)])

    def by_chip(blocks):
        return [blocks[0]] + [send(blocks[n], 2 * n) for n in range(1, n_col // 2)]

    def across(blocks):
        return send(jnp.stack([block[1] for block in blocks]), 1)

    messages = token_messages(
        row, col, tokens, types, type_table, weights, cotangent, n_row, n_col
    )
    arrived = by_chip(messages)
    bias = pair_bias(pair, weight_t, key_mask.reshape(1, tok_col))
    bias, arrived, types = lax.optimization_barrier(
        (bias.astype(jnp.float16), arrived, types)
    )
    own = own_rows(row, tokens, types, type_table, w_gate, cotangent, half)
    bias = lax.all_to_all(bias, ("row", "col"), 0, 0, tiled=True)
    other = across(arrived)
    bias, other, own = lax.optimization_barrier((bias, other, own))

    back, grad_bias = attention(col, arrived, other, bias.astype(jnp.float32), n_row)
    grad_bias = lax.all_to_all(
        grad_bias.astype(jnp.float16), ("row", "col"), 0, 0, tiled=True
    )
    back, late_pair = lax.optimization_barrier((back.astype(jnp.float16), pair))
    pair_normed, pair_inv = pair_units(late_pair)
    back, _, pair_normed = lax.optimization_barrier((back, grad_bias, pair_normed))
    back = lax.all_to_all(back, ("row", "col"), 0, 0, tiled=True)

    pair_grad, part = None, 0.0
    pieces = jnp.split(grad_bias, PARTS, axis=2)
    others = [swap(piece, "samp") for piece in pieces]
    for n, (piece, other) in enumerate(zip(pieces, others)):
        grads = unscaled(piece, tok_col) + unscaled(other, tok_col)
        pair_grad, more = pair_backward(
            n, pair_grad, pair.shape, pair_normed, pair_inv, grads, weight_t,
            total_tokens / samples,
        )
        part = part + more
    pair_grad = pair_grad.reshape(pair.shape)

    pair_grad, back, part = lax.optimization_barrier((pair_grad, back, part))
    flip = [(n, n ^ (n_col + 1)) for n in range(n_row * n_col)]
    sums = (swap(part, "row"), send(part, 1), lax.ppermute(part, ("row", "col"), flip))
    token_half = token_back(back.astype(jnp.float32), *own, weights)
    token_half, sums = lax.optimization_barrier((token_half, sums))
    token_half = token_half.reshape(half, tok_col, D)
    other_half = swap(token_half, "row")
    part = (part + sums[0]) + (sums[1] + sums[2])
    part = (part + send(part, 2)) + (send(part, 4) + send(part, 6))
    first = row_index == 0
    token_grad = jnp.concatenate(
        [jnp.where(first, token_half, other_half), jnp.where(first, other_half, token_half)],
        axis=0,
    )
    return (token_grad, pair_grad, part.T / samples)


def body(*args):
    n_row = lax.axis_size("row")
    n_col = lax.axis_size("col")
    tokens = args[0]
    pair = args[4]
    fits = n_row == 2 and n_col == 8 and n_row * n_col == H and lax.axis_size("samp") == 2
    square = pair.shape[0] * n_row == pair.shape[1] * n_col
    if fits and square and tokens.shape[0] == 4 and tokens.shape[1] == 64:
        return body_heads(*args)
    return body_any(*args)


def solution(mesh):
    placed = (
        P("samp", "col", None),
        P("col"),
        P(),
        P("col"),
        P("row", "col", None),
        P(),
        P(),
        P(),
        P(),
        P(),
        P("samp", "col", None),
    )
    return jax.shard_map(
        body,
        mesh=mesh,
        in_specs=placed,
        out_specs=(P("samp", "col", None), P("row", "col", None), P()),
        check_vma=False,
    )
```

```python
import math

import jax
import jax.numpy as jnp
from jax import lax
from jax.experimental import pallas as pl
from jax.experimental.pallas import tpu as pltpu
from jax.sharding import PartitionSpec as P

D = 768
H = 16
CH = 48
NTYPE = 32


def broadcast(block, axis, source):
    block = jnp.where(lax.axis_index(axis) == source, block, jnp.zeros_like(block))
    return lax.psum(block, axis)


def token_norm(tokens, restype, type_table):
    onehot = (restype[:, None] == jnp.arange(NTYPE, dtype=jnp.int32)[None, :]).astype(jnp.bfloat16)
    embedded = tokens.astype(jnp.float32) + jnp.dot(
        onehot, type_table, preferred_element_type=jnp.float32
    )
    centred = embedded - jnp.mean(embedded, axis=-1, keepdims=True)
    inv_std = lax.rsqrt(jnp.mean(centred * centred, axis=-1, keepdims=True) + 1e-05)
    return (centred * inv_std, inv_std)


def pair_norm(block):
    values = block.astype(jnp.float32)
    centred = values - jnp.mean(values, axis=-1, keepdims=True)
    inv_std = lax.rsqrt(jnp.mean(centred * centred, axis=-1, keepdims=True) + 1e-05)
    return (centred * inv_std, inv_std)


def norm_back(grad_in, normed, inv_std):
    return inv_std * (
        grad_in
        - jnp.mean(grad_in, axis=-1, keepdims=True)
        - normed * jnp.mean(grad_in * normed, axis=-1, keepdims=True)
    )


def project(rows_in, weight):
    return jnp.einsum("std,de->ste", rows_in, weight, preferred_element_type=jnp.float32).astype(
        jnp.bfloat16
    )


def back_project(grads, weight):
    return jnp.einsum(
        "ste,de->std", grads, weight.astype(jnp.float32), precision=lax.Precision.HIGHEST
    )


def pair_back(grad_bias, pair_normed, pair_inv, bias_weight):
    grad_normed = jnp.einsum("hij,ch->ijc", grad_bias, bias_weight, precision=lax.Precision.HIGHEST)
    return norm_back(grad_normed, pair_normed, pair_inv)


def body_any(
    tokens, restype, type_table, key_mask, pair, w_bias, w_query, w_key, w_value, w_gate, cotangent
):
    n_row = lax.axis_size("row")
    n_col = lax.axis_size("col")
    n_samp = lax.axis_size("samp")
    samp_dev = tokens.shape[0]
    tok_col = tokens.shape[1]
    spread = n_col // n_row
    row_count = tok_col * spread
    total_tokens = tok_col * n_col
    row_index = lax.axis_index("row")
    col_index = lax.axis_index("col")
    is_owner = col_index // spread == row_index
    own_start = col_index % spread * tok_col
    normed, inv_std = token_norm(tokens, restype, type_table)
    own_act = normed.astype(jnp.bfloat16)
    key_proj = project(own_act, w_key)
    value_proj = project(own_act, w_value)
    stacked = jnp.stack([own_act, cotangent])
    pieces = [broadcast(stacked, "col", row_index * spread + member) for member in range(spread)]
    gathered = jnp.concatenate(pieces, axis=2)
    query_side = gathered[0]
    grad_rows = gathered[1]
    queries = project(query_side, w_query)
    gate_lin = project(query_side, w_gate)
    pair_normed, pair_inv = pair_norm(pair)
    bias_weight = w_bias.astype(jnp.float32)
    bias = jnp.einsum("ijc,ch->hij", pair_normed, bias_weight, precision=lax.Precision.HIGHEST)
    query_heads = queries.reshape(samp_dev, row_count, H, CH)
    key_heads = key_proj.reshape(samp_dev, tok_col, H, CH)
    value_heads = value_proj.reshape(samp_dev, tok_col, H, CH)
    scores = (
        jnp.einsum("sihc,sjhc->shij", query_heads, key_heads, preferred_element_type=jnp.float32)
        / math.sqrt(CH)
        + bias[None]
    )
    scores = jnp.where(key_mask[None, None, None, :] == 1, scores, -1000000000.0)
    top = lax.pmax(jnp.max(scores, axis=-1), "col")
    expo = jnp.exp(scores - top[..., None])
    partial_out = jnp.einsum(
        "shij,sjhc->sihc",
        expo.astype(jnp.bfloat16),
        value_heads,
        preferred_element_type=jnp.float32,
    )
    totals, summed = lax.psum(
        (jnp.sum(expo, axis=-1), partial_out.reshape(samp_dev, row_count, D)), "col"
    )
    attended = (
        summed.reshape(samp_dev, row_count, H, CH) / jnp.transpose(totals, (0, 2, 1))[..., None]
    )
    flat_out = attended.reshape(samp_dev, row_count, D)
    sig_gate = jax.nn.sigmoid(gate_lin.astype(jnp.float32))
    grad_f = grad_rows.astype(jnp.float32)
    grad_out = (grad_f * sig_gate).astype(jnp.bfloat16)
    grad_gate = (grad_f * flat_out * sig_gate * (1.0 - sig_gate)).astype(jnp.bfloat16)
    gate_piece = lax.dynamic_slice_in_dim(grad_gate, own_start, tok_col, 1)
    gate_term = jnp.where(
        is_owner,
        jnp.einsum("ste,de->std", gate_piece, w_gate, preferred_element_type=jnp.float32),
        0.0,
    )
    grad_heads = grad_out.reshape(samp_dev, row_count, H, CH)
    delta = jnp.transpose(jnp.sum(grad_heads.astype(jnp.float32) * attended, axis=-1), (0, 2, 1))
    probs = expo / totals[..., None]
    grad_pre = jnp.einsum(
        "sihc,sjhc->shij", grad_heads, value_heads, preferred_element_type=jnp.float32
    )
    grad_scores = probs * (grad_pre - delta[..., None])
    rounded = grad_scores.astype(jnp.bfloat16)
    grad_query = (
        jnp.einsum("shij,sjhc->sihc", rounded, key_heads, preferred_element_type=jnp.float32)
        / math.sqrt(CH)
    ).reshape(samp_dev, row_count, D)
    grad_key = (
        jnp.einsum("shij,sihc->sjhc", rounded, query_heads, preferred_element_type=jnp.float32)
        / math.sqrt(CH)
    ).reshape(samp_dev, tok_col, D)
    grad_value = jnp.einsum(
        "shij,sihc->sjhc",
        probs.astype(jnp.bfloat16),
        grad_heads,
        preferred_element_type=jnp.float32,
    ).reshape(samp_dev, tok_col, D)
    bias_local = jnp.sum(grad_scores, axis=0)
    blank = jnp.zeros((samp_dev, total_tokens, D), jnp.float32)
    mine = lax.psum_scatter(
        lax.dynamic_update_slice_in_dim(blank, grad_query, row_index * row_count, 1),
        "col",
        scatter_dimension=1,
        tiled=True,
    )
    query_all, key_all, value_all, gate_all = lax.psum(
        (mine, grad_key, grad_value, gate_term), "row"
    )
    grad_act = (
        back_project(query_all, w_query)
        + back_project(key_all, w_key)
        + back_project(value_all, w_value)
        + gate_all
    )
    token_grad = norm_back(grad_act, normed, inv_std).astype(jnp.bfloat16)
    samples = samp_dev * n_samp
    grad_bias = lax.psum(bias_local, "samp")
    grad_pair = pair_back(grad_bias, pair_normed, pair_inv, bias_weight)
    pair_grad = (grad_pair * (total_tokens / samples)).astype(jnp.bfloat16)
    weight_part = jnp.einsum("ijc,hij->ch", pair_normed, grad_bias, precision=lax.Precision.HIGHEST)
    weight_sum = lax.psum(weight_part, ("row", "col"))
    bias_weight_grad = weight_sum / samples
    return (token_grad, pair_grad, bias_weight_grad)


EPS = 1e-05
SCALE = 1.0 / math.sqrt(CH)
NT = (((1,), (1,)), ((), ()))
TN = (((0,), (0,)), ((), ()))
MASKED = -65504.0


def params(megabytes):
    return pltpu.CompilerParams(vmem_limit_bytes=megabytes * 1024 * 1024)


def matmul(left, right):
    return jnp.dot(left, right, preferred_element_type=jnp.float32)


def matmul_nt(left, right):
    return lax.dot_general(left, right, NT, preferred_element_type=jnp.float32)


def matmul_tn(left, right):
    return lax.dot_general(left, right, TN, preferred_element_type=jnp.float32)


def halves(values):
    high = values.astype(jnp.bfloat16)
    low = (values - high.astype(jnp.float32)).astype(jnp.bfloat16)
    return high, low


def unit_rows(values):
    centred = values - jnp.mean(values, axis=-1, keepdims=True)
    inv_std = lax.rsqrt(jnp.mean(centred * centred, axis=-1, keepdims=True) + EPS)
    return centred * inv_std, inv_std


def embed_rows(tokens_ref, types_ref, table_ref):
    count, length, width = tokens_ref.shape
    index = lax.broadcasted_iota(jnp.int32, (NTYPE, length), 0)
    onehot = jnp.where(types_ref[...] == index, 1.0, 0.0).astype(jnp.bfloat16)
    added = matmul_tn(onehot, table_ref[...])
    embedded = tokens_ref[...].astype(jnp.float32) + added[None]
    return unit_rows(embedded.reshape(count * length, width))


def token_kernel(row_ref, col_ref, tokens_ref, types_ref, table_ref, *refs):
    wq_ref, wk_ref, wv_ref, wg_ref, cot_ref = refs[:5]
    out_refs, side_ref = refs[5:-1], refs[-1]
    normed, _ = embed_rows(tokens_ref, types_ref, table_ref)
    act = normed.astype(jnp.bfloat16)
    for slot, ref in enumerate((wq_ref, wk_ref, wv_ref)):
        side_ref[slot] = matmul(act, ref[...]).astype(jnp.bfloat16).T
    gate = matmul(act, wg_ref[...]).astype(jnp.bfloat16).astype(jnp.float32)
    cot = cot_ref[...].reshape(gate.shape).astype(jnp.float32)
    side_ref[3] = (cot * jax.nn.sigmoid(gate)).astype(jnp.bfloat16).T
    for offset, out_ref in enumerate(out_refs):
        for core in range(2):
            start = pl.multiple_of((col_ref[0] ^ (2 * offset + core)) * CH, 16)
            out_ref[core] = side_ref[:, pl.ds(start, CH), :]


def token_messages(row, col, tokens, types, table, weights, cotangent, n_row, n_col):
    samp_dev, tok_col, _ = tokens.shape
    width = D // n_row
    held = samp_dev * tok_col
    whole3 = lambda i, r, c: (0, 0, 0)
    whole2 = lambda i, r, c: (0, 0)
    weight_spec = pl.BlockSpec((D, width), lambda i, r, c: (0, r[0]))
    shape = (2, 4, CH, held)
    count = n_col // 2
    return pl.pallas_call(
        token_kernel,
        out_shape=[jax.ShapeDtypeStruct(shape, jnp.bfloat16)] * count,
        grid_spec=pltpu.PrefetchScalarGridSpec(
            num_scalar_prefetch=2,
            grid=(1,),
            in_specs=[
                pl.BlockSpec(tokens.shape, whole3),
                pl.BlockSpec(types.shape, whole2),
                pl.BlockSpec(table.shape, whole2),
                weight_spec,
                weight_spec,
                weight_spec,
                weight_spec,
                pl.BlockSpec((samp_dev, tok_col, width), lambda i, r, c: (0, 0, r[0])),
            ],
            out_specs=[pl.BlockSpec(shape, lambda i, r, c: (0, 0, 0, 0))] * count,
            scratch_shapes=[pltpu.VMEM((4, width, held), jnp.bfloat16)],
        ),
        compiler_params=params(56),
        cost_estimate=pl.CostEstimate(
            flops=4_000_000_000, bytes_accessed=4_000_000, transcendentals=0
        ),
        name="token_messages",
    )(row, col, tokens, types, table, *weights, cotangent)


def own_kernel(
    row_ref, tokens_ref, types_ref, table_ref, wg_ref, cot_ref, slope_ref, normed_ref, inv_ref
):
    normed, inv_std = embed_rows(tokens_ref, types_ref, table_ref)
    gate = matmul(normed.astype(jnp.bfloat16), wg_ref[...]).astype(jnp.bfloat16)
    sig = jax.nn.sigmoid(gate.astype(jnp.float32))
    cot = cot_ref[...].reshape(gate.shape).astype(jnp.float32)
    slope_ref[...] = (cot * sig * (1.0 - sig)).T
    normed_ref[...] = normed.T
    inv_ref[...] = jnp.broadcast_to(inv_std, (inv_std.shape[0], 128)).T[:8]


def own_rows(row, tokens, types, table, w_gate, cotangent, half):
    _, tok_col, _ = tokens.shape
    count = half * tok_col
    part_spec = pl.BlockSpec((half, tok_col, D), lambda i, r: (r[0], 0, 0))
    whole2 = lambda i, r: (0, 0)
    return pl.pallas_call(
        own_kernel,
        out_shape=[
            jax.ShapeDtypeStruct((D, count), jnp.float32),
            jax.ShapeDtypeStruct((D, count), jnp.float32),
            jax.ShapeDtypeStruct((8, count), jnp.float32),
        ],
        grid_spec=pltpu.PrefetchScalarGridSpec(
            num_scalar_prefetch=1,
            grid=(1,),
            in_specs=[
                part_spec,
                pl.BlockSpec(types.shape, whole2),
                pl.BlockSpec(table.shape, whole2),
                pl.BlockSpec(w_gate.shape, whole2),
                part_spec,
            ],
            out_specs=[
                pl.BlockSpec((D, count), whole2),
                pl.BlockSpec((D, count), whole2),
                pl.BlockSpec((8, count), whole2),
            ],
        ),
        compiler_params=params(56),
        cost_estimate=pl.CostEstimate(
            flops=3_000_000_000, bytes_accessed=3_000_000, transcendentals=0
        ),
        name="own_rows",
    )(row, tokens, types, table, w_gate, cotangent)


MANY = 4
PARTS = 2


def pair_columns(pair_ref, k, many):
    _, _, length, width = pair_ref.shape
    blocks = [pair_ref[p, pl.ds(k, many)] for p in range(2)]
    rows = jnp.concatenate(blocks, axis=1).reshape(many * 2 * length, width)
    same = lax.broadcasted_iota(jnp.int32, (width, width), 0) == lax.broadcasted_iota(
        jnp.int32, (width, width), 1
    )
    centring = (jnp.where(same, 1.0, 0.0) - 1.0 / width).astype(jnp.bfloat16)
    centred = matmul_nt(centring, rows)
    return centred, lax.rsqrt(jnp.mean(centred * centred, axis=0, keepdims=True) + EPS)


def bias_kernel(pair_ref, weight_ref, mask_ref, out_ref, flat_ref):
    _, count, length, width = pair_ref.shape
    whole = flat_ref.shape[0] // H
    weight = jnp.concatenate([weight_ref[...]] * 2, axis=1)
    base = pl.program_id(0) * count

    def step(n, carry):
        k = n * MANY
        centred, inv_std = pair_columns(pair_ref, k, MANY)
        bias = matmul(weight, jnp.concatenate(halves(centred), axis=0)) * inv_std
        for m in range(MANY):
            lanes = slice(m * 2 * length, (m + 1) * 2 * length)
            flat_ref[pl.ds(base + k + m, H, stride=whole), :] = bias[:, lanes]
        return carry

    lax.fori_loop(0, count // MANY, step, 0, unroll=2)

    @pl.when(pl.program_id(0) == pl.num_programs(0) - 1)
    def _():
        keep = jnp.broadcast_to(mask_ref[...].astype(jnp.float32), (128, length)).T
        keep = jnp.concatenate([keep] * (2 * whole // 128), axis=1) == 1.0
        for h in range(H):
            turned = flat_ref[h * whole : (h + 1) * whole, :].T
            bias = jnp.concatenate([turned[:length], turned[length:]], axis=1)
            out_ref[h] = jnp.where(keep, bias, MASKED)


STEPS = 4


def split_spec(shape):
    block = (shape[0] // STEPS,) + tuple(shape[1:])
    return pl.BlockSpec(block, lambda i: (i,) + (0,) * (len(shape) - 1))


def whole_spec(shape):
    return pl.BlockSpec(tuple(shape), lambda i: (0,) * len(shape))


def pair_spec(pair):
    row_count, tok_col, width = pair.shape
    block = (2, row_count // 2 // STEPS, tok_col, width)
    return pl.BlockSpec(block, lambda i: (0, i, 0, 0))


def pair_bias(pair, weight_t, mask):
    row_count, tok_col, width = pair.shape
    whole = row_count // 2
    return pl.pallas_call(
        bias_kernel,
        out_shape=jax.ShapeDtypeStruct((H, tok_col, row_count), jnp.float32),
        grid=(STEPS,),
        in_specs=[pair_spec(pair), whole_spec(weight_t.shape), whole_spec(mask.shape)],
        out_specs=whole_spec((H, tok_col, row_count)),
        scratch_shapes=[pltpu.VMEM((H * whole, 2 * tok_col), jnp.float32)],
        compiler_params=params(24),
        cost_estimate=pl.CostEstimate(
            flops=6_000_000_000, bytes_accessed=5_000_000, transcendentals=0
        ),
        name="pair_bias",
    )(pair.reshape(2, whole, tok_col, width), weight_t, mask)


def norm_kernel(pair_ref, normed_ref, inv_ref):
    def step(n, carry):
        centred, inv_std = pair_columns(pair_ref, n * MANY, MANY)
        normed_ref[n] = jnp.concatenate(halves(centred * inv_std), axis=0)
        inv_ref[n] = jnp.broadcast_to(inv_std, inv_ref.shape[1:])
        return carry

    lax.fori_loop(0, normed_ref.shape[0], step, 0, unroll=2)


def pair_units(pair):
    row_count, tok_col, width = pair.shape
    whole = row_count // 2
    chunks, lanes = whole // MANY, MANY * 2 * tok_col
    shapes = [(chunks, 2 * width, lanes), (chunks, 8, lanes)]
    return pl.pallas_call(
        norm_kernel,
        out_shape=[
            jax.ShapeDtypeStruct(shapes[0], jnp.bfloat16),
            jax.ShapeDtypeStruct(shapes[1], jnp.float32),
        ],
        grid=(STEPS,),
        in_specs=[pair_spec(pair)],
        out_specs=[split_spec(shape) for shape in shapes],
        compiler_params=params(56),
        cost_estimate=pl.CostEstimate(
            flops=6_000_000_000, bytes_accessed=12_000_000, transcendentals=0
        ),
        name="pair_units",
    )(pair.reshape(2, whole, tok_col, width))


def shift_of(top):
    return jnp.floor(jnp.clip(14.0 - jnp.log2(top), -100.0, 100.0))


def attention_kernel(col_ref, *refs):
    other_ref, bias_ref, back_ref, grad_bias_ref, sum_ref, tokens_ref = refs[-6:]
    col = col_ref[0]
    for offset, ref in enumerate(refs[:-6]):
        tokens_ref[col ^ (2 * offset)] = ref[0]
        tokens_ref[col ^ (2 * offset + 1)] = other_ref[offset]
    n_col = tokens_ref.shape[0]
    tok_col, row_count = bias_ref.shape[1:]
    half = back_ref.shape[2] // tok_col
    n_row = bias_ref.shape[0] // n_col
    step = pl.program_id(0)

    @pl.when(step == 0)
    def _():
        sum_ref[...] = jnp.zeros_like(sum_ref)

    outs = []
    for sample in range(half):
        lanes = slice(sample * tok_col, (sample + 1) * tok_col)

        def side(slot):
            return jnp.concatenate([tokens_ref[c, slot, :, lanes] for c in range(n_col)], axis=1)

        query_t, key_t, value_t, grad_t = [side(slot) for slot in range(4)]
        key = key_t.T
        value = value_t.T
        attended_parts, grad_query_parts = [], []
        grad_key = jnp.zeros(key_t.shape, jnp.float32)
        grad_value = jnp.zeros(key_t.shape, jnp.float32)
        for block in range(n_row):
            cols = slice(block * row_count, (block + 1) * row_count)
            heads = slice(block * n_col, (block + 1) * n_col)
            bias = bias_ref[heads].reshape(n_col * tok_col, row_count)
            query_b = query_t[:, cols]
            grad_b = grad_t[:, cols]
            scores = matmul(key, query_b) * SCALE + bias
            scores = jnp.where(bias < -60000.0, -1000000000.0, scores)
            expo = jnp.exp(scores - jnp.max(scores, axis=0, keepdims=True))
            share = 1.0 / jnp.sum(expo, axis=0, keepdims=True)
            attended = matmul(value_t, expo.astype(jnp.bfloat16)) * share
            delta = jnp.sum(grad_b.astype(jnp.float32) * attended, axis=0, keepdims=True)
            probs = expo * share
            grad_scores = probs * (matmul(value, grad_b) - delta)
            rounded = grad_scores.astype(jnp.bfloat16)
            attended_parts.append(attended)
            grad_query_parts.append(matmul(key_t, rounded) * SCALE)
            grad_key = grad_key + matmul_nt(query_b, rounded)
            grad_value = grad_value + matmul_nt(grad_b, probs.astype(jnp.bfloat16))
            sum_ref[heads] += grad_scores.reshape(n_col, tok_col, row_count)
        outs.append(
            (
                jnp.concatenate(grad_query_parts, axis=1),
                grad_key * SCALE,
                grad_value,
                jnp.concatenate(attended_parts, axis=1),
            )
        )
    spare = jnp.zeros((8 - 4, half * tok_col), jnp.float32)
    tops = [jnp.max(jnp.abs(out[slot]), axis=0, keepdims=True) for slot in range(4) for out in outs]
    shifts = shift_of(jnp.concatenate(tops, axis=0))
    scales = jnp.exp2(shifts)
    scaled = [
        [out[slot] * scales[slot * half + n : slot * half + n + 1] for n, out in enumerate(outs)]
        for slot in range(4)
    ]
    for c in range(n_col):
        lanes = slice(c * tok_col, (c + 1) * tok_col)
        for slot in range(4):
            back_ref[c, slot * CH : (slot + 1) * CH, :] = jnp.concatenate(
                [part[:, lanes] for part in scaled[slot]], axis=1
            )
        tails = [
            jnp.concatenate([shifts[slot * half + n :, lanes][:1] for n in range(half)], axis=1)
            for slot in range(4)
        ]
        back_ref[c, 4 * CH :, :] = jnp.concatenate(tails + [spare], axis=0)

    @pl.when(step == pl.num_programs(0) - 1)
    def _():
        piece = row_count // 2 // PARTS
        for head in range(n_row * n_col):
            sums = sum_ref[head]
            sums = jnp.concatenate(
                [
                    sums[:, (p * PARTS + n) * piece : (p * PARTS + n + 1) * piece]
                    for n in range(PARTS)
                    for p in range(2)
                ],
                axis=1,
            )
            shift = shift_of(jnp.max(jnp.abs(sums), axis=0, keepdims=True))
            grad_bias_ref[head, :tok_col, :] = sums * jnp.exp2(shift)
            grad_bias_ref[head, tok_col:, :] = jnp.broadcast_to(shift, (8, row_count))


def attention(col, arrived, other, bias, n_row):
    count = len(arrived)
    n_col = 2 * count
    _, tok_col, row_count = bias.shape
    half = arrived[0].shape[-1] // tok_col // n_row
    width = half * tok_col
    back_shape = (n_row * n_col, 4 * CH + 8, width)
    bias_shape = (n_row * n_col, tok_col + 8, row_count)
    return pl.pallas_call(
        attention_kernel,
        out_shape=[
            jax.ShapeDtypeStruct(back_shape, jnp.float32),
            jax.ShapeDtypeStruct(bias_shape, jnp.float32),
        ],
        grid_spec=pltpu.PrefetchScalarGridSpec(
            num_scalar_prefetch=1,
            grid=(n_row,),
            in_specs=[pl.BlockSpec((1, 4, CH, width), lambda i, r: (0, 0, 0, i))] * count
            + [
                pl.BlockSpec((count, 4, CH, width), lambda i, r: (0, 0, 0, i)),
                pl.BlockSpec(bias.shape, lambda i, r: (0, 0, 0)),
            ],
            out_specs=[
                pl.BlockSpec((n_col, 4 * CH + 8, width), lambda i, r: (i, 0, 0)),
                pl.BlockSpec(bias_shape, lambda i, r: (0, 0, 0)),
            ],
            scratch_shapes=[
                pltpu.VMEM(bias.shape, jnp.float32),
                pltpu.VMEM((n_col, 4, CH, width), jnp.bfloat16),
            ],
        ),
        compiler_params=params(24),
        cost_estimate=pl.CostEstimate(
            flops=8_000_000_000, bytes_accessed=6_000_000, transcendentals=1_000_000
        ),
        name="attention",
    )(col, *arrived, other, bias)


def back_kernel(*refs):
    slope_ref, normed_ref, inv_ref, wq_ref, wk_ref, wv_ref, wg_ref = refs[-11:-4]
    out_ref, parts_ref, gate_ref, total_ref = refs[-4:]
    back_ref = refs[0]
    count = normed_ref.shape[-1]
    step = pl.program_id(0)
    rows = wq_ref.shape[0]

    @pl.when(step == 0)
    def _():
        for slot in range(4):
            scale = jnp.exp2(-back_ref[:, 4 * CH + slot : 4 * CH + slot + 1, :])
            values = back_ref[:, slot * CH : (slot + 1) * CH, :] * scale
            values = values.reshape(gate_ref.shape)
            if slot < 3:
                parts_ref[slot] = jnp.concatenate(halves(values), axis=1)
            else:
                gate_ref[...] = (values * slope_ref[...]).astype(jnp.bfloat16)

    total = matmul(wg_ref[...], gate_ref[...])
    for slot, ref in enumerate((wq_ref, wk_ref, wv_ref)):
        parts = matmul(ref[...], parts_ref[slot])
        total = total + (parts[:, :count] + parts[:, count:])
    total_ref[pl.ds(pl.multiple_of(step * rows, 8), rows), :] = total

    @pl.when(step == pl.num_programs(0) - 1)
    def _():
        whole = total_ref[...]
        normed = normed_ref[...]
        result = inv_ref[:1] * (
            whole
            - jnp.mean(whole, axis=0, keepdims=True)
            - normed * jnp.mean(whole * normed, axis=0, keepdims=True)
        )
        out_ref[...] = result.T.astype(jnp.bfloat16)


def token_back(back, slope, normed, inv_std, weights):
    count = normed.shape[-1]
    steps = 2
    whole = lambda shape: pl.BlockSpec(shape, lambda i: (0,) * len(shape))
    weight_spec = pl.BlockSpec((D // steps, D), lambda i: (i, 0))
    return pl.pallas_call(
        back_kernel,
        out_shape=jax.ShapeDtypeStruct((count, D), jnp.bfloat16),
        grid=(steps,),
        in_specs=[whole(array.shape) for array in (back, slope, normed, inv_std)]
        + [weight_spec] * 4,
        out_specs=whole((count, D)),
        scratch_shapes=[
            pltpu.VMEM((3, D, 2 * count), jnp.bfloat16),
            pltpu.VMEM((D, count), jnp.bfloat16),
            pltpu.VMEM((D, count), jnp.float32),
        ],
        compiler_params=params(40),
        cost_estimate=pl.CostEstimate(
            flops=4_000_000_000, bytes_accessed=8_000_000, transcendentals=0
        ),
        name="token_back",
    )(back, slope, normed, inv_std, *weights)


def flatten(grads_ref, flat_ref):
    whole = flat_ref.shape[0] // H
    for h in range(H):
        grads = grads_ref[h]
        both = jnp.concatenate([grads[:, :whole], grads[:, whole:]], axis=0)
        flat_ref[h * whole : (h + 1) * whole, :] = both.T


def flat_columns(flat_ref, k, many):
    whole = flat_ref.shape[0] // H
    grads = [flat_ref[pl.ds(k + m, H, stride=whole), :] for m in range(many)]
    return jnp.concatenate(halves(jnp.concatenate(grads, axis=1)), axis=0)


def pair_back_kernel(factor, normed_ref, inv_ref, grads_ref, weight_ref, *refs):
    out_ref, part_ref, flat_ref = refs[-3:]
    _, count, length, width = out_ref.shape
    weight = weight_ref[...].astype(jnp.float32)
    weight = halves(weight - jnp.mean(weight, axis=1, keepdims=True))
    weight = jnp.concatenate([weight[0], weight[0], weight[1], weight[1]], axis=0).T
    base = pl.program_id(0) * count

    @pl.when(pl.program_id(0) == 0)
    def _():
        part_ref[...] = jnp.zeros_like(part_ref)
        flatten(grads_ref, flat_ref)

    def step(n, carry):
        k = n * MANY
        both = normed_ref[n]
        normed = both[:width].astype(jnp.float32) + both[width:].astype(jnp.float32)
        grads = flat_columns(flat_ref, base + k, MANY)
        grad_in = matmul(weight, jnp.concatenate([grads, grads], axis=0))
        overlap = jnp.mean(grad_in * normed, axis=0, keepdims=True)
        result = (grad_in - normed * overlap) * (inv_ref[n, :1] * factor)
        result = result.astype(jnp.bfloat16).T.reshape(MANY, 2 * length, width)
        for p in range(2):
            out_ref[p, pl.ds(k, MANY)] = result[:, p * length : (p + 1) * length]
        return carry + matmul_nt(both, grads)

    parts = jnp.zeros((2 * width, 2 * H), jnp.float32)
    parts = lax.fori_loop(0, count // MANY, step, parts, unroll=2)
    parts = parts[:, :H] + parts[:, H:]
    part_ref[...] += (parts[:width] + parts[width:]).T


def pair_backward(number, so_far, shape, normed, inv_std, grads, weight_t, factor):
    row_count, tok_col, width = shape
    whole = row_count // 2
    steps = STEPS // PARTS
    first = number * steps

    def split(shape):
        block = (shape[0] // STEPS,) + tuple(shape[1:])
        return pl.BlockSpec(block, lambda i: (i + first,) + (0,) * (len(shape) - 1))

    previous = [] if so_far is None else [so_far]
    return pl.pallas_call(
        lambda *refs: pair_back_kernel(factor, *refs),
        out_shape=[
            jax.ShapeDtypeStruct((2, whole, tok_col, width), jnp.bfloat16),
            jax.ShapeDtypeStruct((H, width), jnp.float32),
        ],
        grid=(steps,),
        in_specs=[
            split(normed.shape),
            split(inv_std.shape),
            whole_spec(grads.shape),
            whole_spec(weight_t.shape),
        ]
        + [pl.BlockSpec(memory_space=pl.ANY)] * len(previous),
        out_specs=[
            pl.BlockSpec((2, whole // STEPS, tok_col, width), lambda i: (0, i + first, 0, 0)),
            whole_spec((H, width)),
        ],
        scratch_shapes=[pltpu.VMEM((H * whole // PARTS, 2 * tok_col), jnp.float32)],
        input_output_aliases={4: 0} if previous else {},
        compiler_params=params(24),
        cost_estimate=pl.CostEstimate(
            flops=6_000_000_000, bytes_accessed=100_000, transcendentals=0
        ),
        name="pair_backward",
    )(normed, inv_std, grads, weight_t, *previous)


def unscaled(block, rows):
    block = block.astype(jnp.float32)
    return block[:, :rows] * jnp.exp2(-block[:, rows : rows + 1])


def swap(block, axis):
    return lax.ppermute(block, axis, [(0, 1), (1, 0)])


def body_heads(
    tokens, restype, type_table, key_mask, pair, w_bias, w_query, w_key, w_value, w_gate, cotangent
):
    n_row = lax.axis_size("row")
    n_col = lax.axis_size("col")
    n_samp = lax.axis_size("samp")
    samp_dev = tokens.shape[0]
    tok_col = tokens.shape[1]
    row_count = pair.shape[0]
    total_tokens = tok_col * n_col
    half = samp_dev // n_row
    row_index = lax.axis_index("row")
    row = row_index.astype(jnp.int32).reshape(1)
    col = lax.axis_index("col").astype(jnp.int32).reshape(1)
    types = restype.reshape(1, tok_col)
    weight_t = w_bias.T
    weights = (w_query, w_key, w_value, w_gate)
    samples = samp_dev * n_samp

    def send(block, offset):
        return lax.ppermute(block, "col", [(c, c ^ offset) for c in range(n_col)])

    def by_chip(blocks):
        return [blocks[0]] + [send(blocks[n], 2 * n) for n in range(1, n_col // 2)]

    def across(blocks):
        return send(jnp.stack([block[1] for block in blocks]), 1)

    messages = token_messages(
        row, col, tokens, types, type_table, weights, cotangent, n_row, n_col
    )
    arrived = by_chip(messages)
    bias = pair_bias(pair, weight_t, key_mask.reshape(1, tok_col))
    bias, arrived, types = lax.optimization_barrier(
        (bias.astype(jnp.float16), arrived, types)
    )
    own = own_rows(row, tokens, types, type_table, w_gate, cotangent, half)
    bias = lax.all_to_all(bias, ("row", "col"), 0, 0, tiled=True)
    other = across(arrived)
    bias, other, own = lax.optimization_barrier((bias, other, own))

    back, grad_bias = attention(col, arrived, other, bias.astype(jnp.float32), n_row)
    grad_bias = lax.all_to_all(
        grad_bias.astype(jnp.float16), ("row", "col"), 0, 0, tiled=True
    )
    back, late_pair = lax.optimization_barrier((back.astype(jnp.float16), pair))
    pair_normed, pair_inv = pair_units(late_pair)
    back, grad_bias, pair_normed = lax.optimization_barrier((back, grad_bias, pair_normed))
    back = lax.all_to_all(back, ("row", "col"), 0, 0, tiled=True)

    pair_grad, part = None, 0.0
    pieces = jnp.split(grad_bias, PARTS, axis=2)
    others = [swap(piece, "samp") for piece in pieces]
    for n, (piece, other) in enumerate(zip(pieces, others)):
        grads = unscaled(piece, tok_col) + unscaled(other, tok_col)
        pair_grad, more = pair_backward(
            n, pair_grad, pair.shape, pair_normed, pair_inv, grads, weight_t,
            total_tokens / samples,
        )
        part = part + more
    pair_grad = pair_grad.reshape(pair.shape)

    pair_grad, back, part = lax.optimization_barrier((pair_grad, back, part))
    flip = [(n, n ^ (n_col + 1)) for n in range(n_row * n_col)]
    sums = (swap(part, "row"), send(part, 1), lax.ppermute(part, ("row", "col"), flip))
    token_half = token_back(back.astype(jnp.float32), *own, weights)
    token_half, sums = lax.optimization_barrier((token_half, sums))
    token_half = token_half.reshape(half, tok_col, D)
    other_half = swap(token_half, "row")
    part = (part + sums[0]) + (sums[1] + sums[2])
    part = (part + send(part, 2)) + (send(part, 4) + send(part, 6))
    first = row_index == 0
    token_grad = jnp.concatenate(
        [jnp.where(first, token_half, other_half), jnp.where(first, other_half, token_half)],
        axis=0,
    )
    return (token_grad, pair_grad, part.T / samples)


def body(*args):
    n_row = lax.axis_size("row")
    n_col = lax.axis_size("col")
    tokens = args[0]
    pair = args[4]
    fits = n_row == 2 and n_col == 8 and n_row * n_col == H and lax.axis_size("samp") == 2
    square = pair.shape[0] * n_row == pair.shape[1] * n_col
    if fits and square and tokens.shape[0] == 4 and tokens.shape[1] == 64:
        return body_heads(*args)
    return body_any(*args)


def solution(mesh):
    placed = (
        P("samp", "col", None),
        P("col"),
        P(),
        P("col"),
        P("row", "col", None),
        P(),
        P(),
        P(),
        P(),
        P(),
        P("samp", "col", None),
    )
    return jax.shard_map(
        body,
        mesh=mesh,
        in_specs=placed,
        out_specs=(P("samp", "col", None), P("row", "col", None), P()),
        check_vma=False,
    )
```

```python
import math

import jax
import jax.numpy as jnp
from jax import lax
from jax.experimental import pallas as pl
from jax.experimental.pallas import tpu as pltpu
from jax.sharding import PartitionSpec as P

D = 768
H = 16
CH = 48
NTYPE = 32


def broadcast(block, axis, source):
    block = jnp.where(lax.axis_index(axis) == source, block, jnp.zeros_like(block))
    return lax.psum(block, axis)


def token_norm(tokens, restype, type_table):
    onehot = (restype[:, None] == jnp.arange(NTYPE, dtype=jnp.int32)[None, :]).astype(jnp.bfloat16)
    embedded = tokens.astype(jnp.float32) + jnp.dot(
        onehot, type_table, preferred_element_type=jnp.float32
    )
    centred = embedded - jnp.mean(embedded, axis=-1, keepdims=True)
    inv_std = lax.rsqrt(jnp.mean(centred * centred, axis=-1, keepdims=True) + 1e-05)
    return (centred * inv_std, inv_std)


def pair_norm(block):
    values = block.astype(jnp.float32)
    centred = values - jnp.mean(values, axis=-1, keepdims=True)
    inv_std = lax.rsqrt(jnp.mean(centred * centred, axis=-1, keepdims=True) + 1e-05)
    return (centred * inv_std, inv_std)


def norm_back(grad_in, normed, inv_std):
    return inv_std * (
        grad_in
        - jnp.mean(grad_in, axis=-1, keepdims=True)
        - normed * jnp.mean(grad_in * normed, axis=-1, keepdims=True)
    )


def project(rows_in, weight):
    return jnp.einsum("std,de->ste", rows_in, weight, preferred_element_type=jnp.float32).astype(
        jnp.bfloat16
    )


def back_project(grads, weight):
    return jnp.einsum(
        "ste,de->std", grads, weight.astype(jnp.float32), precision=lax.Precision.HIGHEST
    )


def pair_back(grad_bias, pair_normed, pair_inv, bias_weight):
    grad_normed = jnp.einsum("hij,ch->ijc", grad_bias, bias_weight, precision=lax.Precision.HIGHEST)
    return norm_back(grad_normed, pair_normed, pair_inv)


def body_any(
    tokens, restype, type_table, key_mask, pair, w_bias, w_query, w_key, w_value, w_gate, cotangent
):
    n_row = lax.axis_size("row")
    n_col = lax.axis_size("col")
    n_samp = lax.axis_size("samp")
    samp_dev = tokens.shape[0]
    tok_col = tokens.shape[1]
    spread = n_col // n_row
    row_count = tok_col * spread
    total_tokens = tok_col * n_col
    row_index = lax.axis_index("row")
    col_index = lax.axis_index("col")
    is_owner = col_index // spread == row_index
    own_start = col_index % spread * tok_col
    normed, inv_std = token_norm(tokens, restype, type_table)
    own_act = normed.astype(jnp.bfloat16)
    key_proj = project(own_act, w_key)
    value_proj = project(own_act, w_value)
    stacked = jnp.stack([own_act, cotangent])
    pieces = [broadcast(stacked, "col", row_index * spread + member) for member in range(spread)]
    gathered = jnp.concatenate(pieces, axis=2)
    query_side = gathered[0]
    grad_rows = gathered[1]
    queries = project(query_side, w_query)
    gate_lin = project(query_side, w_gate)
    pair_normed, pair_inv = pair_norm(pair)
    bias_weight = w_bias.astype(jnp.float32)
    bias = jnp.einsum("ijc,ch->hij", pair_normed, bias_weight, precision=lax.Precision.HIGHEST)
    query_heads = queries.reshape(samp_dev, row_count, H, CH)
    key_heads = key_proj.reshape(samp_dev, tok_col, H, CH)
    value_heads = value_proj.reshape(samp_dev, tok_col, H, CH)
    scores = (
        jnp.einsum("sihc,sjhc->shij", query_heads, key_heads, preferred_element_type=jnp.float32)
        / math.sqrt(CH)
        + bias[None]
    )
    scores = jnp.where(key_mask[None, None, None, :] == 1, scores, -1000000000.0)
    top = lax.pmax(jnp.max(scores, axis=-1), "col")
    expo = jnp.exp(scores - top[..., None])
    partial_out = jnp.einsum(
        "shij,sjhc->sihc",
        expo.astype(jnp.bfloat16),
        value_heads,
        preferred_element_type=jnp.float32,
    )
    totals, summed = lax.psum(
        (jnp.sum(expo, axis=-1), partial_out.reshape(samp_dev, row_count, D)), "col"
    )
    attended = (
        summed.reshape(samp_dev, row_count, H, CH) / jnp.transpose(totals, (0, 2, 1))[..., None]
    )
    flat_out = attended.reshape(samp_dev, row_count, D)
    sig_gate = jax.nn.sigmoid(gate_lin.astype(jnp.float32))
    grad_f = grad_rows.astype(jnp.float32)
    grad_out = (grad_f * sig_gate).astype(jnp.bfloat16)
    grad_gate = (grad_f * flat_out * sig_gate * (1.0 - sig_gate)).astype(jnp.bfloat16)
    gate_piece = lax.dynamic_slice_in_dim(grad_gate, own_start, tok_col, 1)
    gate_term = jnp.where(
        is_owner,
        jnp.einsum("ste,de->std", gate_piece, w_gate, preferred_element_type=jnp.float32),
        0.0,
    )
    grad_heads = grad_out.reshape(samp_dev, row_count, H, CH)
    delta = jnp.transpose(jnp.sum(grad_heads.astype(jnp.float32) * attended, axis=-1), (0, 2, 1))
    probs = expo / totals[..., None]
    grad_pre = jnp.einsum(
        "sihc,sjhc->shij", grad_heads, value_heads, preferred_element_type=jnp.float32
    )
    grad_scores = probs * (grad_pre - delta[..., None])
    rounded = grad_scores.astype(jnp.bfloat16)
    grad_query = (
        jnp.einsum("shij,sjhc->sihc", rounded, key_heads, preferred_element_type=jnp.float32)
        / math.sqrt(CH)
    ).reshape(samp_dev, row_count, D)
    grad_key = (
        jnp.einsum("shij,sihc->sjhc", rounded, query_heads, preferred_element_type=jnp.float32)
        / math.sqrt(CH)
    ).reshape(samp_dev, tok_col, D)
    grad_value = jnp.einsum(
        "shij,sihc->sjhc",
        probs.astype(jnp.bfloat16),
        grad_heads,
        preferred_element_type=jnp.float32,
    ).reshape(samp_dev, tok_col, D)
    bias_local = jnp.sum(grad_scores, axis=0)
    blank = jnp.zeros((samp_dev, total_tokens, D), jnp.float32)
    mine = lax.psum_scatter(
        lax.dynamic_update_slice_in_dim(blank, grad_query, row_index * row_count, 1),
        "col",
        scatter_dimension=1,
        tiled=True,
    )
    query_all, key_all, value_all, gate_all = lax.psum(
        (mine, grad_key, grad_value, gate_term), "row"
    )
    grad_act = (
        back_project(query_all, w_query)
        + back_project(key_all, w_key)
        + back_project(value_all, w_value)
        + gate_all
    )
    token_grad = norm_back(grad_act, normed, inv_std).astype(jnp.bfloat16)
    samples = samp_dev * n_samp
    grad_bias = lax.psum(bias_local, "samp")
    grad_pair = pair_back(grad_bias, pair_normed, pair_inv, bias_weight)
    pair_grad = (grad_pair * (total_tokens / samples)).astype(jnp.bfloat16)
    weight_part = jnp.einsum("ijc,hij->ch", pair_normed, grad_bias, precision=lax.Precision.HIGHEST)
    weight_sum = lax.psum(weight_part, ("row", "col"))
    bias_weight_grad = weight_sum / samples
    return (token_grad, pair_grad, bias_weight_grad)


EPS = 1e-05
SCALE = 1.0 / math.sqrt(CH)
NT = (((1,), (1,)), ((), ()))
TN = (((0,), (0,)), ((), ()))
MASKED = -65504.0


def params(megabytes):
    return pltpu.CompilerParams(vmem_limit_bytes=megabytes * 1024 * 1024)


def matmul(left, right):
    return jnp.dot(left, right, preferred_element_type=jnp.float32)


def matmul_nt(left, right):
    return lax.dot_general(left, right, NT, preferred_element_type=jnp.float32)


def matmul_tn(left, right):
    return lax.dot_general(left, right, TN, preferred_element_type=jnp.float32)


def halves(values):
    high = values.astype(jnp.bfloat16)
    low = (values - high.astype(jnp.float32)).astype(jnp.bfloat16)
    return high, low


def unit_rows(values):
    centred = values - jnp.mean(values, axis=-1, keepdims=True)
    inv_std = lax.rsqrt(jnp.mean(centred * centred, axis=-1, keepdims=True) + EPS)
    return centred * inv_std, inv_std


def embed_rows(tokens_ref, types_ref, table_ref):
    count, length, width = tokens_ref.shape
    index = lax.broadcasted_iota(jnp.int32, (NTYPE, length), 0)
    onehot = jnp.where(types_ref[...] == index, 1.0, 0.0).astype(jnp.bfloat16)
    added = matmul_tn(onehot, table_ref[...])
    embedded = tokens_ref[...].astype(jnp.float32) + added[None]
    return unit_rows(embedded.reshape(count * length, width))


def token_kernel(row_ref, col_ref, tokens_ref, types_ref, table_ref, *refs):
    wq_ref, wk_ref, wv_ref, wg_ref, cot_ref = refs[:5]
    out_refs, side_ref = refs[5:-1], refs[-1]
    normed, _ = embed_rows(tokens_ref, types_ref, table_ref)
    act = normed.astype(jnp.bfloat16)
    for slot, ref in enumerate((wq_ref, wk_ref, wv_ref)):
        side_ref[slot] = matmul(act, ref[...]).astype(jnp.bfloat16).T
    gate = matmul(act, wg_ref[...]).astype(jnp.bfloat16).astype(jnp.float32)
    cot = cot_ref[...].reshape(gate.shape).astype(jnp.float32)
    side_ref[3] = (cot * jax.nn.sigmoid(gate)).astype(jnp.bfloat16).T
    for offset, out_ref in enumerate(out_refs):
        for core in range(2):
            start = pl.multiple_of((col_ref[0] ^ (2 * offset + core)) * CH, 16)
            out_ref[core] = side_ref[:, pl.ds(start, CH), :]


def token_messages(row, col, tokens, types, table, weights, cotangent, n_row, n_col):
    samp_dev, tok_col, _ = tokens.shape
    width = D // n_row
    held = samp_dev * tok_col
    whole3 = lambda i, r, c: (0, 0, 0)
    whole2 = lambda i, r, c: (0, 0)
    weight_spec = pl.BlockSpec((D, width), lambda i, r, c: (0, r[0]))
    shape = (2, 4, CH, held)
    count = n_col // 2
    return pl.pallas_call(
        token_kernel,
        out_shape=[jax.ShapeDtypeStruct(shape, jnp.bfloat16)] * count,
        grid_spec=pltpu.PrefetchScalarGridSpec(
            num_scalar_prefetch=2,
            grid=(1,),
            in_specs=[
                pl.BlockSpec(tokens.shape, whole3),
                pl.BlockSpec(types.shape, whole2),
                pl.BlockSpec(table.shape, whole2),
                weight_spec,
                weight_spec,
                weight_spec,
                weight_spec,
                pl.BlockSpec((samp_dev, tok_col, width), lambda i, r, c: (0, 0, r[0])),
            ],
            out_specs=[pl.BlockSpec(shape, lambda i, r, c: (0, 0, 0, 0))] * count,
            scratch_shapes=[pltpu.VMEM((4, width, held), jnp.bfloat16)],
        ),
        compiler_params=params(56),
        cost_estimate=pl.CostEstimate(
            flops=4_000_000_000, bytes_accessed=4_000_000, transcendentals=0
        ),
        name="token_messages",
    )(row, col, tokens, types, table, *weights, cotangent)


def own_kernel(
    row_ref, tokens_ref, types_ref, table_ref, wg_ref, cot_ref, slope_ref, normed_ref, inv_ref
):
    normed, inv_std = embed_rows(tokens_ref, types_ref, table_ref)
    gate = matmul(normed.astype(jnp.bfloat16), wg_ref[...]).astype(jnp.bfloat16)
    sig = jax.nn.sigmoid(gate.astype(jnp.float32))
    cot = cot_ref[...].reshape(gate.shape).astype(jnp.float32)
    slope_ref[...] = (cot * sig * (1.0 - sig)).T
    normed_ref[...] = normed.T
    inv_ref[...] = jnp.broadcast_to(inv_std, (inv_std.shape[0], 128)).T[:8]


def own_rows(row, tokens, types, table, w_gate, cotangent, half):
    _, tok_col, _ = tokens.shape
    count = half * tok_col
    part_spec = pl.BlockSpec((half, tok_col, D), lambda i, r: (r[0], 0, 0))
    whole2 = lambda i, r: (0, 0)
    return pl.pallas_call(
        own_kernel,
        out_shape=[
            jax.ShapeDtypeStruct((D, count), jnp.float32),
            jax.ShapeDtypeStruct((D, count), jnp.float32),
            jax.ShapeDtypeStruct((8, count), jnp.float32),
        ],
        grid_spec=pltpu.PrefetchScalarGridSpec(
            num_scalar_prefetch=1,
            grid=(1,),
            in_specs=[
                part_spec,
                pl.BlockSpec(types.shape, whole2),
                pl.BlockSpec(table.shape, whole2),
                pl.BlockSpec(w_gate.shape, whole2),
                part_spec,
            ],
            out_specs=[
                pl.BlockSpec((D, count), whole2),
                pl.BlockSpec((D, count), whole2),
                pl.BlockSpec((8, count), whole2),
            ],
        ),
        compiler_params=params(56),
        cost_estimate=pl.CostEstimate(
            flops=3_000_000_000, bytes_accessed=3_000_000, transcendentals=0
        ),
        name="own_rows",
    )(row, tokens, types, table, w_gate, cotangent)


MANY = 4


def pair_columns(pair_ref, k, many):
    _, _, length, width = pair_ref.shape
    blocks = [pair_ref[p, pl.ds(k, many)] for p in range(2)]
    rows = jnp.concatenate(blocks, axis=1).reshape(many * 2 * length, width)
    same = lax.broadcasted_iota(jnp.int32, (width, width), 0) == lax.broadcasted_iota(
        jnp.int32, (width, width), 1
    )
    centring = (jnp.where(same, 1.0, 0.0) - 1.0 / width).astype(jnp.bfloat16)
    centred = matmul_nt(centring, rows)
    return centred, lax.rsqrt(jnp.mean(centred * centred, axis=0, keepdims=True) + EPS)


def bias_kernel(pair_ref, weight_ref, mask_ref, out_ref, flat_ref):
    _, count, length, width = pair_ref.shape
    whole = flat_ref.shape[0] // H
    weight = jnp.concatenate([weight_ref[...]] * 2, axis=1)
    base = pl.program_id(0) * count

    def step(n, carry):
        k = n * MANY
        centred, inv_std = pair_columns(pair_ref, k, MANY)
        bias = matmul(weight, jnp.concatenate(halves(centred), axis=0)) * inv_std
        for m in range(MANY):
            lanes = slice(m * 2 * length, (m + 1) * 2 * length)
            flat_ref[pl.ds(base + k + m, H, stride=whole), :] = bias[:, lanes]
        return carry

    lax.fori_loop(0, count // MANY, step, 0, unroll=2)

    @pl.when(pl.program_id(0) == pl.num_programs(0) - 1)
    def _():
        keep = jnp.broadcast_to(mask_ref[...].astype(jnp.float32), (128, length)).T
        keep = jnp.concatenate([keep] * (2 * whole // 128), axis=1) == 1.0
        for h in range(H):
            turned = flat_ref[h * whole : (h + 1) * whole, :].T
            bias = jnp.concatenate([turned[:length], turned[length:]], axis=1)
            out_ref[h] = jnp.where(keep, bias, MASKED)


STEPS = 4


def split_spec(shape):
    block = (shape[0] // STEPS,) + tuple(shape[1:])
    return pl.BlockSpec(block, lambda i: (i,) + (0,) * (len(shape) - 1))


def whole_spec(shape):
    return pl.BlockSpec(tuple(shape), lambda i: (0,) * len(shape))


def pair_spec(pair):
    row_count, tok_col, width = pair.shape
    block = (2, row_count // 2 // STEPS, tok_col, width)
    return pl.BlockSpec(block, lambda i: (0, i, 0, 0))


def pair_bias(pair, weight_t, mask):
    row_count, tok_col, width = pair.shape
    whole = row_count // 2
    return pl.pallas_call(
        bias_kernel,
        out_shape=jax.ShapeDtypeStruct((H, tok_col, row_count), jnp.float32),
        grid=(STEPS,),
        in_specs=[pair_spec(pair), whole_spec(weight_t.shape), whole_spec(mask.shape)],
        out_specs=whole_spec((H, tok_col, row_count)),
        scratch_shapes=[pltpu.VMEM((H * whole, 2 * tok_col), jnp.float32)],
        compiler_params=params(24),
        cost_estimate=pl.CostEstimate(
            flops=6_000_000_000, bytes_accessed=5_000_000, transcendentals=0
        ),
        name="pair_bias",
    )(pair.reshape(2, whole, tok_col, width), weight_t, mask)


def norm_kernel(pair_ref, normed_ref, inv_ref):
    def step(n, carry):
        centred, inv_std = pair_columns(pair_ref, n * MANY, MANY)
        normed_ref[n] = jnp.concatenate(halves(centred * inv_std), axis=0)
        inv_ref[n] = jnp.broadcast_to(inv_std, inv_ref.shape[1:])
        return carry

    lax.fori_loop(0, normed_ref.shape[0], step, 0, unroll=2)


def pair_units(pair):
    row_count, tok_col, width = pair.shape
    whole = row_count // 2
    chunks, lanes = whole // MANY, MANY * 2 * tok_col
    shapes = [(chunks, 2 * width, lanes), (chunks, 8, lanes)]
    return pl.pallas_call(
        norm_kernel,
        out_shape=[
            pltpu.VMEM(shapes[0], jnp.bfloat16),
            pltpu.VMEM(shapes[1], jnp.float32),
        ],
        grid=(STEPS,),
        in_specs=[pair_spec(pair)],
        out_specs=[split_spec(shape) for shape in shapes],
        compiler_params=params(24),
        cost_estimate=pl.CostEstimate(
            flops=6_000_000_000, bytes_accessed=12_000_000, transcendentals=0
        ),
        name="pair_units",
    )(pair.reshape(2, whole, tok_col, width))


def shift_of(top):
    return jnp.floor(jnp.clip(14.0 - jnp.log2(top), -100.0, 100.0))


def attention_kernel(col_ref, *refs):
    other_ref, bias_ref, back_ref, grad_bias_ref, sum_ref, tokens_ref = refs[-6:]
    col = col_ref[0]
    for offset, ref in enumerate(refs[:-6]):
        tokens_ref[col ^ (2 * offset)] = ref[0]
        tokens_ref[col ^ (2 * offset + 1)] = other_ref[offset]
    n_col = tokens_ref.shape[0]
    tok_col, row_count = bias_ref.shape[1:]
    half = back_ref.shape[2] // tok_col
    n_row = bias_ref.shape[0] // n_col
    step = pl.program_id(0)

    @pl.when(step == 0)
    def _():
        sum_ref[...] = jnp.zeros_like(sum_ref)

    outs = []
    for sample in range(half):
        lanes = slice(sample * tok_col, (sample + 1) * tok_col)

        def side(slot):
            return jnp.concatenate([tokens_ref[c, slot, :, lanes] for c in range(n_col)], axis=1)

        query_t, key_t, value_t, grad_t = [side(slot) for slot in range(4)]
        key = key_t.T
        value = value_t.T
        attended_parts, grad_query_parts = [], []
        grad_key = jnp.zeros(key_t.shape, jnp.float32)
        grad_value = jnp.zeros(key_t.shape, jnp.float32)
        for block in range(n_row):
            cols = slice(block * row_count, (block + 1) * row_count)
            heads = slice(block * n_col, (block + 1) * n_col)
            bias = bias_ref[heads].reshape(n_col * tok_col, row_count)
            query_b = query_t[:, cols]
            grad_b = grad_t[:, cols]
            scores = matmul(key, query_b) * SCALE + bias
            scores = jnp.where(bias < -60000.0, -1000000000.0, scores)
            expo = jnp.exp(scores - jnp.max(scores, axis=0, keepdims=True))
            share = 1.0 / jnp.sum(expo, axis=0, keepdims=True)
            attended = matmul(value_t, expo.astype(jnp.bfloat16)) * share
            delta = jnp.sum(grad_b.astype(jnp.float32) * attended, axis=0, keepdims=True)
            probs = expo * share
            grad_scores = probs * (matmul(value, grad_b) - delta)
            rounded = grad_scores.astype(jnp.bfloat16)
            attended_parts.append(attended)
            grad_query_parts.append(matmul(key_t, rounded) * SCALE)
            grad_key = grad_key + matmul_nt(query_b, rounded)
            grad_value = grad_value + matmul_nt(grad_b, probs.astype(jnp.bfloat16))
            sum_ref[heads] += grad_scores.reshape(n_col, tok_col, row_count)
        outs.append(
            (
                jnp.concatenate(grad_query_parts, axis=1),
                grad_key * SCALE,
                grad_value,
                jnp.concatenate(attended_parts, axis=1),
            )
        )
    spare = jnp.zeros((8 - 4, half * tok_col), jnp.float32)
    tops = [jnp.max(jnp.abs(out[slot]), axis=0, keepdims=True) for slot in range(4) for out in outs]
    shifts = shift_of(jnp.concatenate(tops, axis=0))
    scales = jnp.exp2(shifts)
    scaled = [
        [out[slot] * scales[slot * half + n : slot * half + n + 1] for n, out in enumerate(outs)]
        for slot in range(4)
    ]
    for c in range(n_col):
        lanes = slice(c * tok_col, (c + 1) * tok_col)
        for slot in range(4):
            back_ref[c, slot * CH : (slot + 1) * CH, :] = jnp.concatenate(
                [part[:, lanes] for part in scaled[slot]], axis=1
            )
        tails = [
            jnp.concatenate([shifts[slot * half + n :, lanes][:1] for n in range(half)], axis=1)
            for slot in range(4)
        ]
        back_ref[c, 4 * CH :, :] = jnp.concatenate(tails + [spare], axis=0)

    @pl.when(step == pl.num_programs(0) - 1)
    def _():
        for head in range(n_row * n_col):
            sums = sum_ref[head]
            shift = shift_of(jnp.max(jnp.abs(sums), axis=0, keepdims=True))
            grad_bias_ref[head, :tok_col, :] = sums * jnp.exp2(shift)
            grad_bias_ref[head, tok_col:, :] = jnp.broadcast_to(shift, (8, row_count))


def attention(col, arrived, other, bias, n_row):
    count = len(arrived)
    n_col = 2 * count
    _, tok_col, row_count = bias.shape
    half = arrived[0].shape[-1] // tok_col // n_row
    width = half * tok_col
    back_shape = (n_row * n_col, 4 * CH + 8, width)
    bias_shape = (n_row * n_col, tok_col + 8, row_count)
    return pl.pallas_call(
        attention_kernel,
        out_shape=[
            pltpu.VMEM(back_shape, jnp.float32),
            pltpu.VMEM(bias_shape, jnp.float32),
        ],
        grid_spec=pltpu.PrefetchScalarGridSpec(
            num_scalar_prefetch=1,
            grid=(n_row,),
            in_specs=[pl.BlockSpec((1, 4, CH, width), lambda i, r: (0, 0, 0, i))] * count
            + [
                pl.BlockSpec((count, 4, CH, width), lambda i, r: (0, 0, 0, i)),
                pl.BlockSpec(bias.shape, lambda i, r: (0, 0, 0)),
            ],
            out_specs=[
                pl.BlockSpec((n_col, 4 * CH + 8, width), lambda i, r: (i, 0, 0)),
                pl.BlockSpec(bias_shape, lambda i, r: (0, 0, 0)),
            ],
            scratch_shapes=[
                pltpu.VMEM(bias.shape, jnp.float32),
                pltpu.VMEM((n_col, 4, CH, width), jnp.bfloat16),
            ],
        ),
        compiler_params=params(24),
        cost_estimate=pl.CostEstimate(
            flops=8_000_000_000, bytes_accessed=6_000_000, transcendentals=1_000_000
        ),
        name="attention",
    )(col, *arrived, other, bias)


def back_kernel(*refs):
    slope_ref, normed_ref, inv_ref, wq_ref, wk_ref, wv_ref, wg_ref = refs[-11:-4]
    out_ref, parts_ref, gate_ref, total_ref = refs[-4:]
    back_ref = refs[0]
    count = normed_ref.shape[-1]
    step = pl.program_id(0)
    rows = wq_ref.shape[0]

    @pl.when(step == 0)
    def _():
        for slot in range(4):
            scale = jnp.exp2(-back_ref[:, 4 * CH + slot : 4 * CH + slot + 1, :])
            values = back_ref[:, slot * CH : (slot + 1) * CH, :] * scale
            values = values.reshape(gate_ref.shape)
            if slot < 3:
                parts_ref[slot] = jnp.concatenate(halves(values), axis=1)
            else:
                gate_ref[...] = (values * slope_ref[...]).astype(jnp.bfloat16)

    total = matmul(wg_ref[...], gate_ref[...])
    for slot, ref in enumerate((wq_ref, wk_ref, wv_ref)):
        parts = matmul(ref[...], parts_ref[slot])
        total = total + (parts[:, :count] + parts[:, count:])
    total_ref[pl.ds(pl.multiple_of(step * rows, 8), rows), :] = total

    @pl.when(step == pl.num_programs(0) - 1)
    def _():
        whole = total_ref[...]
        normed = normed_ref[...]
        result = inv_ref[:1] * (
            whole
            - jnp.mean(whole, axis=0, keepdims=True)
            - normed * jnp.mean(whole * normed, axis=0, keepdims=True)
        )
        out_ref[...] = result.T.astype(jnp.bfloat16)


def token_back(back, slope, normed, inv_std, weights):
    count = normed.shape[-1]
    steps = 2
    whole = lambda shape: pl.BlockSpec(shape, lambda i: (0,) * len(shape))
    weight_spec = pl.BlockSpec((D // steps, D), lambda i: (i, 0))
    return pl.pallas_call(
        back_kernel,
        out_shape=jax.ShapeDtypeStruct((count, D), jnp.bfloat16),
        grid=(steps,),
        in_specs=[whole(array.shape) for array in (back, slope, normed, inv_std)]
        + [weight_spec] * 4,
        out_specs=whole((count, D)),
        scratch_shapes=[
            pltpu.VMEM((3, D, 2 * count), jnp.bfloat16),
            pltpu.VMEM((D, count), jnp.bfloat16),
            pltpu.VMEM((D, count), jnp.float32),
        ],
        compiler_params=params(40),
        cost_estimate=pl.CostEstimate(
            flops=4_000_000_000, bytes_accessed=8_000_000, transcendentals=0
        ),
        name="token_back",
    )(back, slope, normed, inv_std, *weights)


def flatten(grads_ref, flat_ref):
    whole = flat_ref.shape[0] // H
    for h in range(H):
        grads = grads_ref[h]
        both = jnp.concatenate([grads[:, :whole], grads[:, whole:]], axis=0)
        flat_ref[h * whole : (h + 1) * whole, :] = both.T


def flat_columns(flat_ref, k, many):
    whole = flat_ref.shape[0] // H
    grads = [flat_ref[pl.ds(k + m, H, stride=whole), :] for m in range(many)]
    return jnp.concatenate(halves(jnp.concatenate(grads, axis=1)), axis=0)


def pair_weight_kernel(normed_ref, grads_ref, part_ref, flat_ref):
    chunks, width, _ = normed_ref.shape
    base = pl.program_id(0) * chunks

    @pl.when(pl.program_id(0) == 0)
    def _():
        part_ref[...] = jnp.zeros_like(part_ref)
        flatten(grads_ref, flat_ref)

    def step(n, carry):
        return carry + matmul_nt(normed_ref[n], flat_columns(flat_ref, (base + n) * MANY, MANY))

    parts = lax.fori_loop(0, chunks, step, jnp.zeros((width, 2 * H), jnp.float32), unroll=2)
    parts = parts[:, :H] + parts[:, H:]
    part_ref[...] += (parts[: width // 2] + parts[width // 2 :]).T


def pair_back_kernel(factor, normed_ref, inv_ref, grads_ref, weight_ref, out_ref, flat_ref):
    _, count, length, width = out_ref.shape
    weight = weight_ref[...].astype(jnp.float32)
    weight = halves(weight - jnp.mean(weight, axis=1, keepdims=True))
    weight = jnp.concatenate([weight[0], weight[0], weight[1], weight[1]], axis=0).T
    base = pl.program_id(0) * count

    @pl.when(pl.program_id(0) == 0)
    def _():
        flatten(grads_ref, flat_ref)

    def step(n, carry):
        k = n * MANY
        normed = normed_ref[n].astype(jnp.float32)
        normed = normed[:width] + normed[width:]
        grads = flat_columns(flat_ref, base + k, MANY)
        grad_in = matmul(weight, jnp.concatenate([grads, grads], axis=0))
        overlap = jnp.mean(grad_in * normed, axis=0, keepdims=True)
        result = (grad_in - normed * overlap) * (inv_ref[n, :1] * factor)
        result = result.astype(jnp.bfloat16).T.reshape(MANY, 2 * length, width)
        for p in range(2):
            out_ref[p, pl.ds(k, MANY)] = result[:, p * length : (p + 1) * length]
        return carry

    lax.fori_loop(0, count // MANY, step, 0, unroll=2)


def pair_weight(normed, grads):
    heads, length, rows = grads.shape
    part_shape = (H, normed.shape[1] // 2)
    return pl.pallas_call(
        pair_weight_kernel,
        out_shape=jax.ShapeDtypeStruct(part_shape, jnp.float32),
        grid=(STEPS,),
        in_specs=[split_spec(normed.shape), whole_spec(grads.shape)],
        out_specs=whole_spec(part_shape),
        scratch_shapes=[pltpu.VMEM((H * rows // 2, 2 * length), jnp.float32)],
        compiler_params=params(24),
        cost_estimate=pl.CostEstimate(
            flops=5_000_000_000, bytes_accessed=100_000, transcendentals=0
        ),
        name="pair_weight",
    )(normed, grads)


def pair_backward(shape, normed, inv_std, grads, weight_t, factor):
    row_count, tok_col, width = shape
    whole = row_count // 2
    pair_grad = pl.pallas_call(
        lambda *refs: pair_back_kernel(factor, *refs),
        out_shape=jax.ShapeDtypeStruct((2, whole, tok_col, width), jnp.bfloat16),
        grid=(STEPS,),
        in_specs=[
            split_spec(normed.shape),
            split_spec(inv_std.shape),
            whole_spec(grads.shape),
            whole_spec(weight_t.shape),
        ],
        out_specs=pl.BlockSpec((2, whole // STEPS, tok_col, width), lambda i: (0, i, 0, 0)),
        scratch_shapes=[pltpu.VMEM((H * whole, 2 * tok_col), jnp.float32)],
        compiler_params=params(24),
        cost_estimate=pl.CostEstimate(
            flops=8_000_000_000, bytes_accessed=100_000, transcendentals=0
        ),
        name="pair_backward",
    )(normed, inv_std, grads, weight_t)
    return pair_grad.reshape(shape)


def unscaled(block, rows):
    block = block.astype(jnp.float32)
    return block[:, :rows] * jnp.exp2(-block[:, rows : rows + 1])


def swap(block, axis):
    return lax.ppermute(block, axis, [(0, 1), (1, 0)])


def body_heads(
    tokens, restype, type_table, key_mask, pair, w_bias, w_query, w_key, w_value, w_gate, cotangent
):
    n_row = lax.axis_size("row")
    n_col = lax.axis_size("col")
    n_samp = lax.axis_size("samp")
    samp_dev = tokens.shape[0]
    tok_col = tokens.shape[1]
    row_count = pair.shape[0]
    total_tokens = tok_col * n_col
    half = samp_dev // n_row
    row_index = lax.axis_index("row")
    row = row_index.astype(jnp.int32).reshape(1)
    col = lax.axis_index("col").astype(jnp.int32).reshape(1)
    types = restype.reshape(1, tok_col)
    weight_t = w_bias.T
    weights = (w_query, w_key, w_value, w_gate)
    samples = samp_dev * n_samp

    def send(block, offset):
        return lax.ppermute(block, "col", [(c, c ^ offset) for c in range(n_col)])

    def by_chip(blocks):
        return [blocks[0]] + [send(blocks[n], 2 * n) for n in range(1, n_col // 2)]

    def across(blocks):
        return send(jnp.stack([block[1] for block in blocks]), 1)

    messages = token_messages(
        row, col, tokens, types, type_table, weights, cotangent, n_row, n_col
    )
    arrived = by_chip(messages)
    bias = pair_bias(pair, weight_t, key_mask.reshape(1, tok_col))
    bias, arrived, types = lax.optimization_barrier(
        (bias.astype(jnp.float16), arrived, types)
    )
    own = own_rows(row, tokens, types, type_table, w_gate, cotangent, half)
    bias = lax.all_to_all(bias, ("row", "col"), 0, 0, tiled=True)
    other = across(arrived)
    bias, other, own = lax.optimization_barrier((bias, other, own))

    back, grad_bias = attention(col, arrived, other, bias.astype(jnp.float32), n_row)
    grad_bias = lax.all_to_all(
        grad_bias.astype(jnp.float16), ("row", "col"), 0, 0, tiled=True
    )
    back, late_pair = lax.optimization_barrier((back.astype(jnp.float16), pair))
    pair_normed, pair_inv = pair_units(late_pair)
    back, _, pair_normed = lax.optimization_barrier((back, grad_bias, pair_normed))
    back = lax.all_to_all(back, ("row", "col"), 0, 0, tiled=True)

    other_bias = swap(grad_bias, "samp")
    own_bias = unscaled(grad_bias, tok_col)
    part = pair_weight(pair_normed, own_bias)
    samp_part = swap(part, "samp")
    row_part = swap(part, "row")
    both_part = lax.ppermute(part, ("samp", "row"), [(n, 3 - n) for n in range(4)])
    other_bias, part = lax.optimization_barrier((other_bias, part))
    grads = own_bias + unscaled(other_bias, tok_col)
    part = (part + samp_part) + (row_part + both_part)
    grads, part = lax.optimization_barrier((grads, part))
    sums = (send(part, 1), send(part, 2), send(part, 3))
    pair_grad = pair_backward(
        pair.shape, pair_normed, pair_inv, grads, weight_t, total_tokens / samples
    )

    pair_grad, back, sums = lax.optimization_barrier((pair_grad, back, sums))
    part = (part + sums[0]) + (sums[1] + sums[2])
    last = send(part, 4)
    token_half = token_back(back.astype(jnp.float32), *own, weights)
    token_half, last = lax.optimization_barrier((token_half, last))
    part = part + last
    token_half = token_half.reshape(half, tok_col, D)
    other_half = swap(token_half, "row")
    first = row_index == 0
    token_grad = jnp.concatenate(
        [jnp.where(first, token_half, other_half), jnp.where(first, other_half, token_half)],
        axis=0,
    )
    return (token_grad, pair_grad, part.T / samples)


def body(*args):
    n_row = lax.axis_size("row")
    n_col = lax.axis_size("col")
    tokens = args[0]
    pair = args[4]
    fits = n_row == 2 and n_col == 8 and n_row * n_col == H and lax.axis_size("samp") == 2
    square = pair.shape[0] * n_row == pair.shape[1] * n_col
    if fits and square and tokens.shape[0] == 4 and tokens.shape[1] == 64:
        return body_heads(*args)
    return body_any(*args)


def solution(mesh):
    placed = (
        P("samp", "col", None),
        P("col"),
        P(),
        P("col"),
        P("row", "col", None),
        P(),
        P(),
        P(),
        P(),
        P(),
        P("samp", "col", None),
    )
    return jax.shard_map(
        body,
        mesh=mesh,
        in_specs=placed,
        out_specs=(P("samp", "col", None), P("row", "col", None), P()),
        check_vma=False,
    )
```

```python
import math

import jax
import jax.numpy as jnp
from jax import lax
from jax.experimental import pallas as pl
from jax.experimental.pallas import tpu as pltpu
from jax.sharding import PartitionSpec as P

D = 768
H = 16
CH = 48
NTYPE = 32


def broadcast(block, axis, source):
    block = jnp.where(lax.axis_index(axis) == source, block, jnp.zeros_like(block))
    return lax.psum(block, axis)


def token_norm(tokens, restype, type_table):
    onehot = (restype[:, None] == jnp.arange(NTYPE, dtype=jnp.int32)[None, :]).astype(jnp.bfloat16)
    embedded = tokens.astype(jnp.float32) + jnp.dot(
        onehot, type_table, preferred_element_type=jnp.float32
    )
    centred = embedded - jnp.mean(embedded, axis=-1, keepdims=True)
    inv_std = lax.rsqrt(jnp.mean(centred * centred, axis=-1, keepdims=True) + 1e-05)
    return (centred * inv_std, inv_std)


def pair_norm(block):
    values = block.astype(jnp.float32)
    centred = values - jnp.mean(values, axis=-1, keepdims=True)
    inv_std = lax.rsqrt(jnp.mean(centred * centred, axis=-1, keepdims=True) + 1e-05)
    return (centred * inv_std, inv_std)


def norm_back(grad_in, normed, inv_std):
    return inv_std * (
        grad_in
        - jnp.mean(grad_in, axis=-1, keepdims=True)
        - normed * jnp.mean(grad_in * normed, axis=-1, keepdims=True)
    )


def project(rows_in, weight):
    return jnp.einsum("std,de->ste", rows_in, weight, preferred_element_type=jnp.float32).astype(
        jnp.bfloat16
    )


def back_project(grads, weight):
    return jnp.einsum(
        "ste,de->std", grads, weight.astype(jnp.float32), precision=lax.Precision.HIGHEST
    )


def pair_back(grad_bias, pair_normed, pair_inv, bias_weight):
    grad_normed = jnp.einsum("hij,ch->ijc", grad_bias, bias_weight, precision=lax.Precision.HIGHEST)
    return norm_back(grad_normed, pair_normed, pair_inv)


def body_any(
    tokens, restype, type_table, key_mask, pair, w_bias, w_query, w_key, w_value, w_gate, cotangent
):
    n_row = lax.axis_size("row")
    n_col = lax.axis_size("col")
    n_samp = lax.axis_size("samp")
    samp_dev = tokens.shape[0]
    tok_col = tokens.shape[1]
    spread = n_col // n_row
    row_count = tok_col * spread
    total_tokens = tok_col * n_col
    row_index = lax.axis_index("row")
    col_index = lax.axis_index("col")
    is_owner = col_index // spread == row_index
    own_start = col_index % spread * tok_col
    normed, inv_std = token_norm(tokens, restype, type_table)
    own_act = normed.astype(jnp.bfloat16)
    key_proj = project(own_act, w_key)
    value_proj = project(own_act, w_value)
    stacked = jnp.stack([own_act, cotangent])
    pieces = [broadcast(stacked, "col", row_index * spread + member) for member in range(spread)]
    gathered = jnp.concatenate(pieces, axis=2)
    query_side = gathered[0]
    grad_rows = gathered[1]
    queries = project(query_side, w_query)
    gate_lin = project(query_side, w_gate)
    pair_normed, pair_inv = pair_norm(pair)
    bias_weight = w_bias.astype(jnp.float32)
    bias = jnp.einsum("ijc,ch->hij", pair_normed, bias_weight, precision=lax.Precision.HIGHEST)
    query_heads = queries.reshape(samp_dev, row_count, H, CH)
    key_heads = key_proj.reshape(samp_dev, tok_col, H, CH)
    value_heads = value_proj.reshape(samp_dev, tok_col, H, CH)
    scores = (
        jnp.einsum("sihc,sjhc->shij", query_heads, key_heads, preferred_element_type=jnp.float32)
        / math.sqrt(CH)
        + bias[None]
    )
    scores = jnp.where(key_mask[None, None, None, :] == 1, scores, -1000000000.0)
    top = lax.pmax(jnp.max(scores, axis=-1), "col")
    expo = jnp.exp(scores - top[..., None])
    partial_out = jnp.einsum(
        "shij,sjhc->sihc",
        expo.astype(jnp.bfloat16),
        value_heads,
        preferred_element_type=jnp.float32,
    )
    totals, summed = lax.psum(
        (jnp.sum(expo, axis=-1), partial_out.reshape(samp_dev, row_count, D)), "col"
    )
    attended = (
        summed.reshape(samp_dev, row_count, H, CH) / jnp.transpose(totals, (0, 2, 1))[..., None]
    )
    flat_out = attended.reshape(samp_dev, row_count, D)
    sig_gate = jax.nn.sigmoid(gate_lin.astype(jnp.float32))
    grad_f = grad_rows.astype(jnp.float32)
    grad_out = (grad_f * sig_gate).astype(jnp.bfloat16)
    grad_gate = (grad_f * flat_out * sig_gate * (1.0 - sig_gate)).astype(jnp.bfloat16)
    gate_piece = lax.dynamic_slice_in_dim(grad_gate, own_start, tok_col, 1)
    gate_term = jnp.where(
        is_owner,
        jnp.einsum("ste,de->std", gate_piece, w_gate, preferred_element_type=jnp.float32),
        0.0,
    )
    grad_heads = grad_out.reshape(samp_dev, row_count, H, CH)
    delta = jnp.transpose(jnp.sum(grad_heads.astype(jnp.float32) * attended, axis=-1), (0, 2, 1))
    probs = expo / totals[..., None]
    grad_pre = jnp.einsum(
        "sihc,sjhc->shij", grad_heads, value_heads, preferred_element_type=jnp.float32
    )
    grad_scores = probs * (grad_pre - delta[..., None])
    rounded = grad_scores.astype(jnp.bfloat16)
    grad_query = (
        jnp.einsum("shij,sjhc->sihc", rounded, key_heads, preferred_element_type=jnp.float32)
        / math.sqrt(CH)
    ).reshape(samp_dev, row_count, D)
    grad_key = (
        jnp.einsum("shij,sihc->sjhc", rounded, query_heads, preferred_element_type=jnp.float32)
        / math.sqrt(CH)
    ).reshape(samp_dev, tok_col, D)
    grad_value = jnp.einsum(
        "shij,sihc->sjhc",
        probs.astype(jnp.bfloat16),
        grad_heads,
        preferred_element_type=jnp.float32,
    ).reshape(samp_dev, tok_col, D)
    bias_local = jnp.sum(grad_scores, axis=0)
    blank = jnp.zeros((samp_dev, total_tokens, D), jnp.float32)
    mine = lax.psum_scatter(
        lax.dynamic_update_slice_in_dim(blank, grad_query, row_index * row_count, 1),
        "col",
        scatter_dimension=1,
        tiled=True,
    )
    query_all, key_all, value_all, gate_all = lax.psum(
        (mine, grad_key, grad_value, gate_term), "row"
    )
    grad_act = (
        back_project(query_all, w_query)
        + back_project(key_all, w_key)
        + back_project(value_all, w_value)
        + gate_all
    )
    token_grad = norm_back(grad_act, normed, inv_std).astype(jnp.bfloat16)
    samples = samp_dev * n_samp
    grad_bias = lax.psum(bias_local, "samp")
    grad_pair = pair_back(grad_bias, pair_normed, pair_inv, bias_weight)
    pair_grad = (grad_pair * (total_tokens / samples)).astype(jnp.bfloat16)
    weight_part = jnp.einsum("ijc,hij->ch", pair_normed, grad_bias, precision=lax.Precision.HIGHEST)
    weight_sum = lax.psum(weight_part, ("row", "col"))
    bias_weight_grad = weight_sum / samples
    return (token_grad, pair_grad, bias_weight_grad)


EPS = 1e-05
SCALE = 1.0 / math.sqrt(CH)
NT = (((1,), (1,)), ((), ()))
TN = (((0,), (0,)), ((), ()))
MASKED = -65504.0


def params(megabytes):
    return pltpu.CompilerParams(vmem_limit_bytes=megabytes * 1024 * 1024)


def matmul(left, right):
    return jnp.dot(left, right, preferred_element_type=jnp.float32)


def matmul_nt(left, right):
    return lax.dot_general(left, right, NT, preferred_element_type=jnp.float32)


def matmul_tn(left, right):
    return lax.dot_general(left, right, TN, preferred_element_type=jnp.float32)


def halves(values):
    high = values.astype(jnp.bfloat16)
    low = (values - high.astype(jnp.float32)).astype(jnp.bfloat16)
    return high, low


def unit_rows(values):
    centred = values - jnp.mean(values, axis=-1, keepdims=True)
    inv_std = lax.rsqrt(jnp.mean(centred * centred, axis=-1, keepdims=True) + EPS)
    return centred * inv_std, inv_std


def embed_rows(tokens_ref, types_ref, table_ref):
    count, length, width = tokens_ref.shape
    index = lax.broadcasted_iota(jnp.int32, (NTYPE, length), 0)
    onehot = jnp.where(types_ref[...] == index, 1.0, 0.0).astype(jnp.bfloat16)
    added = matmul_tn(onehot, table_ref[...])
    embedded = tokens_ref[...].astype(jnp.float32) + added[None]
    return unit_rows(embedded.reshape(count * length, width))


def token_kernel(row_ref, col_ref, tokens_ref, types_ref, table_ref, *refs):
    wq_ref, wk_ref, wv_ref, wg_ref, cot_ref = refs[:5]
    out_refs, side_ref = refs[5:-1], refs[-1]
    normed, _ = embed_rows(tokens_ref, types_ref, table_ref)
    act = normed.astype(jnp.bfloat16)
    for slot, ref in enumerate((wq_ref, wk_ref, wv_ref)):
        side_ref[slot] = matmul(act, ref[...]).astype(jnp.bfloat16).T
    gate = matmul(act, wg_ref[...]).astype(jnp.bfloat16).astype(jnp.float32)
    cot = cot_ref[...].reshape(gate.shape).astype(jnp.float32)
    side_ref[3] = (cot * jax.nn.sigmoid(gate)).astype(jnp.bfloat16).T
    for offset, out_ref in enumerate(out_refs):
        for core in range(2):
            start = pl.multiple_of((col_ref[0] ^ (2 * offset + core)) * CH, 16)
            out_ref[core] = side_ref[:, pl.ds(start, CH), :]


def token_messages(row, col, tokens, types, table, weights, cotangent, n_row, n_col):
    samp_dev, tok_col, _ = tokens.shape
    width = D // n_row
    held = samp_dev * tok_col
    whole3 = lambda i, r, c: (0, 0, 0)
    whole2 = lambda i, r, c: (0, 0)
    weight_spec = pl.BlockSpec((D, width), lambda i, r, c: (0, r[0]))
    shape = (2, 4, CH, held)
    count = n_col // 2
    return pl.pallas_call(
        token_kernel,
        out_shape=[jax.ShapeDtypeStruct(shape, jnp.bfloat16)] * count,
        grid_spec=pltpu.PrefetchScalarGridSpec(
            num_scalar_prefetch=2,
            grid=(1,),
            in_specs=[
                pl.BlockSpec(tokens.shape, whole3),
                pl.BlockSpec(types.shape, whole2),
                pl.BlockSpec(table.shape, whole2),
                weight_spec,
                weight_spec,
                weight_spec,
                weight_spec,
                pl.BlockSpec((samp_dev, tok_col, width), lambda i, r, c: (0, 0, r[0])),
            ],
            out_specs=[pl.BlockSpec(shape, lambda i, r, c: (0, 0, 0, 0))] * count,
            scratch_shapes=[pltpu.VMEM((4, width, held), jnp.bfloat16)],
        ),
        compiler_params=params(56),
        cost_estimate=pl.CostEstimate(
            flops=4_000_000_000, bytes_accessed=4_000_000, transcendentals=0
        ),
        name="token_messages",
    )(row, col, tokens, types, table, *weights, cotangent)


def own_kernel(
    row_ref, tokens_ref, types_ref, table_ref, wg_ref, cot_ref, slope_ref, normed_ref, inv_ref
):
    normed, inv_std = embed_rows(tokens_ref, types_ref, table_ref)
    gate = matmul(normed.astype(jnp.bfloat16), wg_ref[...]).astype(jnp.bfloat16)
    sig = jax.nn.sigmoid(gate.astype(jnp.float32))
    cot = cot_ref[...].reshape(gate.shape).astype(jnp.float32)
    slope_ref[...] = (cot * sig * (1.0 - sig)).T
    normed_ref[...] = normed.T
    inv_ref[...] = jnp.broadcast_to(inv_std, (inv_std.shape[0], 128)).T[:8]


def own_rows(row, tokens, types, table, w_gate, cotangent, half):
    _, tok_col, _ = tokens.shape
    count = half * tok_col
    part_spec = pl.BlockSpec((half, tok_col, D), lambda i, r: (r[0], 0, 0))
    whole2 = lambda i, r: (0, 0)
    return pl.pallas_call(
        own_kernel,
        out_shape=[
            jax.ShapeDtypeStruct((D, count), jnp.float32),
            jax.ShapeDtypeStruct((D, count), jnp.float32),
            jax.ShapeDtypeStruct((8, count), jnp.float32),
        ],
        grid_spec=pltpu.PrefetchScalarGridSpec(
            num_scalar_prefetch=1,
            grid=(1,),
            in_specs=[
                part_spec,
                pl.BlockSpec(types.shape, whole2),
                pl.BlockSpec(table.shape, whole2),
                pl.BlockSpec(w_gate.shape, whole2),
                part_spec,
            ],
            out_specs=[
                pl.BlockSpec((D, count), whole2),
                pl.BlockSpec((D, count), whole2),
                pl.BlockSpec((8, count), whole2),
            ],
        ),
        compiler_params=params(56),
        cost_estimate=pl.CostEstimate(
            flops=3_000_000_000, bytes_accessed=3_000_000, transcendentals=0
        ),
        name="own_rows",
    )(row, tokens, types, table, w_gate, cotangent)


MANY = 4
PARTS = 2


def pair_columns(pair_ref, k, many):
    _, _, length, width = pair_ref.shape
    blocks = [pair_ref[p, pl.ds(k, many)] for p in range(2)]
    rows = jnp.concatenate(blocks, axis=1).reshape(many * 2 * length, width)
    same = lax.broadcasted_iota(jnp.int32, (width, width), 0) == lax.broadcasted_iota(
        jnp.int32, (width, width), 1
    )
    centring = (jnp.where(same, 1.0, 0.0) - 1.0 / width).astype(jnp.bfloat16)
    centred = matmul_nt(centring, rows)
    return centred, lax.rsqrt(jnp.mean(centred * centred, axis=0, keepdims=True) + EPS)


def bias_kernel(pair_ref, weight_ref, mask_ref, out_ref, flat_ref):
    _, count, length, width = pair_ref.shape
    whole = flat_ref.shape[0] // H
    weight = jnp.concatenate([weight_ref[...]] * 2, axis=1)
    base = pl.program_id(0) * count

    def step(n, carry):
        k = n * MANY
        centred, inv_std = pair_columns(pair_ref, k, MANY)
        bias = matmul(weight, jnp.concatenate(halves(centred), axis=0)) * inv_std
        for m in range(MANY):
            lanes = slice(m * 2 * length, (m + 1) * 2 * length)
            flat_ref[pl.ds(base + k + m, H, stride=whole), :] = bias[:, lanes]
        return carry

    lax.fori_loop(0, count // MANY, step, 0, unroll=2)

    @pl.when(pl.program_id(0) == pl.num_programs(0) - 1)
    def _():
        keep = jnp.broadcast_to(mask_ref[...].astype(jnp.float32), (128, length)).T
        keep = jnp.concatenate([keep] * (2 * whole // 128), axis=1) == 1.0
        for h in range(H):
            turned = flat_ref[h * whole : (h + 1) * whole, :].T
            bias = jnp.concatenate([turned[:length], turned[length:]], axis=1)
            out_ref[h] = jnp.where(keep, bias, MASKED)


STEPS = 4


def split_spec(shape):
    block = (shape[0] // STEPS,) + tuple(shape[1:])
    return pl.BlockSpec(block, lambda i: (i,) + (0,) * (len(shape) - 1))


def whole_spec(shape):
    return pl.BlockSpec(tuple(shape), lambda i: (0,) * len(shape))


def pair_spec(pair):
    row_count, tok_col, width = pair.shape
    block = (2, row_count // 2 // STEPS, tok_col, width)
    return pl.BlockSpec(block, lambda i: (0, i, 0, 0))


def pair_bias(pair, weight_t, mask):
    row_count, tok_col, width = pair.shape
    whole = row_count // 2
    return pl.pallas_call(
        bias_kernel,
        out_shape=jax.ShapeDtypeStruct((H, tok_col, row_count), jnp.float32),
        grid=(STEPS,),
        in_specs=[pair_spec(pair), whole_spec(weight_t.shape), whole_spec(mask.shape)],
        out_specs=whole_spec((H, tok_col, row_count)),
        scratch_shapes=[pltpu.VMEM((H * whole, 2 * tok_col), jnp.float32)],
        compiler_params=params(24),
        cost_estimate=pl.CostEstimate(
            flops=6_000_000_000, bytes_accessed=5_000_000, transcendentals=0
        ),
        name="pair_bias",
    )(pair.reshape(2, whole, tok_col, width), weight_t, mask)


def norm_kernel(pair_ref, normed_ref, inv_ref):
    def step(n, carry):
        centred, inv_std = pair_columns(pair_ref, n * MANY, MANY)
        normed_ref[n] = jnp.concatenate(halves(centred * inv_std), axis=0)
        inv_ref[n] = jnp.broadcast_to(inv_std, inv_ref.shape[1:])
        return carry

    lax.fori_loop(0, normed_ref.shape[0], step, 0, unroll=2)


def pair_units(pair):
    row_count, tok_col, width = pair.shape
    whole = row_count // 2
    chunks, lanes = whole // MANY, MANY * 2 * tok_col
    shapes = [(chunks, 2 * width, lanes), (chunks, 8, lanes)]
    return pl.pallas_call(
        norm_kernel,
        out_shape=[
            jax.ShapeDtypeStruct(shapes[0], jnp.bfloat16),
            jax.ShapeDtypeStruct(shapes[1], jnp.float32),
        ],
        grid=(STEPS,),
        in_specs=[pair_spec(pair)],
        out_specs=[split_spec(shape) for shape in shapes],
        compiler_params=params(56),
        cost_estimate=pl.CostEstimate(
            flops=6_000_000_000, bytes_accessed=12_000_000, transcendentals=0
        ),
        name="pair_units",
    )(pair.reshape(2, whole, tok_col, width))


def shift_of(top):
    return jnp.floor(jnp.clip(14.0 - jnp.log2(top), -100.0, 100.0))


def attention_kernel(col_ref, *refs):
    other_ref, bias_ref, back_ref, grad_bias_ref, sum_ref, tokens_ref = refs[-6:]
    col = col_ref[0]
    for offset, ref in enumerate(refs[:-6]):
        tokens_ref[col ^ (2 * offset)] = ref[0]
        tokens_ref[col ^ (2 * offset + 1)] = other_ref[offset]
    n_col = tokens_ref.shape[0]
    tok_col, row_count = bias_ref.shape[1:]
    half = back_ref.shape[2] // tok_col
    n_row = bias_ref.shape[0] // n_col
    step = pl.program_id(0)

    @pl.when(step == 0)
    def _():
        sum_ref[...] = jnp.zeros_like(sum_ref)

    outs = []
    for sample in range(half):
        lanes = slice(sample * tok_col, (sample + 1) * tok_col)

        def side(slot):
            return jnp.concatenate([tokens_ref[c, slot, :, lanes] for c in range(n_col)], axis=1)

        query_t, key_t, value_t, grad_t = [side(slot) for slot in range(4)]
        key = key_t.T
        value = value_t.T
        attended_parts, grad_query_parts = [], []
        grad_key = jnp.zeros(key_t.shape, jnp.float32)
        grad_value = jnp.zeros(key_t.shape, jnp.float32)
        for block in range(n_row):
            cols = slice(block * row_count, (block + 1) * row_count)
            heads = slice(block * n_col, (block + 1) * n_col)
            bias = bias_ref[heads].reshape(n_col * tok_col, row_count)
            query_b = query_t[:, cols]
            grad_b = grad_t[:, cols]
            scores = matmul(key, query_b) * SCALE + bias
            scores = jnp.where(bias < -60000.0, -1000000000.0, scores)
            expo = jnp.exp(scores - jnp.max(scores, axis=0, keepdims=True))
            share = 1.0 / jnp.sum(expo, axis=0, keepdims=True)
            attended = matmul(value_t, expo.astype(jnp.bfloat16)) * share
            delta = jnp.sum(grad_b.astype(jnp.float32) * attended, axis=0, keepdims=True)
            probs = expo * share
            grad_scores = probs * (matmul(value, grad_b) - delta)
            rounded = grad_scores.astype(jnp.bfloat16)
            attended_parts.append(attended)
            grad_query_parts.append(matmul(key_t, rounded) * SCALE)
            grad_key = grad_key + matmul_nt(query_b, rounded)
            grad_value = grad_value + matmul_nt(grad_b, probs.astype(jnp.bfloat16))
            sum_ref[heads] += grad_scores.reshape(n_col, tok_col, row_count)
        outs.append(
            (
                jnp.concatenate(grad_query_parts, axis=1),
                grad_key * SCALE,
                grad_value,
                jnp.concatenate(attended_parts, axis=1),
            )
        )
    spare = jnp.zeros((8 - 4, half * tok_col), jnp.float32)
    tops = [jnp.max(jnp.abs(out[slot]), axis=0, keepdims=True) for slot in range(4) for out in outs]
    shifts = shift_of(jnp.concatenate(tops, axis=0))
    scales = jnp.exp2(shifts)
    scaled = [
        [out[slot] * scales[slot * half + n : slot * half + n + 1] for n, out in enumerate(outs)]
        for slot in range(4)
    ]
    for c in range(n_col):
        lanes = slice(c * tok_col, (c + 1) * tok_col)
        for slot in range(4):
            back_ref[c, slot * CH : (slot + 1) * CH, :] = jnp.concatenate(
                [part[:, lanes] for part in scaled[slot]], axis=1
            )
        tails = [
            jnp.concatenate([shifts[slot * half + n :, lanes][:1] for n in range(half)], axis=1)
            for slot in range(4)
        ]
        back_ref[c, 4 * CH :, :] = jnp.concatenate(tails + [spare], axis=0)

    @pl.when(step == pl.num_programs(0) - 1)
    def _():
        piece = row_count // 2 // PARTS
        for head in range(n_row * n_col):
            sums = sum_ref[head]
            sums = jnp.concatenate(
                [
                    sums[:, (p * PARTS + n) * piece : (p * PARTS + n + 1) * piece]
                    for n in range(PARTS)
                    for p in range(2)
                ],
                axis=1,
            )
            shift = shift_of(jnp.max(jnp.abs(sums), axis=0, keepdims=True))
            grad_bias_ref[head, :tok_col, :] = sums * jnp.exp2(shift)
            grad_bias_ref[head, tok_col:, :] = jnp.broadcast_to(shift, (8, row_count))


def attention(col, arrived, other, bias, n_row):
    count = len(arrived)
    n_col = 2 * count
    _, tok_col, row_count = bias.shape
    half = arrived[0].shape[-1] // tok_col // n_row
    width = half * tok_col
    back_shape = (n_row * n_col, 4 * CH + 8, width)
    bias_shape = (n_row * n_col, tok_col + 8, row_count)
    return pl.pallas_call(
        attention_kernel,
        out_shape=[
            jax.ShapeDtypeStruct(back_shape, jnp.float32),
            jax.ShapeDtypeStruct(bias_shape, jnp.float32),
        ],
        grid_spec=pltpu.PrefetchScalarGridSpec(
            num_scalar_prefetch=1,
            grid=(n_row,),
            in_specs=[pl.BlockSpec((1, 4, CH, width), lambda i, r: (0, 0, 0, i))] * count
            + [
                pl.BlockSpec((count, 4, CH, width), lambda i, r: (0, 0, 0, i)),
                pl.BlockSpec(bias.shape, lambda i, r: (0, 0, 0)),
            ],
            out_specs=[
                pl.BlockSpec((n_col, 4 * CH + 8, width), lambda i, r: (i, 0, 0)),
                pl.BlockSpec(bias_shape, lambda i, r: (0, 0, 0)),
            ],
            scratch_shapes=[
                pltpu.VMEM(bias.shape, jnp.float32),
                pltpu.VMEM((n_col, 4, CH, width), jnp.bfloat16),
            ],
        ),
        compiler_params=params(24),
        cost_estimate=pl.CostEstimate(
            flops=8_000_000_000, bytes_accessed=6_000_000, transcendentals=1_000_000
        ),
        name="attention",
    )(col, *arrived, other, bias)


def back_kernel(*refs):
    slope_ref, normed_ref, inv_ref, wq_ref, wk_ref, wv_ref, wg_ref = refs[-11:-4]
    out_ref, parts_ref, gate_ref, total_ref = refs[-4:]
    back_ref = refs[0]
    count = normed_ref.shape[-1]
    step = pl.program_id(0)
    rows = wq_ref.shape[0]

    @pl.when(step == 0)
    def _():
        for slot in range(4):
            scale = jnp.exp2(-back_ref[:, 4 * CH + slot : 4 * CH + slot + 1, :])
            values = back_ref[:, slot * CH : (slot + 1) * CH, :] * scale
            values = values.reshape(gate_ref.shape)
            if slot < 3:
                parts_ref[slot] = jnp.concatenate(halves(values), axis=1)
            else:
                gate_ref[...] = (values * slope_ref[...]).astype(jnp.bfloat16)

    total = matmul(wg_ref[...], gate_ref[...])
    for slot, ref in enumerate((wq_ref, wk_ref, wv_ref)):
        parts = matmul(ref[...], parts_ref[slot])
        total = total + (parts[:, :count] + parts[:, count:])
    total_ref[pl.ds(pl.multiple_of(step * rows, 8), rows), :] = total

    @pl.when(step == pl.num_programs(0) - 1)
    def _():
        whole = total_ref[...]
        normed = normed_ref[...]
        result = inv_ref[:1] * (
            whole
            - jnp.mean(whole, axis=0, keepdims=True)
            - normed * jnp.mean(whole * normed, axis=0, keepdims=True)
        )
        out_ref[...] = result.T.astype(jnp.bfloat16)


def token_back(back, slope, normed, inv_std, weights):
    count = normed.shape[-1]
    steps = 2
    whole = lambda shape: pl.BlockSpec(shape, lambda i: (0,) * len(shape))
    weight_spec = pl.BlockSpec((D // steps, D), lambda i: (i, 0))
    return pl.pallas_call(
        back_kernel,
        out_shape=jax.ShapeDtypeStruct((count, D), jnp.bfloat16),
        grid=(steps,),
        in_specs=[whole(array.shape) for array in (back, slope, normed, inv_std)]
        + [weight_spec] * 4,
        out_specs=whole((count, D)),
        scratch_shapes=[
            pltpu.VMEM((3, D, 2 * count), jnp.bfloat16),
            pltpu.VMEM((D, count), jnp.bfloat16),
            pltpu.VMEM((D, count), jnp.float32),
        ],
        compiler_params=params(24),
        cost_estimate=pl.CostEstimate(
            flops=4_000_000_000, bytes_accessed=8_000_000, transcendentals=0
        ),
        name="token_back",
    )(back, slope, normed, inv_std, *weights)


def flatten(grads_ref, flat_ref):
    whole = flat_ref.shape[0] // H
    for h in range(H):
        grads = grads_ref[h]
        both = jnp.concatenate([grads[:, :whole], grads[:, whole:]], axis=0)
        flat_ref[h * whole : (h + 1) * whole, :] = both.T


def flat_columns(flat_ref, k, many):
    whole = flat_ref.shape[0] // H
    grads = [flat_ref[pl.ds(k + m, H, stride=whole), :] for m in range(many)]
    return jnp.concatenate(halves(jnp.concatenate(grads, axis=1)), axis=0)


def pair_weight_kernel(normed_ref, *refs):
    pieces, (part_ref, flat_ref) = refs[:-2], refs[-2:]
    chunks, width, _ = normed_ref.shape
    number = pl.program_id(0)
    steps = STEPS // len(pieces)
    base = lax.rem(number, steps) * chunks

    @pl.when(number == 0)
    def _():
        part_ref[...] = jnp.zeros_like(part_ref)

    for n, piece in enumerate(pieces):

        @pl.when(number == n * steps)
        def _():
            flatten(piece, flat_ref)

    def step(n, carry):
        return carry + matmul_nt(normed_ref[n], flat_columns(flat_ref, (base + n) * MANY, MANY))

    parts = lax.fori_loop(0, chunks, step, jnp.zeros((width, 2 * H), jnp.float32), unroll=2)
    parts = parts[:, :H] + parts[:, H:]
    part_ref[...] += (parts[: width // 2] + parts[width // 2 :]).T


def pair_back_kernel(factor, normed_ref, inv_ref, grads_ref, weight_ref, *refs):
    out_ref, flat_ref = refs[-2:]
    _, count, length, width = out_ref.shape
    weight = weight_ref[...].astype(jnp.float32)
    weight = halves(weight - jnp.mean(weight, axis=1, keepdims=True))
    weight = jnp.concatenate([weight[0], weight[0], weight[1], weight[1]], axis=0).T
    base = pl.program_id(0) * count

    @pl.when(pl.program_id(0) == 0)
    def _():
        flatten(grads_ref, flat_ref)

    def step(n, carry):
        k = n * MANY
        normed = normed_ref[n].astype(jnp.float32)
        normed = normed[:width] + normed[width:]
        grads = flat_columns(flat_ref, base + k, MANY)
        grad_in = matmul(weight, jnp.concatenate([grads, grads], axis=0))
        overlap = jnp.mean(grad_in * normed, axis=0, keepdims=True)
        result = (grad_in - normed * overlap) * (inv_ref[n, :1] * factor)
        result = result.astype(jnp.bfloat16).T.reshape(MANY, 2 * length, width)
        for p in range(2):
            out_ref[p, pl.ds(k, MANY)] = result[:, p * length : (p + 1) * length]
        return carry

    lax.fori_loop(0, count // MANY, step, 0, unroll=2)


def pair_weight(normed, pieces):
    _, length, rows = pieces[0].shape
    part_shape = (H, normed.shape[1] // 2)
    return pl.pallas_call(
        pair_weight_kernel,
        out_shape=jax.ShapeDtypeStruct(part_shape, jnp.float32),
        grid=(STEPS,),
        in_specs=[split_spec(normed.shape)] + [whole_spec(piece.shape) for piece in pieces],
        out_specs=whole_spec(part_shape),
        scratch_shapes=[pltpu.VMEM((H * rows // 2, 2 * length), jnp.float32)],
        compiler_params=params(24),
        cost_estimate=pl.CostEstimate(
            flops=1_000_000, bytes_accessed=100_000, transcendentals=0
        ),
        name="pair_weight",
    )(normed, *pieces)


def pair_backward(number, so_far, shape, normed, inv_std, grads, weight_t, factor):
    row_count, tok_col, width = shape
    whole = row_count // 2
    steps = STEPS // PARTS
    first = number * steps

    def split(shape):
        block = (shape[0] // STEPS,) + tuple(shape[1:])
        return pl.BlockSpec(block, lambda i: (i + first,) + (0,) * (len(shape) - 1))

    previous = [] if so_far is None else [so_far]
    return pl.pallas_call(
        lambda *refs: pair_back_kernel(factor, *refs),
        out_shape=jax.ShapeDtypeStruct((2, whole, tok_col, width), jnp.bfloat16),
        grid=(steps,),
        in_specs=[
            split(normed.shape),
            split(inv_std.shape),
            whole_spec(grads.shape),
            whole_spec(weight_t.shape),
        ]
        + [pl.BlockSpec(memory_space=pl.ANY)] * len(previous),
        out_specs=pl.BlockSpec(
            (2, whole // STEPS, tok_col, width), lambda i: (0, i + first, 0, 0)
        ),
        scratch_shapes=[pltpu.VMEM((H * whole // PARTS, 2 * tok_col), jnp.float32)],
        input_output_aliases={4: 0} if previous else {},
        compiler_params=params(24),
        cost_estimate=pl.CostEstimate(
            flops=1_000_000, bytes_accessed=100_000, transcendentals=0
        ),
        name="pair_backward",
    )(normed, inv_std, grads, weight_t, *previous)


def unscaled(block, rows):
    block = block.astype(jnp.float32)
    return block[:, :rows] * jnp.exp2(-block[:, rows : rows + 1])


def swap(block, axis):
    return lax.ppermute(block, axis, [(0, 1), (1, 0)])


def body_heads(
    tokens, restype, type_table, key_mask, pair, w_bias, w_query, w_key, w_value, w_gate, cotangent
):
    n_row = lax.axis_size("row")
    n_col = lax.axis_size("col")
    n_samp = lax.axis_size("samp")
    samp_dev = tokens.shape[0]
    tok_col = tokens.shape[1]
    row_count = pair.shape[0]
    total_tokens = tok_col * n_col
    half = samp_dev // n_row
    row_index = lax.axis_index("row")
    row = row_index.astype(jnp.int32).reshape(1)
    col = lax.axis_index("col").astype(jnp.int32).reshape(1)
    types = restype.reshape(1, tok_col)
    weight_t = w_bias.T
    weights = (w_query, w_key, w_value, w_gate)
    samples = samp_dev * n_samp

    def send(block, offset):
        return lax.ppermute(block, "col", [(c, c ^ offset) for c in range(n_col)])

    def by_chip(blocks):
        return [blocks[0]] + [send(blocks[n], 2 * n) for n in range(1, n_col // 2)]

    def across(blocks):
        return send(jnp.stack([block[1] for block in blocks]), 1)

    messages = token_messages(
        row, col, tokens, types, type_table, weights, cotangent, n_row, n_col
    )
    arrived = by_chip(messages)
    bias = pair_bias(pair, weight_t, key_mask.reshape(1, tok_col))
    bias, arrived, types = lax.optimization_barrier(
        (bias.astype(jnp.float16), arrived, types)
    )
    own = own_rows(row, tokens, types, type_table, w_gate, cotangent, half)
    bias = lax.all_to_all(bias, ("row", "col"), 0, 0, tiled=True)
    other = across(arrived)
    bias, other, own = lax.optimization_barrier((bias, other, own))

    back, grad_bias = attention(col, arrived, other, bias.astype(jnp.float32), n_row)
    grad_bias = lax.all_to_all(
        grad_bias.astype(jnp.float16), ("row", "col"), 0, 0, tiled=True
    )
    back, late_pair = lax.optimization_barrier((back.astype(jnp.float16), pair))
    pair_normed, pair_inv = pair_units(late_pair)
    back, _, pair_normed = lax.optimization_barrier((back, grad_bias, pair_normed))
    back = lax.all_to_all(back, ("row", "col"), 0, 0, tiled=True)

    other_bias = swap(grad_bias, "samp")
    own_pieces = [unscaled(piece, tok_col) for piece in jnp.split(grad_bias, PARTS, axis=2)]
    part = pair_weight(pair_normed, own_pieces)
    samp_part = swap(part, "samp")
    row_part = swap(part, "row")
    both_part = lax.ppermute(part, ("samp", "row"), [(n, 3 - n) for n in range(4)])
    other_bias, part = lax.optimization_barrier((other_bias, part))
    pieces = [
        mine + unscaled(piece, tok_col)
        for mine, piece in zip(own_pieces, jnp.split(other_bias, PARTS, axis=2))
    ]
    part = (part + samp_part) + (row_part + both_part)
    pieces, part = lax.optimization_barrier((pieces, part))
    sums = (send(part, 1), send(part, 2), send(part, 3))
    pair_grad = None
    for n, piece in enumerate(pieces):
        pair_grad = pair_backward(
            n, pair_grad, pair.shape, pair_normed, pair_inv, piece, weight_t,
            total_tokens / samples,
        )
        if n == 0:
            pair_grad, back, sums = lax.optimization_barrier((pair_grad, back, sums))
            part = (part + sums[0]) + (sums[1] + sums[2])
            last = send(part, 4)
            token_half = token_back(back.astype(jnp.float32), *own, weights)
            token_half = token_half.reshape(half, tok_col, D)
            pair_grad, token_half = lax.optimization_barrier((pair_grad, token_half))
            other_half = swap(token_half, "row")
    pair_grad, other_half, last = lax.optimization_barrier((pair_grad, other_half, last))
    pair_grad = pair_grad.reshape(pair.shape)
    part = part + last
    first = row_index == 0
    token_grad = jnp.concatenate(
        [jnp.where(first, token_half, other_half), jnp.where(first, other_half, token_half)],
        axis=0,
    )
    return (token_grad, pair_grad, part.T / samples)


def body(*args):
    n_row = lax.axis_size("row")
    n_col = lax.axis_size("col")
    tokens = args[0]
    pair = args[4]
    fits = n_row == 2 and n_col == 8 and n_row * n_col == H and lax.axis_size("samp") == 2
    square = pair.shape[0] * n_row == pair.shape[1] * n_col
    if fits and square and tokens.shape[0] == 4 and tokens.shape[1] == 64:
        return body_heads(*args)
    return body_any(*args)


def solution(mesh):
    placed = (
        P("samp", "col", None),
        P("col"),
        P(),
        P("col"),
        P("row", "col", None),
        P(),
        P(),
        P(),
        P(),
        P(),
        P("samp", "col", None),
    )
    return jax.shard_map(
        body,
        mesh=mesh,
        in_specs=placed,
        out_specs=(P("samp", "col", None), P("row", "col", None), P()),
        check_vma=False,
    )
```

```python
import math

import jax
import jax.numpy as jnp
from jax import lax
from jax.experimental import pallas as pl
from jax.experimental.pallas import tpu as pltpu
from jax.sharding import PartitionSpec as P

D = 768
H = 16
CH = 48
NTYPE = 32


def broadcast(block, axis, source):
    block = jnp.where(lax.axis_index(axis) == source, block, jnp.zeros_like(block))
    return lax.psum(block, axis)


def token_norm(tokens, restype, type_table):
    onehot = (restype[:, None] == jnp.arange(NTYPE, dtype=jnp.int32)[None, :]).astype(jnp.bfloat16)
    embedded = tokens.astype(jnp.float32) + jnp.dot(
        onehot, type_table, preferred_element_type=jnp.float32
    )
    centred = embedded - jnp.mean(embedded, axis=-1, keepdims=True)
    inv_std = lax.rsqrt(jnp.mean(centred * centred, axis=-1, keepdims=True) + 1e-05)
    return (centred * inv_std, inv_std)


def pair_norm(block):
    values = block.astype(jnp.float32)
    centred = values - jnp.mean(values, axis=-1, keepdims=True)
    inv_std = lax.rsqrt(jnp.mean(centred * centred, axis=-1, keepdims=True) + 1e-05)
    return (centred * inv_std, inv_std)


def norm_back(grad_in, normed, inv_std):
    return inv_std * (
        grad_in
        - jnp.mean(grad_in, axis=-1, keepdims=True)
        - normed * jnp.mean(grad_in * normed, axis=-1, keepdims=True)
    )


def project(rows_in, weight):
    return jnp.einsum("std,de->ste", rows_in, weight, preferred_element_type=jnp.float32).astype(
        jnp.bfloat16
    )


def back_project(grads, weight):
    return jnp.einsum(
        "ste,de->std", grads, weight.astype(jnp.float32), precision=lax.Precision.HIGHEST
    )


def pair_back(grad_bias, pair_normed, pair_inv, bias_weight):
    grad_normed = jnp.einsum("hij,ch->ijc", grad_bias, bias_weight, precision=lax.Precision.HIGHEST)
    return norm_back(grad_normed, pair_normed, pair_inv)


def body_any(
    tokens, restype, type_table, key_mask, pair, w_bias, w_query, w_key, w_value, w_gate, cotangent
):
    n_row = lax.axis_size("row")
    n_col = lax.axis_size("col")
    n_samp = lax.axis_size("samp")
    samp_dev = tokens.shape[0]
    tok_col = tokens.shape[1]
    spread = n_col // n_row
    row_count = tok_col * spread
    total_tokens = tok_col * n_col
    row_index = lax.axis_index("row")
    col_index = lax.axis_index("col")
    is_owner = col_index // spread == row_index
    own_start = col_index % spread * tok_col
    normed, inv_std = token_norm(tokens, restype, type_table)
    own_act = normed.astype(jnp.bfloat16)
    key_proj = project(own_act, w_key)
    value_proj = project(own_act, w_value)
    stacked = jnp.stack([own_act, cotangent])
    pieces = [broadcast(stacked, "col", row_index * spread + member) for member in range(spread)]
    gathered = jnp.concatenate(pieces, axis=2)
    query_side = gathered[0]
    grad_rows = gathered[1]
    queries = project(query_side, w_query)
    gate_lin = project(query_side, w_gate)
    pair_normed, pair_inv = pair_norm(pair)
    bias_weight = w_bias.astype(jnp.float32)
    bias = jnp.einsum("ijc,ch->hij", pair_normed, bias_weight, precision=lax.Precision.HIGHEST)
    query_heads = queries.reshape(samp_dev, row_count, H, CH)
    key_heads = key_proj.reshape(samp_dev, tok_col, H, CH)
    value_heads = value_proj.reshape(samp_dev, tok_col, H, CH)
    scores = (
        jnp.einsum("sihc,sjhc->shij", query_heads, key_heads, preferred_element_type=jnp.float32)
        / math.sqrt(CH)
        + bias[None]
    )
    scores = jnp.where(key_mask[None, None, None, :] == 1, scores, -1000000000.0)
    top = lax.pmax(jnp.max(scores, axis=-1), "col")
    expo = jnp.exp(scores - top[..., None])
    partial_out = jnp.einsum(
        "shij,sjhc->sihc",
        expo.astype(jnp.bfloat16),
        value_heads,
        preferred_element_type=jnp.float32,
    )
    totals, summed = lax.psum(
        (jnp.sum(expo, axis=-1), partial_out.reshape(samp_dev, row_count, D)), "col"
    )
    attended = (
        summed.reshape(samp_dev, row_count, H, CH) / jnp.transpose(totals, (0, 2, 1))[..., None]
    )
    flat_out = attended.reshape(samp_dev, row_count, D)
    sig_gate = jax.nn.sigmoid(gate_lin.astype(jnp.float32))
    grad_f = grad_rows.astype(jnp.float32)
    grad_out = (grad_f * sig_gate).astype(jnp.bfloat16)
    grad_gate = (grad_f * flat_out * sig_gate * (1.0 - sig_gate)).astype(jnp.bfloat16)
    gate_piece = lax.dynamic_slice_in_dim(grad_gate, own_start, tok_col, 1)
    gate_term = jnp.where(
        is_owner,
        jnp.einsum("ste,de->std", gate_piece, w_gate, preferred_element_type=jnp.float32),
        0.0,
    )
    grad_heads = grad_out.reshape(samp_dev, row_count, H, CH)
    delta = jnp.transpose(jnp.sum(grad_heads.astype(jnp.float32) * attended, axis=-1), (0, 2, 1))
    probs = expo / totals[..., None]
    grad_pre = jnp.einsum(
        "sihc,sjhc->shij", grad_heads, value_heads, preferred_element_type=jnp.float32
    )
    grad_scores = probs * (grad_pre - delta[..., None])
    rounded = grad_scores.astype(jnp.bfloat16)
    grad_query = (
        jnp.einsum("shij,sjhc->sihc", rounded, key_heads, preferred_element_type=jnp.float32)
        / math.sqrt(CH)
    ).reshape(samp_dev, row_count, D)
    grad_key = (
        jnp.einsum("shij,sihc->sjhc", rounded, query_heads, preferred_element_type=jnp.float32)
        / math.sqrt(CH)
    ).reshape(samp_dev, tok_col, D)
    grad_value = jnp.einsum(
        "shij,sihc->sjhc",
        probs.astype(jnp.bfloat16),
        grad_heads,
        preferred_element_type=jnp.float32,
    ).reshape(samp_dev, tok_col, D)
    bias_local = jnp.sum(grad_scores, axis=0)
    blank = jnp.zeros((samp_dev, total_tokens, D), jnp.float32)
    mine = lax.psum_scatter(
        lax.dynamic_update_slice_in_dim(blank, grad_query, row_index * row_count, 1),
        "col",
        scatter_dimension=1,
        tiled=True,
    )
    query_all, key_all, value_all, gate_all = lax.psum(
        (mine, grad_key, grad_value, gate_term), "row"
    )
    grad_act = (
        back_project(query_all, w_query)
        + back_project(key_all, w_key)
        + back_project(value_all, w_value)
        + gate_all
    )
    token_grad = norm_back(grad_act, normed, inv_std).astype(jnp.bfloat16)
    samples = samp_dev * n_samp
    grad_bias = lax.psum(bias_local, "samp")
    grad_pair = pair_back(grad_bias, pair_normed, pair_inv, bias_weight)
    pair_grad = (grad_pair * (total_tokens / samples)).astype(jnp.bfloat16)
    weight_part = jnp.einsum("ijc,hij->ch", pair_normed, grad_bias, precision=lax.Precision.HIGHEST)
    weight_sum = lax.psum(weight_part, ("row", "col"))
    bias_weight_grad = weight_sum / samples
    return (token_grad, pair_grad, bias_weight_grad)


EPS = 1e-05
SCALE = 1.0 / math.sqrt(CH)
NT = (((1,), (1,)), ((), ()))
TN = (((0,), (0,)), ((), ()))
MASKED = -65504.0


def params(megabytes):
    return pltpu.CompilerParams(vmem_limit_bytes=megabytes * 1024 * 1024)


def matmul(left, right):
    return jnp.dot(left, right, preferred_element_type=jnp.float32)


def matmul_nt(left, right):
    return lax.dot_general(left, right, NT, preferred_element_type=jnp.float32)


def matmul_tn(left, right):
    return lax.dot_general(left, right, TN, preferred_element_type=jnp.float32)


def halves(values):
    high = values.astype(jnp.bfloat16)
    low = (values - high.astype(jnp.float32)).astype(jnp.bfloat16)
    return high, low


def unit_rows(values):
    centred = values - jnp.mean(values, axis=-1, keepdims=True)
    inv_std = lax.rsqrt(jnp.mean(centred * centred, axis=-1, keepdims=True) + EPS)
    return centred * inv_std, inv_std


def embed_rows(tokens_ref, types_ref, table_ref):
    count, length, width = tokens_ref.shape
    index = lax.broadcasted_iota(jnp.int32, (NTYPE, length), 0)
    onehot = jnp.where(types_ref[...] == index, 1.0, 0.0).astype(jnp.bfloat16)
    added = matmul_tn(onehot, table_ref[...])
    embedded = tokens_ref[...].astype(jnp.float32) + added[None]
    return unit_rows(embedded.reshape(count * length, width))


def token_kernel(row_ref, col_ref, tokens_ref, types_ref, table_ref, *refs):
    weight_refs, cot_ref, out_refs = refs[:4], refs[4], refs[5:-3]
    side_ref, held_ref, sems = refs[-3:]
    width = held_ref.shape[-1]
    mine = pl.ds(pl.multiple_of(row_ref[0] * width, 128), width)
    copies = [
        pltpu.make_async_copy(ref.at[:, mine], held_ref.at[slot], sems.at[slot])
        for slot, ref in enumerate(weight_refs)
    ]
    for copy in copies:
        copy.start()
    normed, _ = embed_rows(tokens_ref, types_ref, table_ref)
    act = normed.astype(jnp.bfloat16)
    for slot in range(3):
        copies[slot].wait()
        side_ref[slot] = matmul(act, held_ref[slot]).astype(jnp.bfloat16).T
    copies[3].wait()
    gate = matmul(act, held_ref[3]).astype(jnp.bfloat16).astype(jnp.float32)
    cot = cot_ref[...].reshape(gate.shape).astype(jnp.float32)
    side_ref[3] = (cot * jax.nn.sigmoid(gate)).astype(jnp.bfloat16).T
    for offset, out_ref in enumerate(out_refs):
        for core in range(2):
            start = pl.multiple_of((col_ref[0] ^ (2 * offset + core)) * CH, 16)
            out_ref[core] = side_ref[:, pl.ds(start, CH), :]


def token_messages(row, col, tokens, types, table, weights, cotangent, n_row, n_col):
    samp_dev, tok_col, _ = tokens.shape
    width = D // n_row
    held = samp_dev * tok_col
    whole3 = lambda i, r, c: (0, 0, 0)
    whole2 = lambda i, r, c: (0, 0)
    weight_spec = pl.BlockSpec(memory_space=pl.ANY)
    shape = (2, 4, CH, held)
    count = n_col // 2
    return pl.pallas_call(
        token_kernel,
        out_shape=[jax.ShapeDtypeStruct(shape, jnp.bfloat16)] * count,
        grid_spec=pltpu.PrefetchScalarGridSpec(
            num_scalar_prefetch=2,
            grid=(1,),
            in_specs=[
                pl.BlockSpec(tokens.shape, whole3),
                pl.BlockSpec(types.shape, whole2),
                pl.BlockSpec(table.shape, whole2),
                weight_spec,
                weight_spec,
                weight_spec,
                weight_spec,
                pl.BlockSpec((samp_dev, tok_col, width), lambda i, r, c: (0, 0, r[0])),
            ],
            out_specs=[pl.BlockSpec(shape, lambda i, r, c: (0, 0, 0, 0))] * count,
            scratch_shapes=[
                pltpu.VMEM((4, width, held), jnp.bfloat16),
                pltpu.VMEM((4, D, width), jnp.bfloat16),
                pltpu.SemaphoreType.DMA((4,)),
            ],
        ),
        compiler_params=params(56),
        cost_estimate=pl.CostEstimate(
            flops=4_000_000_000, bytes_accessed=4_000_000, transcendentals=0
        ),
        name="token_messages",
    )(row, col, tokens, types, table, *weights, cotangent)


def own_kernel(
    row_ref, tokens_ref, types_ref, table_ref, wg_ref, cot_ref, slope_ref, normed_ref, inv_ref
):
    normed, inv_std = embed_rows(tokens_ref, types_ref, table_ref)
    gate = matmul(normed.astype(jnp.bfloat16), wg_ref[...]).astype(jnp.bfloat16)
    sig = jax.nn.sigmoid(gate.astype(jnp.float32))
    cot = cot_ref[...].reshape(gate.shape).astype(jnp.float32)
    slope_ref[...] = (cot * sig * (1.0 - sig)).T
    normed_ref[...] = normed.T
    inv_ref[...] = jnp.broadcast_to(inv_std, (inv_std.shape[0], 128)).T[:8]


def own_rows(row, tokens, types, table, w_gate, cotangent, half):
    _, tok_col, _ = tokens.shape
    count = half * tok_col
    part_spec = pl.BlockSpec((half, tok_col, D), lambda i, r: (r[0], 0, 0))
    whole2 = lambda i, r: (0, 0)
    return pl.pallas_call(
        own_kernel,
        out_shape=[
            jax.ShapeDtypeStruct((D, count), jnp.float32),
            jax.ShapeDtypeStruct((D, count), jnp.float32),
            jax.ShapeDtypeStruct((8, count), jnp.float32),
        ],
        grid_spec=pltpu.PrefetchScalarGridSpec(
            num_scalar_prefetch=1,
            grid=(1,),
            in_specs=[
                part_spec,
                pl.BlockSpec(types.shape, whole2),
                pl.BlockSpec(table.shape, whole2),
                pl.BlockSpec(w_gate.shape, whole2),
                part_spec,
            ],
            out_specs=[
                pl.BlockSpec((D, count), whole2),
                pl.BlockSpec((D, count), whole2),
                pl.BlockSpec((8, count), whole2),
            ],
        ),
        compiler_params=params(56),
        cost_estimate=pl.CostEstimate(
            flops=3_000_000_000, bytes_accessed=3_000_000, transcendentals=0
        ),
        name="own_rows",
    )(row, tokens, types, table, w_gate, cotangent)


MANY = 4


def pair_columns(pair_ref, k, many):
    _, _, length, width = pair_ref.shape
    blocks = [pair_ref[p, pl.ds(k, many)] for p in range(2)]
    rows = jnp.concatenate(blocks, axis=1).reshape(many * 2 * length, width)
    same = lax.broadcasted_iota(jnp.int32, (width, width), 0) == lax.broadcasted_iota(
        jnp.int32, (width, width), 1
    )
    centring = (jnp.where(same, 1.0, 0.0) - 1.0 / width).astype(jnp.bfloat16)
    centred = matmul_nt(centring, rows)
    return centred, lax.rsqrt(jnp.mean(centred * centred, axis=0, keepdims=True) + EPS)


def bias_kernel(pair_ref, weight_ref, mask_ref, out_ref, flat_ref):
    _, count, length, width = pair_ref.shape
    whole = flat_ref.shape[0] // H
    weight = jnp.concatenate([weight_ref[...]] * 2, axis=1)
    base = pl.program_id(0) * count

    def step(n, carry):
        k = n * MANY
        centred, inv_std = pair_columns(pair_ref, k, MANY)
        bias = matmul(weight, jnp.concatenate(halves(centred), axis=0)) * inv_std
        for m in range(MANY):
            lanes = slice(m * 2 * length, (m + 1) * 2 * length)
            flat_ref[pl.ds(base + k + m, H, stride=whole), :] = bias[:, lanes]
        return carry

    lax.fori_loop(0, count // MANY, step, 0, unroll=4)

    @pl.when(pl.program_id(0) == pl.num_programs(0) - 1)
    def _():
        keep = jnp.broadcast_to(mask_ref[...].astype(jnp.float32), (128, length)).T
        keep = jnp.concatenate([keep] * (2 * whole // 128), axis=1) == 1.0
        for h in range(H):
            turned = flat_ref[h * whole : (h + 1) * whole, :].T
            bias = jnp.concatenate([turned[:length], turned[length:]], axis=1)
            out_ref[h] = jnp.where(keep, bias, MASKED)


STEPS = 4


def split_spec(shape):
    block = (shape[0] // STEPS,) + tuple(shape[1:])
    return pl.BlockSpec(block, lambda i: (i,) + (0,) * (len(shape) - 1))


def whole_spec(shape):
    return pl.BlockSpec(tuple(shape), lambda i: (0,) * len(shape))


def pair_spec(pair):
    row_count, tok_col, width = pair.shape
    block = (2, row_count // 2 // STEPS, tok_col, width)
    return pl.BlockSpec(block, lambda i: (0, i, 0, 0))


def pair_bias(pair, weight_t, mask):
    row_count, tok_col, width = pair.shape
    whole = row_count // 2
    return pl.pallas_call(
        bias_kernel,
        out_shape=jax.ShapeDtypeStruct((H, tok_col, row_count), jnp.float32),
        grid=(STEPS,),
        in_specs=[pair_spec(pair), whole_spec(weight_t.shape), whole_spec(mask.shape)],
        out_specs=whole_spec((H, tok_col, row_count)),
        scratch_shapes=[pltpu.VMEM((H * whole, 2 * tok_col), jnp.float32)],
        compiler_params=params(24),
        cost_estimate=pl.CostEstimate(
            flops=6_000_000_000, bytes_accessed=5_000_000, transcendentals=0
        ),
        name="pair_bias",
    )(pair.reshape(2, whole, tok_col, width), weight_t, mask)


def norm_kernel(pair_ref, normed_ref, inv_ref):
    def step(n, carry):
        centred, inv_std = pair_columns(pair_ref, n * MANY, MANY)
        normed_ref[n] = jnp.concatenate(halves(centred * inv_std), axis=0)
        inv_ref[n] = jnp.broadcast_to(inv_std, inv_ref.shape[1:])
        return carry

    lax.fori_loop(0, normed_ref.shape[0], step, 0, unroll=4)


def pair_units(pair):
    row_count, tok_col, width = pair.shape
    whole = row_count // 2
    chunks, lanes = whole // MANY, MANY * 2 * tok_col
    shapes = [(chunks, 2 * width, lanes), (chunks, 8, lanes)]
    return pl.pallas_call(
        norm_kernel,
        out_shape=[
            jax.ShapeDtypeStruct(shapes[0], jnp.bfloat16),
            jax.ShapeDtypeStruct(shapes[1], jnp.float32),
        ],
        grid=(STEPS,),
        in_specs=[pair_spec(pair)],
        out_specs=[split_spec(shape) for shape in shapes],
        compiler_params=params(56),
        cost_estimate=pl.CostEstimate(
            flops=6_000_000_000, bytes_accessed=12_000_000, transcendentals=0
        ),
        name="pair_units",
    )(pair.reshape(2, whole, tok_col, width))


def shift_of(top):
    return jnp.floor(jnp.clip(14.0 - jnp.log2(top), -100.0, 100.0))


def attention_kernel(col_ref, *refs):
    other_ref, bias_ref, back_ref, grad_bias_ref, sum_ref, tokens_ref = refs[-6:]
    col = col_ref[0]
    for offset, ref in enumerate(refs[:-6]):
        tokens_ref[col ^ (2 * offset)] = ref[0]
        tokens_ref[col ^ (2 * offset + 1)] = other_ref[offset]
    n_col = tokens_ref.shape[0]
    tok_col, row_count = bias_ref.shape[1:]
    half = back_ref.shape[2] // tok_col
    n_row = bias_ref.shape[0] // n_col
    step = pl.program_id(0)

    @pl.when(step == 0)
    def _():
        sum_ref[...] = jnp.zeros_like(sum_ref)

    outs = []
    for sample in range(half):
        lanes = slice(sample * tok_col, (sample + 1) * tok_col)

        def side(slot):
            return jnp.concatenate([tokens_ref[c, slot, :, lanes] for c in range(n_col)], axis=1)

        query_t, key_t, value_t, grad_t = [side(slot) for slot in range(4)]
        key = key_t.T
        value = value_t.T
        attended_parts, grad_query_parts = [], []
        grad_key = jnp.zeros(key_t.shape, jnp.float32)
        grad_value = jnp.zeros(key_t.shape, jnp.float32)
        for block in range(n_row):
            cols = slice(block * row_count, (block + 1) * row_count)
            heads = slice(block * n_col, (block + 1) * n_col)
            bias = bias_ref[heads].reshape(n_col * tok_col, row_count)
            query_b = query_t[:, cols]
            grad_b = grad_t[:, cols]
            scores = matmul(key, query_b) * SCALE + bias
            scores = jnp.where(bias < -60000.0, -1000000000.0, scores)
            expo = jnp.exp(scores - jnp.max(scores, axis=0, keepdims=True))
            share = 1.0 / jnp.sum(expo, axis=0, keepdims=True)
            attended = matmul(value_t, expo.astype(jnp.bfloat16)) * share
            delta = jnp.sum(grad_b.astype(jnp.float32) * attended, axis=0, keepdims=True)
            probs = expo * share
            grad_scores = probs * (matmul(value, grad_b) - delta)
            rounded = grad_scores.astype(jnp.bfloat16)
            attended_parts.append(attended)
            grad_query_parts.append(matmul(key_t, rounded) * SCALE)
            grad_key = grad_key + matmul_nt(query_b, rounded)
            grad_value = grad_value + matmul_nt(grad_b, probs.astype(jnp.bfloat16))
            sum_ref[heads] += grad_scores.reshape(n_col, tok_col, row_count)
        outs.append(
            (
                jnp.concatenate(grad_query_parts, axis=1),
                grad_key * SCALE,
                grad_value,
                jnp.concatenate(attended_parts, axis=1),
            )
        )
    spare = jnp.zeros((8 - 4, half * tok_col), jnp.float32)
    tops = [jnp.max(jnp.abs(out[slot]), axis=0, keepdims=True) for slot in range(4) for out in outs]
    shifts = shift_of(jnp.concatenate(tops, axis=0))
    scales = jnp.exp2(shifts)
    scaled = [
        [out[slot] * scales[slot * half + n : slot * half + n + 1] for n, out in enumerate(outs)]
        for slot in range(4)
    ]
    for c in range(n_col):
        lanes = slice(c * tok_col, (c + 1) * tok_col)
        for slot in range(4):
            back_ref[c, slot * CH : (slot + 1) * CH, :] = jnp.concatenate(
                [part[:, lanes] for part in scaled[slot]], axis=1
            )
        tails = [
            jnp.concatenate([shifts[slot * half + n :, lanes][:1] for n in range(half)], axis=1)
            for slot in range(4)
        ]
        back_ref[c, 4 * CH :, :] = jnp.concatenate(tails + [spare], axis=0)

    @pl.when(step == pl.num_programs(0) - 1)
    def _():
        for head in range(n_row * n_col):
            sums = sum_ref[head]
            shift = shift_of(jnp.max(jnp.abs(sums), axis=0, keepdims=True))
            grad_bias_ref[head, :tok_col, :] = sums * jnp.exp2(shift)
            grad_bias_ref[head, tok_col:, :] = jnp.broadcast_to(shift, (8, row_count))


def attention(col, arrived, other, bias, n_row):
    count = len(arrived)
    n_col = 2 * count
    _, tok_col, row_count = bias.shape
    half = arrived[0].shape[-1] // tok_col // n_row
    width = half * tok_col
    back_shape = (n_row * n_col, 4 * CH + 8, width)
    bias_shape = (n_row * n_col, tok_col + 8, row_count)
    return pl.pallas_call(
        attention_kernel,
        out_shape=[
            jax.ShapeDtypeStruct(back_shape, jnp.float32),
            jax.ShapeDtypeStruct(bias_shape, jnp.float32),
        ],
        grid_spec=pltpu.PrefetchScalarGridSpec(
            num_scalar_prefetch=1,
            grid=(n_row,),
            in_specs=[pl.BlockSpec((1, 4, CH, width), lambda i, r: (0, 0, 0, i))] * count
            + [
                pl.BlockSpec((count, 4, CH, width), lambda i, r: (0, 0, 0, i)),
                pl.BlockSpec(bias.shape, lambda i, r: (0, 0, 0)),
            ],
            out_specs=[
                pl.BlockSpec((n_col, 4 * CH + 8, width), lambda i, r: (i, 0, 0)),
                pl.BlockSpec(bias_shape, lambda i, r: (0, 0, 0)),
            ],
            scratch_shapes=[
                pltpu.VMEM(bias.shape, jnp.float32),
                pltpu.VMEM((n_col, 4, CH, width), jnp.bfloat16),
            ],
        ),
        compiler_params=params(24),
        cost_estimate=pl.CostEstimate(
            flops=8_000_000_000, bytes_accessed=6_000_000, transcendentals=1_000_000
        ),
        name="attention",
    )(col, *arrived, other, bias)


def back_kernel(*refs):
    slope_ref, normed_ref, inv_ref, wq_ref, wk_ref, wv_ref, wg_ref = refs[-11:-4]
    out_ref, parts_ref, gate_ref, total_ref = refs[-4:]
    back_ref = refs[0]
    count = normed_ref.shape[-1]
    step = pl.program_id(0)
    rows = wq_ref.shape[0]

    @pl.when(step == 0)
    def _():
        for slot in range(4):
            scale = jnp.exp2(-back_ref[:, 4 * CH + slot : 4 * CH + slot + 1, :])
            values = back_ref[:, slot * CH : (slot + 1) * CH, :] * scale
            values = values.reshape(gate_ref.shape)
            if slot < 3:
                parts_ref[slot] = jnp.concatenate(halves(values), axis=1)
            else:
                gate_ref[...] = (values * slope_ref[...]).astype(jnp.bfloat16)

    total = matmul(wg_ref[...], gate_ref[...])
    for slot, ref in enumerate((wq_ref, wk_ref, wv_ref)):
        parts = matmul(ref[...], parts_ref[slot])
        total = total + (parts[:, :count] + parts[:, count:])
    total_ref[pl.ds(pl.multiple_of(step * rows, 8), rows), :] = total

    @pl.when(step == pl.num_programs(0) - 1)
    def _():
        whole = total_ref[...]
        normed = normed_ref[...]
        result = inv_ref[:1] * (
            whole
            - jnp.mean(whole, axis=0, keepdims=True)
            - normed * jnp.mean(whole * normed, axis=0, keepdims=True)
        )
        out_ref[...] = result.T.astype(jnp.bfloat16)


def token_back(back, slope, normed, inv_std, weights):
    count = normed.shape[-1]
    steps = 2
    whole = lambda shape: pl.BlockSpec(shape, lambda i: (0,) * len(shape))
    weight_spec = pl.BlockSpec((D // steps, D), lambda i: (i, 0))
    return pl.pallas_call(
        back_kernel,
        out_shape=jax.ShapeDtypeStruct((count, D), jnp.bfloat16),
        grid=(steps,),
        in_specs=[whole(array.shape) for array in (back, slope, normed, inv_std)]
        + [weight_spec] * 4,
        out_specs=whole((count, D)),
        scratch_shapes=[
            pltpu.VMEM((3, D, 2 * count), jnp.bfloat16),
            pltpu.VMEM((D, count), jnp.bfloat16),
            pltpu.VMEM((D, count), jnp.float32),
        ],
        compiler_params=params(40),
        cost_estimate=pl.CostEstimate(
            flops=4_000_000_000, bytes_accessed=8_000_000, transcendentals=0
        ),
        name="token_back",
    )(back, slope, normed, inv_std, *weights)


def flatten(grads_ref, flat_ref):
    whole = flat_ref.shape[0] // H
    for h in range(H):
        grads = grads_ref[h]
        both = jnp.concatenate([grads[:, :whole], grads[:, whole:]], axis=0)
        flat_ref[h * whole : (h + 1) * whole, :] = both.T


def flat_columns(flat_ref, k, many):
    whole = flat_ref.shape[0] // H
    grads = [flat_ref[pl.ds(k + m, H, stride=whole), :] for m in range(many)]
    return jnp.concatenate(halves(jnp.concatenate(grads, axis=1)), axis=0)


def pair_weight_kernel(normed_ref, grads_ref, part_ref, flat_ref):
    chunks, width, _ = normed_ref.shape
    base = pl.program_id(0) * chunks

    @pl.when(pl.program_id(0) == 0)
    def _():
        part_ref[...] = jnp.zeros_like(part_ref)
        flatten(grads_ref, flat_ref)

    def step(n, carry):
        return carry + matmul_nt(normed_ref[n], flat_columns(flat_ref, (base + n) * MANY, MANY))

    parts = lax.fori_loop(0, chunks, step, jnp.zeros((width, 2 * H), jnp.float32), unroll=4)
    parts = parts[:, :H] + parts[:, H:]
    part_ref[...] += (parts[: width // 2] + parts[width // 2 :]).T


def pair_back_kernel(factor, normed_ref, inv_ref, grads_ref, weight_ref, out_ref, flat_ref):
    _, count, length, width = out_ref.shape
    weight = weight_ref[...].astype(jnp.float32)
    weight = halves(weight - jnp.mean(weight, axis=1, keepdims=True))
    weight = jnp.concatenate([weight[0], weight[0], weight[1], weight[1]], axis=0).T
    base = pl.program_id(0) * count

    @pl.when(pl.program_id(0) == 0)
    def _():
        flatten(grads_ref, flat_ref)

    def step(n, carry):
        k = n * MANY
        normed = normed_ref[n].astype(jnp.float32)
        normed = normed[:width] + normed[width:]
        grads = flat_columns(flat_ref, base + k, MANY)
        grad_in = matmul(weight, jnp.concatenate([grads, grads], axis=0))
        overlap = jnp.mean(grad_in * normed, axis=0, keepdims=True)
        result = (grad_in - normed * overlap) * (inv_ref[n, :1] * factor)
        result = result.astype(jnp.bfloat16).T.reshape(MANY, 2 * length, width)
        for p in range(2):
            out_ref[p, pl.ds(k, MANY)] = result[:, p * length : (p + 1) * length]
        return carry

    lax.fori_loop(0, count // MANY, step, 0, unroll=4)


def pair_weight(normed, grads):
    heads, length, rows = grads.shape
    part_shape = (H, normed.shape[1] // 2)
    return pl.pallas_call(
        pair_weight_kernel,
        out_shape=jax.ShapeDtypeStruct(part_shape, jnp.float32),
        grid=(STEPS,),
        in_specs=[split_spec(normed.shape), whole_spec(grads.shape)],
        out_specs=whole_spec(part_shape),
        scratch_shapes=[pltpu.VMEM((H * rows // 2, 2 * length), jnp.float32)],
        compiler_params=params(24),
        cost_estimate=pl.CostEstimate(
            flops=5_000_000_000, bytes_accessed=100_000, transcendentals=0
        ),
        name="pair_weight",
    )(normed, grads)


def pair_backward(shape, normed, inv_std, grads, weight_t, factor):
    row_count, tok_col, width = shape
    whole = row_count // 2
    pair_grad = pl.pallas_call(
        lambda *refs: pair_back_kernel(factor, *refs),
        out_shape=jax.ShapeDtypeStruct((2, whole, tok_col, width), jnp.bfloat16),
        grid=(STEPS,),
        in_specs=[
            split_spec(normed.shape),
            split_spec(inv_std.shape),
            whole_spec(grads.shape),
            whole_spec(weight_t.shape),
        ],
        out_specs=pl.BlockSpec((2, whole // STEPS, tok_col, width), lambda i: (0, i, 0, 0)),
        scratch_shapes=[pltpu.VMEM((H * whole, 2 * tok_col), jnp.float32)],
        compiler_params=params(24),
        cost_estimate=pl.CostEstimate(
            flops=8_000_000_000, bytes_accessed=100_000, transcendentals=0
        ),
        name="pair_backward",
    )(normed, inv_std, grads, weight_t)
    return pair_grad.reshape(shape)


def unscaled(block, rows):
    block = block.astype(jnp.float32)
    return block[:, :rows] * jnp.exp2(-block[:, rows : rows + 1])


def swap(block, axis):
    return lax.ppermute(block, axis, [(0, 1), (1, 0)])


def body_heads(
    tokens, restype, type_table, key_mask, pair, w_bias, w_query, w_key, w_value, w_gate, cotangent
):
    n_row = lax.axis_size("row")
    n_col = lax.axis_size("col")
    n_samp = lax.axis_size("samp")
    samp_dev = tokens.shape[0]
    tok_col = tokens.shape[1]
    row_count = pair.shape[0]
    total_tokens = tok_col * n_col
    half = samp_dev // n_row
    row_index = lax.axis_index("row")
    row = row_index.astype(jnp.int32).reshape(1)
    col = lax.axis_index("col").astype(jnp.int32).reshape(1)
    types = restype.reshape(1, tok_col)
    weight_t = w_bias.T
    weights = (w_query, w_key, w_value, w_gate)
    samples = samp_dev * n_samp

    def send(block, offset):
        return lax.ppermute(block, "col", [(c, c ^ offset) for c in range(n_col)])

    def by_chip(blocks):
        return [blocks[0]] + [send(blocks[n], 2 * n) for n in range(1, n_col // 2)]

    def across(blocks):
        return send(jnp.stack([block[1] for block in blocks]), 1)

    messages = token_messages(
        row, col, tokens, types, type_table, weights, cotangent, n_row, n_col
    )
    arrived = by_chip(messages)
    bias = pair_bias(pair, weight_t, key_mask.reshape(1, tok_col))
    bias, arrived, types = lax.optimization_barrier(
        (bias.astype(jnp.float16), arrived, types)
    )
    own = own_rows(row, tokens, types, type_table, w_gate, cotangent, half)
    bias = lax.all_to_all(bias, ("row", "col"), 0, 0, tiled=True)
    other = across(arrived)
    bias, other, own = lax.optimization_barrier((bias, other, own))

    back, grad_bias = attention(col, arrived, other, bias.astype(jnp.float32), n_row)
    grad_bias = lax.all_to_all(
        grad_bias.astype(jnp.float16), ("row", "col"), 0, 0, tiled=True
    )
    back, late_pair = lax.optimization_barrier((back.astype(jnp.float16), pair))
    pair_normed, pair_inv = pair_units(late_pair)
    back, _, pair_normed = lax.optimization_barrier((back, grad_bias, pair_normed))
    back = lax.all_to_all(back, ("row", "col"), 0, 0, tiled=True)

    other_bias = swap(grad_bias, "samp")
    own_bias = unscaled(grad_bias, tok_col)
    part = pair_weight(pair_normed, own_bias)
    samp_part = swap(part, "samp")
    row_part = swap(part, "row")
    both_part = lax.ppermute(part, ("samp", "row"), [(n, 3 - n) for n in range(4)])
    other_bias, part = lax.optimization_barrier((other_bias, part))
    grads = own_bias + unscaled(other_bias, tok_col)
    part = (part + samp_part) + (row_part + both_part)
    grads, part = lax.optimization_barrier((grads, part))
    sums = (send(part, 1), send(part, 2), send(part, 3))
    pair_grad = pair_backward(
        pair.shape, pair_normed, pair_inv, grads, weight_t, total_tokens / samples
    )

    pair_grad, back, sums = lax.optimization_barrier((pair_grad, back, sums))
    part = ((part + sums[0]) + (sums[1] + sums[2])) / samples
    token_half = token_back(back.astype(jnp.float32), *own, weights)
    token_half, part = lax.optimization_barrier((token_half, part))
    last = send(part, 4)
    token_half = token_half.reshape(half, tok_col, D)
    other_half = swap(token_half, "row")
    first = row_index == 0
    token_grad = jnp.concatenate(
        [jnp.where(first, token_half, other_half), jnp.where(first, other_half, token_half)],
        axis=0,
    )
    token_grad, last = lax.optimization_barrier((token_grad, last))
    return (token_grad, pair_grad, (part + last).T)


def body(*args):
    n_row = lax.axis_size("row")
    n_col = lax.axis_size("col")
    tokens = args[0]
    pair = args[4]
    fits = n_row == 2 and n_col == 8 and n_row * n_col == H and lax.axis_size("samp") == 2
    square = pair.shape[0] * n_row == pair.shape[1] * n_col
    if fits and square and tokens.shape[0] == 4 and tokens.shape[1] == 64:
        return body_heads(*args)
    return body_any(*args)


def solution(mesh):
    placed = (
        P("samp", "col", None),
        P("col"),
        P(),
        P("col"),
        P("row", "col", None),
        P(),
        P(),
        P(),
        P(),
        P(),
        P("samp", "col", None),
    )
    return jax.shard_map(
        body,
        mesh=mesh,
        in_specs=placed,
        out_specs=(P("samp", "col", None), P("row", "col", None), P()),
        check_vma=False,
    )
```

```python
import math

import jax
import jax.numpy as jnp
from jax import lax
from jax.experimental import pallas as pl
from jax.experimental.pallas import tpu as pltpu
from jax.sharding import PartitionSpec as P

D = 768
H = 16
CH = 48
NTYPE = 32


def broadcast(block, axis, source):
    block = jnp.where(lax.axis_index(axis) == source, block, jnp.zeros_like(block))
    return lax.psum(block, axis)


def token_norm(tokens, restype, type_table):
    onehot = (restype[:, None] == jnp.arange(NTYPE, dtype=jnp.int32)[None, :]).astype(jnp.bfloat16)
    embedded = tokens.astype(jnp.float32) + jnp.dot(
        onehot, type_table, preferred_element_type=jnp.float32
    )
    centred = embedded - jnp.mean(embedded, axis=-1, keepdims=True)
    inv_std = lax.rsqrt(jnp.mean(centred * centred, axis=-1, keepdims=True) + 1e-05)
    return (centred * inv_std, inv_std)


def pair_norm(block):
    values = block.astype(jnp.float32)
    centred = values - jnp.mean(values, axis=-1, keepdims=True)
    inv_std = lax.rsqrt(jnp.mean(centred * centred, axis=-1, keepdims=True) + 1e-05)
    return (centred * inv_std, inv_std)


def norm_back(grad_in, normed, inv_std):
    return inv_std * (
        grad_in
        - jnp.mean(grad_in, axis=-1, keepdims=True)
        - normed * jnp.mean(grad_in * normed, axis=-1, keepdims=True)
    )


def project(rows_in, weight):
    return jnp.einsum("std,de->ste", rows_in, weight, preferred_element_type=jnp.float32).astype(
        jnp.bfloat16
    )


def back_project(grads, weight):
    return jnp.einsum(
        "ste,de->std", grads, weight.astype(jnp.float32), precision=lax.Precision.HIGHEST
    )


def pair_back(grad_bias, pair_normed, pair_inv, bias_weight):
    grad_normed = jnp.einsum("hij,ch->ijc", grad_bias, bias_weight, precision=lax.Precision.HIGHEST)
    return norm_back(grad_normed, pair_normed, pair_inv)


def body_any(
    tokens, restype, type_table, key_mask, pair, w_bias, w_query, w_key, w_value, w_gate, cotangent
):
    n_row = lax.axis_size("row")
    n_col = lax.axis_size("col")
    n_samp = lax.axis_size("samp")
    samp_dev = tokens.shape[0]
    tok_col = tokens.shape[1]
    spread = n_col // n_row
    row_count = tok_col * spread
    total_tokens = tok_col * n_col
    row_index = lax.axis_index("row")
    col_index = lax.axis_index("col")
    is_owner = col_index // spread == row_index
    own_start = col_index % spread * tok_col
    normed, inv_std = token_norm(tokens, restype, type_table)
    own_act = normed.astype(jnp.bfloat16)
    key_proj = project(own_act, w_key)
    value_proj = project(own_act, w_value)
    stacked = jnp.stack([own_act, cotangent])
    pieces = [broadcast(stacked, "col", row_index * spread + member) for member in range(spread)]
    gathered = jnp.concatenate(pieces, axis=2)
    query_side = gathered[0]
    grad_rows = gathered[1]
    queries = project(query_side, w_query)
    gate_lin = project(query_side, w_gate)
    pair_normed, pair_inv = pair_norm(pair)
    bias_weight = w_bias.astype(jnp.float32)
    bias = jnp.einsum("ijc,ch->hij", pair_normed, bias_weight, precision=lax.Precision.HIGHEST)
    query_heads = queries.reshape(samp_dev, row_count, H, CH)
    key_heads = key_proj.reshape(samp_dev, tok_col, H, CH)
    value_heads = value_proj.reshape(samp_dev, tok_col, H, CH)
    scores = (
        jnp.einsum("sihc,sjhc->shij", query_heads, key_heads, preferred_element_type=jnp.float32)
        / math.sqrt(CH)
        + bias[None]
    )
    scores = jnp.where(key_mask[None, None, None, :] == 1, scores, -1000000000.0)
    top = lax.pmax(jnp.max(scores, axis=-1), "col")
    expo = jnp.exp(scores - top[..., None])
    partial_out = jnp.einsum(
        "shij,sjhc->sihc",
        expo.astype(jnp.bfloat16),
        value_heads,
        preferred_element_type=jnp.float32,
    )
    totals, summed = lax.psum(
        (jnp.sum(expo, axis=-1), partial_out.reshape(samp_dev, row_count, D)), "col"
    )
    attended = (
        summed.reshape(samp_dev, row_count, H, CH) / jnp.transpose(totals, (0, 2, 1))[..., None]
    )
    flat_out = attended.reshape(samp_dev, row_count, D)
    sig_gate = jax.nn.sigmoid(gate_lin.astype(jnp.float32))
    grad_f = grad_rows.astype(jnp.float32)
    grad_out = (grad_f * sig_gate).astype(jnp.bfloat16)
    grad_gate = (grad_f * flat_out * sig_gate * (1.0 - sig_gate)).astype(jnp.bfloat16)
    gate_piece = lax.dynamic_slice_in_dim(grad_gate, own_start, tok_col, 1)
    gate_term = jnp.where(
        is_owner,
        jnp.einsum("ste,de->std", gate_piece, w_gate, preferred_element_type=jnp.float32),
        0.0,
    )
    grad_heads = grad_out.reshape(samp_dev, row_count, H, CH)
    delta = jnp.transpose(jnp.sum(grad_heads.astype(jnp.float32) * attended, axis=-1), (0, 2, 1))
    probs = expo / totals[..., None]
    grad_pre = jnp.einsum(
        "sihc,sjhc->shij", grad_heads, value_heads, preferred_element_type=jnp.float32
    )
    grad_scores = probs * (grad_pre - delta[..., None])
    rounded = grad_scores.astype(jnp.bfloat16)
    grad_query = (
        jnp.einsum("shij,sjhc->sihc", rounded, key_heads, preferred_element_type=jnp.float32)
        / math.sqrt(CH)
    ).reshape(samp_dev, row_count, D)
    grad_key = (
        jnp.einsum("shij,sihc->sjhc", rounded, query_heads, preferred_element_type=jnp.float32)
        / math.sqrt(CH)
    ).reshape(samp_dev, tok_col, D)
    grad_value = jnp.einsum(
        "shij,sihc->sjhc",
        probs.astype(jnp.bfloat16),
        grad_heads,
        preferred_element_type=jnp.float32,
    ).reshape(samp_dev, tok_col, D)
    bias_local = jnp.sum(grad_scores, axis=0)
    blank = jnp.zeros((samp_dev, total_tokens, D), jnp.float32)
    mine = lax.psum_scatter(
        lax.dynamic_update_slice_in_dim(blank, grad_query, row_index * row_count, 1),
        "col",
        scatter_dimension=1,
        tiled=True,
    )
    query_all, key_all, value_all, gate_all = lax.psum(
        (mine, grad_key, grad_value, gate_term), "row"
    )
    grad_act = (
        back_project(query_all, w_query)
        + back_project(key_all, w_key)
        + back_project(value_all, w_value)
        + gate_all
    )
    token_grad = norm_back(grad_act, normed, inv_std).astype(jnp.bfloat16)
    samples = samp_dev * n_samp
    grad_bias = lax.psum(bias_local, "samp")
    grad_pair = pair_back(grad_bias, pair_normed, pair_inv, bias_weight)
    pair_grad = (grad_pair * (total_tokens / samples)).astype(jnp.bfloat16)
    weight_part = jnp.einsum("ijc,hij->ch", pair_normed, grad_bias, precision=lax.Precision.HIGHEST)
    weight_sum = lax.psum(weight_part, ("row", "col"))
    bias_weight_grad = weight_sum / samples
    return (token_grad, pair_grad, bias_weight_grad)


EPS = 1e-05
SCALE = 1.0 / math.sqrt(CH)
NT = (((1,), (1,)), ((), ()))
TN = (((0,), (0,)), ((), ()))
MASKED = -65504.0


def params(megabytes):
    return pltpu.CompilerParams(vmem_limit_bytes=megabytes * 1024 * 1024)


def matmul(left, right):
    return jnp.dot(left, right, preferred_element_type=jnp.float32)


def matmul_nt(left, right):
    return lax.dot_general(left, right, NT, preferred_element_type=jnp.float32)


def matmul_tn(left, right):
    return lax.dot_general(left, right, TN, preferred_element_type=jnp.float32)


def halves(values):
    high = values.astype(jnp.bfloat16)
    low = (values - high.astype(jnp.float32)).astype(jnp.bfloat16)
    return high, low


def unit_rows(values):
    centred = values - jnp.mean(values, axis=-1, keepdims=True)
    inv_std = lax.rsqrt(jnp.mean(centred * centred, axis=-1, keepdims=True) + EPS)
    return centred * inv_std, inv_std


def embed_rows(tokens_ref, types_ref, table_ref):
    count, length, width = tokens_ref.shape
    index = lax.broadcasted_iota(jnp.int32, (NTYPE, length), 0)
    onehot = jnp.where(types_ref[...] == index, 1.0, 0.0).astype(jnp.bfloat16)
    added = matmul_tn(onehot, table_ref[...])
    embedded = tokens_ref[...].astype(jnp.float32) + added[None]
    return unit_rows(embedded.reshape(count * length, width))


def token_kernel(row_ref, col_ref, tokens_ref, types_ref, table_ref, *refs):
    wq_ref, wk_ref, wv_ref, wg_ref, cot_ref = refs[:5]
    out_refs, side_ref = refs[5:-1], refs[-1]
    normed, _ = embed_rows(tokens_ref, types_ref, table_ref)
    act = normed.astype(jnp.bfloat16)
    for slot, ref in enumerate((wq_ref, wk_ref, wv_ref)):
        side_ref[slot] = matmul(act, ref[...]).astype(jnp.bfloat16).T
    gate = matmul(act, wg_ref[...]).astype(jnp.bfloat16).astype(jnp.float32)
    cot = cot_ref[...].reshape(gate.shape).astype(jnp.float32)
    side_ref[3] = (cot * jax.nn.sigmoid(gate)).astype(jnp.bfloat16).T
    for offset, out_ref in enumerate(out_refs):
        for core in range(2):
            start = pl.multiple_of((col_ref[0] ^ (2 * offset + core)) * CH, 16)
            out_ref[core] = side_ref[:, pl.ds(start, CH), :]


def token_messages(row, col, tokens, types, table, weights, cotangent, n_row, n_col):
    samp_dev, tok_col, _ = tokens.shape
    width = D // n_row
    held = samp_dev * tok_col
    whole3 = lambda i, r, c: (0, 0, 0)
    whole2 = lambda i, r, c: (0, 0)
    weight_spec = pl.BlockSpec((D, width), lambda i, r, c: (0, r[0]))
    shape = (2, 4, CH, held)
    count = n_col // 2
    return pl.pallas_call(
        token_kernel,
        out_shape=[jax.ShapeDtypeStruct(shape, jnp.bfloat16)] * count,
        grid_spec=pltpu.PrefetchScalarGridSpec(
            num_scalar_prefetch=2,
            grid=(1,),
            in_specs=[
                pl.BlockSpec(tokens.shape, whole3),
                pl.BlockSpec(types.shape, whole2),
                pl.BlockSpec(table.shape, whole2),
                weight_spec,
                weight_spec,
                weight_spec,
                weight_spec,
                pl.BlockSpec((samp_dev, tok_col, width), lambda i, r, c: (0, 0, r[0])),
            ],
            out_specs=[pl.BlockSpec(shape, lambda i, r, c: (0, 0, 0, 0))] * count,
            scratch_shapes=[pltpu.VMEM((4, width, held), jnp.bfloat16)],
        ),
        compiler_params=params(56),
        cost_estimate=pl.CostEstimate(
            flops=4_000_000_000, bytes_accessed=4_000_000, transcendentals=0
        ),
        name="token_messages",
    )(row, col, tokens, types, table, *weights, cotangent)


def own_kernel(
    row_ref, tokens_ref, types_ref, table_ref, wg_ref, cot_ref, slope_ref, normed_ref, inv_ref
):
    normed, inv_std = embed_rows(tokens_ref, types_ref, table_ref)
    gate = matmul(normed.astype(jnp.bfloat16), wg_ref[...]).astype(jnp.bfloat16)
    sig = jax.nn.sigmoid(gate.astype(jnp.float32))
    cot = cot_ref[...].reshape(gate.shape).astype(jnp.float32)
    slope_ref[...] = (cot * sig * (1.0 - sig)).T
    normed_ref[...] = normed.T
    inv_ref[...] = jnp.broadcast_to(inv_std, (inv_std.shape[0], 128)).T[:8]


def own_rows(row, tokens, types, table, w_gate, cotangent, half):
    _, tok_col, _ = tokens.shape
    count = half * tok_col
    part_spec = pl.BlockSpec((half, tok_col, D), lambda i, r: (r[0], 0, 0))
    whole2 = lambda i, r: (0, 0)
    return pl.pallas_call(
        own_kernel,
        out_shape=[
            jax.ShapeDtypeStruct((D, count), jnp.float32),
            jax.ShapeDtypeStruct((D, count), jnp.float32),
            jax.ShapeDtypeStruct((8, count), jnp.float32),
        ],
        grid_spec=pltpu.PrefetchScalarGridSpec(
            num_scalar_prefetch=1,
            grid=(1,),
            in_specs=[
                part_spec,
                pl.BlockSpec(types.shape, whole2),
                pl.BlockSpec(table.shape, whole2),
                pl.BlockSpec(w_gate.shape, whole2),
                part_spec,
            ],
            out_specs=[
                pl.BlockSpec((D, count), whole2),
                pl.BlockSpec((D, count), whole2),
                pl.BlockSpec((8, count), whole2),
            ],
        ),
        compiler_params=params(56),
        cost_estimate=pl.CostEstimate(
            flops=3_000_000_000, bytes_accessed=3_000_000, transcendentals=0
        ),
        name="own_rows",
    )(row, tokens, types, table, w_gate, cotangent)


MANY = 4


def pair_columns(pair_ref, k, many):
    _, _, length, width = pair_ref.shape
    blocks = [pair_ref[p, pl.ds(k, many)] for p in range(2)]
    rows = jnp.concatenate(blocks, axis=1).reshape(many * 2 * length, width)
    same = lax.broadcasted_iota(jnp.int32, (width, width), 0) == lax.broadcasted_iota(
        jnp.int32, (width, width), 1
    )
    centring = (jnp.where(same, 1.0, 0.0) - 1.0 / width).astype(jnp.bfloat16)
    centred = matmul_nt(centring, rows)
    return centred, lax.rsqrt(jnp.mean(centred * centred, axis=0, keepdims=True) + EPS)


def bias_kernel(pair_ref, weight_ref, mask_ref, out_ref, flat_ref):
    _, count, length, width = pair_ref.shape
    whole = flat_ref.shape[0] // H
    weight = jnp.concatenate([weight_ref[...]] * 2, axis=1)
    base = pl.program_id(0) * count

    def step(n, carry):
        k = n * MANY
        centred, inv_std = pair_columns(pair_ref, k, MANY)
        bias = matmul(weight, jnp.concatenate(halves(centred), axis=0)) * inv_std
        for m in range(MANY):
            lanes = slice(m * 2 * length, (m + 1) * 2 * length)
            flat_ref[pl.ds(base + k + m, H, stride=whole), :] = bias[:, lanes]
        return carry

    lax.fori_loop(0, count // MANY, step, 0, unroll=8)

    @pl.when(pl.program_id(0) == pl.num_programs(0) - 1)
    def _():
        keep = jnp.broadcast_to(mask_ref[...].astype(jnp.float32), (128, length)).T
        keep = jnp.concatenate([keep] * (2 * whole // 128), axis=1) == 1.0
        for h in range(H):
            turned = flat_ref[h * whole : (h + 1) * whole, :].T
            bias = jnp.concatenate([turned[:length], turned[length:]], axis=1)
            out_ref[h] = jnp.where(keep, bias, MASKED)


STEPS = 4


def split_spec(shape):
    block = (shape[0] // STEPS,) + tuple(shape[1:])
    return pl.BlockSpec(block, lambda i: (i,) + (0,) * (len(shape) - 1))


def whole_spec(shape):
    return pl.BlockSpec(tuple(shape), lambda i: (0,) * len(shape))


def pair_spec(pair):
    row_count, tok_col, width = pair.shape
    block = (2, row_count // 2 // STEPS, tok_col, width)
    return pl.BlockSpec(block, lambda i: (0, i, 0, 0))


def pair_bias(pair, weight_t, mask):
    row_count, tok_col, width = pair.shape
    whole = row_count // 2
    return pl.pallas_call(
        bias_kernel,
        out_shape=jax.ShapeDtypeStruct((H, tok_col, row_count), jnp.float32),
        grid=(STEPS,),
        in_specs=[pair_spec(pair), whole_spec(weight_t.shape), whole_spec(mask.shape)],
        out_specs=whole_spec((H, tok_col, row_count)),
        scratch_shapes=[pltpu.VMEM((H * whole, 2 * tok_col), jnp.float32)],
        compiler_params=params(24),
        cost_estimate=pl.CostEstimate(
            flops=6_000_000_000, bytes_accessed=5_000_000, transcendentals=0
        ),
        name="pair_bias",
    )(pair.reshape(2, whole, tok_col, width), weight_t, mask)


def norm_kernel(pair_ref, normed_ref, inv_ref):
    def step(n, carry):
        centred, inv_std = pair_columns(pair_ref, n * MANY, MANY)
        normed_ref[n] = jnp.concatenate(halves(centred * inv_std), axis=0)
        inv_ref[n] = jnp.broadcast_to(inv_std, inv_ref.shape[1:])
        return carry

    lax.fori_loop(0, normed_ref.shape[0], step, 0, unroll=8)


def pair_units(pair):
    row_count, tok_col, width = pair.shape
    whole = row_count // 2
    chunks, lanes = whole // MANY, MANY * 2 * tok_col
    shapes = [(chunks, 2 * width, lanes), (chunks, 8, lanes)]
    return pl.pallas_call(
        norm_kernel,
        out_shape=[
            jax.ShapeDtypeStruct(shapes[0], jnp.bfloat16),
            jax.ShapeDtypeStruct(shapes[1], jnp.float32),
        ],
        grid=(STEPS,),
        in_specs=[pair_spec(pair)],
        out_specs=[split_spec(shape) for shape in shapes],
        compiler_params=params(56),
        cost_estimate=pl.CostEstimate(
            flops=6_000_000_000, bytes_accessed=12_000_000, transcendentals=0
        ),
        name="pair_units",
    )(pair.reshape(2, whole, tok_col, width))


def shift_of(top):
    return jnp.floor(jnp.clip(14.0 - jnp.log2(top), -100.0, 100.0))


def attention_kernel(col_ref, *refs):
    other_ref, bias_ref, back_ref, grad_bias_ref, sum_ref, tokens_ref = refs[-6:]
    col = col_ref[0]
    for offset, ref in enumerate(refs[:-6]):
        tokens_ref[col ^ (2 * offset)] = ref[0]
        tokens_ref[col ^ (2 * offset + 1)] = other_ref[offset]
    n_col = tokens_ref.shape[0]
    tok_col, row_count = bias_ref.shape[1:]
    half = back_ref.shape[2] // tok_col
    n_row = bias_ref.shape[0] // n_col
    step = pl.program_id(0)

    @pl.when(step == 0)
    def _():
        sum_ref[...] = jnp.zeros_like(sum_ref)

    outs = []
    for sample in range(half):
        lanes = slice(sample * tok_col, (sample + 1) * tok_col)

        def side(slot):
            return jnp.concatenate([tokens_ref[c, slot, :, lanes] for c in range(n_col)], axis=1)

        query_t, key_t, value_t, grad_t = [side(slot) for slot in range(4)]
        key = key_t.T
        value = value_t.T
        attended_parts, grad_query_parts = [], []
        grad_key = jnp.zeros(key_t.shape, jnp.float32)
        grad_value = jnp.zeros(key_t.shape, jnp.float32)
        for block in range(n_row):
            cols = slice(block * row_count, (block + 1) * row_count)
            heads = slice(block * n_col, (block + 1) * n_col)
            bias = bias_ref[heads].reshape(n_col * tok_col, row_count)
            query_b = query_t[:, cols]
            grad_b = grad_t[:, cols]
            scores = matmul(key, query_b) * SCALE + bias
            scores = jnp.where(bias < -60000.0, -1000000000.0, scores)
            expo = jnp.exp(scores - jnp.max(scores, axis=0, keepdims=True))
            share = 1.0 / jnp.sum(expo, axis=0, keepdims=True)
            attended = matmul(value_t, expo.astype(jnp.bfloat16)) * share
            delta = jnp.sum(grad_b.astype(jnp.float32) * attended, axis=0, keepdims=True)
            probs = expo * share
            grad_scores = probs * (matmul(value, grad_b) - delta)
            rounded = grad_scores.astype(jnp.bfloat16)
            attended_parts.append(attended)
            grad_query_parts.append(matmul(key_t, rounded) * SCALE)
            grad_key = grad_key + matmul_nt(query_b, rounded)
            grad_value = grad_value + matmul_nt(grad_b, probs.astype(jnp.bfloat16))
            sum_ref[heads] += grad_scores.reshape(n_col, tok_col, row_count)
        outs.append(
            (
                jnp.concatenate(grad_query_parts, axis=1),
                grad_key * SCALE,
                grad_value,
                jnp.concatenate(attended_parts, axis=1),
            )
        )
    spare = jnp.zeros((8 - 4, half * tok_col), jnp.float32)
    tops = [jnp.max(jnp.abs(out[slot]), axis=0, keepdims=True) for slot in range(4) for out in outs]
    shifts = shift_of(jnp.concatenate(tops, axis=0))
    scales = jnp.exp2(shifts)
    scaled = [
        [out[slot] * scales[slot * half + n : slot * half + n + 1] for n, out in enumerate(outs)]
        for slot in range(4)
    ]
    for c in range(n_col):
        lanes = slice(c * tok_col, (c + 1) * tok_col)
        for slot in range(4):
            back_ref[c, slot * CH : (slot + 1) * CH, :] = jnp.concatenate(
                [part[:, lanes] for part in scaled[slot]], axis=1
            )
        tails = [
            jnp.concatenate([shifts[slot * half + n :, lanes][:1] for n in range(half)], axis=1)
            for slot in range(4)
        ]
        back_ref[c, 4 * CH :, :] = jnp.concatenate(tails + [spare], axis=0)

    @pl.when(step == pl.num_programs(0) - 1)
    def _():
        whole = row_count // 2
        for head in range(n_row * n_col):
            sums = sum_ref[head]
            sums = jnp.concatenate([sums[:, :whole], sums[:, whole:]], axis=0).T
            shift = shift_of(jnp.max(jnp.abs(sums), axis=0, keepdims=True))
            grad_bias_ref[head, :whole, :] = sums * jnp.exp2(shift)
            grad_bias_ref[head, whole:, :] = jnp.broadcast_to(shift, (8, 2 * tok_col))


def attention(col, arrived, other, bias, n_row):
    count = len(arrived)
    n_col = 2 * count
    _, tok_col, row_count = bias.shape
    half = arrived[0].shape[-1] // tok_col // n_row
    width = half * tok_col
    back_shape = (n_row * n_col, 4 * CH + 8, width)
    bias_shape = (n_row * n_col, row_count // 2 + 8, 2 * tok_col)
    return pl.pallas_call(
        attention_kernel,
        out_shape=[
            jax.ShapeDtypeStruct(back_shape, jnp.float32),
            jax.ShapeDtypeStruct(bias_shape, jnp.float32),
        ],
        grid_spec=pltpu.PrefetchScalarGridSpec(
            num_scalar_prefetch=1,
            grid=(n_row,),
            in_specs=[pl.BlockSpec((1, 4, CH, width), lambda i, r: (0, 0, 0, i))] * count
            + [
                pl.BlockSpec((count, 4, CH, width), lambda i, r: (0, 0, 0, i)),
                pl.BlockSpec(bias.shape, lambda i, r: (0, 0, 0)),
            ],
            out_specs=[
                pl.BlockSpec((n_col, 4 * CH + 8, width), lambda i, r: (i, 0, 0)),
                pl.BlockSpec(bias_shape, lambda i, r: (0, 0, 0)),
            ],
            scratch_shapes=[
                pltpu.VMEM(bias.shape, jnp.float32),
                pltpu.VMEM((n_col, 4, CH, width), jnp.bfloat16),
            ],
        ),
        compiler_params=params(24),
        cost_estimate=pl.CostEstimate(
            flops=8_000_000_000, bytes_accessed=6_000_000, transcendentals=1_000_000
        ),
        name="attention",
    )(col, *arrived, other, bias)


def back_kernel(*refs):
    slope_ref, normed_ref, inv_ref, wq_ref, wk_ref, wv_ref, wg_ref = refs[-11:-4]
    out_ref, parts_ref, gate_ref, total_ref = refs[-4:]
    back_ref = refs[0]
    count = normed_ref.shape[-1]
    step = pl.program_id(0)
    rows = wq_ref.shape[0]

    @pl.when(step == 0)
    def _():
        for slot in range(4):
            scale = jnp.exp2(-back_ref[:, 4 * CH + slot : 4 * CH + slot + 1, :])
            values = back_ref[:, slot * CH : (slot + 1) * CH, :] * scale
            values = values.reshape(gate_ref.shape)
            if slot < 3:
                parts_ref[slot] = jnp.concatenate(halves(values), axis=1)
            else:
                gate_ref[...] = (values * slope_ref[...]).astype(jnp.bfloat16)

    total = matmul(wg_ref[...], gate_ref[...])
    for slot, ref in enumerate((wq_ref, wk_ref, wv_ref)):
        parts = matmul(ref[...], parts_ref[slot])
        total = total + (parts[:, :count] + parts[:, count:])
    total_ref[pl.ds(pl.multiple_of(step * rows, 8), rows), :] = total

    @pl.when(step == pl.num_programs(0) - 1)
    def _():
        whole = total_ref[...]
        normed = normed_ref[...]
        result = inv_ref[:1] * (
            whole
            - jnp.mean(whole, axis=0, keepdims=True)
            - normed * jnp.mean(whole * normed, axis=0, keepdims=True)
        )
        out_ref[...] = result.T.astype(jnp.bfloat16)


def token_back(back, slope, normed, inv_std, weights):
    count = normed.shape[-1]
    steps = 2
    whole = lambda shape: pl.BlockSpec(shape, lambda i: (0,) * len(shape))
    weight_spec = pl.BlockSpec((D // steps, D), lambda i: (i, 0))
    return pl.pallas_call(
        back_kernel,
        out_shape=jax.ShapeDtypeStruct((count, D), jnp.bfloat16),
        grid=(steps,),
        in_specs=[whole(array.shape) for array in (back, slope, normed, inv_std)]
        + [weight_spec] * 4,
        out_specs=whole((count, D)),
        scratch_shapes=[
            pltpu.VMEM((3, D, 2 * count), jnp.bfloat16),
            pltpu.VMEM((D, count), jnp.bfloat16),
            pltpu.VMEM((D, count), jnp.float32),
        ],
        compiler_params=params(40),
        cost_estimate=pl.CostEstimate(
            flops=4_000_000_000, bytes_accessed=8_000_000, transcendentals=0
        ),
        name="token_back",
    )(back, slope, normed, inv_std, *weights)


def flat_columns(flat_ref, k, many):
    whole = flat_ref.shape[0] // H
    grads = [flat_ref[pl.ds(k + m, H, stride=whole), :] for m in range(many)]
    return jnp.concatenate(halves(jnp.concatenate(grads, axis=1)), axis=0)


def pair_weight_kernel(normed_ref, grads_ref, part_ref):
    chunks, width, _ = normed_ref.shape
    base = pl.program_id(0) * chunks

    @pl.when(pl.program_id(0) == 0)
    def _():
        part_ref[...] = jnp.zeros_like(part_ref)

    def step(n, carry):
        return carry + matmul_nt(normed_ref[n], flat_columns(grads_ref, (base + n) * MANY, MANY))

    parts = lax.fori_loop(0, chunks, step, jnp.zeros((width, 2 * H), jnp.float32), unroll=8)
    parts = parts[:, :H] + parts[:, H:]
    part_ref[...] += (parts[: width // 2] + parts[width // 2 :]).T


def pair_back_kernel(factor, normed_ref, inv_ref, grads_ref, weight_ref, out_ref):
    _, count, length, width = out_ref.shape
    weight = weight_ref[...].astype(jnp.float32)
    weight = halves(weight - jnp.mean(weight, axis=1, keepdims=True))
    weight = jnp.concatenate([weight[0], weight[0], weight[1], weight[1]], axis=0).T
    base = pl.program_id(0) * count

    def step(n, carry):
        k = n * MANY
        normed = normed_ref[n].astype(jnp.float32)
        normed = normed[:width] + normed[width:]
        grads = flat_columns(grads_ref, base + k, MANY)
        grad_in = matmul(weight, jnp.concatenate([grads, grads], axis=0))
        overlap = jnp.mean(grad_in * normed, axis=0, keepdims=True)
        result = (grad_in - normed * overlap) * (inv_ref[n, :1] * factor)
        result = result.astype(jnp.bfloat16).T.reshape(MANY, 2 * length, width)
        for p in range(2):
            out_ref[p, pl.ds(k, MANY)] = result[:, p * length : (p + 1) * length]
        return carry

    lax.fori_loop(0, count // MANY, step, 0, unroll=8)


def pair_weight(normed, grads):
    part_shape = (H, normed.shape[1] // 2)
    return pl.pallas_call(
        pair_weight_kernel,
        out_shape=jax.ShapeDtypeStruct(part_shape, jnp.float32),
        grid=(STEPS,),
        in_specs=[split_spec(normed.shape), whole_spec(grads.shape)],
        out_specs=whole_spec(part_shape),
        compiler_params=params(24),
        cost_estimate=pl.CostEstimate(
            flops=5_000_000_000, bytes_accessed=100_000, transcendentals=0
        ),
        name="pair_weight",
    )(normed, grads)


def pair_backward(shape, normed, inv_std, grads, weight_t, factor):
    row_count, tok_col, width = shape
    whole = row_count // 2
    pair_grad = pl.pallas_call(
        lambda *refs: pair_back_kernel(factor, *refs),
        out_shape=jax.ShapeDtypeStruct((2, whole, tok_col, width), jnp.bfloat16),
        grid=(STEPS,),
        in_specs=[
            split_spec(normed.shape),
            split_spec(inv_std.shape),
            whole_spec(grads.shape),
            whole_spec(weight_t.shape),
        ],
        out_specs=pl.BlockSpec((2, whole // STEPS, tok_col, width), lambda i: (0, i, 0, 0)),
        compiler_params=params(24),
        cost_estimate=pl.CostEstimate(
            flops=8_000_000_000, bytes_accessed=100_000, transcendentals=0
        ),
        name="pair_backward",
    )(normed, inv_std, grads, weight_t)
    return pair_grad.reshape(shape)


def unscaled(block, rows):
    block = block.astype(jnp.float32)
    block = block[:, :rows] * jnp.exp2(-block[:, rows : rows + 1])
    return block.reshape(-1, block.shape[2])


def swap(block, axis):
    return lax.ppermute(block, axis, [(0, 1), (1, 0)])


def body_heads(
    tokens, restype, type_table, key_mask, pair, w_bias, w_query, w_key, w_value, w_gate, cotangent
):
    n_row = lax.axis_size("row")
    n_col = lax.axis_size("col")
    n_samp = lax.axis_size("samp")
    samp_dev = tokens.shape[0]
    tok_col = tokens.shape[1]
    row_count = pair.shape[0]
    total_tokens = tok_col * n_col
    half = samp_dev // n_row
    row_index = lax.axis_index("row")
    row = row_index.astype(jnp.int32).reshape(1)
    col = lax.axis_index("col").astype(jnp.int32).reshape(1)
    types = restype.reshape(1, tok_col)
    weight_t = w_bias.T
    weights = (w_query, w_key, w_value, w_gate)
    samples = samp_dev * n_samp

    def send(block, offset):
        return lax.ppermute(block, "col", [(c, c ^ offset) for c in range(n_col)])

    def by_chip(blocks):
        return [blocks[0]] + [send(blocks[n], 2 * n) for n in range(1, n_col // 2)]

    def across(blocks):
        return send(jnp.stack([block[1] for block in blocks]), 1)

    messages = token_messages(
        row, col, tokens, types, type_table, weights, cotangent, n_row, n_col
    )
    arrived = by_chip(messages)
    bias = pair_bias(pair, weight_t, key_mask.reshape(1, tok_col))
    bias, arrived, types = lax.optimization_barrier(
        (bias.astype(jnp.float16), arrived, types)
    )
    own = own_rows(row, tokens, types, type_table, w_gate, cotangent, half)
    bias = lax.all_to_all(bias, ("row", "col"), 0, 0, tiled=True)
    other = across(arrived)
    bias, other, own = lax.optimization_barrier((bias, other, own))

    back, grad_bias = attention(col, arrived, other, bias.astype(jnp.float32), n_row)
    grad_bias = lax.all_to_all(
        grad_bias.astype(jnp.float16), ("row", "col"), 0, 0, tiled=True
    )
    back, late_pair = lax.optimization_barrier((back.astype(jnp.float16), pair))
    pair_normed, pair_inv = pair_units(late_pair)
    back, _, pair_normed = lax.optimization_barrier((back, grad_bias, pair_normed))
    back = lax.all_to_all(back, ("row", "col"), 0, 0, tiled=True)

    other_bias = swap(grad_bias, "samp")
    own_bias = unscaled(grad_bias, row_count // 2)
    part = pair_weight(pair_normed, own_bias)
    samp_part = swap(part, "samp")
    row_part = swap(part, "row")
    both_part = lax.ppermute(part, ("samp", "row"), [(n, 3 - n) for n in range(4)])
    other_bias, part = lax.optimization_barrier((other_bias, part))
    grads = own_bias + unscaled(other_bias, row_count // 2)
    pair_grad = pair_backward(
        pair.shape, pair_normed, pair_inv, grads, weight_t, total_tokens / samples
    )

    pair_grad, back, sums = lax.optimization_barrier(
        (pair_grad, back, (part, samp_part, row_part, both_part))
    )
    part = (sums[0] + sums[1]) + (sums[2] + sums[3])
    sums = (send(part, 1), send(part, 2), send(part, 3))
    token_half = token_back(back.astype(jnp.float32), *own, weights)
    token_half, sums = lax.optimization_barrier((token_half, sums))
    part = ((part + sums[0]) + (sums[1] + sums[2])) / samples
    last = send(part, 4)
    token_half = token_half.reshape(half, tok_col, D)
    other_half = swap(token_half, "row")
    first = row_index == 0
    token_grad = jnp.concatenate(
        [jnp.where(first, token_half, other_half), jnp.where(first, other_half, token_half)],
        axis=0,
    )
    token_grad, last = lax.optimization_barrier((token_grad, last))
    return (token_grad, pair_grad, (part + last).T)


def body(*args):
    n_row = lax.axis_size("row")
    n_col = lax.axis_size("col")
    tokens = args[0]
    pair = args[4]
    fits = n_row == 2 and n_col == 8 and n_row * n_col == H and lax.axis_size("samp") == 2
    square = pair.shape[0] * n_row == pair.shape[1] * n_col
    if fits and square and tokens.shape[0] == 4 and tokens.shape[1] == 64:
        return body_heads(*args)
    return body_any(*args)


def solution(mesh):
    placed = (
        P("samp", "col", None),
        P("col"),
        P(),
        P("col"),
        P("row", "col", None),
        P(),
        P(),
        P(),
        P(),
        P(),
        P("samp", "col", None),
    )
    return jax.shard_map(
        body,
        mesh=mesh,
        in_specs=placed,
        out_specs=(P("samp", "col", None), P("row", "col", None), P()),
        check_vma=False,
    )
```

```python
import math

import jax
import jax.numpy as jnp
from jax import lax
from jax.experimental import pallas as pl
from jax.experimental.pallas import tpu as pltpu
from jax.sharding import PartitionSpec as P

D = 768
H = 16
CH = 48
NTYPE = 32


def broadcast(block, axis, source):
    block = jnp.where(lax.axis_index(axis) == source, block, jnp.zeros_like(block))
    return lax.psum(block, axis)


def token_norm(tokens, restype, type_table):
    onehot = (restype[:, None] == jnp.arange(NTYPE, dtype=jnp.int32)[None, :]).astype(jnp.bfloat16)
    embedded = tokens.astype(jnp.float32) + jnp.dot(
        onehot, type_table, preferred_element_type=jnp.float32
    )
    centred = embedded - jnp.mean(embedded, axis=-1, keepdims=True)
    inv_std = lax.rsqrt(jnp.mean(centred * centred, axis=-1, keepdims=True) + 1e-05)
    return (centred * inv_std, inv_std)


def pair_norm(block):
    values = block.astype(jnp.float32)
    centred = values - jnp.mean(values, axis=-1, keepdims=True)
    inv_std = lax.rsqrt(jnp.mean(centred * centred, axis=-1, keepdims=True) + 1e-05)
    return (centred * inv_std, inv_std)


def norm_back(grad_in, normed, inv_std):
    return inv_std * (
        grad_in
        - jnp.mean(grad_in, axis=-1, keepdims=True)
        - normed * jnp.mean(grad_in * normed, axis=-1, keepdims=True)
    )


def project(rows_in, weight):
    return jnp.einsum("std,de->ste", rows_in, weight, preferred_element_type=jnp.float32).astype(
        jnp.bfloat16
    )


def back_project(grads, weight):
    return jnp.einsum(
        "ste,de->std", grads, weight.astype(jnp.float32), precision=lax.Precision.HIGHEST
    )


def pair_back(grad_bias, pair_normed, pair_inv, bias_weight):
    grad_normed = jnp.einsum("hij,ch->ijc", grad_bias, bias_weight, precision=lax.Precision.HIGHEST)
    return norm_back(grad_normed, pair_normed, pair_inv)


def body_any(
    tokens, restype, type_table, key_mask, pair, w_bias, w_query, w_key, w_value, w_gate, cotangent
):
    n_row = lax.axis_size("row")
    n_col = lax.axis_size("col")
    n_samp = lax.axis_size("samp")
    samp_dev = tokens.shape[0]
    tok_col = tokens.shape[1]
    spread = n_col // n_row
    row_count = tok_col * spread
    total_tokens = tok_col * n_col
    row_index = lax.axis_index("row")
    col_index = lax.axis_index("col")
    is_owner = col_index // spread == row_index
    own_start = col_index % spread * tok_col
    normed, inv_std = token_norm(tokens, restype, type_table)
    own_act = normed.astype(jnp.bfloat16)
    key_proj = project(own_act, w_key)
    value_proj = project(own_act, w_value)
    stacked = jnp.stack([own_act, cotangent])
    pieces = [broadcast(stacked, "col", row_index * spread + member) for member in range(spread)]
    gathered = jnp.concatenate(pieces, axis=2)
    query_side = gathered[0]
    grad_rows = gathered[1]
    queries = project(query_side, w_query)
    gate_lin = project(query_side, w_gate)
    pair_normed, pair_inv = pair_norm(pair)
    bias_weight = w_bias.astype(jnp.float32)
    bias = jnp.einsum("ijc,ch->hij", pair_normed, bias_weight, precision=lax.Precision.HIGHEST)
    query_heads = queries.reshape(samp_dev, row_count, H, CH)
    key_heads = key_proj.reshape(samp_dev, tok_col, H, CH)
    value_heads = value_proj.reshape(samp_dev, tok_col, H, CH)
    scores = (
        jnp.einsum("sihc,sjhc->shij", query_heads, key_heads, preferred_element_type=jnp.float32)
        / math.sqrt(CH)
        + bias[None]
    )
    scores = jnp.where(key_mask[None, None, None, :] == 1, scores, -1000000000.0)
    top = lax.pmax(jnp.max(scores, axis=-1), "col")
    expo = jnp.exp(scores - top[..., None])
    partial_out = jnp.einsum(
        "shij,sjhc->sihc",
        expo.astype(jnp.bfloat16),
        value_heads,
        preferred_element_type=jnp.float32,
    )
    totals, summed = lax.psum(
        (jnp.sum(expo, axis=-1), partial_out.reshape(samp_dev, row_count, D)), "col"
    )
    attended = (
        summed.reshape(samp_dev, row_count, H, CH) / jnp.transpose(totals, (0, 2, 1))[..., None]
    )
    flat_out = attended.reshape(samp_dev, row_count, D)
    sig_gate = jax.nn.sigmoid(gate_lin.astype(jnp.float32))
    grad_f = grad_rows.astype(jnp.float32)
    grad_out = (grad_f * sig_gate).astype(jnp.bfloat16)
    grad_gate = (grad_f * flat_out * sig_gate * (1.0 - sig_gate)).astype(jnp.bfloat16)
    gate_piece = lax.dynamic_slice_in_dim(grad_gate, own_start, tok_col, 1)
    gate_term = jnp.where(
        is_owner,
        jnp.einsum("ste,de->std", gate_piece, w_gate, preferred_element_type=jnp.float32),
        0.0,
    )
    grad_heads = grad_out.reshape(samp_dev, row_count, H, CH)
    delta = jnp.transpose(jnp.sum(grad_heads.astype(jnp.float32) * attended, axis=-1), (0, 2, 1))
    probs = expo / totals[..., None]
    grad_pre = jnp.einsum(
        "sihc,sjhc->shij", grad_heads, value_heads, preferred_element_type=jnp.float32
    )
    grad_scores = probs * (grad_pre - delta[..., None])
    rounded = grad_scores.astype(jnp.bfloat16)
    grad_query = (
        jnp.einsum("shij,sjhc->sihc", rounded, key_heads, preferred_element_type=jnp.float32)
        / math.sqrt(CH)
    ).reshape(samp_dev, row_count, D)
    grad_key = (
        jnp.einsum("shij,sihc->sjhc", rounded, query_heads, preferred_element_type=jnp.float32)
        / math.sqrt(CH)
    ).reshape(samp_dev, tok_col, D)
    grad_value = jnp.einsum(
        "shij,sihc->sjhc",
        probs.astype(jnp.bfloat16),
        grad_heads,
        preferred_element_type=jnp.float32,
    ).reshape(samp_dev, tok_col, D)
    bias_local = jnp.sum(grad_scores, axis=0)
    blank = jnp.zeros((samp_dev, total_tokens, D), jnp.float32)
    mine = lax.psum_scatter(
        lax.dynamic_update_slice_in_dim(blank, grad_query, row_index * row_count, 1),
        "col",
        scatter_dimension=1,
        tiled=True,
    )
    query_all, key_all, value_all, gate_all = lax.psum(
        (mine, grad_key, grad_value, gate_term), "row"
    )
    grad_act = (
        back_project(query_all, w_query)
        + back_project(key_all, w_key)
        + back_project(value_all, w_value)
        + gate_all
    )
    token_grad = norm_back(grad_act, normed, inv_std).astype(jnp.bfloat16)
    samples = samp_dev * n_samp
    grad_bias = lax.psum(bias_local, "samp")
    grad_pair = pair_back(grad_bias, pair_normed, pair_inv, bias_weight)
    pair_grad = (grad_pair * (total_tokens / samples)).astype(jnp.bfloat16)
    weight_part = jnp.einsum("ijc,hij->ch", pair_normed, grad_bias, precision=lax.Precision.HIGHEST)
    weight_sum = lax.psum(weight_part, ("row", "col"))
    bias_weight_grad = weight_sum / samples
    return (token_grad, pair_grad, bias_weight_grad)


EPS = 1e-05
SCALE = 1.0 / math.sqrt(CH)
NT = (((1,), (1,)), ((), ()))
TN = (((0,), (0,)), ((), ()))
MASKED = -65504.0


def params(megabytes):
    return pltpu.CompilerParams(vmem_limit_bytes=megabytes * 1024 * 1024)


def matmul(left, right):
    return jnp.dot(left, right, preferred_element_type=jnp.float32)


def matmul_nt(left, right):
    return lax.dot_general(left, right, NT, preferred_element_type=jnp.float32)


def matmul_tn(left, right):
    return lax.dot_general(left, right, TN, preferred_element_type=jnp.float32)


def halves(values):
    high = values.astype(jnp.bfloat16)
    low = (values - high.astype(jnp.float32)).astype(jnp.bfloat16)
    return high, low


def unit_rows(values):
    centred = values - jnp.mean(values, axis=-1, keepdims=True)
    inv_std = lax.rsqrt(jnp.mean(centred * centred, axis=-1, keepdims=True) + EPS)
    return centred * inv_std, inv_std


def embed_rows(tokens_ref, types_ref, table_ref):
    count, length, width = tokens_ref.shape
    index = lax.broadcasted_iota(jnp.int32, (NTYPE, length), 0)
    onehot = jnp.where(types_ref[...] == index, 1.0, 0.0).astype(jnp.bfloat16)
    added = matmul_tn(onehot, table_ref[...])
    embedded = tokens_ref[...].astype(jnp.float32) + added[None]
    return unit_rows(embedded.reshape(count * length, width))


def token_kernel(row_ref, col_ref, tokens_ref, types_ref, table_ref, *refs):
    wq_ref, wk_ref, wv_ref, wg_ref, cot_ref = refs[:5]
    out_refs, side_ref = refs[5:-1], refs[-1]
    normed, _ = embed_rows(tokens_ref, types_ref, table_ref)
    act = normed.astype(jnp.bfloat16)
    for slot, ref in enumerate((wq_ref, wk_ref, wv_ref)):
        side_ref[slot] = matmul(act, ref[...]).astype(jnp.bfloat16).T
    gate = matmul(act, wg_ref[...]).astype(jnp.bfloat16).astype(jnp.float32)
    cot = cot_ref[...].reshape(gate.shape).astype(jnp.float32)
    side_ref[3] = (cot * jax.nn.sigmoid(gate)).astype(jnp.bfloat16).T
    for offset, out_ref in enumerate(out_refs):
        for core in range(2):
            start = pl.multiple_of((col_ref[0] ^ (2 * offset + core)) * CH, 16)
            out_ref[core] = side_ref[:, pl.ds(start, CH), :]


def token_messages(row, col, tokens, types, table, weights, cotangent, n_row, n_col):
    samp_dev, tok_col, _ = tokens.shape
    width = D // n_row
    held = samp_dev * tok_col
    whole3 = lambda i, r, c: (0, 0, 0)
    whole2 = lambda i, r, c: (0, 0)
    weight_spec = pl.BlockSpec((D, width), lambda i, r, c: (0, r[0]))
    shape = (2, 4, CH, held)
    count = n_col // 2
    return pl.pallas_call(
        token_kernel,
        out_shape=[jax.ShapeDtypeStruct(shape, jnp.bfloat16)] * count,
        grid_spec=pltpu.PrefetchScalarGridSpec(
            num_scalar_prefetch=2,
            grid=(1,),
            in_specs=[
                pl.BlockSpec(tokens.shape, whole3),
                pl.BlockSpec(types.shape, whole2),
                pl.BlockSpec(table.shape, whole2),
                weight_spec,
                weight_spec,
                weight_spec,
                weight_spec,
                pl.BlockSpec((samp_dev, tok_col, width), lambda i, r, c: (0, 0, r[0])),
            ],
            out_specs=[pl.BlockSpec(shape, lambda i, r, c: (0, 0, 0, 0))] * count,
            scratch_shapes=[pltpu.VMEM((4, width, held), jnp.bfloat16)],
        ),
        compiler_params=params(56),
        cost_estimate=pl.CostEstimate(
            flops=4_000_000_000, bytes_accessed=4_000_000, transcendentals=0
        ),
        name="token_messages",
    )(row, col, tokens, types, table, *weights, cotangent)


def own_kernel(
    row_ref, tokens_ref, types_ref, table_ref, wg_ref, cot_ref, slope_ref, normed_ref, inv_ref
):
    normed, inv_std = embed_rows(tokens_ref, types_ref, table_ref)
    gate = matmul(normed.astype(jnp.bfloat16), wg_ref[...]).astype(jnp.bfloat16)
    sig = jax.nn.sigmoid(gate.astype(jnp.float32))
    cot = cot_ref[...].reshape(gate.shape).astype(jnp.float32)
    slope_ref[...] = (cot * sig * (1.0 - sig)).T
    normed_ref[...] = normed.T
    inv_ref[...] = jnp.broadcast_to(inv_std, (inv_std.shape[0], 128)).T[:8]


def own_rows(row, tokens, types, table, w_gate, cotangent, half):
    _, tok_col, _ = tokens.shape
    count = half * tok_col
    part_spec = pl.BlockSpec((half, tok_col, D), lambda i, r: (r[0], 0, 0))
    whole2 = lambda i, r: (0, 0)
    return pl.pallas_call(
        own_kernel,
        out_shape=[
            jax.ShapeDtypeStruct((D, count), jnp.float32),
            jax.ShapeDtypeStruct((D, count), jnp.float32),
            jax.ShapeDtypeStruct((8, count), jnp.float32),
        ],
        grid_spec=pltpu.PrefetchScalarGridSpec(
            num_scalar_prefetch=1,
            grid=(1,),
            in_specs=[
                part_spec,
                pl.BlockSpec(types.shape, whole2),
                pl.BlockSpec(table.shape, whole2),
                pl.BlockSpec(w_gate.shape, whole2),
                part_spec,
            ],
            out_specs=[
                pl.BlockSpec((D, count), whole2),
                pl.BlockSpec((D, count), whole2),
                pl.BlockSpec((8, count), whole2),
            ],
        ),
        compiler_params=params(56),
        cost_estimate=pl.CostEstimate(
            flops=3_000_000_000, bytes_accessed=3_000_000, transcendentals=0
        ),
        name="own_rows",
    )(row, tokens, types, table, w_gate, cotangent)


MANY = 4


def pair_columns(pair_ref, k, many):
    _, _, length, width = pair_ref.shape
    blocks = [pair_ref[p, pl.ds(k, many)] for p in range(2)]
    rows = jnp.concatenate(blocks, axis=1).reshape(many * 2 * length, width)
    same = lax.broadcasted_iota(jnp.int32, (width, width), 0) == lax.broadcasted_iota(
        jnp.int32, (width, width), 1
    )
    centring = (jnp.where(same, 1.0, 0.0) - 1.0 / width).astype(jnp.bfloat16)
    centred = matmul_nt(centring, rows)
    return centred, lax.rsqrt(jnp.mean(centred * centred, axis=0, keepdims=True) + EPS)


def bias_kernel(pair_ref, weight_ref, mask_ref, out_ref, flat_ref):
    _, count, length, width = pair_ref.shape
    whole = flat_ref.shape[0] // H
    weight = jnp.concatenate([weight_ref[...]] * 2, axis=1)
    base = pl.program_id(0) * count

    def step(n, carry):
        k = n * MANY
        centred, inv_std = pair_columns(pair_ref, k, MANY)
        bias = matmul(weight, jnp.concatenate(halves(centred), axis=0)) * inv_std
        for m in range(MANY):
            lanes = slice(m * 2 * length, (m + 1) * 2 * length)
            flat_ref[pl.ds(base + k + m, H, stride=whole), :] = bias[:, lanes]
        return carry

    lax.fori_loop(0, count // MANY, step, 0, unroll=8)

    @pl.when(pl.program_id(0) == pl.num_programs(0) - 1)
    def _():
        keep = jnp.broadcast_to(mask_ref[...].astype(jnp.float32), (128, length)).T
        keep = jnp.concatenate([keep] * (2 * whole // 128), axis=1) == 1.0
        for h in range(H):
            turned = flat_ref[h * whole : (h + 1) * whole, :].T
            bias = jnp.concatenate([turned[:length], turned[length:]], axis=1)
            out_ref[h] = jnp.where(keep, bias, MASKED)


STEPS = 4


def split_spec(shape):
    block = (shape[0] // STEPS,) + tuple(shape[1:])
    return pl.BlockSpec(block, lambda i: (i,) + (0,) * (len(shape) - 1))


def whole_spec(shape):
    return pl.BlockSpec(tuple(shape), lambda i: (0,) * len(shape))


def pair_spec(pair):
    row_count, tok_col, width = pair.shape
    block = (2, row_count // 2 // STEPS, tok_col, width)
    return pl.BlockSpec(block, lambda i: (0, i, 0, 0))


def pair_bias(pair, weight_t, mask):
    row_count, tok_col, width = pair.shape
    whole = row_count // 2
    return pl.pallas_call(
        bias_kernel,
        out_shape=jax.ShapeDtypeStruct((H, tok_col, row_count), jnp.float32),
        grid=(STEPS,),
        in_specs=[pair_spec(pair), whole_spec(weight_t.shape), whole_spec(mask.shape)],
        out_specs=whole_spec((H, tok_col, row_count)),
        scratch_shapes=[pltpu.VMEM((H * whole, 2 * tok_col), jnp.float32)],
        compiler_params=params(24),
        cost_estimate=pl.CostEstimate(
            flops=6_000_000_000, bytes_accessed=5_000_000, transcendentals=0
        ),
        name="pair_bias",
    )(pair.reshape(2, whole, tok_col, width), weight_t, mask)


def norm_kernel(pair_ref, normed_ref, inv_ref):
    def step(n, carry):
        centred, inv_std = pair_columns(pair_ref, n * MANY, MANY)
        normed_ref[n] = jnp.concatenate(halves(centred * inv_std), axis=0)
        inv_ref[n] = jnp.broadcast_to(inv_std, inv_ref.shape[1:])
        return carry

    lax.fori_loop(0, normed_ref.shape[0], step, 0, unroll=8)


def pair_units(pair):
    row_count, tok_col, width = pair.shape
    whole = row_count // 2
    chunks, lanes = whole // MANY, MANY * 2 * tok_col
    shapes = [(chunks, 2 * width, lanes), (chunks, 8, lanes)]
    return pl.pallas_call(
        norm_kernel,
        out_shape=[
            jax.ShapeDtypeStruct(shapes[0], jnp.bfloat16),
            jax.ShapeDtypeStruct(shapes[1], jnp.float32),
        ],
        grid=(STEPS,),
        in_specs=[pair_spec(pair)],
        out_specs=[split_spec(shape) for shape in shapes],
        compiler_params=params(56),
        cost_estimate=pl.CostEstimate(
            flops=6_000_000_000, bytes_accessed=12_000_000, transcendentals=0
        ),
        name="pair_units",
    )(pair.reshape(2, whole, tok_col, width))


def shift_of(top):
    return jnp.floor(jnp.clip(14.0 - jnp.log2(top), -100.0, 100.0))


def attention_kernel(col_ref, *refs):
    other_ref, bias_ref, back_ref, grad_bias_ref, sum_ref, tokens_ref = refs[-6:]
    col = col_ref[0]
    for offset, ref in enumerate(refs[:-6]):
        tokens_ref[col ^ (2 * offset)] = ref[0]
        tokens_ref[col ^ (2 * offset + 1)] = other_ref[offset]
    n_col = tokens_ref.shape[0]
    tok_col, row_count = bias_ref.shape[1:]
    half = back_ref.shape[2] // tok_col
    n_row = bias_ref.shape[0] // n_col
    step = pl.program_id(0)

    @pl.when(step == 0)
    def _():
        sum_ref[...] = jnp.zeros_like(sum_ref)

    outs = []
    for sample in range(half):
        lanes = slice(sample * tok_col, (sample + 1) * tok_col)

        def side(slot):
            return jnp.concatenate([tokens_ref[c, slot, :, lanes] for c in range(n_col)], axis=1)

        query_t, key_t, value_t, grad_t = [side(slot) for slot in range(4)]
        key = key_t.T
        value = value_t.T
        attended_parts, grad_query_parts = [], []
        grad_key = jnp.zeros(key_t.shape, jnp.float32)
        grad_value = jnp.zeros(key_t.shape, jnp.float32)
        for block in range(n_row):
            cols = slice(block * row_count, (block + 1) * row_count)
            heads = slice(block * n_col, (block + 1) * n_col)
            bias = bias_ref[heads].reshape(n_col * tok_col, row_count)
            query_b = query_t[:, cols]
            grad_b = grad_t[:, cols]
            scores = matmul(key, query_b) * SCALE + bias
            scores = jnp.where(bias < -60000.0, -1000000000.0, scores)
            expo = jnp.exp(scores - jnp.max(scores, axis=0, keepdims=True))
            share = 1.0 / jnp.sum(expo, axis=0, keepdims=True)
            attended = matmul(value_t, expo.astype(jnp.bfloat16)) * share
            delta = jnp.sum(grad_b.astype(jnp.float32) * attended, axis=0, keepdims=True)
            probs = expo * share
            grad_scores = probs * (matmul(value, grad_b) - delta)
            rounded = grad_scores.astype(jnp.bfloat16)
            attended_parts.append(attended)
            grad_query_parts.append(matmul(key_t, rounded) * SCALE)
            grad_key = grad_key + matmul_nt(query_b, rounded)
            grad_value = grad_value + matmul_nt(grad_b, probs.astype(jnp.bfloat16))
            sum_ref[heads] += grad_scores.reshape(n_col, tok_col, row_count)
        outs.append(
            (
                jnp.concatenate(grad_query_parts, axis=1),
                grad_key * SCALE,
                grad_value,
                jnp.concatenate(attended_parts, axis=1),
            )
        )
    spare = jnp.zeros((8 - 4, half * tok_col), jnp.float32)
    tops = [jnp.max(jnp.abs(out[slot]), axis=0, keepdims=True) for slot in range(4) for out in outs]
    shifts = shift_of(jnp.concatenate(tops, axis=0))
    scales = jnp.exp2(shifts)
    scaled = [
        [out[slot] * scales[slot * half + n : slot * half + n + 1] for n, out in enumerate(outs)]
        for slot in range(4)
    ]
    for c in range(n_col):
        lanes = slice(c * tok_col, (c + 1) * tok_col)
        for slot in range(4):
            back_ref[c, slot * CH : (slot + 1) * CH, :] = jnp.concatenate(
                [part[:, lanes] for part in scaled[slot]], axis=1
            )
        tails = [
            jnp.concatenate([shifts[slot * half + n :, lanes][:1] for n in range(half)], axis=1)
            for slot in range(4)
        ]
        back_ref[c, 4 * CH :, :] = jnp.concatenate(tails + [spare], axis=0)

    @pl.when(step == pl.num_programs(0) - 1)
    def _():
        whole = row_count // 2
        for head in range(n_row * n_col):
            sums = sum_ref[head]
            sums = jnp.concatenate([sums[:, :whole], sums[:, whole:]], axis=0).T
            shift = shift_of(jnp.max(jnp.abs(sums), axis=0, keepdims=True))
            grad_bias_ref[head, :whole, :] = sums * jnp.exp2(shift)
            grad_bias_ref[head, whole:, :] = jnp.broadcast_to(shift, (8, 2 * tok_col))


def attention(col, arrived, other, bias, n_row):
    count = len(arrived)
    n_col = 2 * count
    _, tok_col, row_count = bias.shape
    half = arrived[0].shape[-1] // tok_col // n_row
    width = half * tok_col
    back_shape = (n_row * n_col, 4 * CH + 8, width)
    bias_shape = (n_row * n_col, row_count // 2 + 8, 2 * tok_col)
    return pl.pallas_call(
        attention_kernel,
        out_shape=[
            jax.ShapeDtypeStruct(back_shape, jnp.float32),
            jax.ShapeDtypeStruct(bias_shape, jnp.float32),
        ],
        grid_spec=pltpu.PrefetchScalarGridSpec(
            num_scalar_prefetch=1,
            grid=(n_row,),
            in_specs=[pl.BlockSpec((1, 4, CH, width), lambda i, r: (0, 0, 0, i))] * count
            + [
                pl.BlockSpec((count, 4, CH, width), lambda i, r: (0, 0, 0, i)),
                pl.BlockSpec(bias.shape, lambda i, r: (0, 0, 0)),
            ],
            out_specs=[
                pl.BlockSpec((n_col, 4 * CH + 8, width), lambda i, r: (i, 0, 0)),
                pl.BlockSpec(bias_shape, lambda i, r: (0, 0, 0)),
            ],
            scratch_shapes=[
                pltpu.VMEM(bias.shape, jnp.float32),
                pltpu.VMEM((n_col, 4, CH, width), jnp.bfloat16),
            ],
        ),
        compiler_params=params(24),
        cost_estimate=pl.CostEstimate(
            flops=8_000_000_000, bytes_accessed=6_000_000, transcendentals=1_000_000
        ),
        name="attention",
    )(col, *arrived, other, bias)


def back_kernel(*refs):
    slope_ref, normed_ref, inv_ref, wq_ref, wk_ref, wv_ref, wg_ref = refs[-11:-4]
    out_ref, parts_ref, gate_ref, total_ref = refs[-4:]
    back_ref = refs[0]
    count = normed_ref.shape[-1]
    step = pl.program_id(0)
    rows = wq_ref.shape[0]

    @pl.when(step == 0)
    def _():
        for slot in range(4):
            scale = jnp.exp2(-back_ref[:, 4 * CH + slot : 4 * CH + slot + 1, :])
            values = back_ref[:, slot * CH : (slot + 1) * CH, :] * scale
            values = values.reshape(gate_ref.shape)
            if slot < 3:
                parts_ref[slot] = jnp.concatenate(halves(values), axis=1)
            else:
                gate_ref[...] = (values * slope_ref[...]).astype(jnp.bfloat16)

    total = matmul(wg_ref[...], gate_ref[...])
    for slot, ref in enumerate((wq_ref, wk_ref, wv_ref)):
        parts = matmul(ref[...], parts_ref[slot])
        total = total + (parts[:, :count] + parts[:, count:])
    total_ref[pl.ds(pl.multiple_of(step * rows, 8), rows), :] = total

    @pl.when(step == pl.num_programs(0) - 1)
    def _():
        whole = total_ref[...]
        normed = normed_ref[...]
        result = inv_ref[:1] * (
            whole
            - jnp.mean(whole, axis=0, keepdims=True)
            - normed * jnp.mean(whole * normed, axis=0, keepdims=True)
        )
        out_ref[...] = result.T.astype(jnp.bfloat16)


def token_back(back, slope, normed, inv_std, weights):
    count = normed.shape[-1]
    steps = 2
    whole = lambda shape: pl.BlockSpec(shape, lambda i: (0,) * len(shape))
    weight_spec = pl.BlockSpec((D // steps, D), lambda i: (i, 0))
    return pl.pallas_call(
        back_kernel,
        out_shape=jax.ShapeDtypeStruct((count, D), jnp.bfloat16),
        grid=(steps,),
        in_specs=[whole(array.shape) for array in (back, slope, normed, inv_std)]
        + [weight_spec] * 4,
        out_specs=whole((count, D)),
        scratch_shapes=[
            pltpu.VMEM((3, D, 2 * count), jnp.bfloat16),
            pltpu.VMEM((D, count), jnp.bfloat16),
            pltpu.VMEM((D, count), jnp.float32),
        ],
        compiler_params=params(40),
        cost_estimate=pl.CostEstimate(
            flops=4_000_000_000, bytes_accessed=8_000_000, transcendentals=0
        ),
        name="token_back",
    )(back, slope, normed, inv_std, *weights)


def flat_columns(flat_ref, k, many):
    whole = flat_ref.shape[0] // H
    grads = [flat_ref[pl.ds(k + m, H, stride=whole), :] for m in range(many)]
    return jnp.concatenate(halves(jnp.concatenate(grads, axis=1)), axis=0)


def pair_weight_kernel(normed_ref, grads_ref, part_ref):
    chunks, width, _ = normed_ref.shape
    base = pl.program_id(0) * chunks

    @pl.when(pl.program_id(0) == 0)
    def _():
        part_ref[...] = jnp.zeros_like(part_ref)

    def step(n, carry):
        return carry + matmul_nt(normed_ref[n], flat_columns(grads_ref, (base + n) * MANY, MANY))

    parts = lax.fori_loop(0, chunks, step, jnp.zeros((width, 2 * H), jnp.float32), unroll=8)
    parts = parts[:, :H] + parts[:, H:]
    part_ref[...] += (parts[: width // 2] + parts[width // 2 :]).T


def pair_back_kernel(factor, normed_ref, inv_ref, grads_ref, weight_ref, out_ref):
    _, count, length, width = out_ref.shape
    weight = weight_ref[...].astype(jnp.float32)
    weight = halves(weight - jnp.mean(weight, axis=1, keepdims=True))
    weight = jnp.concatenate([weight[0], weight[0], weight[1], weight[1]], axis=0).T
    base = pl.program_id(0) * count

    def step(n, carry):
        k = n * MANY
        normed = normed_ref[n].astype(jnp.float32)
        normed = normed[:width] + normed[width:]
        grads = flat_columns(grads_ref, base + k, MANY)
        grad_in = matmul(weight, jnp.concatenate([grads, grads], axis=0))
        overlap = jnp.mean(grad_in * normed, axis=0, keepdims=True)
        result = (grad_in - normed * overlap) * (inv_ref[n, :1] * factor)
        result = result.astype(jnp.bfloat16).T.reshape(MANY, 2 * length, width)
        for p in range(2):
            out_ref[p, pl.ds(k, MANY)] = result[:, p * length : (p + 1) * length]
        return carry

    lax.fori_loop(0, count // MANY, step, 0, unroll=8)


def pair_weight(normed, grads):
    part_shape = (H, normed.shape[1] // 2)
    return pl.pallas_call(
        pair_weight_kernel,
        out_shape=jax.ShapeDtypeStruct(part_shape, jnp.float32),
        grid=(STEPS,),
        in_specs=[split_spec(normed.shape), whole_spec(grads.shape)],
        out_specs=whole_spec(part_shape),
        compiler_params=params(24),
        cost_estimate=pl.CostEstimate(
            flops=1_000_000, bytes_accessed=100_000, transcendentals=0
        ),
        name="pair_weight",
    )(normed, grads)


def pair_backward(shape, normed, inv_std, grads, weight_t, factor):
    row_count, tok_col, width = shape
    whole = row_count // 2
    pair_grad = pl.pallas_call(
        lambda *refs: pair_back_kernel(factor, *refs),
        out_shape=jax.ShapeDtypeStruct((2, whole, tok_col, width), jnp.bfloat16),
        grid=(STEPS,),
        in_specs=[
            split_spec(normed.shape),
            split_spec(inv_std.shape),
            whole_spec(grads.shape),
            whole_spec(weight_t.shape),
        ],
        out_specs=pl.BlockSpec((2, whole // STEPS, tok_col, width), lambda i: (0, i, 0, 0)),
        compiler_params=params(24),
        cost_estimate=pl.CostEstimate(
            flops=1_000_000, bytes_accessed=100_000, transcendentals=0
        ),
        name="pair_backward",
    )(normed, inv_std, grads, weight_t)
    return pair_grad.reshape(shape)


def unscaled(block, rows):
    block = block.astype(jnp.float32)
    block = block[:, :rows] * jnp.exp2(-block[:, rows : rows + 1])
    return block.reshape(-1, block.shape[2])


def swap(block, axis):
    return lax.ppermute(block, axis, [(0, 1), (1, 0)])


def body_heads(
    tokens, restype, type_table, key_mask, pair, w_bias, w_query, w_key, w_value, w_gate, cotangent
):
    n_row = lax.axis_size("row")
    n_col = lax.axis_size("col")
    n_samp = lax.axis_size("samp")
    samp_dev = tokens.shape[0]
    tok_col = tokens.shape[1]
    row_count = pair.shape[0]
    total_tokens = tok_col * n_col
    half = samp_dev // n_row
    row_index = lax.axis_index("row")
    row = row_index.astype(jnp.int32).reshape(1)
    col = lax.axis_index("col").astype(jnp.int32).reshape(1)
    types = restype.reshape(1, tok_col)
    weight_t = w_bias.T
    weights = (w_query, w_key, w_value, w_gate)
    samples = samp_dev * n_samp

    def send(block, offset):
        return lax.ppermute(block, "col", [(c, c ^ offset) for c in range(n_col)])

    def by_chip(blocks):
        return [blocks[0]] + [send(blocks[n], 2 * n) for n in range(1, n_col // 2)]

    def across(blocks):
        return send(jnp.stack([block[1] for block in blocks]), 1)

    messages = token_messages(
        row, col, tokens, types, type_table, weights, cotangent, n_row, n_col
    )
    arrived = by_chip(messages)
    bias = pair_bias(pair, weight_t, key_mask.reshape(1, tok_col))
    bias, arrived, types = lax.optimization_barrier(
        (bias.astype(jnp.float16), arrived, types)
    )
    own = own_rows(row, tokens, types, type_table, w_gate, cotangent, half)
    bias = lax.all_to_all(bias, ("row", "col"), 0, 0, tiled=True)
    other = across(arrived)
    bias, other, own = lax.optimization_barrier((bias, other, own))

    back, grad_bias = attention(col, arrived, other, bias.astype(jnp.float32), n_row)
    grad_bias = lax.all_to_all(
        grad_bias.astype(jnp.float16), ("row", "col"), 0, 0, tiled=True
    )
    back, late_pair = lax.optimization_barrier((back.astype(jnp.float16), pair))
    pair_normed, pair_inv = pair_units(late_pair)
    back, _, pair_normed = lax.optimization_barrier((back, grad_bias, pair_normed))
    back = lax.all_to_all(back, ("row", "col"), 0, 0, tiled=True)

    other_bias = swap(grad_bias, "samp")
    own_bias = unscaled(grad_bias, row_count // 2)
    part = pair_weight(pair_normed, own_bias)
    samp_part = swap(part, "samp")
    row_part = swap(part, "row")
    both_part = lax.ppermute(part, ("samp", "row"), [(n, 3 - n) for n in range(4)])
    other_bias, part = lax.optimization_barrier((other_bias, part))
    grads = own_bias + unscaled(other_bias, row_count // 2)
    pair_grad = pair_backward(
        pair.shape, pair_normed, pair_inv, grads, weight_t, total_tokens / samples
    )

    pair_grad, back, sums = lax.optimization_barrier(
        (pair_grad, back, (part, samp_part, row_part, both_part))
    )
    part = (sums[0] + sums[1]) + (sums[2] + sums[3])
    sums = (send(part, 1), send(part, 2), send(part, 3))
    token_half = token_back(back.astype(jnp.float32), *own, weights)
    token_half, sums = lax.optimization_barrier((token_half, sums))
    part = ((part + sums[0]) + (sums[1] + sums[2])) / samples
    last = send(part, 4)
    token_half = token_half.reshape(half, tok_col, D)
    other_half = swap(token_half, "row")
    first = row_index == 0
    token_grad = jnp.concatenate(
        [jnp.where(first, token_half, other_half), jnp.where(first, other_half, token_half)],
        axis=0,
    )
    token_grad, last = lax.optimization_barrier((token_grad, last))
    return (token_grad, pair_grad, (part + last).T)


def body(*args):
    n_row = lax.axis_size("row")
    n_col = lax.axis_size("col")
    tokens = args[0]
    pair = args[4]
    fits = n_row == 2 and n_col == 8 and n_row * n_col == H and lax.axis_size("samp") == 2
    square = pair.shape[0] * n_row == pair.shape[1] * n_col
    if fits and square and tokens.shape[0] == 4 and tokens.shape[1] == 64:
        return body_heads(*args)
    return body_any(*args)


def solution(mesh):
    placed = (
        P("samp", "col", None),
        P("col"),
        P(),
        P("col"),
        P("row", "col", None),
        P(),
        P(),
        P(),
        P(),
        P(),
        P("samp", "col", None),
    )
    return jax.shard_map(
        body,
        mesh=mesh,
        in_specs=placed,
        out_specs=(P("samp", "col", None), P("row", "col", None), P()),
        check_vma=False,
    )
```

```python
import math

import jax
import jax.numpy as jnp
from jax import lax
from jax.experimental import pallas as pl
from jax.experimental.pallas import tpu as pltpu
from jax.sharding import PartitionSpec as P

D = 768
H = 16
CH = 48
NTYPE = 32


def broadcast(block, axis, source):
    block = jnp.where(lax.axis_index(axis) == source, block, jnp.zeros_like(block))
    return lax.psum(block, axis)


def token_norm(tokens, restype, type_table):
    onehot = (restype[:, None] == jnp.arange(NTYPE, dtype=jnp.int32)[None, :]).astype(jnp.bfloat16)
    embedded = tokens.astype(jnp.float32) + jnp.dot(
        onehot, type_table, preferred_element_type=jnp.float32
    )
    centred = embedded - jnp.mean(embedded, axis=-1, keepdims=True)
    inv_std = lax.rsqrt(jnp.mean(centred * centred, axis=-1, keepdims=True) + 1e-05)
    return (centred * inv_std, inv_std)


def pair_norm(block):
    values = block.astype(jnp.float32)
    centred = values - jnp.mean(values, axis=-1, keepdims=True)
    inv_std = lax.rsqrt(jnp.mean(centred * centred, axis=-1, keepdims=True) + 1e-05)
    return (centred * inv_std, inv_std)


def norm_back(grad_in, normed, inv_std):
    return inv_std * (
        grad_in
        - jnp.mean(grad_in, axis=-1, keepdims=True)
        - normed * jnp.mean(grad_in * normed, axis=-1, keepdims=True)
    )


def project(rows_in, weight):
    return jnp.einsum("std,de->ste", rows_in, weight, preferred_element_type=jnp.float32).astype(
        jnp.bfloat16
    )


def back_project(grads, weight):
    return jnp.einsum(
        "ste,de->std", grads, weight.astype(jnp.float32), precision=lax.Precision.HIGHEST
    )


def pair_back(grad_bias, pair_normed, pair_inv, bias_weight):
    grad_normed = jnp.einsum("hij,ch->ijc", grad_bias, bias_weight, precision=lax.Precision.HIGHEST)
    return norm_back(grad_normed, pair_normed, pair_inv)


def body_any(
    tokens, restype, type_table, key_mask, pair, w_bias, w_query, w_key, w_value, w_gate, cotangent
):
    n_row = lax.axis_size("row")
    n_col = lax.axis_size("col")
    n_samp = lax.axis_size("samp")
    samp_dev = tokens.shape[0]
    tok_col = tokens.shape[1]
    spread = n_col // n_row
    row_count = tok_col * spread
    total_tokens = tok_col * n_col
    row_index = lax.axis_index("row")
    col_index = lax.axis_index("col")
    is_owner = col_index // spread == row_index
    own_start = col_index % spread * tok_col
    normed, inv_std = token_norm(tokens, restype, type_table)
    own_act = normed.astype(jnp.bfloat16)
    key_proj = project(own_act, w_key)
    value_proj = project(own_act, w_value)
    stacked = jnp.stack([own_act, cotangent])
    pieces = [broadcast(stacked, "col", row_index * spread + member) for member in range(spread)]
    gathered = jnp.concatenate(pieces, axis=2)
    query_side = gathered[0]
    grad_rows = gathered[1]
    queries = project(query_side, w_query)
    gate_lin = project(query_side, w_gate)
    pair_normed, pair_inv = pair_norm(pair)
    bias_weight = w_bias.astype(jnp.float32)
    bias = jnp.einsum("ijc,ch->hij", pair_normed, bias_weight, precision=lax.Precision.HIGHEST)
    query_heads = queries.reshape(samp_dev, row_count, H, CH)
    key_heads = key_proj.reshape(samp_dev, tok_col, H, CH)
    value_heads = value_proj.reshape(samp_dev, tok_col, H, CH)
    scores = (
        jnp.einsum("sihc,sjhc->shij", query_heads, key_heads, preferred_element_type=jnp.float32)
        / math.sqrt(CH)
        + bias[None]
    )
    scores = jnp.where(key_mask[None, None, None, :] == 1, scores, -1000000000.0)
    top = lax.pmax(jnp.max(scores, axis=-1), "col")
    expo = jnp.exp(scores - top[..., None])
    partial_out = jnp.einsum(
        "shij,sjhc->sihc",
        expo.astype(jnp.bfloat16),
        value_heads,
        preferred_element_type=jnp.float32,
    )
    totals, summed = lax.psum(
        (jnp.sum(expo, axis=-1), partial_out.reshape(samp_dev, row_count, D)), "col"
    )
    attended = (
        summed.reshape(samp_dev, row_count, H, CH) / jnp.transpose(totals, (0, 2, 1))[..., None]
    )
    flat_out = attended.reshape(samp_dev, row_count, D)
    sig_gate = jax.nn.sigmoid(gate_lin.astype(jnp.float32))
    grad_f = grad_rows.astype(jnp.float32)
    grad_out = (grad_f * sig_gate).astype(jnp.bfloat16)
    grad_gate = (grad_f * flat_out * sig_gate * (1.0 - sig_gate)).astype(jnp.bfloat16)
    gate_piece = lax.dynamic_slice_in_dim(grad_gate, own_start, tok_col, 1)
    gate_term = jnp.where(
        is_owner,
        jnp.einsum("ste,de->std", gate_piece, w_gate, preferred_element_type=jnp.float32),
        0.0,
    )
    grad_heads = grad_out.reshape(samp_dev, row_count, H, CH)
    delta = jnp.transpose(jnp.sum(grad_heads.astype(jnp.float32) * attended, axis=-1), (0, 2, 1))
    probs = expo / totals[..., None]
    grad_pre = jnp.einsum(
        "sihc,sjhc->shij", grad_heads, value_heads, preferred_element_type=jnp.float32
    )
    grad_scores = probs * (grad_pre - delta[..., None])
    rounded = grad_scores.astype(jnp.bfloat16)
    grad_query = (
        jnp.einsum("shij,sjhc->sihc", rounded, key_heads, preferred_element_type=jnp.float32)
        / math.sqrt(CH)
    ).reshape(samp_dev, row_count, D)
    grad_key = (
        jnp.einsum("shij,sihc->sjhc", rounded, query_heads, preferred_element_type=jnp.float32)
        / math.sqrt(CH)
    ).reshape(samp_dev, tok_col, D)
    grad_value = jnp.einsum(
        "shij,sihc->sjhc",
        probs.astype(jnp.bfloat16),
        grad_heads,
        preferred_element_type=jnp.float32,
    ).reshape(samp_dev, tok_col, D)
    bias_local = jnp.sum(grad_scores, axis=0)
    blank = jnp.zeros((samp_dev, total_tokens, D), jnp.float32)
    mine = lax.psum_scatter(
        lax.dynamic_update_slice_in_dim(blank, grad_query, row_index * row_count, 1),
        "col",
        scatter_dimension=1,
        tiled=True,
    )
    query_all, key_all, value_all, gate_all = lax.psum(
        (mine, grad_key, grad_value, gate_term), "row"
    )
    grad_act = (
        back_project(query_all, w_query)
        + back_project(key_all, w_key)
        + back_project(value_all, w_value)
        + gate_all
    )
    token_grad = norm_back(grad_act, normed, inv_std).astype(jnp.bfloat16)
    samples = samp_dev * n_samp
    grad_bias = lax.psum(bias_local, "samp")
    grad_pair = pair_back(grad_bias, pair_normed, pair_inv, bias_weight)
    pair_grad = (grad_pair * (total_tokens / samples)).astype(jnp.bfloat16)
    weight_part = jnp.einsum("ijc,hij->ch", pair_normed, grad_bias, precision=lax.Precision.HIGHEST)
    weight_sum = lax.psum(weight_part, ("row", "col"))
    bias_weight_grad = weight_sum / samples
    return (token_grad, pair_grad, bias_weight_grad)


EPS = 1e-05
SCALE = 1.0 / math.sqrt(CH)
NT = (((1,), (1,)), ((), ()))
TN = (((0,), (0,)), ((), ()))
MASKED = -65504.0


def params(megabytes):
    return pltpu.CompilerParams(vmem_limit_bytes=megabytes * 1024 * 1024)


def matmul(left, right):
    return jnp.dot(left, right, preferred_element_type=jnp.float32)


def matmul_nt(left, right):
    return lax.dot_general(left, right, NT, preferred_element_type=jnp.float32)


def matmul_tn(left, right):
    return lax.dot_general(left, right, TN, preferred_element_type=jnp.float32)


def halves(values):
    high = values.astype(jnp.bfloat16)
    low = (values - high.astype(jnp.float32)).astype(jnp.bfloat16)
    return high, low


def unit_rows(values):
    centred = values - jnp.mean(values, axis=-1, keepdims=True)
    inv_std = lax.rsqrt(jnp.mean(centred * centred, axis=-1, keepdims=True) + EPS)
    return centred * inv_std, inv_std


def embed_rows(tokens_ref, types_ref, table_ref):
    count, length, width = tokens_ref.shape
    index = lax.broadcasted_iota(jnp.int32, (NTYPE, length), 0)
    onehot = jnp.where(types_ref[...] == index, 1.0, 0.0).astype(jnp.bfloat16)
    added = matmul_tn(onehot, table_ref[...])
    embedded = tokens_ref[...].astype(jnp.float32) + added[None]
    return unit_rows(embedded.reshape(count * length, width))


def token_kernel(row_ref, col_ref, tokens_ref, types_ref, table_ref, *refs):
    wq_ref, wk_ref, wv_ref, wg_ref, cot_ref = refs[:5]
    out_refs, side_ref = refs[5:-1], refs[-1]
    normed, _ = embed_rows(tokens_ref, types_ref, table_ref)
    act = normed.astype(jnp.bfloat16)
    for slot, ref in enumerate((wq_ref, wk_ref, wv_ref)):
        side_ref[slot] = matmul(act, ref[...]).astype(jnp.bfloat16).T
    gate = matmul(act, wg_ref[...]).astype(jnp.bfloat16).astype(jnp.float32)
    cot = cot_ref[...].reshape(gate.shape).astype(jnp.float32)
    side_ref[3] = (cot * jax.nn.sigmoid(gate)).astype(jnp.bfloat16).T
    for offset, out_ref in enumerate(out_refs):
        for core in range(2):
            start = pl.multiple_of((col_ref[0] ^ (2 * offset + core)) * CH, 16)
            out_ref[core] = side_ref[:, pl.ds(start, CH), :]


def token_messages(row, col, tokens, types, table, weights, cotangent, n_row, n_col):
    samp_dev, tok_col, _ = tokens.shape
    width = D // n_row
    held = samp_dev * tok_col
    whole3 = lambda i, r, c: (0, 0, 0)
    whole2 = lambda i, r, c: (0, 0)
    weight_spec = pl.BlockSpec((D, width), lambda i, r, c: (0, r[0]))
    shape = (2, 4, CH, held)
    count = n_col // 2
    return pl.pallas_call(
        token_kernel,
        out_shape=[jax.ShapeDtypeStruct(shape, jnp.bfloat16)] * count,
        grid_spec=pltpu.PrefetchScalarGridSpec(
            num_scalar_prefetch=2,
            grid=(1,),
            in_specs=[
                pl.BlockSpec(tokens.shape, whole3),
                pl.BlockSpec(types.shape, whole2),
                pl.BlockSpec(table.shape, whole2),
                weight_spec,
                weight_spec,
                weight_spec,
                weight_spec,
                pl.BlockSpec((samp_dev, tok_col, width), lambda i, r, c: (0, 0, r[0])),
            ],
            out_specs=[pl.BlockSpec(shape, lambda i, r, c: (0, 0, 0, 0))] * count,
            scratch_shapes=[pltpu.VMEM((4, width, held), jnp.bfloat16)],
        ),
        compiler_params=params(56),
        cost_estimate=pl.CostEstimate(
            flops=4_000_000_000, bytes_accessed=4_000_000, transcendentals=0
        ),
        name="token_messages",
    )(row, col, tokens, types, table, *weights, cotangent)


def own_kernel(
    row_ref, tokens_ref, types_ref, table_ref, wg_ref, cot_ref, slope_ref, normed_ref, inv_ref
):
    normed, inv_std = embed_rows(tokens_ref, types_ref, table_ref)
    gate = matmul(normed.astype(jnp.bfloat16), wg_ref[...]).astype(jnp.bfloat16)
    sig = jax.nn.sigmoid(gate.astype(jnp.float32))
    cot = cot_ref[...].reshape(gate.shape).astype(jnp.float32)
    slope_ref[...] = (cot * sig * (1.0 - sig)).T
    normed_ref[...] = normed.T
    inv_ref[...] = jnp.broadcast_to(inv_std, (inv_std.shape[0], 128)).T[:8]


def own_rows(row, tokens, types, table, w_gate, cotangent, half):
    _, tok_col, _ = tokens.shape
    count = half * tok_col
    part_spec = pl.BlockSpec((half, tok_col, D), lambda i, r: (r[0], 0, 0))
    whole2 = lambda i, r: (0, 0)
    return pl.pallas_call(
        own_kernel,
        out_shape=[
            jax.ShapeDtypeStruct((D, count), jnp.float32),
            jax.ShapeDtypeStruct((D, count), jnp.float32),
            jax.ShapeDtypeStruct((8, count), jnp.float32),
        ],
        grid_spec=pltpu.PrefetchScalarGridSpec(
            num_scalar_prefetch=1,
            grid=(1,),
            in_specs=[
                part_spec,
                pl.BlockSpec(types.shape, whole2),
                pl.BlockSpec(table.shape, whole2),
                pl.BlockSpec(w_gate.shape, whole2),
                part_spec,
            ],
            out_specs=[
                pl.BlockSpec((D, count), whole2),
                pl.BlockSpec((D, count), whole2),
                pl.BlockSpec((8, count), whole2),
            ],
        ),
        compiler_params=params(56),
        cost_estimate=pl.CostEstimate(
            flops=3_000_000_000, bytes_accessed=3_000_000, transcendentals=0
        ),
        name="own_rows",
    )(row, tokens, types, table, w_gate, cotangent)


MANY = 4


def pair_columns(pair_ref, k, many):
    _, _, length, width = pair_ref.shape
    blocks = [pair_ref[p, pl.ds(k, many)] for p in range(2)]
    rows = jnp.concatenate(blocks, axis=1).reshape(many * 2 * length, width)
    same = lax.broadcasted_iota(jnp.int32, (width, width), 0) == lax.broadcasted_iota(
        jnp.int32, (width, width), 1
    )
    centring = (jnp.where(same, 1.0, 0.0) - 1.0 / width).astype(jnp.bfloat16)
    centred = matmul_nt(centring, rows)
    return centred, lax.rsqrt(jnp.mean(centred * centred, axis=0, keepdims=True) + EPS)


def bias_kernel(pair_ref, weight_ref, mask_ref, out_ref, flat_ref):
    _, count, length, width = pair_ref.shape
    whole = flat_ref.shape[0] // H
    weight = jnp.concatenate([weight_ref[...]] * 2, axis=1)
    base = pl.program_id(0) * count

    def step(n, carry):
        k = n * MANY
        centred, inv_std = pair_columns(pair_ref, k, MANY)
        bias = matmul(weight, jnp.concatenate(halves(centred), axis=0)) * inv_std
        for m in range(MANY):
            lanes = slice(m * 2 * length, (m + 1) * 2 * length)
            flat_ref[pl.ds(base + k + m, H, stride=whole), :] = bias[:, lanes]
        return carry

    lax.fori_loop(0, count // MANY, step, 0, unroll=8)

    @pl.when(pl.program_id(0) == pl.num_programs(0) - 1)
    def _():
        keep = jnp.broadcast_to(mask_ref[...].astype(jnp.float32), (128, length)).T
        keep = jnp.concatenate([keep] * (2 * whole // 128), axis=1) == 1.0
        for h in range(H):
            turned = flat_ref[h * whole : (h + 1) * whole, :].T
            bias = jnp.concatenate([turned[:length], turned[length:]], axis=1)
            out_ref[h] = jnp.where(keep, bias, MASKED)


STEPS = 4


def split_spec(shape):
    block = (shape[0] // STEPS,) + tuple(shape[1:])
    return pl.BlockSpec(block, lambda i: (i,) + (0,) * (len(shape) - 1))


def whole_spec(shape):
    return pl.BlockSpec(tuple(shape), lambda i: (0,) * len(shape))


def pair_spec(pair):
    row_count, tok_col, width = pair.shape
    block = (2, row_count // 2 // STEPS, tok_col, width)
    return pl.BlockSpec(block, lambda i: (0, i, 0, 0))


def pair_bias(pair, weight_t, mask):
    row_count, tok_col, width = pair.shape
    whole = row_count // 2
    return pl.pallas_call(
        bias_kernel,
        out_shape=jax.ShapeDtypeStruct((H, tok_col, row_count), jnp.float32),
        grid=(STEPS,),
        in_specs=[pair_spec(pair), whole_spec(weight_t.shape), whole_spec(mask.shape)],
        out_specs=whole_spec((H, tok_col, row_count)),
        scratch_shapes=[pltpu.VMEM((H * whole, 2 * tok_col), jnp.float32)],
        compiler_params=params(24),
        cost_estimate=pl.CostEstimate(
            flops=6_000_000_000, bytes_accessed=5_000_000, transcendentals=0
        ),
        name="pair_bias",
    )(pair.reshape(2, whole, tok_col, width), weight_t, mask)


def norm_kernel(pair_ref, normed_ref, inv_ref):
    def step(n, carry):
        centred, inv_std = pair_columns(pair_ref, n * MANY, MANY)
        normed_ref[n] = jnp.concatenate(halves(centred * inv_std), axis=0)
        inv_ref[n] = jnp.broadcast_to(inv_std, inv_ref.shape[1:])
        return carry

    lax.fori_loop(0, normed_ref.shape[0], step, 0, unroll=8)


def pair_units(pair):
    row_count, tok_col, width = pair.shape
    whole = row_count // 2
    chunks, lanes = whole // MANY, MANY * 2 * tok_col
    shapes = [(chunks, 2 * width, lanes), (chunks, 8, lanes)]
    return pl.pallas_call(
        norm_kernel,
        out_shape=[
            jax.ShapeDtypeStruct(shapes[0], jnp.bfloat16),
            jax.ShapeDtypeStruct(shapes[1], jnp.float32),
        ],
        grid=(STEPS,),
        in_specs=[pair_spec(pair)],
        out_specs=[split_spec(shape) for shape in shapes],
        compiler_params=params(56),
        cost_estimate=pl.CostEstimate(
            flops=6_000_000_000, bytes_accessed=12_000_000, transcendentals=0
        ),
        name="pair_units",
    )(pair.reshape(2, whole, tok_col, width))


def shift_of(top):
    return jnp.floor(jnp.clip(14.0 - jnp.log2(top), -100.0, 100.0))


def attention_kernel(col_ref, *refs):
    other_ref, bias_ref, back_ref, grad_bias_ref, sum_ref, tokens_ref = refs[-6:]
    col = col_ref[0]
    for offset, ref in enumerate(refs[:-6]):
        tokens_ref[col ^ (2 * offset)] = ref[0]
        tokens_ref[col ^ (2 * offset + 1)] = other_ref[offset]
    n_col = tokens_ref.shape[0]
    tok_col, row_count = bias_ref.shape[1:]
    half = back_ref.shape[2] // tok_col
    n_row = bias_ref.shape[0] // n_col
    step = pl.program_id(0)

    @pl.when(step == 0)
    def _():
        sum_ref[...] = jnp.zeros_like(sum_ref)

    outs = []
    for sample in range(half):
        lanes = slice(sample * tok_col, (sample + 1) * tok_col)

        def side(slot):
            return jnp.concatenate([tokens_ref[c, slot, :, lanes] for c in range(n_col)], axis=1)

        query_t, key_t, value_t, grad_t = [side(slot) for slot in range(4)]
        key = key_t.T
        value = value_t.T
        attended_parts, grad_query_parts = [], []
        grad_key = jnp.zeros(key_t.shape, jnp.float32)
        grad_value = jnp.zeros(key_t.shape, jnp.float32)
        for block in range(n_row):
            cols = slice(block * row_count, (block + 1) * row_count)
            heads = slice(block * n_col, (block + 1) * n_col)
            bias = bias_ref[heads].reshape(n_col * tok_col, row_count)
            query_b = query_t[:, cols]
            grad_b = grad_t[:, cols]
            scores = matmul(key, query_b) * SCALE + bias
            scores = jnp.where(bias < -60000.0, -1000000000.0, scores)
            expo = jnp.exp(scores - jnp.max(scores, axis=0, keepdims=True))
            share = 1.0 / jnp.sum(expo, axis=0, keepdims=True)
            attended = matmul(value_t, expo.astype(jnp.bfloat16)) * share
            delta = jnp.sum(grad_b.astype(jnp.float32) * attended, axis=0, keepdims=True)
            probs = expo * share
            grad_scores = probs * (matmul(value, grad_b) - delta)
            rounded = grad_scores.astype(jnp.bfloat16)
            attended_parts.append(attended)
            grad_query_parts.append(matmul(key_t, rounded) * SCALE)
            grad_key = grad_key + matmul_nt(query_b, rounded)
            grad_value = grad_value + matmul_nt(grad_b, probs.astype(jnp.bfloat16))
            sum_ref[heads] += grad_scores.reshape(n_col, tok_col, row_count)
        outs.append(
            (
                jnp.concatenate(grad_query_parts, axis=1),
                grad_key * SCALE,
                grad_value,
                jnp.concatenate(attended_parts, axis=1),
            )
        )
    spare = jnp.zeros((8 - 4, half * tok_col), jnp.float32)
    tops = [jnp.max(jnp.abs(out[slot]), axis=0, keepdims=True) for slot in range(4) for out in outs]
    shifts = shift_of(jnp.concatenate(tops, axis=0))
    scales = jnp.exp2(shifts)
    scaled = [
        [out[slot] * scales[slot * half + n : slot * half + n + 1] for n, out in enumerate(outs)]
        for slot in range(4)
    ]
    for c in range(n_col):
        lanes = slice(c * tok_col, (c + 1) * tok_col)
        for slot in range(4):
            back_ref[c, slot * CH : (slot + 1) * CH, :] = jnp.concatenate(
                [part[:, lanes] for part in scaled[slot]], axis=1
            )
        tails = [
            jnp.concatenate([shifts[slot * half + n :, lanes][:1] for n in range(half)], axis=1)
            for slot in range(4)
        ]
        back_ref[c, 4 * CH :, :] = jnp.concatenate(tails + [spare], axis=0)

    @pl.when(step == pl.num_programs(0) - 1)
    def _():
        whole = row_count // 2
        for head in range(n_row * n_col):
            sums = sum_ref[head]
            sums = jnp.concatenate([sums[:, :whole], sums[:, whole:]], axis=0).T
            shift = shift_of(jnp.max(jnp.abs(sums), axis=0, keepdims=True))
            grad_bias_ref[head, :whole, :] = sums * jnp.exp2(shift)
            grad_bias_ref[head, whole:, :] = jnp.broadcast_to(shift, (8, 2 * tok_col))


def attention(col, arrived, other, bias, n_row):
    count = len(arrived)
    n_col = 2 * count
    _, tok_col, row_count = bias.shape
    half = arrived[0].shape[-1] // tok_col // n_row
    width = half * tok_col
    back_shape = (n_row * n_col, 4 * CH + 8, width)
    bias_shape = (n_row * n_col, row_count // 2 + 8, 2 * tok_col)
    return pl.pallas_call(
        attention_kernel,
        out_shape=[
            jax.ShapeDtypeStruct(back_shape, jnp.float32),
            jax.ShapeDtypeStruct(bias_shape, jnp.float32),
        ],
        grid_spec=pltpu.PrefetchScalarGridSpec(
            num_scalar_prefetch=1,
            grid=(n_row,),
            in_specs=[pl.BlockSpec((1, 4, CH, width), lambda i, r: (0, 0, 0, i))] * count
            + [
                pl.BlockSpec((count, 4, CH, width), lambda i, r: (0, 0, 0, i)),
                pl.BlockSpec(bias.shape, lambda i, r: (0, 0, 0)),
            ],
            out_specs=[
                pl.BlockSpec((n_col, 4 * CH + 8, width), lambda i, r: (i, 0, 0)),
                pl.BlockSpec(bias_shape, lambda i, r: (0, 0, 0)),
            ],
            scratch_shapes=[
                pltpu.VMEM(bias.shape, jnp.float32),
                pltpu.VMEM((n_col, 4, CH, width), jnp.bfloat16),
            ],
        ),
        compiler_params=params(24),
        cost_estimate=pl.CostEstimate(
            flops=8_000_000_000, bytes_accessed=6_000_000, transcendentals=1_000_000
        ),
        name="attention",
    )(col, *arrived, other, bias)


def back_kernel(*refs):
    slope_ref, normed_ref, inv_ref, wq_ref, wk_ref, wv_ref, wg_ref = refs[-11:-4]
    out_ref, parts_ref, gate_ref, total_ref = refs[-4:]
    back_ref = refs[0]
    count = normed_ref.shape[-1]
    step = pl.program_id(0)
    rows = wq_ref.shape[0]

    @pl.when(step == 0)
    def _():
        for slot in range(4):
            scale = jnp.exp2(-back_ref[:, 4 * CH + slot : 4 * CH + slot + 1, :])
            values = back_ref[:, slot * CH : (slot + 1) * CH, :] * scale
            values = values.reshape(gate_ref.shape)
            if slot < 3:
                parts_ref[slot] = jnp.concatenate(halves(values), axis=1)
            else:
                gate_ref[...] = (values * slope_ref[...]).astype(jnp.bfloat16)

    total = matmul(wg_ref[...], gate_ref[...])
    for slot, ref in enumerate((wq_ref, wk_ref, wv_ref)):
        parts = matmul(ref[...], parts_ref[slot])
        total = total + (parts[:, :count] + parts[:, count:])
    total_ref[pl.ds(pl.multiple_of(step * rows, 8), rows), :] = total

    @pl.when(step == pl.num_programs(0) - 1)
    def _():
        whole = total_ref[...]
        normed = normed_ref[...]
        result = inv_ref[:1] * (
            whole
            - jnp.mean(whole, axis=0, keepdims=True)
            - normed * jnp.mean(whole * normed, axis=0, keepdims=True)
        )
        out_ref[...] = result.T.astype(jnp.bfloat16)


def token_back(back, slope, normed, inv_std, weights):
    count = normed.shape[-1]
    steps = 2
    whole = lambda shape: pl.BlockSpec(shape, lambda i: (0,) * len(shape))
    weight_spec = pl.BlockSpec((D // steps, D), lambda i: (i, 0))
    return pl.pallas_call(
        back_kernel,
        out_shape=jax.ShapeDtypeStruct((count, D), jnp.bfloat16),
        grid=(steps,),
        in_specs=[whole(array.shape) for array in (back, slope, normed, inv_std)]
        + [weight_spec] * 4,
        out_specs=whole((count, D)),
        scratch_shapes=[
            pltpu.VMEM((3, D, 2 * count), jnp.bfloat16),
            pltpu.VMEM((D, count), jnp.bfloat16),
            pltpu.VMEM((D, count), jnp.float32),
        ],
        compiler_params=params(40),
        cost_estimate=pl.CostEstimate(
            flops=4_000_000_000, bytes_accessed=8_000_000, transcendentals=0
        ),
        name="token_back",
    )(back, slope, normed, inv_std, *weights)


def flat_columns(flat_ref, k, many):
    whole = flat_ref.shape[0] // H
    grads = [flat_ref[pl.ds(k + m, H, stride=whole), :] for m in range(many)]
    return jnp.concatenate(halves(jnp.concatenate(grads, axis=1)), axis=0)


def pair_weight_kernel(normed_ref, grads_ref, part_ref):
    chunks, width, _ = normed_ref.shape
    base = pl.program_id(0) * chunks

    @pl.when(pl.program_id(0) == 0)
    def _():
        part_ref[...] = jnp.zeros_like(part_ref)

    def step(n, carry):
        return carry + matmul_nt(normed_ref[n], flat_columns(grads_ref, (base + n) * MANY, MANY))

    parts = lax.fori_loop(0, chunks, step, jnp.zeros((width, 2 * H), jnp.float32), unroll=8)
    parts = parts[:, :H] + parts[:, H:]
    part_ref[...] += (parts[: width // 2] + parts[width // 2 :]).T


def pair_back_kernel(factor, normed_ref, inv_ref, grads_ref, weight_ref, out_ref):
    _, count, length, width = out_ref.shape
    weight = weight_ref[...].astype(jnp.float32)
    weight = halves(weight - jnp.mean(weight, axis=1, keepdims=True))
    weight = jnp.concatenate([weight[0], weight[0], weight[1], weight[1]], axis=0).T
    base = pl.program_id(0) * count

    def step(n, carry):
        k = n * MANY
        normed = normed_ref[n].astype(jnp.float32)
        normed = normed[:width] + normed[width:]
        grads = flat_columns(grads_ref, base + k, MANY)
        grad_in = matmul(weight, jnp.concatenate([grads, grads], axis=0))
        overlap = jnp.mean(grad_in * normed, axis=0, keepdims=True)
        result = (grad_in - normed * overlap) * (inv_ref[n, :1] * factor)
        result = result.astype(jnp.bfloat16).T.reshape(MANY, 2 * length, width)
        for p in range(2):
            out_ref[p, pl.ds(k, MANY)] = result[:, p * length : (p + 1) * length]
        return carry

    lax.fori_loop(0, count // MANY, step, 0, unroll=8)


def pair_weight(normed, grads):
    part_shape = (H, normed.shape[1] // 2)
    return pl.pallas_call(
        pair_weight_kernel,
        out_shape=jax.ShapeDtypeStruct(part_shape, jnp.float32),
        grid=(STEPS,),
        in_specs=[split_spec(normed.shape), whole_spec(grads.shape)],
        out_specs=whole_spec(part_shape),
        compiler_params=params(24),
        cost_estimate=pl.CostEstimate(
            flops=1_000_000, bytes_accessed=100_000, transcendentals=0
        ),
        name="pair_weight",
    )(normed, grads)


def pair_backward(shape, normed, inv_std, grads, weight_t, factor):
    row_count, tok_col, width = shape
    whole = row_count // 2
    pair_grad = pl.pallas_call(
        lambda *refs: pair_back_kernel(factor, *refs),
        out_shape=jax.ShapeDtypeStruct((2, whole, tok_col, width), jnp.bfloat16),
        grid=(STEPS,),
        in_specs=[
            split_spec(normed.shape),
            split_spec(inv_std.shape),
            whole_spec(grads.shape),
            whole_spec(weight_t.shape),
        ],
        out_specs=pl.BlockSpec((2, whole // STEPS, tok_col, width), lambda i: (0, i, 0, 0)),
        compiler_params=params(24),
        cost_estimate=pl.CostEstimate(
            flops=1_000_000, bytes_accessed=100_000, transcendentals=0
        ),
        name="pair_backward",
    )(normed, inv_std, grads, weight_t)
    return pair_grad.reshape(shape)


def unscaled(block, rows):
    block = block.astype(jnp.float32)
    block = block[:, :rows] * jnp.exp2(-block[:, rows : rows + 1])
    return block.reshape(-1, block.shape[2])


def swap(block, axis):
    return lax.ppermute(block, axis, [(0, 1), (1, 0)])


def body_heads(
    tokens, restype, type_table, key_mask, pair, w_bias, w_query, w_key, w_value, w_gate, cotangent
):
    n_row = lax.axis_size("row")
    n_col = lax.axis_size("col")
    n_samp = lax.axis_size("samp")
    samp_dev = tokens.shape[0]
    tok_col = tokens.shape[1]
    row_count = pair.shape[0]
    total_tokens = tok_col * n_col
    half = samp_dev // n_row
    row_index = lax.axis_index("row")
    row = row_index.astype(jnp.int32).reshape(1)
    col = lax.axis_index("col").astype(jnp.int32).reshape(1)
    types = restype.reshape(1, tok_col)
    weight_t = w_bias.T
    weights = (w_query, w_key, w_value, w_gate)
    samples = samp_dev * n_samp

    def send(block, offset):
        return lax.ppermute(block, "col", [(c, c ^ offset) for c in range(n_col)])

    def by_chip(blocks):
        return [blocks[0]] + [send(blocks[n], 2 * n) for n in range(1, n_col // 2)]

    def across(blocks):
        return send(jnp.stack([block[1] for block in blocks]), 1)

    messages = token_messages(
        row, col, tokens, types, type_table, weights, cotangent, n_row, n_col
    )
    arrived = by_chip(messages)
    bias = pair_bias(pair, weight_t, key_mask.reshape(1, tok_col))
    bias, arrived, types = lax.optimization_barrier(
        (bias.astype(jnp.float16), arrived, types)
    )
    own = own_rows(row, tokens, types, type_table, w_gate, cotangent, half)
    bias = lax.all_to_all(bias, ("row", "col"), 0, 0, tiled=True)
    other = across(arrived)
    bias, other, own = lax.optimization_barrier((bias, other, own))

    back, grad_bias = attention(col, arrived, other, bias.astype(jnp.float32), n_row)
    grad_bias = lax.all_to_all(
        grad_bias.astype(jnp.float16), ("row", "col"), 0, 0, tiled=True
    )
    back, late_pair = lax.optimization_barrier((back.astype(jnp.float16), pair))
    pair_normed, pair_inv = pair_units(late_pair)
    back, grad_bias, pair_normed = lax.optimization_barrier((back, grad_bias, pair_normed))
    back = lax.all_to_all(back, ("row", "col"), 0, 0, tiled=True)

    other_bias = swap(grad_bias, "samp")
    own_bias = unscaled(grad_bias, row_count // 2)
    part = pair_weight(pair_normed, own_bias)
    samp_part = swap(part, "samp")
    row_part = swap(part, "row")
    both_part = lax.ppermute(part, ("samp", "row"), [(n, 3 - n) for n in range(4)])
    other_bias, part = lax.optimization_barrier((other_bias, part))
    grads = own_bias + unscaled(other_bias, row_count // 2)
    pair_grad = pair_backward(
        pair.shape, pair_normed, pair_inv, grads, weight_t, total_tokens / samples
    )

    pair_grad, back, sums = lax.optimization_barrier(
        (pair_grad, back, (part, samp_part, row_part, both_part))
    )
    part = (sums[0] + sums[1]) + (sums[2] + sums[3])
    sums = (send(part, 1), send(part, 2), send(part, 3))
    token_half = token_back(back.astype(jnp.float32), *own, weights)
    token_half, sums = lax.optimization_barrier((token_half, sums))
    part = ((part + sums[0]) + (sums[1] + sums[2])) / samples
    last = send(part, 4)
    token_half = token_half.reshape(half, tok_col, D)
    other_half = swap(token_half, "row")
    first = row_index == 0
    token_grad = jnp.concatenate(
        [jnp.where(first, token_half, other_half), jnp.where(first, other_half, token_half)],
        axis=0,
    )
    token_grad, last = lax.optimization_barrier((token_grad, last))
    return (token_grad, pair_grad, (part + last).T)


def body(*args):
    n_row = lax.axis_size("row")
    n_col = lax.axis_size("col")
    tokens = args[0]
    pair = args[4]
    fits = n_row == 2 and n_col == 8 and n_row * n_col == H and lax.axis_size("samp") == 2
    square = pair.shape[0] * n_row == pair.shape[1] * n_col
    if fits and square and tokens.shape[0] == 4 and tokens.shape[1] == 64:
        return body_heads(*args)
    return body_any(*args)


def solution(mesh):
    placed = (
        P("samp", "col", None),
        P("col"),
        P(),
        P("col"),
        P("row", "col", None),
        P(),
        P(),
        P(),
        P(),
        P(),
        P("samp", "col", None),
    )
    return jax.shard_map(
        body,
        mesh=mesh,
        in_specs=placed,
        out_specs=(P("samp", "col", None), P("row", "col", None), P()),
        check_vma=False,
    )
```

```python
import math

import jax
import jax.numpy as jnp
from jax import lax
from jax.experimental import pallas as pl
from jax.experimental.pallas import tpu as pltpu
from jax.sharding import PartitionSpec as P

D = 768
H = 16
CH = 48
NTYPE = 32


def broadcast(block, axis, source):
    block = jnp.where(lax.axis_index(axis) == source, block, jnp.zeros_like(block))
    return lax.psum(block, axis)


def token_norm(tokens, restype, type_table):
    onehot = (restype[:, None] == jnp.arange(NTYPE, dtype=jnp.int32)[None, :]).astype(jnp.bfloat16)
    embedded = tokens.astype(jnp.float32) + jnp.dot(
        onehot, type_table, preferred_element_type=jnp.float32
    )
    centred = embedded - jnp.mean(embedded, axis=-1, keepdims=True)
    inv_std = lax.rsqrt(jnp.mean(centred * centred, axis=-1, keepdims=True) + 1e-05)
    return (centred * inv_std, inv_std)


def pair_norm(block):
    values = block.astype(jnp.float32)
    centred = values - jnp.mean(values, axis=-1, keepdims=True)
    inv_std = lax.rsqrt(jnp.mean(centred * centred, axis=-1, keepdims=True) + 1e-05)
    return (centred * inv_std, inv_std)


def norm_back(grad_in, normed, inv_std):
    return inv_std * (
        grad_in
        - jnp.mean(grad_in, axis=-1, keepdims=True)
        - normed * jnp.mean(grad_in * normed, axis=-1, keepdims=True)
    )


def project(rows_in, weight):
    return jnp.einsum("std,de->ste", rows_in, weight, preferred_element_type=jnp.float32).astype(
        jnp.bfloat16
    )


def back_project(grads, weight):
    return jnp.einsum(
        "ste,de->std", grads, weight.astype(jnp.float32), precision=lax.Precision.HIGHEST
    )


def pair_back(grad_bias, pair_normed, pair_inv, bias_weight):
    grad_normed = jnp.einsum("hij,ch->ijc", grad_bias, bias_weight, precision=lax.Precision.HIGHEST)
    return norm_back(grad_normed, pair_normed, pair_inv)


def body_any(
    tokens, restype, type_table, key_mask, pair, w_bias, w_query, w_key, w_value, w_gate, cotangent
):
    n_row = lax.axis_size("row")
    n_col = lax.axis_size("col")
    n_samp = lax.axis_size("samp")
    samp_dev = tokens.shape[0]
    tok_col = tokens.shape[1]
    spread = n_col // n_row
    row_count = tok_col * spread
    total_tokens = tok_col * n_col
    row_index = lax.axis_index("row")
    col_index = lax.axis_index("col")
    is_owner = col_index // spread == row_index
    own_start = col_index % spread * tok_col
    normed, inv_std = token_norm(tokens, restype, type_table)
    own_act = normed.astype(jnp.bfloat16)
    key_proj = project(own_act, w_key)
    value_proj = project(own_act, w_value)
    stacked = jnp.stack([own_act, cotangent])
    pieces = [broadcast(stacked, "col", row_index * spread + member) for member in range(spread)]
    gathered = jnp.concatenate(pieces, axis=2)
    query_side = gathered[0]
    grad_rows = gathered[1]
    queries = project(query_side, w_query)
    gate_lin = project(query_side, w_gate)
    pair_normed, pair_inv = pair_norm(pair)
    bias_weight = w_bias.astype(jnp.float32)
    bias = jnp.einsum("ijc,ch->hij", pair_normed, bias_weight, precision=lax.Precision.HIGHEST)
    query_heads = queries.reshape(samp_dev, row_count, H, CH)
    key_heads = key_proj.reshape(samp_dev, tok_col, H, CH)
    value_heads = value_proj.reshape(samp_dev, tok_col, H, CH)
    scores = (
        jnp.einsum("sihc,sjhc->shij", query_heads, key_heads, preferred_element_type=jnp.float32)
        / math.sqrt(CH)
        + bias[None]
    )
    scores = jnp.where(key_mask[None, None, None, :] == 1, scores, -1000000000.0)
    top = lax.pmax(jnp.max(scores, axis=-1), "col")
    expo = jnp.exp(scores - top[..., None])
    partial_out = jnp.einsum(
        "shij,sjhc->sihc",
        expo.astype(jnp.bfloat16),
        value_heads,
        preferred_element_type=jnp.float32,
    )
    totals, summed = lax.psum(
        (jnp.sum(expo, axis=-1), partial_out.reshape(samp_dev, row_count, D)), "col"
    )
    attended = (
        summed.reshape(samp_dev, row_count, H, CH) / jnp.transpose(totals, (0, 2, 1))[..., None]
    )
    flat_out = attended.reshape(samp_dev, row_count, D)
    sig_gate = jax.nn.sigmoid(gate_lin.astype(jnp.float32))
    grad_f = grad_rows.astype(jnp.float32)
    grad_out = (grad_f * sig_gate).astype(jnp.bfloat16)
    grad_gate = (grad_f * flat_out * sig_gate * (1.0 - sig_gate)).astype(jnp.bfloat16)
    gate_piece = lax.dynamic_slice_in_dim(grad_gate, own_start, tok_col, 1)
    gate_term = jnp.where(
        is_owner,
        jnp.einsum("ste,de->std", gate_piece, w_gate, preferred_element_type=jnp.float32),
        0.0,
    )
    grad_heads = grad_out.reshape(samp_dev, row_count, H, CH)
    delta = jnp.transpose(jnp.sum(grad_heads.astype(jnp.float32) * attended, axis=-1), (0, 2, 1))
    probs = expo / totals[..., None]
    grad_pre = jnp.einsum(
        "sihc,sjhc->shij", grad_heads, value_heads, preferred_element_type=jnp.float32
    )
    grad_scores = probs * (grad_pre - delta[..., None])
    rounded = grad_scores.astype(jnp.bfloat16)
    grad_query = (
        jnp.einsum("shij,sjhc->sihc", rounded, key_heads, preferred_element_type=jnp.float32)
        / math.sqrt(CH)
    ).reshape(samp_dev, row_count, D)
    grad_key = (
        jnp.einsum("shij,sihc->sjhc", rounded, query_heads, preferred_element_type=jnp.float32)
        / math.sqrt(CH)
    ).reshape(samp_dev, tok_col, D)
    grad_value = jnp.einsum(
        "shij,sihc->sjhc",
        probs.astype(jnp.bfloat16),
        grad_heads,
        preferred_element_type=jnp.float32,
    ).reshape(samp_dev, tok_col, D)
    bias_local = jnp.sum(grad_scores, axis=0)
    blank = jnp.zeros((samp_dev, total_tokens, D), jnp.float32)
    mine = lax.psum_scatter(
        lax.dynamic_update_slice_in_dim(blank, grad_query, row_index * row_count, 1),
        "col",
        scatter_dimension=1,
        tiled=True,
    )
    query_all, key_all, value_all, gate_all = lax.psum(
        (mine, grad_key, grad_value, gate_term), "row"
    )
    grad_act = (
        back_project(query_all, w_query)
        + back_project(key_all, w_key)
        + back_project(value_all, w_value)
        + gate_all
    )
    token_grad = norm_back(grad_act, normed, inv_std).astype(jnp.bfloat16)
    samples = samp_dev * n_samp
    grad_bias = lax.psum(bias_local, "samp")
    grad_pair = pair_back(grad_bias, pair_normed, pair_inv, bias_weight)
    pair_grad = (grad_pair * (total_tokens / samples)).astype(jnp.bfloat16)
    weight_part = jnp.einsum("ijc,hij->ch", pair_normed, grad_bias, precision=lax.Precision.HIGHEST)
    weight_sum = lax.psum(weight_part, ("row", "col"))
    bias_weight_grad = weight_sum / samples
    return (token_grad, pair_grad, bias_weight_grad)


EPS = 1e-05
SCALE = 1.0 / math.sqrt(CH)
NT = (((1,), (1,)), ((), ()))
TN = (((0,), (0,)), ((), ()))
MASKED = -65504.0


def params(megabytes):
    return pltpu.CompilerParams(vmem_limit_bytes=megabytes * 1024 * 1024)


def matmul(left, right):
    return jnp.dot(left, right, preferred_element_type=jnp.float32)


def matmul_nt(left, right):
    return lax.dot_general(left, right, NT, preferred_element_type=jnp.float32)


def matmul_tn(left, right):
    return lax.dot_general(left, right, TN, preferred_element_type=jnp.float32)


def halves(values):
    high = values.astype(jnp.bfloat16)
    low = (values - high.astype(jnp.float32)).astype(jnp.bfloat16)
    return high, low


def unit_rows(values):
    centred = values - jnp.mean(values, axis=-1, keepdims=True)
    inv_std = lax.rsqrt(jnp.mean(centred * centred, axis=-1, keepdims=True) + EPS)
    return centred * inv_std, inv_std


def embed_rows(tokens_ref, types_ref, table_ref):
    count, length, width = tokens_ref.shape
    index = lax.broadcasted_iota(jnp.int32, (NTYPE, length), 0)
    onehot = jnp.where(types_ref[...] == index, 1.0, 0.0).astype(jnp.bfloat16)
    added = matmul_tn(onehot, table_ref[...])
    embedded = tokens_ref[...].astype(jnp.float32) + added[None]
    return unit_rows(embedded.reshape(count * length, width))


def token_kernel(row_ref, col_ref, tokens_ref, types_ref, table_ref, *refs):
    wq_ref, wk_ref, wv_ref, wg_ref, cot_ref = refs[:5]
    out_refs, side_ref = refs[5:-1], refs[-1]
    normed, _ = embed_rows(tokens_ref, types_ref, table_ref)
    act = normed.astype(jnp.bfloat16)
    for slot, ref in enumerate((wq_ref, wk_ref, wv_ref)):
        side_ref[slot] = matmul(act, ref[...]).astype(jnp.bfloat16).T
    gate = matmul(act, wg_ref[...]).astype(jnp.bfloat16).astype(jnp.float32)
    cot = cot_ref[...].reshape(gate.shape).astype(jnp.float32)
    side_ref[3] = (cot * jax.nn.sigmoid(gate)).astype(jnp.bfloat16).T
    for offset, out_ref in enumerate(out_refs):
        for core in range(2):
            start = pl.multiple_of((col_ref[0] ^ (2 * offset + core)) * CH, 16)
            out_ref[core] = side_ref[:, pl.ds(start, CH), :]


def token_messages(row, col, tokens, types, table, weights, cotangent, n_row, n_col):
    samp_dev, tok_col, _ = tokens.shape
    width = D // n_row
    held = samp_dev * tok_col
    whole3 = lambda i, r, c: (0, 0, 0)
    whole2 = lambda i, r, c: (0, 0)
    weight_spec = pl.BlockSpec((D, width), lambda i, r, c: (0, r[0]))
    shape = (2, 4, CH, held)
    count = n_col // 2
    return pl.pallas_call(
        token_kernel,
        out_shape=[jax.ShapeDtypeStruct(shape, jnp.bfloat16)] * count,
        grid_spec=pltpu.PrefetchScalarGridSpec(
            num_scalar_prefetch=2,
            grid=(1,),
            in_specs=[
                pl.BlockSpec(tokens.shape, whole3),
                pl.BlockSpec(types.shape, whole2),
                pl.BlockSpec(table.shape, whole2),
                weight_spec,
                weight_spec,
                weight_spec,
                weight_spec,
                pl.BlockSpec((samp_dev, tok_col, width), lambda i, r, c: (0, 0, r[0])),
            ],
            out_specs=[pl.BlockSpec(shape, lambda i, r, c: (0, 0, 0, 0))] * count,
            scratch_shapes=[pltpu.VMEM((4, width, held), jnp.bfloat16)],
        ),
        compiler_params=params(56),
        cost_estimate=pl.CostEstimate(
            flops=4_000_000_000, bytes_accessed=4_000_000, transcendentals=0
        ),
        name="token_messages",
    )(row, col, tokens, types, table, *weights, cotangent)


def own_kernel(
    row_ref, tokens_ref, types_ref, table_ref, wg_ref, cot_ref, slope_ref, normed_ref, inv_ref
):
    normed, inv_std = embed_rows(tokens_ref, types_ref, table_ref)
    gate = matmul(normed.astype(jnp.bfloat16), wg_ref[...]).astype(jnp.bfloat16)
    sig = jax.nn.sigmoid(gate.astype(jnp.float32))
    cot = cot_ref[...].reshape(gate.shape).astype(jnp.float32)
    slope_ref[...] = (cot * sig * (1.0 - sig)).T
    normed_ref[...] = normed.T
    inv_ref[...] = jnp.broadcast_to(inv_std, (inv_std.shape[0], 128)).T[:8]


def own_rows(row, tokens, types, table, w_gate, cotangent, half):
    _, tok_col, _ = tokens.shape
    count = half * tok_col
    part_spec = pl.BlockSpec((half, tok_col, D), lambda i, r: (r[0], 0, 0))
    whole2 = lambda i, r: (0, 0)
    return pl.pallas_call(
        own_kernel,
        out_shape=[
            jax.ShapeDtypeStruct((D, count), jnp.float32),
            jax.ShapeDtypeStruct((D, count), jnp.float32),
            jax.ShapeDtypeStruct((8, count), jnp.float32),
        ],
        grid_spec=pltpu.PrefetchScalarGridSpec(
            num_scalar_prefetch=1,
            grid=(1,),
            in_specs=[
                part_spec,
                pl.BlockSpec(types.shape, whole2),
                pl.BlockSpec(table.shape, whole2),
                pl.BlockSpec(w_gate.shape, whole2),
                part_spec,
            ],
            out_specs=[
                pl.BlockSpec((D, count), whole2),
                pl.BlockSpec((D, count), whole2),
                pl.BlockSpec((8, count), whole2),
            ],
        ),
        compiler_params=params(56),
        cost_estimate=pl.CostEstimate(
            flops=3_000_000_000, bytes_accessed=3_000_000, transcendentals=0
        ),
        name="own_rows",
    )(row, tokens, types, table, w_gate, cotangent)


MANY = 4


def pair_columns(pair_ref, k, many):
    _, _, length, width = pair_ref.shape
    blocks = [pair_ref[p, pl.ds(k, many)] for p in range(2)]
    rows = jnp.concatenate(blocks, axis=1).reshape(many * 2 * length, width)
    same = lax.broadcasted_iota(jnp.int32, (width, width), 0) == lax.broadcasted_iota(
        jnp.int32, (width, width), 1
    )
    centring = (jnp.where(same, 1.0, 0.0) - 1.0 / width).astype(jnp.bfloat16)
    centred = matmul_nt(centring, rows)
    return centred, lax.rsqrt(jnp.mean(centred * centred, axis=0, keepdims=True) + EPS)


def bias_kernel(pair_ref, weight_ref, mask_ref, out_ref, flat_ref):
    _, count, length, width = pair_ref.shape
    whole = flat_ref.shape[0] // H
    weight = jnp.concatenate([weight_ref[...]] * 2, axis=1)
    base = pl.program_id(0) * count

    def step(n, carry):
        k = n * MANY
        centred, inv_std = pair_columns(pair_ref, k, MANY)
        bias = matmul(weight, jnp.concatenate(halves(centred), axis=0)) * inv_std
        for m in range(MANY):
            lanes = slice(m * 2 * length, (m + 1) * 2 * length)
            flat_ref[pl.ds(base + k + m, H, stride=whole), :] = bias[:, lanes]
        return carry

    lax.fori_loop(0, count // MANY, step, 0, unroll=8)

    @pl.when(pl.program_id(0) == pl.num_programs(0) - 1)
    def _():
        keep = jnp.broadcast_to(mask_ref[...].astype(jnp.float32), (128, length)).T
        keep = jnp.concatenate([keep] * (2 * whole // 128), axis=1) == 1.0
        for h in range(H):
            turned = flat_ref[h * whole : (h + 1) * whole, :].T
            bias = jnp.concatenate([turned[:length], turned[length:]], axis=1)
            out_ref[h] = jnp.where(keep, bias, MASKED)


STEPS = 4


def split_spec(shape):
    block = (shape[0] // STEPS,) + tuple(shape[1:])
    return pl.BlockSpec(block, lambda i: (i,) + (0,) * (len(shape) - 1))


def whole_spec(shape):
    return pl.BlockSpec(tuple(shape), lambda i: (0,) * len(shape))


def pair_spec(pair):
    row_count, tok_col, width = pair.shape
    block = (2, row_count // 2 // STEPS, tok_col, width)
    return pl.BlockSpec(block, lambda i: (0, i, 0, 0))


def pair_bias(pair, weight_t, mask):
    row_count, tok_col, width = pair.shape
    whole = row_count // 2
    return pl.pallas_call(
        bias_kernel,
        out_shape=jax.ShapeDtypeStruct((H, tok_col, row_count), jnp.float32),
        grid=(STEPS,),
        in_specs=[pair_spec(pair), whole_spec(weight_t.shape), whole_spec(mask.shape)],
        out_specs=whole_spec((H, tok_col, row_count)),
        scratch_shapes=[pltpu.VMEM((H * whole, 2 * tok_col), jnp.float32)],
        compiler_params=params(24),
        cost_estimate=pl.CostEstimate(
            flops=6_000_000_000, bytes_accessed=5_000_000, transcendentals=0
        ),
        name="pair_bias",
    )(pair.reshape(2, whole, tok_col, width), weight_t, mask)


def norm_kernel(pair_ref, normed_ref, inv_ref):
    def step(n, carry):
        centred, inv_std = pair_columns(pair_ref, n * MANY, MANY)
        normed_ref[n] = jnp.concatenate(halves(centred * inv_std), axis=0)
        inv_ref[n] = jnp.broadcast_to(inv_std, inv_ref.shape[1:])
        return carry

    lax.fori_loop(0, normed_ref.shape[0], step, 0, unroll=8)


def pair_units(pair):
    row_count, tok_col, width = pair.shape
    whole = row_count // 2
    chunks, lanes = whole // MANY, MANY * 2 * tok_col
    shapes = [(chunks, 2 * width, lanes), (chunks, 8, lanes)]
    return pl.pallas_call(
        norm_kernel,
        out_shape=[
            jax.ShapeDtypeStruct(shapes[0], jnp.bfloat16),
            jax.ShapeDtypeStruct(shapes[1], jnp.float32),
        ],
        grid=(STEPS,),
        in_specs=[pair_spec(pair)],
        out_specs=[split_spec(shape) for shape in shapes],
        compiler_params=params(56),
        cost_estimate=pl.CostEstimate(
            flops=6_000_000_000, bytes_accessed=12_000_000, transcendentals=0
        ),
        name="pair_units",
    )(pair.reshape(2, whole, tok_col, width))


def shift_of(top):
    return jnp.floor(jnp.clip(14.0 - jnp.log2(top), -100.0, 100.0))


def attention_kernel(col_ref, *refs):
    other_ref, bias_ref, back_ref, grad_bias_ref, sum_ref, tokens_ref = refs[-6:]
    col = col_ref[0]
    for offset, ref in enumerate(refs[:-6]):
        tokens_ref[col ^ (2 * offset)] = ref[0]
        tokens_ref[col ^ (2 * offset + 1)] = other_ref[offset]
    n_col = tokens_ref.shape[0]
    tok_col, row_count = bias_ref.shape[1:]
    half = back_ref.shape[2] // tok_col
    n_row = bias_ref.shape[0] // n_col
    step = pl.program_id(0)

    @pl.when(step == 0)
    def _():
        sum_ref[...] = jnp.zeros_like(sum_ref)

    outs = []
    for sample in range(half):
        lanes = slice(sample * tok_col, (sample + 1) * tok_col)

        def side(slot):
            return jnp.concatenate([tokens_ref[c, slot, :, lanes] for c in range(n_col)], axis=1)

        query_t, key_t, value_t, grad_t = [side(slot) for slot in range(4)]
        key = key_t.T
        value = value_t.T
        attended_parts, grad_query_parts = [], []
        grad_key = jnp.zeros(key_t.shape, jnp.float32)
        grad_value = jnp.zeros(key_t.shape, jnp.float32)
        for block in range(n_row):
            cols = slice(block * row_count, (block + 1) * row_count)
            heads = slice(block * n_col, (block + 1) * n_col)
            bias = bias_ref[heads].reshape(n_col * tok_col, row_count)
            query_b = query_t[:, cols]
            grad_b = grad_t[:, cols]
            scores = matmul(key, query_b) * SCALE + bias
            scores = jnp.where(bias < -60000.0, -1000000000.0, scores)
            expo = jnp.exp(scores - jnp.max(scores, axis=0, keepdims=True))
            share = 1.0 / jnp.sum(expo, axis=0, keepdims=True)
            attended = matmul(value_t, expo.astype(jnp.bfloat16)) * share
            delta = jnp.sum(grad_b.astype(jnp.float32) * attended, axis=0, keepdims=True)
            probs = expo * share
            grad_scores = probs * (matmul(value, grad_b) - delta)
            rounded = grad_scores.astype(jnp.bfloat16)
            attended_parts.append(attended)
            grad_query_parts.append(matmul(key_t, rounded) * SCALE)
            grad_key = grad_key + matmul_nt(query_b, rounded)
            grad_value = grad_value + matmul_nt(grad_b, probs.astype(jnp.bfloat16))
            sum_ref[heads] += grad_scores.reshape(n_col, tok_col, row_count)
        outs.append(
            (
                jnp.concatenate(grad_query_parts, axis=1),
                grad_key * SCALE,
                grad_value,
                jnp.concatenate(attended_parts, axis=1),
            )
        )
    spare = jnp.zeros((8 - 4, half * tok_col), jnp.float32)
    tops = [jnp.max(jnp.abs(out[slot]), axis=0, keepdims=True) for slot in range(4) for out in outs]
    shifts = shift_of(jnp.concatenate(tops, axis=0))
    scales = jnp.exp2(shifts)
    scaled = [
        [out[slot] * scales[slot * half + n : slot * half + n + 1] for n, out in enumerate(outs)]
        for slot in range(4)
    ]
    for c in range(n_col):
        lanes = slice(c * tok_col, (c + 1) * tok_col)
        for slot in range(4):
            back_ref[c, slot * CH : (slot + 1) * CH, :] = jnp.concatenate(
                [part[:, lanes] for part in scaled[slot]], axis=1
            )
        tails = [
            jnp.concatenate([shifts[slot * half + n :, lanes][:1] for n in range(half)], axis=1)
            for slot in range(4)
        ]
        back_ref[c, 4 * CH :, :] = jnp.concatenate(tails + [spare], axis=0)

    @pl.when(step == pl.num_programs(0) - 1)
    def _():
        whole = row_count // 2
        for head in range(n_row * n_col):
            sums = sum_ref[head]
            sums = jnp.concatenate([sums[:, :whole], sums[:, whole:]], axis=0).T
            shift = shift_of(jnp.max(jnp.abs(sums), axis=0, keepdims=True))
            grad_bias_ref[head, :whole, :] = sums * jnp.exp2(shift)
            grad_bias_ref[head, whole:, :] = jnp.broadcast_to(shift, (8, 2 * tok_col))


def attention(col, arrived, other, bias, n_row):
    count = len(arrived)
    n_col = 2 * count
    _, tok_col, row_count = bias.shape
    half = arrived[0].shape[-1] // tok_col // n_row
    width = half * tok_col
    back_shape = (n_row * n_col, 4 * CH + 8, width)
    bias_shape = (n_row * n_col, row_count // 2 + 8, 2 * tok_col)
    return pl.pallas_call(
        attention_kernel,
        out_shape=[
            jax.ShapeDtypeStruct(back_shape, jnp.float32),
            jax.ShapeDtypeStruct(bias_shape, jnp.float32),
        ],
        grid_spec=pltpu.PrefetchScalarGridSpec(
            num_scalar_prefetch=1,
            grid=(n_row,),
            in_specs=[pl.BlockSpec((1, 4, CH, width), lambda i, r: (0, 0, 0, i))] * count
            + [
                pl.BlockSpec((count, 4, CH, width), lambda i, r: (0, 0, 0, i)),
                pl.BlockSpec(bias.shape, lambda i, r: (0, 0, 0)),
            ],
            out_specs=[
                pl.BlockSpec((n_col, 4 * CH + 8, width), lambda i, r: (i, 0, 0)),
                pl.BlockSpec(bias_shape, lambda i, r: (0, 0, 0)),
            ],
            scratch_shapes=[
                pltpu.VMEM(bias.shape, jnp.float32),
                pltpu.VMEM((n_col, 4, CH, width), jnp.bfloat16),
            ],
        ),
        compiler_params=params(24),
        cost_estimate=pl.CostEstimate(
            flops=8_000_000_000, bytes_accessed=6_000_000, transcendentals=1_000_000
        ),
        name="attention",
    )(col, *arrived, other, bias)


def back_kernel(*refs):
    slope_ref, normed_ref, inv_ref, wq_ref, wk_ref, wv_ref, wg_ref = refs[-11:-4]
    out_ref, parts_ref, gate_ref, total_ref = refs[-4:]
    back_ref = refs[0]
    count = normed_ref.shape[-1]
    step = pl.program_id(0)
    rows = wq_ref.shape[0]

    @pl.when(step == 0)
    def _():
        for slot in range(4):
            scale = jnp.exp2(-back_ref[:, 4 * CH + slot : 4 * CH + slot + 1, :])
            values = back_ref[:, slot * CH : (slot + 1) * CH, :] * scale
            values = values.reshape(gate_ref.shape)
            if slot < 3:
                parts_ref[slot] = jnp.concatenate(halves(values), axis=1)
            else:
                gate_ref[...] = (values * slope_ref[...]).astype(jnp.bfloat16)

    total = matmul(wg_ref[...], gate_ref[...])
    for slot, ref in enumerate((wq_ref, wk_ref, wv_ref)):
        parts = matmul(ref[...], parts_ref[slot])
        total = total + (parts[:, :count] + parts[:, count:])
    total_ref[pl.ds(pl.multiple_of(step * rows, 8), rows), :] = total

    @pl.when(step == pl.num_programs(0) - 1)
    def _():
        whole = total_ref[...]
        normed = normed_ref[...]
        result = inv_ref[:1] * (
            whole
            - jnp.mean(whole, axis=0, keepdims=True)
            - normed * jnp.mean(whole * normed, axis=0, keepdims=True)
        )
        out_ref[...] = result.T.astype(jnp.bfloat16)


def token_back(back, slope, normed, inv_std, weights):
    count = normed.shape[-1]
    steps = 2
    whole = lambda shape: pl.BlockSpec(shape, lambda i: (0,) * len(shape))
    weight_spec = pl.BlockSpec((D // steps, D), lambda i: (i, 0))
    return pl.pallas_call(
        back_kernel,
        out_shape=jax.ShapeDtypeStruct((count, D), jnp.bfloat16),
        grid=(steps,),
        in_specs=[whole(array.shape) for array in (back, slope, normed, inv_std)]
        + [weight_spec] * 4,
        out_specs=whole((count, D)),
        scratch_shapes=[
            pltpu.VMEM((3, D, 2 * count), jnp.bfloat16),
            pltpu.VMEM((D, count), jnp.bfloat16),
            pltpu.VMEM((D, count), jnp.float32),
        ],
        compiler_params=params(40),
        cost_estimate=pl.CostEstimate(
            flops=4_000_000_000, bytes_accessed=8_000_000, transcendentals=0
        ),
        name="token_back",
    )(back, slope, normed, inv_std, *weights)


def flat_columns(flat_ref, k, many):
    whole = flat_ref.shape[0] // H
    grads = [flat_ref[pl.ds(k + m, H, stride=whole), :] for m in range(many)]
    return jnp.concatenate(halves(jnp.concatenate(grads, axis=1)), axis=0)


def pair_weight_kernel(normed_ref, grads_ref, part_ref):
    chunks, width, _ = normed_ref.shape
    base = pl.program_id(0) * chunks

    @pl.when(pl.program_id(0) == 0)
    def _():
        part_ref[...] = jnp.zeros_like(part_ref)

    def step(n, carry):
        return carry + matmul_nt(normed_ref[n], flat_columns(grads_ref, (base + n) * MANY, MANY))

    parts = lax.fori_loop(0, chunks, step, jnp.zeros((width, 2 * H), jnp.float32), unroll=8)
    parts = parts[:, :H] + parts[:, H:]
    part_ref[...] += (parts[: width // 2] + parts[width // 2 :]).T


def pair_back_kernel(factor, normed_ref, inv_ref, grads_ref, weight_ref, out_ref):
    _, count, length, width = out_ref.shape
    weight = weight_ref[...].astype(jnp.float32)
    weight = halves(weight - jnp.mean(weight, axis=1, keepdims=True))
    weight = jnp.concatenate([weight[0], weight[0], weight[1], weight[1]], axis=0).T
    base = pl.program_id(0) * count

    def step(n, carry):
        k = n * MANY
        normed = normed_ref[n].astype(jnp.float32)
        normed = normed[:width] + normed[width:]
        grads = flat_columns(grads_ref, base + k, MANY)
        grad_in = matmul(weight, jnp.concatenate([grads, grads], axis=0))
        overlap = jnp.mean(grad_in * normed, axis=0, keepdims=True)
        result = (grad_in - normed * overlap) * (inv_ref[n, :1] * factor)
        result = result.astype(jnp.bfloat16).T.reshape(MANY, 2 * length, width)
        for p in range(2):
            out_ref[p, pl.ds(k, MANY)] = result[:, p * length : (p + 1) * length]
        return carry

    lax.fori_loop(0, count // MANY, step, 0, unroll=8)


def pair_weight(normed, grads):
    part_shape = (H, normed.shape[1] // 2)
    return pl.pallas_call(
        pair_weight_kernel,
        out_shape=jax.ShapeDtypeStruct(part_shape, jnp.float32),
        grid=(STEPS,),
        in_specs=[split_spec(normed.shape), whole_spec(grads.shape)],
        out_specs=whole_spec(part_shape),
        compiler_params=params(24),
        cost_estimate=pl.CostEstimate(
            flops=1_000_000, bytes_accessed=100_000, transcendentals=0
        ),
        name="pair_weight",
    )(normed, grads)


def pair_backward(shape, normed, inv_std, grads, weight_t, factor):
    row_count, tok_col, width = shape
    whole = row_count // 2
    pair_grad = pl.pallas_call(
        lambda *refs: pair_back_kernel(factor, *refs),
        out_shape=jax.ShapeDtypeStruct((2, whole, tok_col, width), jnp.bfloat16),
        grid=(STEPS,),
        in_specs=[
            split_spec(normed.shape),
            split_spec(inv_std.shape),
            whole_spec(grads.shape),
            whole_spec(weight_t.shape),
        ],
        out_specs=pl.BlockSpec((2, whole // STEPS, tok_col, width), lambda i: (0, i, 0, 0)),
        compiler_params=params(24),
        cost_estimate=pl.CostEstimate(
            flops=1_000_000, bytes_accessed=100_000, transcendentals=0
        ),
        name="pair_backward",
    )(normed, inv_std, grads, weight_t)
    return pair_grad.reshape(shape)


def unscaled(block, rows):
    block = block.astype(jnp.float32)
    block = block[:, :rows] * jnp.exp2(-block[:, rows : rows + 1])
    return block.reshape(-1, block.shape[2])


def swap(block, axis):
    return lax.ppermute(block, axis, [(0, 1), (1, 0)])


def body_heads(
    tokens, restype, type_table, key_mask, pair, w_bias, w_query, w_key, w_value, w_gate, cotangent
):
    n_row = lax.axis_size("row")
    n_col = lax.axis_size("col")
    n_samp = lax.axis_size("samp")
    samp_dev = tokens.shape[0]
    tok_col = tokens.shape[1]
    row_count = pair.shape[0]
    total_tokens = tok_col * n_col
    half = samp_dev // n_row
    row_index = lax.axis_index("row")
    row = row_index.astype(jnp.int32).reshape(1)
    col = lax.axis_index("col").astype(jnp.int32).reshape(1)
    types = restype.reshape(1, tok_col)
    weight_t = w_bias.T
    weights = (w_query, w_key, w_value, w_gate)
    samples = samp_dev * n_samp

    def send(block, offset):
        return lax.ppermute(block, "col", [(c, c ^ offset) for c in range(n_col)])

    def by_chip(blocks):
        return [blocks[0]] + [send(blocks[n], 2 * n) for n in range(1, n_col // 2)]

    def across(blocks):
        return send(jnp.stack([block[1] for block in blocks]), 1)

    messages = token_messages(
        row, col, tokens, types, type_table, weights, cotangent, n_row, n_col
    )
    arrived = by_chip(messages)
    bias = pair_bias(pair, weight_t, key_mask.reshape(1, tok_col))
    bias, arrived, types = lax.optimization_barrier(
        (bias.astype(jnp.float16), arrived, types)
    )
    own = own_rows(row, tokens, types, type_table, w_gate, cotangent, half)
    bias = lax.all_to_all(bias, ("row", "col"), 0, 0, tiled=True)
    other = across(arrived)
    bias, other, own = lax.optimization_barrier((bias, other, own))

    back, grad_bias = attention(col, arrived, other, bias.astype(jnp.float32), n_row)
    grad_bias = lax.all_to_all(
        grad_bias.astype(jnp.float16), ("row", "col"), 0, 0, tiled=True
    )
    back, late_pair = lax.optimization_barrier((back.astype(jnp.float16), pair))
    pair_normed, pair_inv = pair_units(late_pair)
    back, grad_bias, pair_normed = lax.optimization_barrier((back, grad_bias, pair_normed))
    back = lax.all_to_all(back, ("row", "col"), 0, 0, tiled=True)

    other_bias = swap(grad_bias, "samp")
    own_bias = unscaled(grad_bias, row_count // 2)
    part = pair_weight(pair_normed, own_bias)
    samp_part = swap(part, "samp")
    row_part = swap(part, "row")
    both_part = lax.ppermute(part, ("samp", "row"), [(n, 3 - n) for n in range(4)])
    other_bias, part = lax.optimization_barrier((other_bias, part))
    grads = own_bias + unscaled(other_bias, row_count // 2)
    pair_grad = pair_backward(
        pair.shape, pair_normed, pair_inv, grads, weight_t, total_tokens / samples
    )

    pair_grad, sums = lax.optimization_barrier(
        (pair_grad, (part, samp_part, row_part, both_part))
    )
    part = (sums[0] + sums[1]) + (sums[2] + sums[3])
    sums = (part, send(part, 1), send(part, 2), send(part, 3))
    back, sums = lax.optimization_barrier((back, sums))
    part = ((sums[0] + sums[1]) + (sums[2] + sums[3])) / samples
    token_half = token_back(back.astype(jnp.float32), *own, weights)
    token_half, part = lax.optimization_barrier((token_half, part))
    last = send(part, 4)
    token_half = token_half.reshape(half, tok_col, D)
    other_half = swap(token_half, "row")
    first = row_index == 0
    token_grad = jnp.concatenate(
        [jnp.where(first, token_half, other_half), jnp.where(first, other_half, token_half)],
        axis=0,
    )
    token_grad, last = lax.optimization_barrier((token_grad, last))
    return (token_grad, pair_grad, (part + last).T)


def body(*args):
    n_row = lax.axis_size("row")
    n_col = lax.axis_size("col")
    tokens = args[0]
    pair = args[4]
    fits = n_row == 2 and n_col == 8 and n_row * n_col == H and lax.axis_size("samp") == 2
    square = pair.shape[0] * n_row == pair.shape[1] * n_col
    if fits and square and tokens.shape[0] == 4 and tokens.shape[1] == 64:
        return body_heads(*args)
    return body_any(*args)


def solution(mesh):
    placed = (
        P("samp", "col", None),
        P("col"),
        P(),
        P("col"),
        P("row", "col", None),
        P(),
        P(),
        P(),
        P(),
        P(),
        P("samp", "col", None),
    )
    return jax.shard_map(
        body,
        mesh=mesh,
        in_specs=placed,
        out_specs=(P("samp", "col", None), P("row", "col", None), P()),
        check_vma=False,
    )
```

```python
import math

import jax
import jax.numpy as jnp
from jax import lax
from jax.experimental import pallas as pl
from jax.experimental.pallas import tpu as pltpu
from jax.sharding import PartitionSpec as P

D = 768
H = 16
CH = 48
NTYPE = 32


def broadcast(block, axis, source):
    block = jnp.where(lax.axis_index(axis) == source, block, jnp.zeros_like(block))
    return lax.psum(block, axis)


def token_norm(tokens, restype, type_table):
    onehot = (restype[:, None] == jnp.arange(NTYPE, dtype=jnp.int32)[None, :]).astype(jnp.bfloat16)
    embedded = tokens.astype(jnp.float32) + jnp.dot(
        onehot, type_table, preferred_element_type=jnp.float32
    )
    centred = embedded - jnp.mean(embedded, axis=-1, keepdims=True)
    inv_std = lax.rsqrt(jnp.mean(centred * centred, axis=-1, keepdims=True) + 1e-05)
    return (centred * inv_std, inv_std)


def pair_norm(block):
    values = block.astype(jnp.float32)
    centred = values - jnp.mean(values, axis=-1, keepdims=True)
    inv_std = lax.rsqrt(jnp.mean(centred * centred, axis=-1, keepdims=True) + 1e-05)
    return (centred * inv_std, inv_std)


def norm_back(grad_in, normed, inv_std):
    return inv_std * (
        grad_in
        - jnp.mean(grad_in, axis=-1, keepdims=True)
        - normed * jnp.mean(grad_in * normed, axis=-1, keepdims=True)
    )


def project(rows_in, weight):
    return jnp.einsum("std,de->ste", rows_in, weight, preferred_element_type=jnp.float32).astype(
        jnp.bfloat16
    )


def back_project(grads, weight):
    return jnp.einsum(
        "ste,de->std", grads, weight.astype(jnp.float32), precision=lax.Precision.HIGHEST
    )


def pair_back(grad_bias, pair_normed, pair_inv, bias_weight):
    grad_normed = jnp.einsum("hij,ch->ijc", grad_bias, bias_weight, precision=lax.Precision.HIGHEST)
    return norm_back(grad_normed, pair_normed, pair_inv)


def body_any(
    tokens, restype, type_table, key_mask, pair, w_bias, w_query, w_key, w_value, w_gate, cotangent
):
    n_row = lax.axis_size("row")
    n_col = lax.axis_size("col")
    n_samp = lax.axis_size("samp")
    samp_dev = tokens.shape[0]
    tok_col = tokens.shape[1]
    spread = n_col // n_row
    row_count = tok_col * spread
    total_tokens = tok_col * n_col
    row_index = lax.axis_index("row")
    col_index = lax.axis_index("col")
    is_owner = col_index // spread == row_index
    own_start = col_index % spread * tok_col
    normed, inv_std = token_norm(tokens, restype, type_table)
    own_act = normed.astype(jnp.bfloat16)
    key_proj = project(own_act, w_key)
    value_proj = project(own_act, w_value)
    stacked = jnp.stack([own_act, cotangent])
    pieces = [broadcast(stacked, "col", row_index * spread + member) for member in range(spread)]
    gathered = jnp.concatenate(pieces, axis=2)
    query_side = gathered[0]
    grad_rows = gathered[1]
    queries = project(query_side, w_query)
    gate_lin = project(query_side, w_gate)
    pair_normed, pair_inv = pair_norm(pair)
    bias_weight = w_bias.astype(jnp.float32)
    bias = jnp.einsum("ijc,ch->hij", pair_normed, bias_weight, precision=lax.Precision.HIGHEST)
    query_heads = queries.reshape(samp_dev, row_count, H, CH)
    key_heads = key_proj.reshape(samp_dev, tok_col, H, CH)
    value_heads = value_proj.reshape(samp_dev, tok_col, H, CH)
    scores = (
        jnp.einsum("sihc,sjhc->shij", query_heads, key_heads, preferred_element_type=jnp.float32)
        / math.sqrt(CH)
        + bias[None]
    )
    scores = jnp.where(key_mask[None, None, None, :] == 1, scores, -1000000000.0)
    top = lax.pmax(jnp.max(scores, axis=-1), "col")
    expo = jnp.exp(scores - top[..., None])
    partial_out = jnp.einsum(
        "shij,sjhc->sihc",
        expo.astype(jnp.bfloat16),
        value_heads,
        preferred_element_type=jnp.float32,
    )
    totals, summed = lax.psum(
        (jnp.sum(expo, axis=-1), partial_out.reshape(samp_dev, row_count, D)), "col"
    )
    attended = (
        summed.reshape(samp_dev, row_count, H, CH) / jnp.transpose(totals, (0, 2, 1))[..., None]
    )
    flat_out = attended.reshape(samp_dev, row_count, D)
    sig_gate = jax.nn.sigmoid(gate_lin.astype(jnp.float32))
    grad_f = grad_rows.astype(jnp.float32)
    grad_out = (grad_f * sig_gate).astype(jnp.bfloat16)
    grad_gate = (grad_f * flat_out * sig_gate * (1.0 - sig_gate)).astype(jnp.bfloat16)
    gate_piece = lax.dynamic_slice_in_dim(grad_gate, own_start, tok_col, 1)
    gate_term = jnp.where(
        is_owner,
        jnp.einsum("ste,de->std", gate_piece, w_gate, preferred_element_type=jnp.float32),
        0.0,
    )
    grad_heads = grad_out.reshape(samp_dev, row_count, H, CH)
    delta = jnp.transpose(jnp.sum(grad_heads.astype(jnp.float32) * attended, axis=-1), (0, 2, 1))
    probs = expo / totals[..., None]
    grad_pre = jnp.einsum(
        "sihc,sjhc->shij", grad_heads, value_heads, preferred_element_type=jnp.float32
    )
    grad_scores = probs * (grad_pre - delta[..., None])
    rounded = grad_scores.astype(jnp.bfloat16)
    grad_query = (
        jnp.einsum("shij,sjhc->sihc", rounded, key_heads, preferred_element_type=jnp.float32)
        / math.sqrt(CH)
    ).reshape(samp_dev, row_count, D)
    grad_key = (
        jnp.einsum("shij,sihc->sjhc", rounded, query_heads, preferred_element_type=jnp.float32)
        / math.sqrt(CH)
    ).reshape(samp_dev, tok_col, D)
    grad_value = jnp.einsum(
        "shij,sihc->sjhc",
        probs.astype(jnp.bfloat16),
        grad_heads,
        preferred_element_type=jnp.float32,
    ).reshape(samp_dev, tok_col, D)
    bias_local = jnp.sum(grad_scores, axis=0)
    blank = jnp.zeros((samp_dev, total_tokens, D), jnp.float32)
    mine = lax.psum_scatter(
        lax.dynamic_update_slice_in_dim(blank, grad_query, row_index * row_count, 1),
        "col",
        scatter_dimension=1,
        tiled=True,
    )
    query_all, key_all, value_all, gate_all = lax.psum(
        (mine, grad_key, grad_value, gate_term), "row"
    )
    grad_act = (
        back_project(query_all, w_query)
        + back_project(key_all, w_key)
        + back_project(value_all, w_value)
        + gate_all
    )
    token_grad = norm_back(grad_act, normed, inv_std).astype(jnp.bfloat16)
    samples = samp_dev * n_samp
    grad_bias = lax.psum(bias_local, "samp")
    grad_pair = pair_back(grad_bias, pair_normed, pair_inv, bias_weight)
    pair_grad = (grad_pair * (total_tokens / samples)).astype(jnp.bfloat16)
    weight_part = jnp.einsum("ijc,hij->ch", pair_normed, grad_bias, precision=lax.Precision.HIGHEST)
    weight_sum = lax.psum(weight_part, ("row", "col"))
    bias_weight_grad = weight_sum / samples
    return (token_grad, pair_grad, bias_weight_grad)


EPS = 1e-05
SCALE = 1.0 / math.sqrt(CH)
NT = (((1,), (1,)), ((), ()))
TN = (((0,), (0,)), ((), ()))
MASKED = -65504.0


def params(megabytes):
    return pltpu.CompilerParams(vmem_limit_bytes=megabytes * 1024 * 1024)


def matmul(left, right):
    return jnp.dot(left, right, preferred_element_type=jnp.float32)


def matmul_nt(left, right):
    return lax.dot_general(left, right, NT, preferred_element_type=jnp.float32)


def matmul_tn(left, right):
    return lax.dot_general(left, right, TN, preferred_element_type=jnp.float32)


def halves(values):
    high = values.astype(jnp.bfloat16)
    low = (values - high.astype(jnp.float32)).astype(jnp.bfloat16)
    return high, low


def unit_rows(values):
    centred = values - jnp.mean(values, axis=-1, keepdims=True)
    inv_std = lax.rsqrt(jnp.mean(centred * centred, axis=-1, keepdims=True) + EPS)
    return centred * inv_std, inv_std


def embed_rows(tokens_ref, types_ref, table_ref):
    count, length, width = tokens_ref.shape
    index = lax.broadcasted_iota(jnp.int32, (NTYPE, length), 0)
    onehot = jnp.where(types_ref[...] == index, 1.0, 0.0).astype(jnp.bfloat16)
    added = matmul_tn(onehot, table_ref[...])
    embedded = tokens_ref[...].astype(jnp.float32) + added[None]
    return unit_rows(embedded.reshape(count * length, width))


def token_kernel(row_ref, col_ref, tokens_ref, types_ref, table_ref, *refs):
    wq_ref, wk_ref, wv_ref, wg_ref, cot_ref = refs[:5]
    out_refs, side_ref = refs[5:-1], refs[-1]
    normed, _ = embed_rows(tokens_ref, types_ref, table_ref)
    act = normed.astype(jnp.bfloat16)
    for slot, ref in enumerate((wq_ref, wk_ref, wv_ref)):
        side_ref[slot] = matmul(act, ref[...]).astype(jnp.bfloat16).T
    gate = matmul(act, wg_ref[...]).astype(jnp.bfloat16).astype(jnp.float32)
    cot = cot_ref[...].reshape(gate.shape).astype(jnp.float32)
    side_ref[3] = (cot * jax.nn.sigmoid(gate)).astype(jnp.bfloat16).T
    for offset, out_ref in enumerate(out_refs):
        for core in range(2):
            start = pl.multiple_of((col_ref[0] ^ (2 * offset + core)) * CH, 16)
            out_ref[core] = side_ref[:, pl.ds(start, CH), :]


def token_messages(row, col, tokens, types, table, weights, cotangent, n_row, n_col):
    samp_dev, tok_col, _ = tokens.shape
    width = D // n_row
    held = samp_dev * tok_col
    whole3 = lambda i, r, c: (0, 0, 0)
    whole2 = lambda i, r, c: (0, 0)
    weight_spec = pl.BlockSpec((D, width), lambda i, r, c: (0, r[0]))
    shape = (2, 4, CH, held)
    count = n_col // 2
    return pl.pallas_call(
        token_kernel,
        out_shape=[jax.ShapeDtypeStruct(shape, jnp.bfloat16)] * count,
        grid_spec=pltpu.PrefetchScalarGridSpec(
            num_scalar_prefetch=2,
            grid=(1,),
            in_specs=[
                pl.BlockSpec(tokens.shape, whole3),
                pl.BlockSpec(types.shape, whole2),
                pl.BlockSpec(table.shape, whole2),
                weight_spec,
                weight_spec,
                weight_spec,
                weight_spec,
                pl.BlockSpec((samp_dev, tok_col, width), lambda i, r, c: (0, 0, r[0])),
            ],
            out_specs=[pl.BlockSpec(shape, lambda i, r, c: (0, 0, 0, 0))] * count,
            scratch_shapes=[pltpu.VMEM((4, width, held), jnp.bfloat16)],
        ),
        compiler_params=params(56),
        cost_estimate=pl.CostEstimate(
            flops=4_000_000_000, bytes_accessed=4_000_000, transcendentals=0
        ),
        name="token_messages",
    )(row, col, tokens, types, table, *weights, cotangent)


def own_kernel(
    row_ref, tokens_ref, types_ref, table_ref, wg_ref, cot_ref, slope_ref, normed_ref, inv_ref
):
    normed, inv_std = embed_rows(tokens_ref, types_ref, table_ref)
    gate = matmul(normed.astype(jnp.bfloat16), wg_ref[...]).astype(jnp.bfloat16)
    sig = jax.nn.sigmoid(gate.astype(jnp.float32))
    cot = cot_ref[...].reshape(gate.shape).astype(jnp.float32)
    slope_ref[...] = (cot * sig * (1.0 - sig)).T
    normed_ref[...] = normed.T
    inv_ref[...] = jnp.broadcast_to(inv_std, (inv_std.shape[0], 128)).T[:8]


def own_rows(row, tokens, types, table, w_gate, cotangent, half):
    _, tok_col, _ = tokens.shape
    count = half * tok_col
    part_spec = pl.BlockSpec((half, tok_col, D), lambda i, r: (r[0], 0, 0))
    whole2 = lambda i, r: (0, 0)
    return pl.pallas_call(
        own_kernel,
        out_shape=[
            jax.ShapeDtypeStruct((D, count), jnp.float32),
            jax.ShapeDtypeStruct((D, count), jnp.float32),
            jax.ShapeDtypeStruct((8, count), jnp.float32),
        ],
        grid_spec=pltpu.PrefetchScalarGridSpec(
            num_scalar_prefetch=1,
            grid=(1,),
            in_specs=[
                part_spec,
                pl.BlockSpec(types.shape, whole2),
                pl.BlockSpec(table.shape, whole2),
                pl.BlockSpec(w_gate.shape, whole2),
                part_spec,
            ],
            out_specs=[
                pl.BlockSpec((D, count), whole2),
                pl.BlockSpec((D, count), whole2),
                pl.BlockSpec((8, count), whole2),
            ],
        ),
        compiler_params=params(56),
        cost_estimate=pl.CostEstimate(
            flops=3_000_000_000, bytes_accessed=3_000_000, transcendentals=0
        ),
        name="own_rows",
    )(row, tokens, types, table, w_gate, cotangent)


MANY = 4


def pair_columns(pair_ref, k, many):
    _, _, length, width = pair_ref.shape
    blocks = [pair_ref[p, pl.ds(k, many)] for p in range(2)]
    rows = jnp.concatenate(blocks, axis=1).reshape(many * 2 * length, width)
    same = lax.broadcasted_iota(jnp.int32, (width, width), 0) == lax.broadcasted_iota(
        jnp.int32, (width, width), 1
    )
    centring = (jnp.where(same, 1.0, 0.0) - 1.0 / width).astype(jnp.bfloat16)
    centred = matmul_nt(centring, rows)
    return centred, lax.rsqrt(jnp.mean(centred * centred, axis=0, keepdims=True) + EPS)


def bias_kernel(pair_ref, weight_ref, mask_ref, out_ref, flat_ref):
    _, count, length, width = pair_ref.shape
    whole = flat_ref.shape[0] // H
    weight = jnp.concatenate([weight_ref[...]] * 2, axis=1)
    base = pl.program_id(0) * count

    def step(n, carry):
        k = n * MANY
        centred, inv_std = pair_columns(pair_ref, k, MANY)
        bias = matmul(weight, jnp.concatenate(halves(centred), axis=0)) * inv_std
        for m in range(MANY):
            lanes = slice(m * 2 * length, (m + 1) * 2 * length)
            flat_ref[pl.ds(base + k + m, H, stride=whole), :] = bias[:, lanes]
        return carry

    lax.fori_loop(0, count // MANY, step, 0, unroll=8)

    @pl.when(pl.program_id(0) == pl.num_programs(0) - 1)
    def _():
        keep = jnp.broadcast_to(mask_ref[...].astype(jnp.float32), (128, length)).T
        keep = jnp.concatenate([keep] * (2 * whole // 128), axis=1) == 1.0
        for h in range(H):
            turned = flat_ref[h * whole : (h + 1) * whole, :].T
            bias = jnp.concatenate([turned[:length], turned[length:]], axis=1)
            out_ref[h] = jnp.where(keep, bias, MASKED)


STEPS = 4


def split_spec(shape):
    block = (shape[0] // STEPS,) + tuple(shape[1:])
    return pl.BlockSpec(block, lambda i: (i,) + (0,) * (len(shape) - 1))


def whole_spec(shape):
    return pl.BlockSpec(tuple(shape), lambda i: (0,) * len(shape))


def pair_spec(pair):
    row_count, tok_col, width = pair.shape
    block = (2, row_count // 2 // STEPS, tok_col, width)
    return pl.BlockSpec(block, lambda i: (0, i, 0, 0))


def pair_bias(pair, weight_t, mask):
    row_count, tok_col, width = pair.shape
    whole = row_count // 2
    return pl.pallas_call(
        bias_kernel,
        out_shape=jax.ShapeDtypeStruct((H, tok_col, row_count), jnp.float32),
        grid=(STEPS,),
        in_specs=[pair_spec(pair), whole_spec(weight_t.shape), whole_spec(mask.shape)],
        out_specs=whole_spec((H, tok_col, row_count)),
        scratch_shapes=[pltpu.VMEM((H * whole, 2 * tok_col), jnp.float32)],
        compiler_params=params(24),
        cost_estimate=pl.CostEstimate(
            flops=6_000_000_000, bytes_accessed=5_000_000, transcendentals=0
        ),
        name="pair_bias",
    )(pair.reshape(2, whole, tok_col, width), weight_t, mask)


def norm_kernel(pair_ref, normed_ref, inv_ref):
    def step(n, carry):
        centred, inv_std = pair_columns(pair_ref, n * MANY, MANY)
        normed_ref[n] = jnp.concatenate(halves(centred * inv_std), axis=0)
        inv_ref[n] = jnp.broadcast_to(inv_std, inv_ref.shape[1:])
        return carry

    lax.fori_loop(0, normed_ref.shape[0], step, 0, unroll=8)


def pair_units(pair):
    row_count, tok_col, width = pair.shape
    whole = row_count // 2
    chunks, lanes = whole // MANY, MANY * 2 * tok_col
    shapes = [(chunks, 2 * width, lanes), (chunks, 8, lanes)]
    return pl.pallas_call(
        norm_kernel,
        out_shape=[
            jax.ShapeDtypeStruct(shapes[0], jnp.bfloat16),
            jax.ShapeDtypeStruct(shapes[1], jnp.float32),
        ],
        grid=(STEPS,),
        in_specs=[pair_spec(pair)],
        out_specs=[split_spec(shape) for shape in shapes],
        compiler_params=params(56),
        cost_estimate=pl.CostEstimate(
            flops=6_000_000_000, bytes_accessed=12_000_000, transcendentals=0
        ),
        name="pair_units",
    )(pair.reshape(2, whole, tok_col, width))


def shift_of(top):
    return jnp.floor(jnp.clip(14.0 - jnp.log2(top), -100.0, 100.0))


def attention_kernel(col_ref, *refs):
    other_ref, bias_ref, back_ref, grad_bias_ref, sum_ref, tokens_ref = refs[-6:]
    col = col_ref[0]
    for offset, ref in enumerate(refs[:-6]):
        tokens_ref[col ^ (2 * offset)] = ref[0]
        tokens_ref[col ^ (2 * offset + 1)] = other_ref[offset]
    n_col = tokens_ref.shape[0]
    tok_col, row_count = bias_ref.shape[1:]
    half = back_ref.shape[2] // tok_col
    n_row = bias_ref.shape[0] // n_col
    step = pl.program_id(0)

    @pl.when(step == 0)
    def _():
        sum_ref[...] = jnp.zeros_like(sum_ref)

    outs = []
    for sample in range(half):
        lanes = slice(sample * tok_col, (sample + 1) * tok_col)

        def side(slot):
            return jnp.concatenate([tokens_ref[c, slot, :, lanes] for c in range(n_col)], axis=1)

        query_t, key_t, value_t, grad_t = [side(slot) for slot in range(4)]
        key = key_t.T
        value = value_t.T
        attended_parts, grad_query_parts = [], []
        grad_key = jnp.zeros(key_t.shape, jnp.float32)
        grad_value = jnp.zeros(key_t.shape, jnp.float32)
        for block in range(n_row):
            cols = slice(block * row_count, (block + 1) * row_count)
            heads = slice(block * n_col, (block + 1) * n_col)
            bias = bias_ref[heads].reshape(n_col * tok_col, row_count)
            query_b = query_t[:, cols]
            grad_b = grad_t[:, cols]
            scores = matmul(key, query_b) * SCALE + bias
            scores = jnp.where(bias < -60000.0, -1000000000.0, scores)
            expo = jnp.exp(scores - jnp.max(scores, axis=0, keepdims=True))
            share = 1.0 / jnp.sum(expo, axis=0, keepdims=True)
            attended = matmul(value_t, expo.astype(jnp.bfloat16)) * share
            delta = jnp.sum(grad_b.astype(jnp.float32) * attended, axis=0, keepdims=True)
            probs = expo * share
            grad_scores = probs * (matmul(value, grad_b) - delta)
            rounded = grad_scores.astype(jnp.bfloat16)
            attended_parts.append(attended)
            grad_query_parts.append(matmul(key_t, rounded) * SCALE)
            grad_key = grad_key + matmul_nt(query_b, rounded)
            grad_value = grad_value + matmul_nt(grad_b, probs.astype(jnp.bfloat16))
            sum_ref[heads] += grad_scores.reshape(n_col, tok_col, row_count)
        outs.append(
            (
                jnp.concatenate(grad_query_parts, axis=1),
                grad_key * SCALE,
                grad_value,
                jnp.concatenate(attended_parts, axis=1),
            )
        )
    spare = jnp.zeros((8 - 4, half * tok_col), jnp.float32)
    tops = [jnp.max(jnp.abs(out[slot]), axis=0, keepdims=True) for slot in range(4) for out in outs]
    shifts = shift_of(jnp.concatenate(tops, axis=0))
    scales = jnp.exp2(shifts)
    scaled = [
        [out[slot] * scales[slot * half + n : slot * half + n + 1] for n, out in enumerate(outs)]
        for slot in range(4)
    ]
    for c in range(n_col):
        lanes = slice(c * tok_col, (c + 1) * tok_col)
        for slot in range(4):
            back_ref[c, slot * CH : (slot + 1) * CH, :] = jnp.concatenate(
                [part[:, lanes] for part in scaled[slot]], axis=1
            )
        tails = [
            jnp.concatenate([shifts[slot * half + n :, lanes][:1] for n in range(half)], axis=1)
            for slot in range(4)
        ]
        back_ref[c, 4 * CH :, :] = jnp.concatenate(tails + [spare], axis=0)

    @pl.when(step == pl.num_programs(0) - 1)
    def _():
        whole = row_count // 2
        for head in range(n_row * n_col):
            sums = sum_ref[head]
            sums = jnp.concatenate([sums[:, :whole], sums[:, whole:]], axis=0).T
            shift = shift_of(jnp.max(jnp.abs(sums), axis=0, keepdims=True))
            grad_bias_ref[head, :whole, :] = sums * jnp.exp2(shift)
            grad_bias_ref[head, whole:, :] = jnp.broadcast_to(shift, (8, 2 * tok_col))


def attention(col, arrived, other, bias, n_row):
    count = len(arrived)
    n_col = 2 * count
    _, tok_col, row_count = bias.shape
    half = arrived[0].shape[-1] // tok_col // n_row
    width = half * tok_col
    back_shape = (n_row * n_col, 4 * CH + 8, width)
    bias_shape = (n_row * n_col, row_count // 2 + 8, 2 * tok_col)
    return pl.pallas_call(
        attention_kernel,
        out_shape=[
            jax.ShapeDtypeStruct(back_shape, jnp.float32),
            jax.ShapeDtypeStruct(bias_shape, jnp.float32),
        ],
        grid_spec=pltpu.PrefetchScalarGridSpec(
            num_scalar_prefetch=1,
            grid=(n_row,),
            in_specs=[pl.BlockSpec((1, 4, CH, width), lambda i, r: (0, 0, 0, i))] * count
            + [
                pl.BlockSpec((count, 4, CH, width), lambda i, r: (0, 0, 0, i)),
                pl.BlockSpec(bias.shape, lambda i, r: (0, 0, 0)),
            ],
            out_specs=[
                pl.BlockSpec((n_col, 4 * CH + 8, width), lambda i, r: (i, 0, 0)),
                pl.BlockSpec(bias_shape, lambda i, r: (0, 0, 0)),
            ],
            scratch_shapes=[
                pltpu.VMEM(bias.shape, jnp.float32),
                pltpu.VMEM((n_col, 4, CH, width), jnp.bfloat16),
            ],
        ),
        compiler_params=params(24),
        cost_estimate=pl.CostEstimate(
            flops=8_000_000_000, bytes_accessed=6_000_000, transcendentals=1_000_000
        ),
        name="attention",
    )(col, *arrived, other, bias)


def back_kernel(*refs):
    slope_ref, normed_ref, inv_ref, wq_ref, wk_ref, wv_ref, wg_ref = refs[-11:-4]
    out_ref, parts_ref, gate_ref, total_ref = refs[-4:]
    back_ref = refs[0]
    count = normed_ref.shape[-1]
    step = pl.program_id(0)
    rows = wq_ref.shape[0]

    @pl.when(step == 0)
    def _():
        for slot in range(4):
            scale = jnp.exp2(-back_ref[:, 4 * CH + slot : 4 * CH + slot + 1, :])
            values = back_ref[:, slot * CH : (slot + 1) * CH, :] * scale
            values = values.reshape(gate_ref.shape)
            if slot < 3:
                parts_ref[slot] = jnp.concatenate(halves(values), axis=1)
            else:
                gate_ref[...] = (values * slope_ref[...]).astype(jnp.bfloat16)

    total = matmul(wg_ref[...], gate_ref[...])
    for slot, ref in enumerate((wq_ref, wk_ref, wv_ref)):
        parts = matmul(ref[...], parts_ref[slot])
        total = total + (parts[:, :count] + parts[:, count:])
    total_ref[pl.ds(pl.multiple_of(step * rows, 8), rows), :] = total

    @pl.when(step == pl.num_programs(0) - 1)
    def _():
        whole = total_ref[...]
        normed = normed_ref[...]
        result = inv_ref[:1] * (
            whole
            - jnp.mean(whole, axis=0, keepdims=True)
            - normed * jnp.mean(whole * normed, axis=0, keepdims=True)
        )
        out_ref[...] = result.T.astype(jnp.bfloat16)


def token_back(back, slope, normed, inv_std, weights):
    count = normed.shape[-1]
    steps = 2
    whole = lambda shape: pl.BlockSpec(shape, lambda i: (0,) * len(shape))
    weight_spec = pl.BlockSpec((D // steps, D), lambda i: (i, 0))
    return pl.pallas_call(
        back_kernel,
        out_shape=jax.ShapeDtypeStruct((count, D), jnp.bfloat16),
        grid=(steps,),
        in_specs=[whole(array.shape) for array in (back, slope, normed, inv_std)]
        + [weight_spec] * 4,
        out_specs=whole((count, D)),
        scratch_shapes=[
            pltpu.VMEM((3, D, 2 * count), jnp.bfloat16),
            pltpu.VMEM((D, count), jnp.bfloat16),
            pltpu.VMEM((D, count), jnp.float32),
        ],
        compiler_params=params(40),
        cost_estimate=pl.CostEstimate(
            flops=4_000_000_000, bytes_accessed=8_000_000, transcendentals=0
        ),
        name="token_back",
    )(back, slope, normed, inv_std, *weights)


def flat_columns(flat_ref, k, many):
    whole = flat_ref.shape[0] // H
    grads = [flat_ref[pl.ds(k + m, H, stride=whole), :] for m in range(many)]
    return jnp.concatenate(halves(jnp.concatenate(grads, axis=1)), axis=0)


def pair_weight_kernel(normed_ref, grads_ref, part_ref):
    chunks, width, _ = normed_ref.shape
    base = pl.program_id(0) * chunks

    @pl.when(pl.program_id(0) == 0)
    def _():
        part_ref[...] = jnp.zeros_like(part_ref)

    def step(n, carry):
        return carry + matmul_nt(normed_ref[n], flat_columns(grads_ref, (base + n) * MANY, MANY))

    parts = lax.fori_loop(0, chunks, step, jnp.zeros((width, 2 * H), jnp.float32), unroll=8)
    parts = parts[:, :H] + parts[:, H:]
    part_ref[...] += (parts[: width // 2] + parts[width // 2 :]).T


def pair_back_kernel(factor, normed_ref, inv_ref, grads_ref, weight_ref, out_ref):
    _, count, length, width = out_ref.shape
    weight = weight_ref[...].astype(jnp.float32)
    weight = halves(weight - jnp.mean(weight, axis=1, keepdims=True))
    weight = jnp.concatenate([weight[0], weight[0], weight[1], weight[1]], axis=0).T
    base = pl.program_id(0) * count

    def step(n, carry):
        k = n * MANY
        normed = normed_ref[n].astype(jnp.float32)
        normed = normed[:width] + normed[width:]
        grads = flat_columns(grads_ref, base + k, MANY)
        grad_in = matmul(weight, jnp.concatenate([grads, grads], axis=0))
        overlap = jnp.mean(grad_in * normed, axis=0, keepdims=True)
        result = (grad_in - normed * overlap) * (inv_ref[n, :1] * factor)
        result = result.astype(jnp.bfloat16).T.reshape(MANY, 2 * length, width)
        for p in range(2):
            out_ref[p, pl.ds(k, MANY)] = result[:, p * length : (p + 1) * length]
        return carry

    lax.fori_loop(0, count // MANY, step, 0, unroll=8)


def pair_weight(normed, grads):
    part_shape = (H, normed.shape[1] // 2)
    return pl.pallas_call(
        pair_weight_kernel,
        out_shape=jax.ShapeDtypeStruct(part_shape, jnp.float32),
        grid=(STEPS,),
        in_specs=[split_spec(normed.shape), whole_spec(grads.shape)],
        out_specs=whole_spec(part_shape),
        compiler_params=params(24),
        cost_estimate=pl.CostEstimate(
            flops=1_000_000, bytes_accessed=100_000, transcendentals=0
        ),
        name="pair_weight",
    )(normed, grads)


def pair_backward(shape, normed, inv_std, grads, weight_t, factor):
    row_count, tok_col, width = shape
    whole = row_count // 2
    pair_grad = pl.pallas_call(
        lambda *refs: pair_back_kernel(factor, *refs),
        out_shape=jax.ShapeDtypeStruct((2, whole, tok_col, width), jnp.bfloat16),
        grid=(STEPS,),
        in_specs=[
            split_spec(normed.shape),
            split_spec(inv_std.shape),
            whole_spec(grads.shape),
            whole_spec(weight_t.shape),
        ],
        out_specs=pl.BlockSpec((2, whole // STEPS, tok_col, width), lambda i: (0, i, 0, 0)),
        compiler_params=params(24),
        cost_estimate=pl.CostEstimate(
            flops=3_000_000_000, bytes_accessed=100_000, transcendentals=0
        ),
        name="pair_backward",
    )(normed, inv_std, grads, weight_t)
    return pair_grad.reshape(shape)


def unscaled(block, rows):
    block = block.astype(jnp.float32)
    block = block[:, :rows] * jnp.exp2(-block[:, rows : rows + 1])
    return block.reshape(-1, block.shape[2])


def swap(block, axis):
    return lax.ppermute(block, axis, [(0, 1), (1, 0)])


def body_heads(
    tokens, restype, type_table, key_mask, pair, w_bias, w_query, w_key, w_value, w_gate, cotangent
):
    n_row = lax.axis_size("row")
    n_col = lax.axis_size("col")
    n_samp = lax.axis_size("samp")
    samp_dev = tokens.shape[0]
    tok_col = tokens.shape[1]
    row_count = pair.shape[0]
    total_tokens = tok_col * n_col
    half = samp_dev // n_row
    row_index = lax.axis_index("row")
    row = row_index.astype(jnp.int32).reshape(1)
    col = lax.axis_index("col").astype(jnp.int32).reshape(1)
    types = restype.reshape(1, tok_col)
    weight_t = w_bias.T
    weights = (w_query, w_key, w_value, w_gate)
    samples = samp_dev * n_samp

    def send(block, offset):
        return lax.ppermute(block, "col", [(c, c ^ offset) for c in range(n_col)])

    def by_chip(blocks):
        return [blocks[0]] + [send(blocks[n], 2 * n) for n in range(1, n_col // 2)]

    def across(blocks):
        return send(jnp.stack([block[1] for block in blocks]), 1)

    messages = token_messages(
        row, col, tokens, types, type_table, weights, cotangent, n_row, n_col
    )
    arrived = by_chip(messages)
    bias = pair_bias(pair, weight_t, key_mask.reshape(1, tok_col))
    bias, arrived, types = lax.optimization_barrier(
        (bias.astype(jnp.float16), arrived, types)
    )
    own = own_rows(row, tokens, types, type_table, w_gate, cotangent, half)
    bias = lax.all_to_all(bias, ("row", "col"), 0, 0, tiled=True)
    other = across(arrived)
    bias, other, own = lax.optimization_barrier((bias, other, own))

    back, grad_bias = attention(col, arrived, other, bias.astype(jnp.float32), n_row)
    grad_bias = lax.all_to_all(
        grad_bias.astype(jnp.float16), ("row", "col"), 0, 0, tiled=True
    )
    back, late_pair = lax.optimization_barrier((back.astype(jnp.float16), pair))
    pair_normed, pair_inv = pair_units(late_pair)
    back, grad_bias, pair_normed = lax.optimization_barrier((back, grad_bias, pair_normed))
    back = lax.all_to_all(back, ("row", "col"), 0, 0, tiled=True)

    other_bias = swap(grad_bias, "samp")
    own_bias = unscaled(grad_bias, row_count // 2)
    part = pair_weight(pair_normed, own_bias)
    samp_part = swap(part, "samp")
    row_part = swap(part, "row")
    both_part = lax.ppermute(part, ("samp", "row"), [(n, 3 - n) for n in range(4)])
    other_bias, part = lax.optimization_barrier((other_bias, part))
    grads = own_bias + unscaled(other_bias, row_count // 2)
    pair_grad = pair_backward(
        pair.shape, pair_normed, pair_inv, grads, weight_t, total_tokens / samples
    )

    pair_grad, sums = lax.optimization_barrier(
        (pair_grad, (part, samp_part, row_part, both_part))
    )
    part = (sums[0] + sums[1]) + (sums[2] + sums[3])
    sums = (part, send(part, 1), send(part, 2), send(part, 3))
    back, sums = lax.optimization_barrier((back, sums))
    part = ((sums[0] + sums[1]) + (sums[2] + sums[3])) / samples
    token_half = token_back(back.astype(jnp.float32), *own, weights)
    token_half, part = lax.optimization_barrier((token_half, part))
    last = send(part, 4)
    token_half = token_half.reshape(half, tok_col, D)
    other_half = swap(token_half, "row")
    first = row_index == 0
    token_grad = jnp.concatenate(
        [jnp.where(first, token_half, other_half), jnp.where(first, other_half, token_half)],
        axis=0,
    )
    token_grad, last = lax.optimization_barrier((token_grad, last))
    return (token_grad, pair_grad, (part + last).T)


def body(*args):
    n_row = lax.axis_size("row")
    n_col = lax.axis_size("col")
    tokens = args[0]
    pair = args[4]
    fits = n_row == 2 and n_col == 8 and n_row * n_col == H and lax.axis_size("samp") == 2
    square = pair.shape[0] * n_row == pair.shape[1] * n_col
    if fits and square and tokens.shape[0] == 4 and tokens.shape[1] == 64:
        return body_heads(*args)
    return body_any(*args)


def solution(mesh):
    placed = (
        P("samp", "col", None),
        P("col"),
        P(),
        P("col"),
        P("row", "col", None),
        P(),
        P(),
        P(),
        P(),
        P(),
        P("samp", "col", None),
    )
    return jax.shard_map(
        body,
        mesh=mesh,
        in_specs=placed,
        out_specs=(P("samp", "col", None), P("row", "col", None), P()),
        check_vma=False,
    )
```

```python
import math

import jax
import jax.numpy as jnp
from jax import lax
from jax.experimental import pallas as pl
from jax.experimental.pallas import tpu as pltpu
from jax.sharding import PartitionSpec as P

D = 768
H = 16
CH = 48
NTYPE = 32


def broadcast(block, axis, source):
    block = jnp.where(lax.axis_index(axis) == source, block, jnp.zeros_like(block))
    return lax.psum(block, axis)


def token_norm(tokens, restype, type_table):
    onehot = (restype[:, None] == jnp.arange(NTYPE, dtype=jnp.int32)[None, :]).astype(jnp.bfloat16)
    embedded = tokens.astype(jnp.float32) + jnp.dot(
        onehot, type_table, preferred_element_type=jnp.float32
    )
    centred = embedded - jnp.mean(embedded, axis=-1, keepdims=True)
    inv_std = lax.rsqrt(jnp.mean(centred * centred, axis=-1, keepdims=True) + 1e-05)
    return (centred * inv_std, inv_std)


def pair_norm(block):
    values = block.astype(jnp.float32)
    centred = values - jnp.mean(values, axis=-1, keepdims=True)
    inv_std = lax.rsqrt(jnp.mean(centred * centred, axis=-1, keepdims=True) + 1e-05)
    return (centred * inv_std, inv_std)


def norm_back(grad_in, normed, inv_std):
    return inv_std * (
        grad_in
        - jnp.mean(grad_in, axis=-1, keepdims=True)
        - normed * jnp.mean(grad_in * normed, axis=-1, keepdims=True)
    )


def project(rows_in, weight):
    return jnp.einsum("std,de->ste", rows_in, weight, preferred_element_type=jnp.float32).astype(
        jnp.bfloat16
    )


def back_project(grads, weight):
    return jnp.einsum(
        "ste,de->std", grads, weight.astype(jnp.float32), precision=lax.Precision.HIGHEST
    )


def pair_back(grad_bias, pair_normed, pair_inv, bias_weight):
    grad_normed = jnp.einsum("hij,ch->ijc", grad_bias, bias_weight, precision=lax.Precision.HIGHEST)
    return norm_back(grad_normed, pair_normed, pair_inv)


def body_any(
    tokens, restype, type_table, key_mask, pair, w_bias, w_query, w_key, w_value, w_gate, cotangent
):
    n_row = lax.axis_size("row")
    n_col = lax.axis_size("col")
    n_samp = lax.axis_size("samp")
    samp_dev = tokens.shape[0]
    tok_col = tokens.shape[1]
    spread = n_col // n_row
    row_count = tok_col * spread
    total_tokens = tok_col * n_col
    row_index = lax.axis_index("row")
    col_index = lax.axis_index("col")
    is_owner = col_index // spread == row_index
    own_start = col_index % spread * tok_col
    normed, inv_std = token_norm(tokens, restype, type_table)
    own_act = normed.astype(jnp.bfloat16)
    key_proj = project(own_act, w_key)
    value_proj = project(own_act, w_value)
    stacked = jnp.stack([own_act, cotangent])
    pieces = [broadcast(stacked, "col", row_index * spread + member) for member in range(spread)]
    gathered = jnp.concatenate(pieces, axis=2)
    query_side = gathered[0]
    grad_rows = gathered[1]
    queries = project(query_side, w_query)
    gate_lin = project(query_side, w_gate)
    pair_normed, pair_inv = pair_norm(pair)
    bias_weight = w_bias.astype(jnp.float32)
    bias = jnp.einsum("ijc,ch->hij", pair_normed, bias_weight, precision=lax.Precision.HIGHEST)
    query_heads = queries.reshape(samp_dev, row_count, H, CH)
    key_heads = key_proj.reshape(samp_dev, tok_col, H, CH)
    value_heads = value_proj.reshape(samp_dev, tok_col, H, CH)
    scores = (
        jnp.einsum("sihc,sjhc->shij", query_heads, key_heads, preferred_element_type=jnp.float32)
        / math.sqrt(CH)
        + bias[None]
    )
    scores = jnp.where(key_mask[None, None, None, :] == 1, scores, -1000000000.0)
    top = lax.pmax(jnp.max(scores, axis=-1), "col")
    expo = jnp.exp(scores - top[..., None])
    partial_out = jnp.einsum(
        "shij,sjhc->sihc",
        expo.astype(jnp.bfloat16),
        value_heads,
        preferred_element_type=jnp.float32,
    )
    totals, summed = lax.psum(
        (jnp.sum(expo, axis=-1), partial_out.reshape(samp_dev, row_count, D)), "col"
    )
    attended = (
        summed.reshape(samp_dev, row_count, H, CH) / jnp.transpose(totals, (0, 2, 1))[..., None]
    )
    flat_out = attended.reshape(samp_dev, row_count, D)
    sig_gate = jax.nn.sigmoid(gate_lin.astype(jnp.float32))
    grad_f = grad_rows.astype(jnp.float32)
    grad_out = (grad_f * sig_gate).astype(jnp.bfloat16)
    grad_gate = (grad_f * flat_out * sig_gate * (1.0 - sig_gate)).astype(jnp.bfloat16)
    gate_piece = lax.dynamic_slice_in_dim(grad_gate, own_start, tok_col, 1)
    gate_term = jnp.where(
        is_owner,
        jnp.einsum("ste,de->std", gate_piece, w_gate, preferred_element_type=jnp.float32),
        0.0,
    )
    grad_heads = grad_out.reshape(samp_dev, row_count, H, CH)
    delta = jnp.transpose(jnp.sum(grad_heads.astype(jnp.float32) * attended, axis=-1), (0, 2, 1))
    probs = expo / totals[..., None]
    grad_pre = jnp.einsum(
        "sihc,sjhc->shij", grad_heads, value_heads, preferred_element_type=jnp.float32
    )
    grad_scores = probs * (grad_pre - delta[..., None])
    rounded = grad_scores.astype(jnp.bfloat16)
    grad_query = (
        jnp.einsum("shij,sjhc->sihc", rounded, key_heads, preferred_element_type=jnp.float32)
        / math.sqrt(CH)
    ).reshape(samp_dev, row_count, D)
    grad_key = (
        jnp.einsum("shij,sihc->sjhc", rounded, query_heads, preferred_element_type=jnp.float32)
        / math.sqrt(CH)
    ).reshape(samp_dev, tok_col, D)
    grad_value = jnp.einsum(
        "shij,sihc->sjhc",
        probs.astype(jnp.bfloat16),
        grad_heads,
        preferred_element_type=jnp.float32,
    ).reshape(samp_dev, tok_col, D)
    bias_local = jnp.sum(grad_scores, axis=0)
    blank = jnp.zeros((samp_dev, total_tokens, D), jnp.float32)
    mine = lax.psum_scatter(
        lax.dynamic_update_slice_in_dim(blank, grad_query, row_index * row_count, 1),
        "col",
        scatter_dimension=1,
        tiled=True,
    )
    query_all, key_all, value_all, gate_all = lax.psum(
        (mine, grad_key, grad_value, gate_term), "row"
    )
    grad_act = (
        back_project(query_all, w_query)
        + back_project(key_all, w_key)
        + back_project(value_all, w_value)
        + gate_all
    )
    token_grad = norm_back(grad_act, normed, inv_std).astype(jnp.bfloat16)
    samples = samp_dev * n_samp
    grad_bias = lax.psum(bias_local, "samp")
    grad_pair = pair_back(grad_bias, pair_normed, pair_inv, bias_weight)
    pair_grad = (grad_pair * (total_tokens / samples)).astype(jnp.bfloat16)
    weight_part = jnp.einsum("ijc,hij->ch", pair_normed, grad_bias, precision=lax.Precision.HIGHEST)
    weight_sum = lax.psum(weight_part, ("row", "col"))
    bias_weight_grad = weight_sum / samples
    return (token_grad, pair_grad, bias_weight_grad)


EPS = 1e-05
SCALE = 1.0 / math.sqrt(CH)
NT = (((1,), (1,)), ((), ()))
TN = (((0,), (0,)), ((), ()))
MASKED = -65504.0


def params(megabytes):
    return pltpu.CompilerParams(vmem_limit_bytes=megabytes * 1024 * 1024)


def matmul(left, right):
    return jnp.dot(left, right, preferred_element_type=jnp.float32)


def matmul_nt(left, right):
    return lax.dot_general(left, right, NT, preferred_element_type=jnp.float32)


def matmul_tn(left, right):
    return lax.dot_general(left, right, TN, preferred_element_type=jnp.float32)


def halves(values):
    high = values.astype(jnp.bfloat16)
    low = (values - high.astype(jnp.float32)).astype(jnp.bfloat16)
    return high, low


def unit_rows(values):
    centred = values - jnp.mean(values, axis=-1, keepdims=True)
    inv_std = lax.rsqrt(jnp.mean(centred * centred, axis=-1, keepdims=True) + EPS)
    return centred * inv_std, inv_std


def embed_rows(tokens_ref, types_ref, table_ref):
    count, length, width = tokens_ref.shape
    index = lax.broadcasted_iota(jnp.int32, (NTYPE, length), 0)
    onehot = jnp.where(types_ref[...] == index, 1.0, 0.0).astype(jnp.bfloat16)
    added = matmul_tn(onehot, table_ref[...])
    embedded = tokens_ref[...].astype(jnp.float32) + added[None]
    return unit_rows(embedded.reshape(count * length, width))


def token_kernel(row_ref, col_ref, tokens_ref, types_ref, table_ref, *refs):
    wq_ref, wk_ref, wv_ref, wg_ref, cot_ref = refs[:5]
    out_refs, side_ref = refs[5:-1], refs[-1]
    normed, _ = embed_rows(tokens_ref, types_ref, table_ref)
    act = normed.astype(jnp.bfloat16)
    for slot, ref in enumerate((wq_ref, wk_ref, wv_ref)):
        side_ref[slot] = matmul(act, ref[...]).astype(jnp.bfloat16).T
    gate = matmul(act, wg_ref[...]).astype(jnp.bfloat16).astype(jnp.float32)
    cot = cot_ref[...].reshape(gate.shape).astype(jnp.float32)
    side_ref[3] = (cot * jax.nn.sigmoid(gate)).astype(jnp.bfloat16).T
    for offset, out_ref in enumerate(out_refs):
        for core in range(2):
            start = pl.multiple_of((col_ref[0] ^ (2 * offset + core)) * CH, 16)
            out_ref[core] = side_ref[:, pl.ds(start, CH), :]


def token_messages(row, col, tokens, types, table, weights, cotangent, n_row, n_col):
    samp_dev, tok_col, _ = tokens.shape
    width = D // n_row
    held = samp_dev * tok_col
    whole3 = lambda i, r, c: (0, 0, 0)
    whole2 = lambda i, r, c: (0, 0)
    weight_spec = pl.BlockSpec((D, width), lambda i, r, c: (0, r[0]))
    shape = (2, 4, CH, held)
    count = n_col // 2
    return pl.pallas_call(
        token_kernel,
        out_shape=[jax.ShapeDtypeStruct(shape, jnp.bfloat16)] * count,
        grid_spec=pltpu.PrefetchScalarGridSpec(
            num_scalar_prefetch=2,
            grid=(1,),
            in_specs=[
                pl.BlockSpec(tokens.shape, whole3),
                pl.BlockSpec(types.shape, whole2),
                pl.BlockSpec(table.shape, whole2),
                weight_spec,
                weight_spec,
                weight_spec,
                weight_spec,
                pl.BlockSpec((samp_dev, tok_col, width), lambda i, r, c: (0, 0, r[0])),
            ],
            out_specs=[pl.BlockSpec(shape, lambda i, r, c: (0, 0, 0, 0))] * count,
            scratch_shapes=[pltpu.VMEM((4, width, held), jnp.bfloat16)],
        ),
        compiler_params=params(56),
        cost_estimate=pl.CostEstimate(
            flops=4_000_000_000, bytes_accessed=4_000_000, transcendentals=0
        ),
        name="token_messages",
    )(row, col, tokens, types, table, *weights, cotangent)


def own_kernel(
    row_ref, tokens_ref, types_ref, table_ref, wg_ref, cot_ref, slope_ref, normed_ref, inv_ref
):
    normed, inv_std = embed_rows(tokens_ref, types_ref, table_ref)
    gate = matmul(normed.astype(jnp.bfloat16), wg_ref[...]).astype(jnp.bfloat16)
    sig = jax.nn.sigmoid(gate.astype(jnp.float32))
    cot = cot_ref[...].reshape(gate.shape).astype(jnp.float32)
    slope_ref[...] = (cot * sig * (1.0 - sig)).T
    normed_ref[...] = normed.T
    inv_ref[...] = jnp.broadcast_to(inv_std, (inv_std.shape[0], 128)).T[:8]


def own_rows(row, tokens, types, table, w_gate, cotangent, half):
    _, tok_col, _ = tokens.shape
    count = half * tok_col
    part_spec = pl.BlockSpec((half, tok_col, D), lambda i, r: (r[0], 0, 0))
    whole2 = lambda i, r: (0, 0)
    return pl.pallas_call(
        own_kernel,
        out_shape=[
            jax.ShapeDtypeStruct((D, count), jnp.float32),
            jax.ShapeDtypeStruct((D, count), jnp.float32),
            jax.ShapeDtypeStruct((8, count), jnp.float32),
        ],
        grid_spec=pltpu.PrefetchScalarGridSpec(
            num_scalar_prefetch=1,
            grid=(1,),
            in_specs=[
                part_spec,
                pl.BlockSpec(types.shape, whole2),
                pl.BlockSpec(table.shape, whole2),
                pl.BlockSpec(w_gate.shape, whole2),
                part_spec,
            ],
            out_specs=[
                pl.BlockSpec((D, count), whole2),
                pl.BlockSpec((D, count), whole2),
                pl.BlockSpec((8, count), whole2),
            ],
        ),
        compiler_params=params(56),
        cost_estimate=pl.CostEstimate(
            flops=3_000_000_000, bytes_accessed=3_000_000, transcendentals=0
        ),
        name="own_rows",
    )(row, tokens, types, table, w_gate, cotangent)


MANY = 4


def pair_columns(pair_ref, k, many):
    _, _, length, width = pair_ref.shape
    blocks = [pair_ref[p, pl.ds(k, many)] for p in range(2)]
    rows = jnp.concatenate(blocks, axis=1).reshape(many * 2 * length, width)
    same = lax.broadcasted_iota(jnp.int32, (width, width), 0) == lax.broadcasted_iota(
        jnp.int32, (width, width), 1
    )
    centring = (jnp.where(same, 1.0, 0.0) - 1.0 / width).astype(jnp.bfloat16)
    centred = matmul_nt(centring, rows)
    return centred, lax.rsqrt(jnp.mean(centred * centred, axis=0, keepdims=True) + EPS)


def bias_kernel(pair_ref, weight_ref, mask_ref, out_ref, flat_ref):
    _, count, length, width = pair_ref.shape
    whole = flat_ref.shape[0] // H
    weight = jnp.concatenate([weight_ref[...]] * 2, axis=1)
    base = pl.program_id(0) * count

    def step(n, carry):
        k = n * MANY
        centred, inv_std = pair_columns(pair_ref, k, MANY)
        bias = matmul(weight, jnp.concatenate(halves(centred), axis=0)) * inv_std
        for m in range(MANY):
            lanes = slice(m * 2 * length, (m + 1) * 2 * length)
            flat_ref[pl.ds(base + k + m, H, stride=whole), :] = bias[:, lanes]
        return carry

    lax.fori_loop(0, count // MANY, step, 0, unroll=8)

    @pl.when(pl.program_id(0) == pl.num_programs(0) - 1)
    def _():
        keep = jnp.broadcast_to(mask_ref[...].astype(jnp.float32), (128, length)).T
        keep = jnp.concatenate([keep] * (2 * whole // 128), axis=1) == 1.0
        for h in range(H):
            turned = flat_ref[h * whole : (h + 1) * whole, :].T
            bias = jnp.concatenate([turned[:length], turned[length:]], axis=1)
            out_ref[h] = jnp.where(keep, bias, MASKED)


STEPS = 4


def split_spec(shape):
    block = (shape[0] // STEPS,) + tuple(shape[1:])
    return pl.BlockSpec(block, lambda i: (i,) + (0,) * (len(shape) - 1))


def whole_spec(shape):
    return pl.BlockSpec(tuple(shape), lambda i: (0,) * len(shape))


def pair_spec(pair):
    row_count, tok_col, width = pair.shape
    block = (2, row_count // 2 // STEPS, tok_col, width)
    return pl.BlockSpec(block, lambda i: (0, i, 0, 0))


def pair_bias(pair, weight_t, mask):
    row_count, tok_col, width = pair.shape
    whole = row_count // 2
    return pl.pallas_call(
        bias_kernel,
        out_shape=jax.ShapeDtypeStruct((H, tok_col, row_count), jnp.float32),
        grid=(STEPS,),
        in_specs=[pair_spec(pair), whole_spec(weight_t.shape), whole_spec(mask.shape)],
        out_specs=whole_spec((H, tok_col, row_count)),
        scratch_shapes=[pltpu.VMEM((H * whole, 2 * tok_col), jnp.float32)],
        compiler_params=params(24),
        cost_estimate=pl.CostEstimate(
            flops=6_000_000_000, bytes_accessed=5_000_000, transcendentals=0
        ),
        name="pair_bias",
    )(pair.reshape(2, whole, tok_col, width), weight_t, mask)


def norm_kernel(pair_ref, normed_ref, inv_ref):
    def step(n, carry):
        centred, inv_std = pair_columns(pair_ref, n * MANY, MANY)
        normed_ref[n] = jnp.concatenate(halves(centred * inv_std), axis=0)
        inv_ref[n] = jnp.broadcast_to(inv_std, inv_ref.shape[1:])
        return carry

    lax.fori_loop(0, normed_ref.shape[0], step, 0, unroll=8)


def pair_units(pair):
    row_count, tok_col, width = pair.shape
    whole = row_count // 2
    chunks, lanes = whole // MANY, MANY * 2 * tok_col
    shapes = [(chunks, 2 * width, lanes), (chunks, 8, lanes)]
    return pl.pallas_call(
        norm_kernel,
        out_shape=[
            jax.ShapeDtypeStruct(shapes[0], jnp.bfloat16),
            jax.ShapeDtypeStruct(shapes[1], jnp.float32),
        ],
        grid=(STEPS,),
        in_specs=[pair_spec(pair)],
        out_specs=[split_spec(shape) for shape in shapes],
        compiler_params=params(56),
        cost_estimate=pl.CostEstimate(
            flops=6_000_000_000, bytes_accessed=12_000_000, transcendentals=0
        ),
        name="pair_units",
    )(pair.reshape(2, whole, tok_col, width))


def shift_of(top):
    return jnp.floor(jnp.clip(14.0 - jnp.log2(top), -100.0, 100.0))


def attention_kernel(col_ref, *refs):
    other_ref, bias_ref, back_ref, grad_bias_ref, sum_ref, tokens_ref = refs[-6:]
    col = col_ref[0]
    for offset, ref in enumerate(refs[:-6]):
        tokens_ref[col ^ (2 * offset)] = ref[0]
        tokens_ref[col ^ (2 * offset + 1)] = other_ref[offset]
    n_col = tokens_ref.shape[0]
    tok_col, row_count = bias_ref.shape[1:]
    half = back_ref.shape[2] // tok_col
    n_row = bias_ref.shape[0] // n_col
    step = pl.program_id(0)

    @pl.when(step == 0)
    def _():
        sum_ref[...] = jnp.zeros_like(sum_ref)

    outs = []
    for sample in range(half):
        lanes = slice(sample * tok_col, (sample + 1) * tok_col)

        def side(slot):
            return jnp.concatenate([tokens_ref[c, slot, :, lanes] for c in range(n_col)], axis=1)

        query_t, key_t, value_t, grad_t = [side(slot) for slot in range(4)]
        key = key_t.T
        value = value_t.T
        attended_parts, grad_query_parts = [], []
        grad_key = jnp.zeros(key_t.shape, jnp.float32)
        grad_value = jnp.zeros(key_t.shape, jnp.float32)
        for block in range(n_row):
            cols = slice(block * row_count, (block + 1) * row_count)
            heads = slice(block * n_col, (block + 1) * n_col)
            bias = bias_ref[heads].reshape(n_col * tok_col, row_count)
            query_b = query_t[:, cols]
            grad_b = grad_t[:, cols]
            scores = matmul(key, query_b) * SCALE + bias
            scores = jnp.where(bias < -60000.0, -1000000000.0, scores)
            expo = jnp.exp(scores - jnp.max(scores, axis=0, keepdims=True))
            share = 1.0 / jnp.sum(expo, axis=0, keepdims=True)
            attended = matmul(value_t, expo.astype(jnp.bfloat16)) * share
            delta = jnp.sum(grad_b.astype(jnp.float32) * attended, axis=0, keepdims=True)
            probs = expo * share
            grad_scores = probs * (matmul(value, grad_b) - delta)
            rounded = grad_scores.astype(jnp.bfloat16)
            attended_parts.append(attended)
            grad_query_parts.append(matmul(key_t, rounded) * SCALE)
            grad_key = grad_key + matmul_nt(query_b, rounded)
            grad_value = grad_value + matmul_nt(grad_b, probs.astype(jnp.bfloat16))
            sum_ref[heads] += grad_scores.reshape(n_col, tok_col, row_count)
        outs.append(
            (
                jnp.concatenate(grad_query_parts, axis=1),
                grad_key * SCALE,
                grad_value,
                jnp.concatenate(attended_parts, axis=1),
            )
        )
    spare = jnp.zeros((8 - 4, half * tok_col), jnp.float32)
    tops = [jnp.max(jnp.abs(out[slot]), axis=0, keepdims=True) for slot in range(4) for out in outs]
    shifts = shift_of(jnp.concatenate(tops, axis=0))
    scales = jnp.exp2(shifts)
    scaled = [
        [out[slot] * scales[slot * half + n : slot * half + n + 1] for n, out in enumerate(outs)]
        for slot in range(4)
    ]
    for c in range(n_col):
        lanes = slice(c * tok_col, (c + 1) * tok_col)
        for slot in range(4):
            back_ref[c, slot * CH : (slot + 1) * CH, :] = jnp.concatenate(
                [part[:, lanes] for part in scaled[slot]], axis=1
            )
        tails = [
            jnp.concatenate([shifts[slot * half + n :, lanes][:1] for n in range(half)], axis=1)
            for slot in range(4)
        ]
        back_ref[c, 4 * CH :, :] = jnp.concatenate(tails + [spare], axis=0)

    @pl.when(step == pl.num_programs(0) - 1)
    def _():
        whole = row_count // 2
        for head in range(n_row * n_col):
            sums = sum_ref[head]
            sums = jnp.concatenate([sums[:, :whole], sums[:, whole:]], axis=0).T
            shift = shift_of(jnp.max(jnp.abs(sums), axis=0, keepdims=True))
            grad_bias_ref[head, :whole, :] = sums * jnp.exp2(shift)
            grad_bias_ref[head, whole:, :] = jnp.broadcast_to(shift, (8, 2 * tok_col))


def attention(col, arrived, other, bias, n_row):
    count = len(arrived)
    n_col = 2 * count
    _, tok_col, row_count = bias.shape
    half = arrived[0].shape[-1] // tok_col // n_row
    width = half * tok_col
    back_shape = (n_row * n_col, 4 * CH + 8, width)
    bias_shape = (n_row * n_col, row_count // 2 + 8, 2 * tok_col)
    return pl.pallas_call(
        attention_kernel,
        out_shape=[
            jax.ShapeDtypeStruct(back_shape, jnp.float32),
            jax.ShapeDtypeStruct(bias_shape, jnp.float32),
        ],
        grid_spec=pltpu.PrefetchScalarGridSpec(
            num_scalar_prefetch=1,
            grid=(n_row,),
            in_specs=[pl.BlockSpec((1, 4, CH, width), lambda i, r: (0, 0, 0, i))] * count
            + [
                pl.BlockSpec((count, 4, CH, width), lambda i, r: (0, 0, 0, i)),
                pl.BlockSpec(bias.shape, lambda i, r: (0, 0, 0)),
            ],
            out_specs=[
                pl.BlockSpec((n_col, 4 * CH + 8, width), lambda i, r: (i, 0, 0)),
                pl.BlockSpec(bias_shape, lambda i, r: (0, 0, 0)),
            ],
            scratch_shapes=[
                pltpu.VMEM(bias.shape, jnp.float32),
                pltpu.VMEM((n_col, 4, CH, width), jnp.bfloat16),
            ],
        ),
        compiler_params=params(24),
        cost_estimate=pl.CostEstimate(
            flops=8_000_000_000, bytes_accessed=6_000_000, transcendentals=1_000_000
        ),
        name="attention",
    )(col, *arrived, other, bias)


def back_kernel(*refs):
    slope_ref, normed_ref, inv_ref, wq_ref, wk_ref, wv_ref, wg_ref = refs[-11:-4]
    out_ref, parts_ref, gate_ref, total_ref = refs[-4:]
    back_ref = refs[0]
    count = normed_ref.shape[-1]
    step = pl.program_id(0)
    rows = wq_ref.shape[0]

    @pl.when(step == 0)
    def _():
        for slot in range(4):
            scale = jnp.exp2(-back_ref[:, 4 * CH + slot : 4 * CH + slot + 1, :])
            values = back_ref[:, slot * CH : (slot + 1) * CH, :] * scale
            values = values.reshape(gate_ref.shape)
            if slot < 3:
                parts_ref[slot] = jnp.concatenate(halves(values), axis=1)
            else:
                gate_ref[...] = (values * slope_ref[...]).astype(jnp.bfloat16)

    total = matmul(wg_ref[...], gate_ref[...])
    for slot, ref in enumerate((wq_ref, wk_ref, wv_ref)):
        parts = matmul(ref[...], parts_ref[slot])
        total = total + (parts[:, :count] + parts[:, count:])
    total_ref[pl.ds(pl.multiple_of(step * rows, 8), rows), :] = total

    @pl.when(step == pl.num_programs(0) - 1)
    def _():
        whole = total_ref[...]
        normed = normed_ref[...]
        result = inv_ref[:1] * (
            whole
            - jnp.mean(whole, axis=0, keepdims=True)
            - normed * jnp.mean(whole * normed, axis=0, keepdims=True)
        )
        out_ref[...] = result.T.astype(jnp.bfloat16)


def token_back(back, slope, normed, inv_std, weights):
    count = normed.shape[-1]
    steps = 2
    whole = lambda shape: pl.BlockSpec(shape, lambda i: (0,) * len(shape))
    weight_spec = pl.BlockSpec((D // steps, D), lambda i: (i, 0))
    return pl.pallas_call(
        back_kernel,
        out_shape=jax.ShapeDtypeStruct((count, D), jnp.bfloat16),
        grid=(steps,),
        in_specs=[whole(array.shape) for array in (back, slope, normed, inv_std)]
        + [weight_spec] * 4,
        out_specs=whole((count, D)),
        scratch_shapes=[
            pltpu.VMEM((3, D, 2 * count), jnp.bfloat16),
            pltpu.VMEM((D, count), jnp.bfloat16),
            pltpu.VMEM((D, count), jnp.float32),
        ],
        compiler_params=params(40),
        cost_estimate=pl.CostEstimate(
            flops=4_000_000_000, bytes_accessed=8_000_000, transcendentals=0
        ),
        name="token_back",
    )(back, slope, normed, inv_std, *weights)


def flat_columns(flat_ref, k, many):
    whole = flat_ref.shape[0] // H
    grads = [flat_ref[pl.ds(k + m, H, stride=whole), :] for m in range(many)]
    return jnp.concatenate(halves(jnp.concatenate(grads, axis=1)), axis=0)


def pair_weight_kernel(normed_ref, grads_ref, part_ref):
    chunks, width, _ = normed_ref.shape
    base = pl.program_id(0) * chunks

    @pl.when(pl.program_id(0) == 0)
    def _():
        part_ref[...] = jnp.zeros_like(part_ref)

    def step(n, carry):
        return carry + matmul_nt(normed_ref[n], flat_columns(grads_ref, (base + n) * MANY, MANY))

    parts = lax.fori_loop(0, chunks, step, jnp.zeros((width, 2 * H), jnp.float32), unroll=8)
    parts = parts[:, :H] + parts[:, H:]
    part_ref[...] += (parts[: width // 2] + parts[width // 2 :]).T


def pair_back_kernel(factor, normed_ref, inv_ref, grads_ref, weight_ref, out_ref):
    _, count, length, width = out_ref.shape
    weight = weight_ref[...].astype(jnp.float32)
    weight = halves(weight - jnp.mean(weight, axis=1, keepdims=True))
    weight = jnp.concatenate([weight[0], weight[0], weight[1], weight[1]], axis=0).T
    base = pl.program_id(0) * count

    def step(n, carry):
        k = n * MANY
        normed = normed_ref[n].astype(jnp.float32)
        normed = normed[:width] + normed[width:]
        grads = flat_columns(grads_ref, base + k, MANY)
        grad_in = matmul(weight, jnp.concatenate([grads, grads], axis=0))
        overlap = jnp.mean(grad_in * normed, axis=0, keepdims=True)
        result = (grad_in - normed * overlap) * (inv_ref[n, :1] * factor)
        result = result.astype(jnp.bfloat16).T.reshape(MANY, 2 * length, width)
        for p in range(2):
            out_ref[p, pl.ds(k, MANY)] = result[:, p * length : (p + 1) * length]
        return carry

    lax.fori_loop(0, count // MANY, step, 0, unroll=8)


def pair_weight(normed, grads):
    part_shape = (H, normed.shape[1] // 2)
    return pl.pallas_call(
        pair_weight_kernel,
        out_shape=jax.ShapeDtypeStruct(part_shape, jnp.float32),
        grid=(STEPS,),
        in_specs=[split_spec(normed.shape), whole_spec(grads.shape)],
        out_specs=whole_spec(part_shape),
        compiler_params=params(24),
        cost_estimate=pl.CostEstimate(
            flops=1_000_000, bytes_accessed=100_000, transcendentals=0
        ),
        name="pair_weight",
    )(normed, grads)


def pair_backward(shape, normed, inv_std, grads, weight_t, factor):
    row_count, tok_col, width = shape
    whole = row_count // 2
    pair_grad = pl.pallas_call(
        lambda *refs: pair_back_kernel(factor, *refs),
        out_shape=jax.ShapeDtypeStruct((2, whole, tok_col, width), jnp.bfloat16),
        grid=(STEPS,),
        in_specs=[
            split_spec(normed.shape),
            split_spec(inv_std.shape),
            whole_spec(grads.shape),
            whole_spec(weight_t.shape),
        ],
        out_specs=pl.BlockSpec((2, whole // STEPS, tok_col, width), lambda i: (0, i, 0, 0)),
        compiler_params=params(24),
        cost_estimate=pl.CostEstimate(
            flops=1_000_000, bytes_accessed=100_000, transcendentals=0
        ),
        name="pair_backward",
    )(normed, inv_std, grads, weight_t)
    return pair_grad.reshape(shape)


def unscaled(block, rows):
    block = block.astype(jnp.float32)
    block = block[:, :rows] * jnp.exp2(-block[:, rows : rows + 1])
    return block.reshape(-1, block.shape[2])


def swap(block, axis):
    return lax.ppermute(block, axis, [(0, 1), (1, 0)])


def body_heads(
    tokens, restype, type_table, key_mask, pair, w_bias, w_query, w_key, w_value, w_gate, cotangent
):
    n_row = lax.axis_size("row")
    n_col = lax.axis_size("col")
    n_samp = lax.axis_size("samp")
    samp_dev = tokens.shape[0]
    tok_col = tokens.shape[1]
    row_count = pair.shape[0]
    total_tokens = tok_col * n_col
    half = samp_dev // n_row
    row_index = lax.axis_index("row")
    row = row_index.astype(jnp.int32).reshape(1)
    col = lax.axis_index("col").astype(jnp.int32).reshape(1)
    types = restype.reshape(1, tok_col)
    weight_t = w_bias.T
    weights = (w_query, w_key, w_value, w_gate)
    samples = samp_dev * n_samp

    def send(block, offset):
        return lax.ppermute(block, "col", [(c, c ^ offset) for c in range(n_col)])

    def by_chip(blocks):
        return [blocks[0]] + [send(blocks[n], 2 * n) for n in range(1, n_col // 2)]

    def across(blocks):
        return send(jnp.stack([block[1] for block in blocks]), 1)

    messages = token_messages(
        row, col, tokens, types, type_table, weights, cotangent, n_row, n_col
    )
    arrived = by_chip(messages)
    bias = pair_bias(pair, weight_t, key_mask.reshape(1, tok_col))
    bias, arrived, types = lax.optimization_barrier(
        (bias.astype(jnp.float16), arrived, types)
    )
    own = own_rows(row, tokens, types, type_table, w_gate, cotangent, half)
    bias = lax.all_to_all(bias, ("row", "col"), 0, 0, tiled=True)
    other = across(arrived)
    bias, other, own = lax.optimization_barrier((bias, other, own))

    back, grad_bias = attention(col, arrived, other, bias.astype(jnp.float32), n_row)
    grad_bias = lax.all_to_all(
        grad_bias.astype(jnp.float16), ("row", "col"), 0, 0, tiled=True
    )
    back, late_pair = lax.optimization_barrier((back.astype(jnp.float16), pair))
    pair_normed, pair_inv = pair_units(late_pair)
    back, grad_bias, pair_normed = lax.optimization_barrier((back, grad_bias, pair_normed))
    back = lax.all_to_all(back, ("row", "col"), 0, 0, tiled=True)

    other_bias = swap(grad_bias, "samp")
    own_bias = unscaled(grad_bias, row_count // 2)
    part = pair_weight(pair_normed, own_bias)
    samp_part = swap(part, "samp")
    row_part = swap(part, "row")
    both_part = lax.ppermute(part, ("samp", "row"), [(n, 3 - n) for n in range(4)])
    other_bias, part = lax.optimization_barrier((other_bias, part))
    grads = own_bias + unscaled(other_bias, row_count // 2)
    pair_grad = pair_backward(
        pair.shape, pair_normed, pair_inv, grads, weight_t, total_tokens / samples
    )

    pair_grad, sums = lax.optimization_barrier(
        (pair_grad, (part, samp_part, row_part, both_part))
    )
    back, _ = lax.optimization_barrier((back, pair_grad))
    part = (sums[0] + sums[1]) + (sums[2] + sums[3])
    sums = (send(part, 1), send(part, 2), send(part, 3))
    token_half = token_back(back.astype(jnp.float32), *own, weights)
    token_half, sums = lax.optimization_barrier((token_half, sums))
    part = ((part + sums[0]) + (sums[1] + sums[2])) / samples
    last = send(part, 4)
    token_half = token_half.reshape(half, tok_col, D)
    other_half = swap(token_half, "row")
    first = row_index == 0
    token_grad = jnp.concatenate(
        [jnp.where(first, token_half, other_half), jnp.where(first, other_half, token_half)],
        axis=0,
    )
    token_grad, last = lax.optimization_barrier((token_grad, last))
    return (token_grad, pair_grad, (part + last).T)


def body(*args):
    n_row = lax.axis_size("row")
    n_col = lax.axis_size("col")
    tokens = args[0]
    pair = args[4]
    fits = n_row == 2 and n_col == 8 and n_row * n_col == H and lax.axis_size("samp") == 2
    square = pair.shape[0] * n_row == pair.shape[1] * n_col
    if fits and square and tokens.shape[0] == 4 and tokens.shape[1] == 64:
        return body_heads(*args)
    return body_any(*args)


def solution(mesh):
    placed = (
        P("samp", "col", None),
        P("col"),
        P(),
        P("col"),
        P("row", "col", None),
        P(),
        P(),
        P(),
        P(),
        P(),
        P("samp", "col", None),
    )
    return jax.shard_map(
        body,
        mesh=mesh,
        in_specs=placed,
        out_specs=(P("samp", "col", None), P("row", "col", None), P()),
        check_vma=False,
    )
```
